32 devices in a mesh: seq: 8 (over y, x, core), head: 4 (over z).
Axes of the slice: x: 2, y: 2, z: 4, core: 2. Of those that a mesh axis runs over, the one named last changes fastest.
Arguments:
- tokens: bfloat16 [4096, 1152], P(('seq', 'head')), may hold values from -6 to 6
- segment_ids: int32 [4096], replicated, may hold values from 0 to 5, as said below
- w_query: bfloat16 [1152, 1024], replicated, may hold values from -0.1875 to 0.1875
- w_key: bfloat16 [1152, 256], replicated, may hold values from -0.1875 to 0.1875
- w_value: bfloat16 [1152, 256], replicated, may hold values from -0.1875 to 0.1875
- w_out: bfloat16 [1024, 1152], replicated, may hold values from -0.1875 to 0.1875
- w_gate: bfloat16 [1152, 6912], P(None, 'head'), may hold values from -0.1875 to 0.1875
- w_up: bfloat16 [1152, 6912], P(None, 'head'), may hold values from -0.1875 to 0.1875
- w_down: bfloat16 [6912, 1152], P('head'), may hold values from -0.078125 to 0.078125
- gain_attn_in: float32 [1152], replicated, may hold values from 0.25 to 1.75
- gain_attn_out: float32 [1152], replicated, may hold values from 0.25 to 1.75
- gain_ffn_in: float32 [1152], replicated, may hold values from 0.25 to 1.75
- gain_ffn_out: float32 [1152], replicated, may hold values from 0.25 to 1.75
- gain_query: float32 [256], replicated, may hold values from 0.25 to 1.75
- gain_key: float32 [256], replicated, may hold values from 0.25 to 1.75
- cotangent: bfloat16 [4096, 1152], P(('seq', 'head'))
Outputs:
- output: bfloat16 [4096, 1152], P(('seq', 'head'))
- grad_tokens: bfloat16 [4096, 1152], P(('seq', 'head'))
- grad_w_query: float32 [1152, 1024], P(('seq', 'head'))
- grad_w_key: float32 [1152, 256], P(('seq', 'head'))
- grad_w_value: float32 [1152, 256], P(('seq', 'head'))
- grad_w_out: float32 [1024, 1152], P(('seq', 'head'))
- grad_w_gate: float32 [1152, 6912], P('seq', 'head')
- grad_w_up: float32 [1152, 6912], P('seq', 'head')
- grad_w_down: float32 [6912, 1152], P('head', 'seq')
- grad_gain_attn_in: float32 [1152], P(('seq', 'head'))
- grad_gain_attn_out: float32 [1152], P(('seq', 'head'))
- grad_gain_ffn_in: float32 [1152], P(('seq', 'head'))
- grad_gain_ffn_out: float32 [1152], P(('seq', 'head'))
- grad_gain_query: float32 [256], P(('seq', 'head'))
- grad_gain_key: float32 [256], P(('seq', 'head'))
The draws below stay inside these ranges and needn't reach their ends.
Inputs may be any that keep to these rules, and one draw needn't show every extreme that they name: `segment_ids`: nonzero ids never decrease and each forms one run; id 0 marks padding, one run at the end of the row; id 2 runs from within the first 512 tokens into the last 512.
All inputs are finite; a program needn't handle non-finite values.
Results may differ from the reference program's by a relative error of at most 0.024.
Values may be sent and summed in bfloat16 or wider, within the bound.
A program may use at most 192 MiB of HBM per device.

```python
import math
import jax
import jax.numpy as jnp
from jax import lax

D = 1152
QH = 4
HD = 256
FF = 6912
GROUP = 512
TOKENS = 4096


def draw_segment_ids(key, part):
    key = jax.random.fold_in(key, 11)
    keys = jax.random.split(key, 5)
    start_long = jax.random.randint(keys[0], (), 1, GROUP // 2)
    end_long = TOKENS - GROUP + jax.random.randint(keys[1], (), GROUP // 4, GROUP // 2)
    rest = TOKENS - end_long
    cut_one = jax.random.randint(keys[2], (), 1, rest // 3 + 1)
    cut_two = cut_one + jax.random.randint(keys[3], (), 1, rest // 3 + 1)
    cut_three = rest - jax.random.randint(keys[4], (), 1, rest // 4 + 1)
    index = jnp.arange(TOKENS, dtype=jnp.int32)
    offset = index - end_long
    tail = jnp.where(offset < cut_one, 3, jnp.where(offset < cut_two, 4, jnp.where(offset < cut_three, 5, 0)))
    ids = jnp.where(index < start_long, 1, jnp.where(index < end_long, 2, tail))
    return ids.astype(jnp.int32)


def draw_cotangent(key, part):
    key = jax.random.fold_in(key, 23)
    rising = 0.6 + 1.2 * jnp.arange(TOKENS, dtype=jnp.float32) / TOKENS
    base = jax.random.normal(key, (TOKENS, D), jnp.float32)
    return (base * rising[:, None]).astype(jnp.bfloat16)


def steps_of(stream_key, extent, pieces, least, largest):
    def one(position, blocks):
        heights = jax.random.uniform(jax.random.fold_in(jax.random.fold_in(stream_key, 6), position), (blocks,), jnp.float32, least / len(pieces), largest / len(pieces))
        return jnp.repeat(jnp.exp(heights), extent[position] // blocks).reshape((-1,) + (1,) * (len(extent) - position - 1))

    factor_of = one(*pieces[0])
    for cut in pieces[1:]:
        factor_of = factor_of * one(*cut)
    return factor_of


def centred(key, shape, scale, bound, cuts=(), held_as=jnp.bfloat16):
    array = scale * jax.random.normal(key, shape, jnp.float32)
    if cuts:
        array = array * steps_of(key, shape, cuts, -0.22, 0.18)
    return jnp.clip(array, -bound, bound).astype(held_as)


def setup_inputs(seed: int = 0) -> dict:
    streams_of = jax.random.split(jax.random.key(seed), 17)
    return {
        "tokens": centred(streams_of[0], (TOKENS, D), 1.0, 6.0, ((0, 32),)),
        "segment_ids": draw_segment_ids(jax.random.fold_in(streams_of[16], 71), 0),
        "w_query": centred(streams_of[2], (D, QH * HD), D ** -0.5, 0.1875),
        "w_key": centred(streams_of[3], (D, HD), D ** -0.5, 0.1875),
        "w_value": centred(streams_of[4], (D, HD), D ** -0.5, 0.1875),
        "w_out": centred(streams_of[5], (QH * HD, D), (QH * HD) ** -0.5, 0.1875),
        "w_gate": centred(streams_of[6], (D, FF), D ** -0.5, 0.1875, ((1, 4),)),
        "w_up": centred(streams_of[7], (D, FF), D ** -0.5, 0.1875, ((1, 4),)),
        "w_down": centred(streams_of[8], (FF, D), FF ** -0.5, 0.078125, ((0, 4),)),
        "gain_attn_in": jnp.clip(1.0 + 0.15 * jax.random.normal(streams_of[9], (D,), jnp.float32), 0.25, 1.75),
        "gain_attn_out": jnp.clip(1.0 + 0.15 * jax.random.normal(streams_of[10], (D,), jnp.float32), 0.25, 1.75),
        "gain_ffn_in": jnp.clip(1.0 + 0.15 * jax.random.normal(streams_of[11], (D,), jnp.float32), 0.25, 1.75),
        "gain_ffn_out": jnp.clip(1.0 + 0.15 * jax.random.normal(streams_of[12], (D,), jnp.float32), 0.25, 1.75),
        "gain_query": jnp.clip(1.0 + 0.15 * jax.random.normal(streams_of[13], (HD,), jnp.float32), 0.25, 1.75),
        "gain_key": jnp.clip(1.0 + 0.15 * jax.random.normal(streams_of[14], (HD,), jnp.float32), 0.25, 1.75),
        "cotangent": draw_cotangent(jax.random.fold_in(streams_of[16], 71), 0),
    }


EPS = 1e-06
NEG = -1e+30
HIGH = lax.Precision.HIGHEST

@jax.custom_vjp
def low(v):
    return lax.optimization_barrier(v.astype(jnp.bfloat16)).astype(jnp.float32)

@jax.custom_vjp
def low_back(v):
    return v

def low_keep(v):
    return (low(v), None)

def low_pass(kept, grad):
    return (grad,)

def back_keep(v):
    return (v, None)

def back_low(kept, grad):
    return (low(grad),)
low.defvjp(low_keep, low_pass)
low_back.defvjp(back_keep, back_low)

def matmul(left, right):
    return jnp.dot(left, right, precision=HIGH, preferred_element_type=jnp.float32)

def norm_rows(v, gain):
    return v * lax.rsqrt(lax.optimization_barrier(jnp.mean(v * v, axis=-1, keepdims=True)) + EPS) * gain

def rotate(v, cosines, sines):
    half = v.shape[-1] // 2
    first = v[..., :half]
    second = v[..., half:]
    return jnp.concatenate([first * cosines - second * sines, second * cosines + first * sines], axis=-1)

def rope_tables(positions, width):
    half = width // 2
    freq = jnp.exp(jnp.arange(half, dtype=jnp.float32) * (-2.0 * math.log(1000000.0) / width))
    angle = positions.astype(jnp.float32)[:, None] * freq[None, :]
    return (jnp.cos(angle), jnp.sin(angle))

def row_positions(segment_ids):
    total = segment_ids.shape[0]
    index = jnp.arange(total, dtype=jnp.int32)
    change = jnp.concatenate([jnp.ones((1,), dtype=bool), segment_ids[1:] != segment_ids[:-1]])
    starts = lax.cummax(jnp.where(change, index, 0), axis=0)
    return (index - starts).astype(jnp.int32)

def reference(tokens, segment_ids, w_query, w_key, w_value, w_out, w_gate, w_up, w_down, gain_attn_in, gain_attn_out, gain_ffn_in, gain_ffn_out, gain_query, gain_key, cotangent):
    positions = row_positions(segment_ids)
    cosines, sines = rope_tables(positions, HD)
    key_index = jnp.arange(TOKENS, dtype=jnp.int32)
    scale = 1.0 / math.sqrt(HD)
    qblock = min(512, TOKENS)
    nblocks = TOKENS // qblock
    starts = jnp.tile(jnp.arange(nblocks, dtype=jnp.int32) * qblock, QH)

    def forward(x, wq, wk, wv, wo, wg, wu, wd, g1, g2, g3, g4, gq, gk):
        a = low(norm_rows(x, g1))
        query_lin = low_back(matmul(a, wq)).reshape(TOKENS, QH, HD)
        queries = low(rotate(norm_rows(query_lin, gq), cosines[:, None, :], sines[:, None, :]))
        key_lin = low_back(matmul(a, wk))
        keys = low(rotate(norm_rows(key_lin, gk), cosines, sines))
        values = low(low_back(matmul(a, wv)))

        def block_fn(args):
            rows, start = args
            query_index = start + jnp.arange(qblock, dtype=jnp.int32)
            query_seg = lax.dynamic_slice_in_dim(segment_ids, start, qblock)
            raw = low_back(matmul(rows, keys.T))
            allowed = (query_seg[:, None] == segment_ids[None, :]) & (key_index[None, :] <= query_index[:, None])
            scores = jnp.where(allowed, raw * scale, NEG)
            top = lax.optimization_barrier(jnp.max(scores, axis=1, keepdims=True))
            weights = jnp.exp(scores - top)
            probs = weights / lax.optimization_barrier(jnp.sum(weights, axis=1, keepdims=True))
            return matmul(low(probs), values)
        blocks = jnp.transpose(queries, (1, 0, 2)).reshape(QH * nblocks, qblock, HD)
        attended = lax.map(jax.checkpoint(block_fn), (blocks, starts))
        attended = jnp.transpose(attended.reshape(QH, TOKENS, HD), (1, 0, 2)).reshape(TOKENS, QH * HD)
        attended = low(low_back(attended))
        projected = low_back(matmul(attended, wo))
        hidden = x + norm_rows(projected, g2)
        ffn_in = low(norm_rows(hidden, g3))
        gate = low_back(matmul(ffn_in, wg))
        up = low_back(matmul(ffn_in, wu))
        activated = low(jax.nn.gelu(gate, approximate=True) * up)
        ffn_out = low_back(matmul(activated, wd))
        return hidden + norm_rows(ffn_out, g4)
    floats = tuple((item.astype(jnp.float32) for item in (tokens, w_query, w_key, w_value, w_out, w_gate, w_up, w_down, gain_attn_in, gain_attn_out, gain_ffn_in, gain_ffn_out, gain_query, gain_key)))
    output, pullback = jax.vjp(forward, *floats)
    grads = pullback(cotangent.astype(jnp.float32))
    return (output.astype(jnp.bfloat16), grads[0].astype(jnp.bfloat16), grads[1], grads[2], grads[3], grads[4], grads[5], grads[6], grads[7], grads[8], grads[9], grads[10], grads[11], grads[12], grads[13])
```

```python
import functools
import math

import jax
import jax.numpy as jnp
from jax import lax
from jax.experimental import pallas as pl
from jax.experimental.pallas import tpu as pltpu
from jax.sharding import PartitionSpec as P

EPS = 1e-06
MESH = pl.DeviceIdType.MESH
VMEM = pltpu.VMEM
LIMIT = 56 * 2**20


def norm_rows(v, gain):
    return v * lax.rsqrt(jnp.mean(v * v, axis=-1, keepdims=True) + EPS) * gain


def rotate(v, cosines, sines):
    half = v.shape[-1] // 2
    first = v[..., :half]
    second = v[..., half:]
    return jnp.concatenate(
        [first * cosines - second * sines, second * cosines + first * sines], axis=-1
    )


def rope_tables(positions, width):
    half = width // 2
    freq = jnp.exp(jnp.arange(half, dtype=jnp.float32) * (-2.0 * math.log(1000000.0) / width))
    angle = positions.astype(jnp.float32)[:, None] * freq[None, :]
    return (jnp.cos(angle), jnp.sin(angle))


def contract_first(left, right):
    return lax.dot_general(
        left, right, (((0,), (0,)), ((), ())), preferred_element_type=jnp.float32
    )


def contract_last(left, right):
    return lax.dot_general(
        left, right, (((1,), (1,)), ((), ())), preferred_element_type=jnp.float32
    )


def place():
    return lax.axis_index("seq"), lax.axis_index("head")


def related(s, mask):
    out = s
    bit = 0
    while mask >> bit:
        if (mask >> bit) & 1:
            step = 1 << bit
            out = out + (1 - 2 * ((s // step) % 2)) * step
        bit += 1
    return out


def subsets(bits):
    out = [0]
    for bit in bits:
        out = out + [m | (1 << bit) for m in out]
    return out


def greet(targets):
    barrier = pltpu.get_barrier_semaphore()
    for target in targets:
        pl.semaphore_signal(barrier, inc=1, device_id=target, device_id_type=MESH)
    pl.semaphore_wait(barrier, len(targets))


def remote(src, dst, send, recv, target):
    return pltpu.make_async_remote_copy(
        src_ref=src,
        dst_ref=dst,
        send_sem=send,
        recv_sem=recv,
        device_id=target,
        device_id_type=MESH,
    )


def seq_orders(bits):
    upper = list(range(1, bits))
    return upper, upper[::-1]


def gather_kernel(nseq, heads, local_refs, out_refs, send, recv):
    bits = nseq.bit_length() - 1
    s, h = place()
    others = [lax.rem(h + d, heads) for d in range(1, heads)]
    greet([(related(s, 1 << b), h) for b in range(bits)] + [(s, o) for o in others])
    count = [0]
    started = []

    def go(src, dst, target):
        k = count[0]
        count[0] += 1
        copy = remote(src, dst, send.at[k], recv.at[k], target)
        copy.start()
        started.append(copy)
        return copy

    first = []
    for a in range(len(out_refs)):
        out_refs[a][s, h] = local_refs[a][...]
        first.append(
            [go(local_refs[a], out_refs[a].at[s, h], (s, o)) for o in others]
        )
    orders = [o + [0] for o in seq_orders(bits)]
    held = [{0: first[a]} for a in range(len(out_refs))]
    for stage in range(bits):
        for a in range(len(out_refs)):
            bit = orders[a % 2][stage]
            target = (related(s, 1 << bit), h)
            arrived = {}
            for mask in list(held[a]):
                for copy in held[a][mask]:
                    copy.wait_recv()
                held[a][mask] = []
                group = related(s, mask)
                copy = go(out_refs[a].at[group], out_refs[a].at[group], target)
                arrived[mask | (1 << bit)] = [copy]
            held[a].update(arrived)
    for a in range(len(out_refs)):
        for mask in held[a]:
            for copy in held[a][mask]:
                copy.wait_recv()
    for copy in started:
        copy.wait_send()


def gather_all(arrays, nseq, heads, cid):
    n = len(arrays)
    total = n * (heads - 1 + nseq - 1)

    def kernel(*refs):
        gather_kernel(nseq, heads, refs[:n], refs[n : 2 * n], refs[2 * n], refs[2 * n + 1])

    return pl.pallas_call(
        kernel,
        out_shape=[jax.ShapeDtypeStruct((nseq, heads) + a.shape, a.dtype) for a in arrays],
        in_specs=[pl.BlockSpec(memory_space=VMEM)] * n,
        out_specs=[pl.BlockSpec(memory_space=VMEM)] * n,
        scratch_shapes=[pltpu.SemaphoreType.DMA((total,)), pltpu.SemaphoreType.DMA((total,))],
        name="gather_all",
        compiler_params=pltpu.CompilerParams(
            collective_id=cid, has_side_effects=True, vmem_limit_bytes=LIMIT
        ),
    )(*arrays)


def line_gather_kernel(heads, x_ref, out_ref, send, recv):
    s, h = place()
    right = (s, lax.rem(h + 1, heads))
    left = (s, lax.rem(h + heads - 1, heads))
    greet([right, left])
    out_ref[h] = x_ref[...]
    for step in range(heads - 1):
        to_right = remote(
            out_ref.at[jnp.maximum(h - step, 0)],
            out_ref.at[jnp.maximum(h - step, 0)],
            send.at[0, step],
            recv.at[0, step],
            right,
        )
        to_left = remote(
            out_ref.at[jnp.minimum(h + step, heads - 1)],
            out_ref.at[jnp.minimum(h + step, heads - 1)],
            send.at[1, step],
            recv.at[1, step],
            left,
        )
        pl.when((h - step >= 0) & (h < heads - 1))(to_right.start)
        pl.when((h + step <= heads - 1) & (h > 0))(to_left.start)
        pl.when(h - 1 - step >= 0)(
            remote(
                out_ref.at[jnp.maximum(h - 1 - step, 0)],
                out_ref.at[jnp.maximum(h - 1 - step, 0)],
                send.at[0, step],
                recv.at[0, step],
                right,
            ).wait_recv
        )
        pl.when(h + 1 + step <= heads - 1)(
            remote(
                out_ref.at[jnp.minimum(h + 1 + step, heads - 1)],
                out_ref.at[jnp.minimum(h + 1 + step, heads - 1)],
                send.at[1, step],
                recv.at[1, step],
                left,
            ).wait_recv
        )
        pl.when((h - step >= 0) & (h < heads - 1))(to_right.wait_send)
        pl.when((h + step <= heads - 1) & (h > 0))(to_left.wait_send)


def line_gather(x, heads, cid):
    return pl.pallas_call(
        functools.partial(line_gather_kernel, heads),
        out_shape=jax.ShapeDtypeStruct((heads,) + x.shape, x.dtype),
        in_specs=[pl.BlockSpec(memory_space=VMEM)],
        out_specs=pl.BlockSpec(memory_space=VMEM),
        scratch_shapes=[
            pltpu.SemaphoreType.DMA((2, heads - 1)),
            pltpu.SemaphoreType.DMA((2, heads - 1)),
        ],
        name="line_gather",
        compiler_params=pltpu.CompilerParams(
            collective_id=cid, has_side_effects=True, vmem_limit_bytes=LIMIT
        ),
    )(x)


def line_scatter_kernel(heads, parts, out_ref, from_left, from_right, send, recv):
    s, h = place()
    last = heads - 1
    right = (s, lax.rem(h + 1, heads))
    left = (s, lax.rem(h + heads - 1, heads))
    greet([right, left])
    f32 = jnp.float32
    for step in range(heads - 1):
        r_dest = jnp.clip(last - (step - h), 0, last)
        l_dest = jnp.clip(step - (last - h), 0, last)
        r_on = (step >= h) & (h < last)
        l_on = (step >= last - h) & (h > 0)
        for on, dest, box, lane, target, first in (
            (r_on, r_dest, from_left, 0, right, step == h),
            (l_on, l_dest, from_right, 1, left, step == last - h),
        ):
            at_end = (h == 0) if lane == 0 else (h == last)
            if step > 0:

                def add(box=box, dest=dest):
                    box[step - 1] = (
                        box[step - 1].astype(f32) + parts[dest].astype(f32)
                    ).astype(box.dtype)

                pl.when(on & jnp.logical_not(at_end))(add)
                pl.when(on & jnp.logical_not(at_end))(
                    remote(
                        box.at[step - 1], box.at[step], send.at[lane, step], recv.at[lane, step], target
                    ).start
                )
            pl.when(on & at_end)(
                remote(
                    parts.at[dest], box.at[step], send.at[lane, step], recv.at[lane, step], target
                ).start
            )
        r_in = (step >= h - 1) & (h > 0)
        l_in = (step >= last - h - 1) & (h < last)
        pl.when(r_in)(
            remote(
                from_left.at[step], from_left.at[step], send.at[0, step], recv.at[0, step], right
            ).wait_recv
        )
        pl.when(l_in)(
            remote(
                from_right.at[step], from_right.at[step], send.at[1, step], recv.at[1, step], left
            ).wait_recv
        )
    for step in range(heads - 1):
        for on, box, lane, target in (
            ((step >= h) & (h < last), from_left, 0, right),
            ((step >= last - h) & (h > 0), from_right, 1, left),
        ):
            pl.when(on)(
                remote(
                    box.at[step], box.at[step], send.at[lane, step], recv.at[lane, step], target
                ).wait_send
            )
    out_ref[...] = parts[h].astype(f32)

    def add_left():
        out_ref[...] += from_left[heads - 2].astype(f32)

    def add_right():
        out_ref[...] += from_right[heads - 2].astype(f32)

    pl.when(h > 0)(add_left)
    pl.when(h < last)(add_right)


def line_scatter(parts, heads, cid):
    block = parts.shape[1:]
    return pl.pallas_call(
        functools.partial(line_scatter_kernel, heads),
        out_shape=jax.ShapeDtypeStruct(block, jnp.float32),
        in_specs=[pl.BlockSpec(memory_space=VMEM)],
        out_specs=pl.BlockSpec(memory_space=VMEM),
        scratch_shapes=[
            VMEM((heads - 1,) + block, parts.dtype),
            VMEM((heads - 1,) + block, parts.dtype),
            pltpu.SemaphoreType.DMA((2, heads - 1)),
            pltpu.SemaphoreType.DMA((2, heads - 1)),
        ],
        name="line_scatter",
        compiler_params=pltpu.CompilerParams(
            collective_id=cid, has_side_effects=True, vmem_limit_bytes=LIMIT
        ),
    )(parts)


def scatter_kernel(nseq, heads, zs, orders, parts, outs, boxes, zboxes, send, recv):
    bits = nseq.bit_length() - 1
    s, h = place()
    f32 = jnp.float32
    others = [lax.rem(h + d, heads) for d in range(1, heads)]
    greet(
        [(related(s, 1 << b), h) for b in range(bits)]
        + ([(s, o) for o in others] if any(zs) else [])
    )
    count = [0]
    started = []

    def go(src, dst, target):
        k = count[0]
        count[0] += 1
        copy = remote(src, dst, send.at[k], recv.at[k], target)
        copy.start()
        started.append(copy)
        return copy

    n = len(parts)
    offsets = [0] * n
    slot = [{} for _ in range(n)]
    waiting = [{} for _ in range(n)]

    def current(a, mask):
        if mask in slot[a]:
            return boxes[a].at[slot[a][mask]]
        return parts[a].at[related(s, mask)]

    def launch(a, stage):
        bit = orders[a][stage]
        rest = orders[a][stage + 1 :]
        target = (related(s, 1 << bit), h)
        after = 1 << rest[0] if rest else 0
        masks = sorted(subsets(rest), key=lambda m: 0 if m & after else 1)
        for mask in masks:
            where = offsets[a]
            offsets[a] += 1
            waiting[a][mask] = (
                go(current(a, mask | (1 << bit)), boxes[a].at[where], target),
                where,
            )

    def settle(a, mask):
        copy, where = waiting[a].pop(mask)
        mine = current(a, mask)
        copy.wait_recv()
        boxes[a][where] = (boxes[a][where].astype(f32) + mine[...].astype(f32)).astype(
            boxes[a].dtype
        )
        slot[a][mask] = where

    for a in range(n):
        launch(a, 0)
    for stage in range(bits):
        for a in range(n):
            for mask in list(waiting[a]):
                settle(a, mask)
            if stage + 1 < bits:
                launch(a, stage + 1)
    arriving = []
    for a in range(n):
        if not zs[a]:
            continue
        mine = current(a, 0)
        arriving.append(
            [
                go(mine.at[o], zboxes[a].at[d], (s, o))
                for d, o in enumerate(others)
            ]
        )
    z = 0
    for a in range(n):
        if zs[a]:
            total = current(a, 0)[h].astype(f32)
            for d, copy in enumerate(arriving[z]):
                copy.wait_recv()
                total = total + zboxes[a][d].astype(f32)
            outs[a][...] = total
            z += 1
        else:
            outs[a][...] = current(a, 0)[...].astype(f32)
    for copy in started:
        copy.wait_send()


def scatter_all(arrays, zs, orders, nseq, heads, cid, name):
    n = len(arrays)
    total = sum((nseq - 1) + (heads - 1 if z else 0) for z in zs)
    blocks = [a.shape[2:] if z else a.shape[1:] for a, z in zip(arrays, zs)]

    def kernel(*refs):
        scatter_kernel(
            nseq,
            heads,
            zs,
            orders,
            refs[:n],
            refs[n : 2 * n],
            refs[2 * n : 3 * n],
            refs[3 * n : 4 * n],
            refs[4 * n],
            refs[4 * n + 1],
        )

    return pl.pallas_call(
        kernel,
        out_shape=[jax.ShapeDtypeStruct(b, jnp.float32) for b in blocks],
        in_specs=[pl.BlockSpec(memory_space=VMEM)] * n,
        out_specs=[pl.BlockSpec(memory_space=VMEM)] * n,
        scratch_shapes=[VMEM((nseq - 1,) + a.shape[1:], a.dtype) for a in arrays]
        + [
            VMEM((heads - 1,) + b, a.dtype) if z else VMEM((8, 128), jnp.float32)
            for a, b, z in zip(arrays, blocks, zs)
        ]
        + [pltpu.SemaphoreType.DMA((total,)), pltpu.SemaphoreType.DMA((total,))],
        name=name,
        compiler_params=pltpu.CompilerParams(
            collective_id=cid, has_side_effects=True, vmem_limit_bytes=LIMIT
        ),
    )(*arrays)


def attend_kernel(q_ref, k_ref, v_ref, start_ref, index_ref, out_ref, log_ref):
    s = lax.axis_index("seq")
    span = k_ref.shape[1]
    start = start_ref[...]
    index = index_ref[...]
    queries = q_ref[...]
    rows = queries.shape[0]
    out_ref[...] = jnp.zeros_like(out_ref)

    def step(g, mass):
        scores = contract_last(k_ref[g], queries)
        key = g * span + lax.broadcasted_iota(jnp.int32, (span, rows), 0)
        terms = jnp.where((key >= start) & (key <= index), jnp.exp(scores), 0.0)
        out_ref[...] += contract_first(v_ref[g], terms.astype(jnp.bfloat16))
        return mass + jnp.sum(terms, axis=0, keepdims=True)

    mass = lax.fori_loop(0, s + 1, step, jnp.zeros((1, rows), jnp.float32))
    out_ref[...] = out_ref[...] / mass
    log_ref[...] = jnp.log(mass)


def attend(q, k, v, start, index):
    rows, width = q.shape
    return pl.pallas_call(
        attend_kernel,
        out_shape=[
            jax.ShapeDtypeStruct((width, rows), jnp.float32),
            jax.ShapeDtypeStruct((1, rows), jnp.float32),
        ],
        in_specs=[pl.BlockSpec(memory_space=VMEM)] * 5,
        out_specs=[pl.BlockSpec(memory_space=VMEM)] * 2,
        name="attend",
        compiler_params=pltpu.CompilerParams(vmem_limit_bytes=LIMIT),
    )(q, k, v, start, index)


def attend_back_kernel(
    q_ref, k_ref, v_ref, start_ref, index_ref, log_ref, dots_ref, d_ref, dq_ref, dk_ref, dv_ref
):
    s = lax.axis_index("seq")
    groups, span = k_ref.shape[:2]
    start = start_ref[...]
    index = index_ref[...]
    log_total = log_ref[...]
    dots = dots_ref[...]
    queries = q_ref[...]
    grads = d_ref[...]
    rows = queries.shape[0]
    dq_ref[...] = jnp.zeros_like(dq_ref)

    def step(g, carry):
        keys = k_ref[g]
        scores = contract_last(keys, queries)
        key = g * span + lax.broadcasted_iota(jnp.int32, (span, rows), 0)
        probs = jnp.where((key >= start) & (key <= index), jnp.exp(scores - log_total), 0.0)
        d_probs = contract_last(v_ref[g], grads)
        d_scores = (probs * (d_probs - dots)).astype(jnp.bfloat16)
        dv_ref[g] = jnp.dot(
            probs.astype(jnp.bfloat16), grads, preferred_element_type=jnp.float32
        ).astype(dv_ref.dtype)
        dk_ref[g] = jnp.dot(d_scores, queries, preferred_element_type=jnp.float32).astype(
            dk_ref.dtype
        )
        dq_ref[...] += contract_first(keys, d_scores)
        return carry

    lax.fori_loop(0, s + 1, step, 0)

    def blank(g, carry):
        dk_ref[g] = jnp.zeros(dk_ref.shape[1:], dk_ref.dtype)
        dv_ref[g] = jnp.zeros(dv_ref.shape[1:], dv_ref.dtype)
        return carry

    lax.fori_loop(s + 1, groups, blank, 0)


def attend_back(q, k, v, start, index, log_total, dots, grads):
    rows, width = q.shape
    return pl.pallas_call(
        attend_back_kernel,
        out_shape=[
            jax.ShapeDtypeStruct((width, rows), jnp.float32),
            jax.ShapeDtypeStruct(k.shape, jnp.bfloat16),
            jax.ShapeDtypeStruct(v.shape, jnp.bfloat16),
        ],
        in_specs=[pl.BlockSpec(memory_space=VMEM)] * 8,
        out_specs=[pl.BlockSpec(memory_space=VMEM)] * 3,
        name="attend_back",
        compiler_params=pltpu.CompilerParams(vmem_limit_bytes=LIMIT),
    )(q, k, v, start, index, log_total, dots, grads)


def local(
    tokens,
    segment_ids,
    w_query,
    w_key,
    w_value,
    w_out,
    w_gate,
    w_up,
    w_down,
    gain_attn_in,
    gain_attn_out,
    gain_ffn_in,
    gain_ffn_out,
    gain_query,
    gain_key,
    cotangent,
):
    heads = lax.axis_size("head")
    nseq = lax.axis_size("seq")
    head_index = lax.axis_index("head")
    seq_index = lax.axis_index("seq")
    bits = nseq.bit_length() - 1
    local_rows, model = tokens.shape
    width = gain_query.shape[0]
    qcount = w_query.shape[1] // width
    group = local_rows * heads
    total = segment_ids.shape[0]
    hidden_units = w_gate.shape[1]
    scale = 1.0 / math.sqrt(width)
    bf16 = jnp.bfloat16
    first_row = (seq_index * heads + head_index) * local_rows
    my_index = first_row + jnp.arange(local_rows, dtype=jnp.int32)
    my_ids = lax.dynamic_slice_in_dim(segment_ids, first_row, local_rows)
    my_starts = jnp.min(
        jnp.where(
            my_ids[:, None] == segment_ids[None, :],
            jnp.arange(total, dtype=jnp.int32)[None, :],
            total,
        ),
        axis=1,
    )
    cosines, sines = rope_tables(my_index - my_starts, width)

    def query_path(linear, gain):
        shaped = linear.reshape(local_rows, qcount, width)
        turned = rotate(norm_rows(shaped, gain), cosines[:, None, :], sines[:, None, :])
        return turned.reshape(local_rows, qcount * width)

    def key_path(linear, gain):
        return rotate(norm_rows(linear, gain), cosines, sines)

    def gated(gate, up):
        return jax.nn.gelu(gate, approximate=True) * up

    def stacked(v):
        return v.reshape(local_rows, qcount, width).transpose(1, 0, 2).reshape(-1, width)

    def unstacked(v):
        return v.reshape(qcount, local_rows, width).transpose(1, 0, 2).reshape(local_rows, -1)

    inputs = tokens.astype(jnp.float32)
    attn_in = norm_rows(inputs, gain_attn_in).astype(bf16)
    k_linear = jnp.dot(attn_in, w_key, preferred_element_type=jnp.float32)
    keys_local = key_path(k_linear, gain_key).astype(bf16)
    values_local = jnp.dot(attn_in, w_value, preferred_element_type=jnp.float32).astype(bf16)
    q_linear = jnp.dot(attn_in, w_query, preferred_element_type=jnp.float32)
    queries_local = query_path(q_linear, gain_query).astype(bf16)
    queries = stacked(queries_local) * jnp.asarray(scale, bf16)
    keys, values = gather_all([keys_local, values_local], nseq, heads, 1)
    keys = keys.reshape(nseq, group, width)
    values = values.reshape(nseq, group, width)
    starts = jnp.tile(my_starts, qcount)[None, :]
    index = jnp.tile(my_index, qcount)[None, :]
    attended_t, log_total = attend(queries, keys, values, starts, index)
    attended = attended_t.T
    mixed_local = unstacked(attended.astype(bf16))
    projected = jnp.dot(mixed_local, w_out, preferred_element_type=jnp.float32)
    hidden = inputs + norm_rows(projected, gain_attn_out)
    ffn_in = norm_rows(hidden, gain_ffn_in).astype(bf16)
    ffn_rows = line_gather(ffn_in, heads, 2).reshape(group, model)
    gate = jnp.dot(ffn_rows, w_gate, preferred_element_type=jnp.float32)
    up = jnp.dot(ffn_rows, w_up, preferred_element_type=jnp.float32)
    activated = gated(gate, up).astype(bf16)
    ffn_out = line_scatter(
        jnp.dot(activated, w_down, preferred_element_type=jnp.float32)
        .astype(bf16)
        .reshape(heads, local_rows, model),
        heads,
        3,
    )
    output = hidden + norm_rows(ffn_out, gain_ffn_out)
    upstream = cotangent.astype(jnp.float32)
    unused, back_four = jax.vjp(norm_rows, ffn_out, gain_ffn_out)
    d_ffn_out, d_gain_four = back_four(upstream)
    d_ffn_rows = line_gather(d_ffn_out.astype(bf16), heads, 4).reshape(group, model)
    d_activated = contract_last(d_ffn_rows, w_down)
    d_w_down = contract_first(d_ffn_rows, activated)
    unused, back_gate = jax.vjp(gated, gate, up)
    d_gate, d_up = back_gate(d_activated)
    d_gate = d_gate.astype(bf16)
    d_up = d_up.astype(bf16)
    d_ffn_in = line_scatter(
        (contract_last(d_gate, w_gate) + contract_last(d_up, w_up))
        .astype(bf16)
        .reshape(heads, local_rows, model),
        heads,
        5,
    )
    d_w_gate = contract_first(ffn_rows, d_gate)
    d_w_up = contract_first(ffn_rows, d_up)
    unused, back_three = jax.vjp(norm_rows, hidden, gain_ffn_in)
    d_hidden_part, d_gain_three = back_three(d_ffn_in)
    d_hidden = upstream + d_hidden_part
    unused, back_two = jax.vjp(norm_rows, projected, gain_attn_out)
    d_projected, d_gain_two = back_two(d_hidden)
    d_projected = d_projected.astype(bf16)
    d_w_out = contract_first(mixed_local, d_projected)
    d_mixed = contract_last(d_projected, w_out).astype(bf16)
    grad_attended = stacked(d_mixed)
    row_dots = jnp.sum(grad_attended.astype(jnp.float32) * attended, axis=1)[None, :]
    d_queries_t, d_keys, d_values = attend_back(
        queries, keys, values, starts, index, log_total, row_dots, grad_attended
    )
    shape = (nseq, heads, local_rows, width)
    ups, downs = seq_orders(bits)
    d_keys, d_values = scatter_all(
        [d_keys.reshape(shape), d_values.reshape(shape)],
        [True, True],
        [[0] + ups, [0] + downs],
        nseq,
        heads,
        6,
        "scatter_keys",
    )
    d_query_rot = unstacked((d_queries_t.T * scale).astype(bf16)).astype(jnp.float32)
    unused, back_query = jax.vjp(query_path, q_linear, gain_query)
    d_q_linear, d_gain_query = back_query(d_query_rot)
    unused, back_key = jax.vjp(key_path, k_linear, gain_key)
    d_k_linear, d_gain_key = back_key(d_keys)
    d_qkv = jnp.concatenate([d_q_linear, d_k_linear, d_values], axis=1).astype(bf16)
    qw = qcount * width
    d_w_qkv = contract_first(attn_in, d_qkv)
    d_attn_in = (
        contract_last(d_qkv[:, :qw], w_query)
        + contract_last(d_qkv[:, qw : qw + width], w_key)
        + contract_last(d_qkv[:, qw + width :], w_value)
    )
    unused, back_one = jax.vjp(norm_rows, inputs, gain_attn_in)
    d_inputs, d_gain_one = back_one(d_attn_in)
    grad_tokens = (d_hidden + d_inputs).astype(bf16)

    def cut(v):
        return v.reshape(nseq, heads, -1)

    wide = jnp.stack([cut(d_gain_one), cut(d_gain_two), cut(d_gain_three), cut(d_gain_four)], 2)
    narrow = jnp.stack([cut(d_gain_query), cut(d_gain_key)], 2)
    each, few = wide.shape[-1], narrow.shape[-1]
    gains = jnp.concatenate(
        [
            jnp.pad(wide, ((0, 0), (0, 0), (0, 0), (0, 128 - each))),
            jnp.pad(narrow, ((0, 0), (0, 0), (0, 2), (0, 128 - few))),
        ],
        axis=2,
    )
    sum_qkv, sum_out, sum_gains = scatter_all(
        [
            d_w_qkv.astype(bf16).reshape(nseq, heads, -1, d_qkv.shape[1]),
            d_w_out.astype(bf16).reshape(nseq, heads, -1, model),
            gains,
        ],
        [True, True, True],
        [[0] + ups, [0] + downs, [0] + downs],
        nseq,
        heads,
        7,
        "scatter_attn",
    )
    sum_gate, sum_up, sum_down = scatter_all(
        [
            d.astype(bf16).reshape(nseq, model // nseq, hidden_units)
            for d in (d_w_gate, d_w_up, d_w_down)
        ],
        [False, False, False],
        [[0] + ups, [0] + downs, [0] + ups],
        nseq,
        heads,
        8,
        "scatter_ffn",
    )
    return (
        output.astype(bf16),
        grad_tokens,
        sum_qkv[:, :qw],
        sum_qkv[:, qw : qw + width],
        sum_qkv[:, qw + width :],
        sum_out,
        sum_gate,
        sum_up,
        sum_down.T,
        sum_gains[0, :each],
        sum_gains[1, :each],
        sum_gains[2, :each],
        sum_gains[3, :each],
        sum_gains[4, :few],
        sum_gains[5, :few],
    )


def solution(mesh):
    rows = P(("seq", "head"), None)
    in_specs = (
        rows,
        P(),
        P(),
        P(),
        P(),
        P(),
        P(None, "head"),
        P(None, "head"),
        P("head", None),
        P(),
        P(),
        P(),
        P(),
        P(),
        P(),
        rows,
    )
    out_specs = (
        rows,
        rows,
        rows,
        rows,
        rows,
        rows,
        P("seq", "head"),
        P("seq", "head"),
        P("head", "seq"),
    ) + (P(("seq", "head")),) * 6
    return jax.shard_map(local, mesh=mesh, in_specs=in_specs, out_specs=out_specs, check_vma=False)
```

```python
import functools
import math

import jax
import jax.numpy as jnp
from jax import lax
from jax.experimental import pallas as pl
from jax.experimental.pallas import tpu as pltpu
from jax.sharding import PartitionSpec as P

EPS = 1e-06
MESH = pl.DeviceIdType.MESH
VMEM = pltpu.VMEM
LIMIT = 56 * 2**20


def norm_rows(v, gain):
    return v * lax.rsqrt(jnp.mean(v * v, axis=-1, keepdims=True) + EPS) * gain


def rotate(v, cosines, sines):
    half = v.shape[-1] // 2
    first = v[..., :half]
    second = v[..., half:]
    return jnp.concatenate(
        [first * cosines - second * sines, second * cosines + first * sines], axis=-1
    )


def rope_tables(positions, width):
    half = width // 2
    freq = jnp.exp(jnp.arange(half, dtype=jnp.float32) * (-2.0 * math.log(1000000.0) / width))
    angle = positions.astype(jnp.float32)[:, None] * freq[None, :]
    return (jnp.cos(angle), jnp.sin(angle))


def contract_first(left, right):
    return lax.dot_general(
        left, right, (((0,), (0,)), ((), ())), preferred_element_type=jnp.float32
    )


def contract_last(left, right):
    return lax.dot_general(
        left, right, (((1,), (1,)), ((), ())), preferred_element_type=jnp.float32
    )


def place():
    return lax.axis_index("seq"), lax.axis_index("head")


def related(s, mask):
    out = s
    bit = 0
    while mask >> bit:
        if (mask >> bit) & 1:
            step = 1 << bit
            out = out + (1 - 2 * ((s // step) % 2)) * step
        bit += 1
    return out


def subsets(bits):
    out = [0]
    for bit in bits:
        out = out + [m | (1 << bit) for m in out]
    return out


def greet(targets):
    barrier = pltpu.get_barrier_semaphore()
    for target in targets:
        pl.semaphore_signal(barrier, inc=1, device_id=target, device_id_type=MESH)
    pl.semaphore_wait(barrier, len(targets))


def remote(src, dst, send, recv, target):
    return pltpu.make_async_remote_copy(
        src_ref=src,
        dst_ref=dst,
        send_sem=send,
        recv_sem=recv,
        device_id=target,
        device_id_type=MESH,
    )


def seq_orders(bits):
    upper = list(range(1, bits))
    return upper, upper[::-1]


def gather_kernel(nseq, heads, local_refs, out_refs, send, recv):
    bits = nseq.bit_length() - 1
    s, h = place()
    others = [lax.rem(h + d, heads) for d in range(1, heads)]
    greet([(related(s, 1 << b), h) for b in range(bits)] + [(s, o) for o in others])
    count = [0]
    started = []

    def go(src, dst, target):
        k = count[0]
        count[0] += 1
        copy = remote(src, dst, send.at[k], recv.at[k], target)
        copy.start()
        started.append(copy)
        return copy

    first = []
    for a in range(len(out_refs)):
        out_refs[a][s, h] = local_refs[a][...]
        first.append(
            [go(local_refs[a], out_refs[a].at[s, h], (s, o)) for o in others]
        )
    orders = [o + [0] for o in seq_orders(bits)]
    held = [{0: first[a]} for a in range(len(out_refs))]
    for stage in range(bits):
        for a in range(len(out_refs)):
            bit = orders[a % 2][stage]
            target = (related(s, 1 << bit), h)
            arrived = {}
            for mask in list(held[a]):
                for copy in held[a][mask]:
                    copy.wait_recv()
                held[a][mask] = []
                group = related(s, mask)
                copy = go(out_refs[a].at[group], out_refs[a].at[group], target)
                arrived[mask | (1 << bit)] = [copy]
            held[a].update(arrived)
    for a in range(len(out_refs)):
        for mask in held[a]:
            for copy in held[a][mask]:
                copy.wait_recv()
    for copy in started:
        copy.wait_send()


def gather_all(arrays, nseq, heads, cid):
    n = len(arrays)
    total = n * (heads - 1 + nseq - 1)

    def kernel(*refs):
        gather_kernel(nseq, heads, refs[:n], refs[n : 2 * n], refs[2 * n], refs[2 * n + 1])

    return pl.pallas_call(
        kernel,
        out_shape=[jax.ShapeDtypeStruct((nseq, heads) + a.shape, a.dtype) for a in arrays],
        in_specs=[pl.BlockSpec(memory_space=VMEM)] * n,
        out_specs=[pl.BlockSpec(memory_space=VMEM)] * n,
        scratch_shapes=[pltpu.SemaphoreType.DMA((total,)), pltpu.SemaphoreType.DMA((total,))],
        name="gather_all",
        compiler_params=pltpu.CompilerParams(
            collective_id=cid, has_side_effects=True, vmem_limit_bytes=LIMIT
        ),
    )(*arrays)


def line_gather_kernel(heads, x_ref, out_ref, send, recv):
    s, h = place()
    right = (s, lax.rem(h + 1, heads))
    left = (s, lax.rem(h + heads - 1, heads))
    greet([right, left])
    out_ref[h] = x_ref[...]
    for step in range(heads - 1):
        to_right = remote(
            out_ref.at[jnp.maximum(h - step, 0)],
            out_ref.at[jnp.maximum(h - step, 0)],
            send.at[0, step],
            recv.at[0, step],
            right,
        )
        to_left = remote(
            out_ref.at[jnp.minimum(h + step, heads - 1)],
            out_ref.at[jnp.minimum(h + step, heads - 1)],
            send.at[1, step],
            recv.at[1, step],
            left,
        )
        pl.when((h - step >= 0) & (h < heads - 1))(to_right.start)
        pl.when((h + step <= heads - 1) & (h > 0))(to_left.start)
        pl.when(h - 1 - step >= 0)(
            remote(
                out_ref.at[jnp.maximum(h - 1 - step, 0)],
                out_ref.at[jnp.maximum(h - 1 - step, 0)],
                send.at[0, step],
                recv.at[0, step],
                right,
            ).wait_recv
        )
        pl.when(h + 1 + step <= heads - 1)(
            remote(
                out_ref.at[jnp.minimum(h + 1 + step, heads - 1)],
                out_ref.at[jnp.minimum(h + 1 + step, heads - 1)],
                send.at[1, step],
                recv.at[1, step],
                left,
            ).wait_recv
        )
        pl.when((h - step >= 0) & (h < heads - 1))(to_right.wait_send)
        pl.when((h + step <= heads - 1) & (h > 0))(to_left.wait_send)


def line_gather(x, heads, cid):
    return pl.pallas_call(
        functools.partial(line_gather_kernel, heads),
        out_shape=jax.ShapeDtypeStruct((heads,) + x.shape, x.dtype),
        in_specs=[pl.BlockSpec(memory_space=VMEM)],
        out_specs=pl.BlockSpec(memory_space=VMEM),
        scratch_shapes=[
            pltpu.SemaphoreType.DMA((2, heads - 1)),
            pltpu.SemaphoreType.DMA((2, heads - 1)),
        ],
        name="line_gather",
        compiler_params=pltpu.CompilerParams(
            collective_id=cid, has_side_effects=True, vmem_limit_bytes=LIMIT
        ),
    )(x)


def line_scatter_kernel(heads, parts, out_ref, from_left, from_right, send, recv):
    s, h = place()
    last = heads - 1
    right = (s, lax.rem(h + 1, heads))
    left = (s, lax.rem(h + heads - 1, heads))
    greet([right, left])
    f32 = jnp.float32
    for step in range(heads - 1):
        r_dest = jnp.clip(last - (step - h), 0, last)
        l_dest = jnp.clip(step - (last - h), 0, last)
        r_on = (step >= h) & (h < last)
        l_on = (step >= last - h) & (h > 0)
        for on, dest, box, lane, target, first in (
            (r_on, r_dest, from_left, 0, right, step == h),
            (l_on, l_dest, from_right, 1, left, step == last - h),
        ):
            at_end = (h == 0) if lane == 0 else (h == last)
            if step > 0:

                def add(box=box, dest=dest):
                    box[step - 1] = (
                        box[step - 1].astype(f32) + parts[dest].astype(f32)
                    ).astype(box.dtype)

                pl.when(on & jnp.logical_not(at_end))(add)
                pl.when(on & jnp.logical_not(at_end))(
                    remote(
                        box.at[step - 1], box.at[step], send.at[lane, step], recv.at[lane, step], target
                    ).start
                )
            pl.when(on & at_end)(
                remote(
                    parts.at[dest], box.at[step], send.at[lane, step], recv.at[lane, step], target
                ).start
            )
        r_in = (step >= h - 1) & (h > 0)
        l_in = (step >= last - h - 1) & (h < last)
        pl.when(r_in)(
            remote(
                from_left.at[step], from_left.at[step], send.at[0, step], recv.at[0, step], right
            ).wait_recv
        )
        pl.when(l_in)(
            remote(
                from_right.at[step], from_right.at[step], send.at[1, step], recv.at[1, step], left
            ).wait_recv
        )
    for step in range(heads - 1):
        for on, box, lane, target in (
            ((step >= h) & (h < last), from_left, 0, right),
            ((step >= last - h) & (h > 0), from_right, 1, left),
        ):
            pl.when(on)(
                remote(
                    box.at[step], box.at[step], send.at[lane, step], recv.at[lane, step], target
                ).wait_send
            )
    out_ref[...] = parts[h].astype(f32)

    def add_left():
        out_ref[...] += from_left[heads - 2].astype(f32)

    def add_right():
        out_ref[...] += from_right[heads - 2].astype(f32)

    pl.when(h > 0)(add_left)
    pl.when(h < last)(add_right)


def line_scatter(parts, heads, cid):
    block = parts.shape[1:]
    return pl.pallas_call(
        functools.partial(line_scatter_kernel, heads),
        out_shape=jax.ShapeDtypeStruct(block, jnp.float32),
        in_specs=[pl.BlockSpec(memory_space=VMEM)],
        out_specs=pl.BlockSpec(memory_space=VMEM),
        scratch_shapes=[
            VMEM((heads - 1,) + block, parts.dtype),
            VMEM((heads - 1,) + block, parts.dtype),
            pltpu.SemaphoreType.DMA((2, heads - 1)),
            pltpu.SemaphoreType.DMA((2, heads - 1)),
        ],
        name="line_scatter",
        compiler_params=pltpu.CompilerParams(
            collective_id=cid, has_side_effects=True, vmem_limit_bytes=LIMIT
        ),
    )(parts)


def scatter_kernel(nseq, heads, zs, orders, parts, outs, boxes, zboxes, send, recv):
    bits = nseq.bit_length() - 1
    s, h = place()
    f32 = jnp.float32
    others = [lax.rem(h + d, heads) for d in range(1, heads)]
    greet(
        [(related(s, 1 << b), h) for b in range(bits)]
        + ([(s, o) for o in others] if any(zs) else [])
    )
    count = [0]
    started = []

    def go(src, dst, target):
        k = count[0]
        count[0] += 1
        copy = remote(src, dst, send.at[k], recv.at[k], target)
        copy.start()
        started.append(copy)
        return copy

    n = len(parts)
    offsets = [0] * n
    slot = [{} for _ in range(n)]
    waiting = [{} for _ in range(n)]

    def current(a, mask):
        if mask in slot[a]:
            return boxes[a].at[slot[a][mask]]
        return parts[a].at[related(s, mask)]

    def launch(a, stage):
        bit = orders[a][stage]
        rest = orders[a][stage + 1 :]
        target = (related(s, 1 << bit), h)
        after = 1 << rest[0] if rest else 0
        masks = sorted(subsets(rest), key=lambda m: 0 if m & after else 1)
        for mask in masks:
            where = offsets[a]
            offsets[a] += 1
            waiting[a][mask] = (
                go(current(a, mask | (1 << bit)), boxes[a].at[where], target),
                where,
            )

    def settle(a, mask):
        copy, where = waiting[a].pop(mask)
        mine = current(a, mask)
        copy.wait_recv()
        boxes[a][where] = (boxes[a][where].astype(f32) + mine[...].astype(f32)).astype(
            boxes[a].dtype
        )
        slot[a][mask] = where

    for a in range(n):
        launch(a, 0)
    for stage in range(bits):
        for a in range(n):
            for mask in list(waiting[a]):
                settle(a, mask)
            if stage + 1 < bits:
                launch(a, stage + 1)
    arriving = []
    for a in range(n):
        if not zs[a]:
            continue
        mine = current(a, 0)
        arriving.append(
            [
                go(mine.at[o], zboxes[a].at[d], (s, o))
                for d, o in enumerate(others)
            ]
        )
    z = 0
    for a in range(n):
        if zs[a]:
            total = current(a, 0)[h].astype(f32)
            for d, copy in enumerate(arriving[z]):
                copy.wait_recv()
                total = total + zboxes[a][d].astype(f32)
            outs[a][...] = total
            z += 1
        else:
            outs[a][...] = current(a, 0)[...].astype(f32)
    for copy in started:
        copy.wait_send()


def scatter_all(arrays, zs, orders, nseq, heads, cid, name):
    n = len(arrays)
    total = sum((nseq - 1) + (heads - 1 if z else 0) for z in zs)
    blocks = [a.shape[2:] if z else a.shape[1:] for a, z in zip(arrays, zs)]

    def kernel(*refs):
        scatter_kernel(
            nseq,
            heads,
            zs,
            orders,
            refs[:n],
            refs[n : 2 * n],
            refs[2 * n : 3 * n],
            refs[3 * n : 4 * n],
            refs[4 * n],
            refs[4 * n + 1],
        )

    return pl.pallas_call(
        kernel,
        out_shape=[jax.ShapeDtypeStruct(b, jnp.float32) for b in blocks],
        in_specs=[pl.BlockSpec(memory_space=VMEM)] * n,
        out_specs=[pl.BlockSpec(memory_space=VMEM)] * n,
        scratch_shapes=[VMEM((nseq - 1,) + a.shape[1:], a.dtype) for a in arrays]
        + [
            VMEM((heads - 1,) + b, a.dtype) if z else VMEM((8, 128), jnp.float32)
            for a, b, z in zip(arrays, blocks, zs)
        ]
        + [pltpu.SemaphoreType.DMA((total,)), pltpu.SemaphoreType.DMA((total,))],
        name=name,
        compiler_params=pltpu.CompilerParams(
            collective_id=cid, has_side_effects=True, vmem_limit_bytes=LIMIT
        ),
    )(*arrays)


def attend_kernel(q_ref, k_ref, v_ref, start_ref, index_ref, out_ref, log_ref):
    s = lax.axis_index("seq")
    span = k_ref.shape[1]
    start = start_ref[...]
    index = index_ref[...]
    queries = q_ref[...]
    rows = queries.shape[0]
    out_ref[...] = jnp.zeros_like(out_ref)

    def step(g, mass):
        scores = contract_last(k_ref[g], queries)
        key = g * span + lax.broadcasted_iota(jnp.int32, (span, rows), 0)
        terms = jnp.where((key >= start) & (key <= index), jnp.exp(scores), 0.0)
        out_ref[...] += contract_first(v_ref[g], terms.astype(jnp.bfloat16))
        return mass + jnp.sum(terms, axis=0, keepdims=True)

    mass = lax.fori_loop(0, s + 1, step, jnp.zeros((1, rows), jnp.float32))
    out_ref[...] = out_ref[...] / mass
    log_ref[...] = jnp.log(mass)


def attend(q, k, v, start, index):
    rows, width = q.shape
    return pl.pallas_call(
        attend_kernel,
        out_shape=[
            jax.ShapeDtypeStruct((width, rows), jnp.float32),
            jax.ShapeDtypeStruct((1, rows), jnp.float32),
        ],
        in_specs=[pl.BlockSpec(memory_space=VMEM)] * 5,
        out_specs=[pl.BlockSpec(memory_space=VMEM)] * 2,
        name="attend",
        compiler_params=pltpu.CompilerParams(vmem_limit_bytes=LIMIT),
    )(q, k, v, start, index)


def attend_back_kernel(
    q_ref, k_ref, v_ref, start_ref, index_ref, log_ref, dots_ref, d_ref, dq_ref, dk_ref, dv_ref
):
    s = lax.axis_index("seq")
    groups, span = k_ref.shape[:2]
    start = start_ref[...]
    index = index_ref[...]
    log_total = log_ref[...]
    dots = dots_ref[...]
    queries = q_ref[...]
    grads = d_ref[...]
    rows = queries.shape[0]
    dq_ref[...] = jnp.zeros_like(dq_ref)

    def step(g, carry):
        keys = k_ref[g]
        scores = contract_last(keys, queries)
        key = g * span + lax.broadcasted_iota(jnp.int32, (span, rows), 0)
        probs = jnp.where((key >= start) & (key <= index), jnp.exp(scores - log_total), 0.0)
        d_probs = contract_last(v_ref[g], grads)
        d_scores = (probs * (d_probs - dots)).astype(jnp.bfloat16)
        dv_ref[g] = jnp.dot(
            probs.astype(jnp.bfloat16), grads, preferred_element_type=jnp.float32
        ).astype(dv_ref.dtype)
        dk_ref[g] = jnp.dot(d_scores, queries, preferred_element_type=jnp.float32).astype(
            dk_ref.dtype
        )
        dq_ref[...] += contract_first(keys, d_scores)
        return carry

    lax.fori_loop(0, s + 1, step, 0)

    def blank(g, carry):
        dk_ref[g] = jnp.zeros(dk_ref.shape[1:], dk_ref.dtype)
        dv_ref[g] = jnp.zeros(dv_ref.shape[1:], dv_ref.dtype)
        return carry

    lax.fori_loop(s + 1, groups, blank, 0)


def attend_back(q, k, v, start, index, log_total, dots, grads):
    rows, width = q.shape
    return pl.pallas_call(
        attend_back_kernel,
        out_shape=[
            jax.ShapeDtypeStruct((width, rows), jnp.float32),
            jax.ShapeDtypeStruct(k.shape, jnp.bfloat16),
            jax.ShapeDtypeStruct(v.shape, jnp.bfloat16),
        ],
        in_specs=[pl.BlockSpec(memory_space=VMEM)] * 8,
        out_specs=[pl.BlockSpec(memory_space=VMEM)] * 3,
        name="attend_back",
        compiler_params=pltpu.CompilerParams(vmem_limit_bytes=LIMIT),
    )(q, k, v, start, index, log_total, dots, grads)


class Sum:
    def __init__(self, links, part, boxes, order):
        self.links, self.part, self.boxes, self.order = links, part, boxes, order
        self.stage = 0
        self.used = 0
        self.slot = {}
        self.waiting = {}

    def current(self, mask):
        if mask in self.slot:
            return self.boxes.at[self.slot[mask]]
        return self.part(mask)

    def launch(self):
        bit = self.order[self.stage]
        rest = self.order[self.stage + 1 :]
        target = self.links.across(bit)
        after = 1 << rest[0] if rest else 0
        for mask in sorted(subsets(rest), key=lambda m: 0 if m & after else 1):
            where = self.used
            self.used += 1
            copy = self.links.go(self.current(mask | (1 << bit)), self.boxes.at[where], target)
            self.waiting[mask] = (copy, where)
        self.stage += 1

    def settle(self, kept=None):
        for mask in list(self.waiting):
            copy, where = self.waiting.pop(mask)
            mine = kept(mask) if kept is not None else self.current(mask)
            copy.wait_recv()
            self.boxes[where] = self.boxes[where] + mine[...]
            self.slot[mask] = where

    def last(self, kept=None):
        ((mask, (copy, where)),) = self.waiting.items()
        self.waiting = {}
        mine = kept(mask) if kept is not None else self.current(mask)
        copy.wait_recv()
        return self.boxes[where].astype(jnp.float32) + mine[...].astype(jnp.float32)


class Links:
    def __init__(self, nseq, heads, send, recv):
        self.s, self.h = place()
        self.nseq, self.heads = nseq, heads
        self.send, self.recv = send, recv
        self.count = 0
        self.started = []
        self.others = [lax.rem(self.h + d, heads) for d in range(1, heads)]

    def greet(self):
        bits = self.nseq.bit_length() - 1
        greet([self.across(b) for b in range(bits)] + [(self.s, o) for o in self.others])

    def across(self, bit):
        return (related(self.s, 1 << bit), self.h)

    def go(self, src, dst, target):
        k = self.count
        self.count += 1
        copy = remote(src, dst, self.send.at[k], self.recv.at[k], target)
        copy.start()
        self.started.append(copy)
        return copy

    def over_heads(self, src, boxes):
        return [self.go(src.at[o], boxes.at[d], (self.s, o)) for d, o in enumerate(self.others)]

    def finish(self):
        for copy in self.started:
            copy.wait_send()


def back_norm(v, gain, d_out):
    scale = lax.rsqrt(jnp.mean(v * v, axis=-1, keepdims=True) + EPS)
    unit = v * scale
    inner = d_out * gain
    d_v = scale * (inner - unit * jnp.mean(inner * unit, axis=-1, keepdims=True))
    return d_v, jnp.sum(d_out * unit, axis=0, keepdims=True)


def back_rotate(d, cosines, sines):
    half = d.shape[-1] // 2
    first, second = d[:, :half], d[:, half:]
    return jnp.concatenate(
        [first * cosines + second * sines, second * cosines - first * sines], axis=-1
    )


def tail_kernel(
    nseq,
    heads,
    qcount,
    scale,
    q_ref,
    k_ref,
    v_ref,
    start_ref,
    index_ref,
    log_ref,
    att_ref,
    mixed_t_ref,
    d_proj_ref,
    w_out_ref,
    q_lin_ref,
    k_lin_ref,
    cos_ref,
    sin_ref,
    gain_q_ref,
    gain_k_ref,
    attn_t_ref,
    w_qkv_ref,
    x_ref,
    gain_in_ref,
    d_hid_ref,
    gains_ref,
    d_gate_ref,
    d_up_ref,
    d_down_ref,
    o_tokens,
    o_qkv,
    o_out,
    o_gate,
    o_up,
    o_down,
    o_gains,
    dk,
    dv,
    dq_t,
    grads,
    grads_t,
    box_k,
    box_v,
    zbox_k,
    zbox_v,
    dw_out,
    box_out,
    zsrc_out,
    zbox_out,
    dw_a,
    dw_b,
    box_a,
    box_b,
    zsrc_qkv,
    zbox_qkv,
    d_qkv,
    keep_gate,
    keep_up,
    keep_down,
    box_gate,
    box_up,
    box_down,
    gsum,
    gbox,
    gzbox,
    send,
    recv,
    local_sem,
):
    f32, bf16 = jnp.float32, jnp.bfloat16
    bits = nseq.bit_length() - 1
    ups, downs = seq_orders(bits)
    links = Links(nseq, heads, send, recv)
    s, h = links.s, links.h
    rows = d_proj_ref.shape[0]
    width = gain_q_ref.shape[1]
    groups, span = k_ref.shape[:2]
    links.greet()

    ffn = []
    kept_copies = []
    kept_masks = subsets(ups)
    for n, (src, keep, box, order) in enumerate(
        (
            (d_gate_ref, keep_gate, box_gate, ups),
            (d_up_ref, keep_up, box_up, downs),
            (d_down_ref, keep_down, box_down, ups),
        )
    ):
        total = Sum(links, lambda m, src=src: src.at[related(s, m)], box, [0] + order)
        total.launch()
        total.kept = lambda m, keep=keep: keep.at[kept_masks.index(m)]
        ffn.append(total)
        for i, m in enumerate(kept_masks):
            copy = pltpu.make_async_copy(src.at[related(s, m)], keep.at[i], local_sem.at[n, i])
            copy.start()
            kept_copies.append(copy)

    d_proj = d_proj_ref[...]

    def out_block(j, carry):
        dw_out[j] = jnp.dot(mixed_t_ref[j], d_proj, preferred_element_type=f32).astype(bf16)
        return carry

    lax.fori_loop(0, nseq, out_block, 0)
    sum_out = Sum(links, lambda m: dw_out.at[related(s, m)], box_out, [0] + downs)
    sum_out.launch()

    for j in range(qcount):
        part = w_out_ref[pl.ds(j * width, width), :]
        grads[pl.ds(j * rows, rows), :] = contract_last(d_proj, part).astype(bf16)
        grads_t[:, pl.ds(j * rows, rows)] = contract_last(part, d_proj).astype(bf16)
    dots = jnp.sum(grads_t[...].astype(f32) * att_ref[...], axis=0, keepdims=True)
    start = start_ref[...]
    index = index_ref[...]
    log_total = log_ref[...]
    dq_t[...] = jnp.zeros_like(dq_t)

    def step(g, carry):
        keys = k_ref[g]
        queries = q_ref[...]
        scores = contract_last(keys, queries)
        key = g * span + lax.broadcasted_iota(jnp.int32, scores.shape, 0)
        probs = jnp.where((key >= start) & (key <= index), jnp.exp(scores - log_total), 0.0)
        d_probs = jnp.dot(v_ref[g], grads_t[...], preferred_element_type=f32)
        d_scores = (probs * (d_probs - dots)).astype(bf16)
        dv[g] = (
            jnp.dot(probs.astype(bf16), grads[...], preferred_element_type=f32)
            .astype(bf16)
            .reshape(dv.shape[1:])
        )
        dk[g] = (
            jnp.dot(d_scores, queries, preferred_element_type=f32)
            .astype(bf16)
            .reshape(dk.shape[1:])
        )
        dq_t[...] += contract_first(keys, d_scores)
        return carry

    lax.fori_loop(0, s + 1, step, 0)

    def blank(g, carry):
        dk[g] = jnp.zeros(dk.shape[1:], bf16)
        dv[g] = jnp.zeros(dv.shape[1:], bf16)
        return carry

    lax.fori_loop(s + 1, groups, blank, 0)
    sum_k = Sum(links, lambda m: dk.at[related(s, m)], box_k, [0] + ups)
    sum_v = Sum(links, lambda m: dv.at[related(s, m)], box_v, [0] + downs)
    sum_k.launch()
    sum_v.launch()

    for copy in kept_copies:
        copy.wait()
    gate, up, down = ffn
    gate.settle(gate.kept)
    gate.launch()
    up.settle(up.kept)
    up.launch()
    sum_k.settle()
    sum_k.launch()
    sum_v.settle()
    sum_v.launch()
    sum_out.settle()
    sum_out.launch()

    cosines, sines = cos_ref[...], sin_ref[...]
    d_gain_q = jnp.zeros((1, width), f32)
    for j in range(qcount):
        d_rot = dq_t[:, pl.ds(j * rows, rows)].T * scale
        d_lin, terms = back_norm(
            q_lin_ref[:, pl.ds(j * width, width)],
            gain_q_ref[...],
            back_rotate(d_rot, cosines, sines),
        )
        d_qkv[:, pl.ds(j * width, width)] = d_lin.astype(bf16)
        d_gain_q = d_gain_q + terms

    sum_k.settle()
    sum_k.launch()
    sum_v.settle()
    sum_v.launch()
    down.settle(down.kept)
    down.launch()
    heads_shape = dk.shape[2:]

    def over(total, zbox, shape):
        where = total.waiting[0][1]
        total.settle()
        return links.over_heads(total.boxes.at[where], zbox), total.boxes.at[where]

    z_k, own_k = over(sum_k, zbox_k, heads_shape)
    z_v, own_v = over(sum_v, zbox_v, heads_shape)
    sum_out.settle()
    sum_out.launch()

    def gathered(copies, zbox, own):
        total = own[h].astype(f32)
        for d, copy in enumerate(copies):
            copy.wait_recv()
            total = total + zbox[d].astype(f32)
        return total

    d_keys = gathered(z_k, zbox_k, own_k)
    d_values = gathered(z_v, zbox_v, own_v)
    d_lin, d_gain_k = back_norm(
        k_lin_ref[...], gain_k_ref[...], back_rotate(d_keys, cosines, sines)
    )
    qw = qcount * width
    d_qkv[:, pl.ds(qw, width)] = d_lin.astype(bf16)
    d_qkv[:, pl.ds(qw + width, width)] = d_values.astype(bf16)
    cut_at = dw_a.shape[2]

    def qkv_block(j, carry):
        dw_a[j] = jnp.dot(
            attn_t_ref[j], d_qkv[:, :cut_at], preferred_element_type=f32
        ).astype(bf16)
        dw_b[j] = jnp.dot(
            attn_t_ref[j], d_qkv[:, cut_at:], preferred_element_type=f32
        ).astype(bf16)
        return carry

    lax.fori_loop(0, nseq, qkv_block, 0)
    sum_a = Sum(links, lambda m: dw_a.at[related(s, m)], box_a, [0] + ups)
    sum_b = Sum(links, lambda m: dw_b.at[related(s, m)], box_b, [0] + downs)
    sum_a.launch()
    sum_b.launch()

    d_attn_in = contract_last(d_qkv[...], w_qkv_ref[...])
    d_x, d_gain_in = back_norm(x_ref[...].astype(f32), gain_in_ref[...], d_attn_in)
    o_tokens[...] = (d_hid_ref[...] + d_x).astype(o_tokens.dtype)

    gsum[0] = gains_ref[...]
    gsum[0, 0:1, :] = d_gain_in
    gsum[0, 4:5, :width] = d_gain_q
    gsum[0, 5:6, :width] = d_gain_k
    gain_copies = [links.go(gsum.at[0], gbox.at[0], links.across(0))]

    sum_a.settle()
    sum_a.launch()
    sum_b.settle()
    sum_b.launch()
    for bit in range(bits):
        gain_copies[-1].wait_recv()
        gsum[bit + 1] = gsum[bit] + gbox[bit]
        if bit + 1 < bits:
            gain_copies.append(
                links.go(gsum.at[bit + 1], gbox.at[bit + 1], links.across(bit + 1))
            )
    gain_z = [
        links.go(gsum.at[bits], gzbox.at[d], (s, o)) for d, o in enumerate(links.others)
    ]

    def pieces(total, zsrc, col, size):
        value = total.last()
        each = value.shape[0] // heads
        for p in range(heads):
            zsrc[p, :, pl.ds(col, size)] = value[p * each : (p + 1) * each].astype(bf16)

    pieces(sum_out, zsrc_out, 0, dw_out.shape[2])
    z_out = links.over_heads(zsrc_out, zbox_out)
    gate.settle()
    gate.launch()
    up.settle()
    up.launch()
    sum_a.settle()
    sum_a.launch()
    sum_b.settle()
    sum_b.launch()
    pieces(sum_a, zsrc_qkv, 0, cut_at)
    pieces(sum_b, zsrc_qkv, cut_at, dw_b.shape[2])
    z_qkv = links.over_heads(zsrc_qkv, zbox_qkv)
    down.settle()
    down.launch()
    o_gate[...] = gate.last()
    o_up[...] = up.last()
    total = gsum[bits]
    for d, copy in enumerate(gain_z):
        copy.wait_recv()
        total = total + gzbox[d]
    o_gains[...] = total
    o_out[...] = gathered(z_out, zbox_out, zsrc_out)
    o_qkv[...] = gathered(z_qkv, zbox_qkv, zsrc_qkv)
    o_down[...] = down.last()
    links.finish()


def tail(nseq, heads, qcount, scale, cid, *arrays):
    (q, k, v, _, _, _, att, mixed_t, d_proj, w_out, q_lin, k_lin, _, _, gain_q, _) = arrays[:16]
    (attn_t, w_qkv, x, gain_in, d_hid, gains, d_gate, d_up, d_down) = arrays[16:]
    f32, bf16 = jnp.float32, jnp.bfloat16
    rows, model = d_proj.shape
    width = gain_q.shape[1]
    cols = w_qkv.shape[1]
    cut_at = cols // 2
    out_rows, qkv_rows = mixed_t.shape[1], attn_t.shape[1]
    pieces_kv = (heads, rows, width)
    ffn_block = d_gate.shape[1:]
    some, all_but = nseq // 2, nseq - 1
    bits = nseq.bit_length() - 1
    copies = 8 * all_but + 5 * (heads - 1) + bits
    vm = pl.BlockSpec(memory_space=VMEM)
    anywhere = pl.BlockSpec(memory_space=pl.ANY)

    def kernel(*refs):
        tail_kernel(nseq, heads, qcount, scale, *refs)

    return pl.pallas_call(
        kernel,
        out_shape=[
            jax.ShapeDtypeStruct((rows, model), bf16),
            jax.ShapeDtypeStruct((qkv_rows // heads, cols), f32),
            jax.ShapeDtypeStruct((out_rows // heads, model), f32),
            jax.ShapeDtypeStruct(ffn_block, f32),
            jax.ShapeDtypeStruct(ffn_block, f32),
            jax.ShapeDtypeStruct(ffn_block, f32),
            jax.ShapeDtypeStruct(gains.shape, f32),
        ],
        in_specs=[vm] * (len(arrays) - 3) + [anywhere] * 3,
        out_specs=[vm] * 7,
        scratch_shapes=[
            VMEM((nseq,) + pieces_kv, bf16),
            VMEM((nseq,) + pieces_kv, bf16),
            VMEM((width, qcount * rows), f32),
            VMEM((qcount * rows, width), bf16),
            VMEM((width, qcount * rows), bf16),
            VMEM((all_but,) + pieces_kv, bf16),
            VMEM((all_but,) + pieces_kv, bf16),
            VMEM((heads - 1, rows, width), bf16),
            VMEM((heads - 1, rows, width), bf16),
            VMEM((nseq, out_rows, model), bf16),
            VMEM((all_but, out_rows, model), bf16),
            VMEM((heads, out_rows // heads, model), bf16),
            VMEM((heads - 1, out_rows // heads, model), bf16),
            VMEM((nseq, qkv_rows, cut_at), bf16),
            VMEM((nseq, qkv_rows, cols - cut_at), bf16),
            VMEM((all_but, qkv_rows, cut_at), bf16),
            VMEM((all_but, qkv_rows, cols - cut_at), bf16),
            VMEM((heads, qkv_rows // heads, cols), bf16),
            VMEM((heads - 1, qkv_rows // heads, cols), bf16),
            VMEM((rows, cols), bf16),
        ]
        + [VMEM((some,) + ffn_block, bf16)] * 3
        + [VMEM((all_but,) + ffn_block, bf16)] * 3
        + [
            VMEM((bits + 1,) + gains.shape, f32),
            VMEM((bits,) + gains.shape, f32),
            VMEM((heads - 1,) + gains.shape, f32),
            pltpu.SemaphoreType.DMA((copies,)),
            pltpu.SemaphoreType.DMA((copies,)),
            pltpu.SemaphoreType.DMA((3, some)),
        ],
        name="tail",
        compiler_params=pltpu.CompilerParams(
            collective_id=cid, has_side_effects=True, vmem_limit_bytes=62 * 2**20
        ),
    )(*arrays)


def local(
    tokens,
    segment_ids,
    w_query,
    w_key,
    w_value,
    w_out,
    w_gate,
    w_up,
    w_down,
    gain_attn_in,
    gain_attn_out,
    gain_ffn_in,
    gain_ffn_out,
    gain_query,
    gain_key,
    cotangent,
):
    heads = lax.axis_size("head")
    nseq = lax.axis_size("seq")
    head_index = lax.axis_index("head")
    seq_index = lax.axis_index("seq")
    bits = nseq.bit_length() - 1
    local_rows, model = tokens.shape
    width = gain_query.shape[0]
    qcount = w_query.shape[1] // width
    group = local_rows * heads
    total = segment_ids.shape[0]
    hidden_units = w_gate.shape[1]
    scale = 1.0 / math.sqrt(width)
    bf16 = jnp.bfloat16
    first_row = (seq_index * heads + head_index) * local_rows
    my_index = first_row + jnp.arange(local_rows, dtype=jnp.int32)
    my_ids = lax.dynamic_slice_in_dim(segment_ids, first_row, local_rows)
    my_starts = jnp.min(
        jnp.where(
            my_ids[:, None] == segment_ids[None, :],
            jnp.arange(total, dtype=jnp.int32)[None, :],
            total,
        ),
        axis=1,
    )
    cosines, sines = rope_tables(my_index - my_starts, width)

    def query_path(linear, gain):
        shaped = linear.reshape(local_rows, qcount, width)
        turned = rotate(norm_rows(shaped, gain), cosines[:, None, :], sines[:, None, :])
        return turned.reshape(local_rows, qcount * width)

    def key_path(linear, gain):
        return rotate(norm_rows(linear, gain), cosines, sines)

    def gated(gate, up):
        return jax.nn.gelu(gate, approximate=True) * up

    def stacked(v):
        return v.reshape(local_rows, qcount, width).transpose(1, 0, 2).reshape(-1, width)

    def unstacked(v):
        return v.reshape(qcount, local_rows, width).transpose(1, 0, 2).reshape(local_rows, -1)

    inputs = tokens.astype(jnp.float32)
    attn_in = norm_rows(inputs, gain_attn_in).astype(bf16)
    k_linear = jnp.dot(attn_in, w_key, preferred_element_type=jnp.float32)
    keys_local = key_path(k_linear, gain_key).astype(bf16)
    values_local = jnp.dot(attn_in, w_value, preferred_element_type=jnp.float32).astype(bf16)
    q_linear = jnp.dot(attn_in, w_query, preferred_element_type=jnp.float32)
    queries_local = query_path(q_linear, gain_query).astype(bf16)
    queries = stacked(queries_local) * jnp.asarray(scale, bf16)
    keys, values = gather_all([keys_local, values_local], nseq, heads, 1)
    keys = keys.reshape(nseq, group, width)
    values = values.reshape(nseq, group, width)
    starts = jnp.tile(my_starts, qcount)[None, :]
    index = jnp.tile(my_index, qcount)[None, :]
    attended_t, log_total = attend(queries, keys, values, starts, index)
    attended = attended_t.T
    mixed_local = unstacked(attended.astype(bf16))
    projected = jnp.dot(mixed_local, w_out, preferred_element_type=jnp.float32)
    hidden = inputs + norm_rows(projected, gain_attn_out)
    ffn_in = norm_rows(hidden, gain_ffn_in).astype(bf16)
    ffn_rows = line_gather(ffn_in, heads, 2).reshape(group, model)
    gate = jnp.dot(ffn_rows, w_gate, preferred_element_type=jnp.float32)
    up = jnp.dot(ffn_rows, w_up, preferred_element_type=jnp.float32)
    activated = gated(gate, up).astype(bf16)
    ffn_out = line_scatter(
        jnp.dot(activated, w_down, preferred_element_type=jnp.float32)
        .astype(bf16)
        .reshape(heads, local_rows, model),
        heads,
        3,
    )
    output = hidden + norm_rows(ffn_out, gain_ffn_out)
    upstream = cotangent.astype(jnp.float32)
    unused, back_four = jax.vjp(norm_rows, ffn_out, gain_ffn_out)
    d_ffn_out, d_gain_four = back_four(upstream)
    d_ffn_rows = line_gather(d_ffn_out.astype(bf16), heads, 4).reshape(group, model)
    d_activated = contract_last(d_ffn_rows, w_down)
    d_w_down = contract_first(d_ffn_rows, activated)
    unused, back_gate = jax.vjp(gated, gate, up)
    d_gate, d_up = back_gate(d_activated)
    d_gate = d_gate.astype(bf16)
    d_up = d_up.astype(bf16)
    d_ffn_in = line_scatter(
        (contract_last(d_gate, w_gate) + contract_last(d_up, w_up))
        .astype(bf16)
        .reshape(heads, local_rows, model),
        heads,
        5,
    )
    d_w_gate = contract_first(ffn_rows, d_gate)
    d_w_up = contract_first(ffn_rows, d_up)
    unused, back_three = jax.vjp(norm_rows, hidden, gain_ffn_in)
    d_hidden_part, d_gain_three = back_three(d_ffn_in)
    d_hidden = upstream + d_hidden_part
    unused, back_two = jax.vjp(norm_rows, projected, gain_attn_out)
    d_projected, d_gain_two = back_two(d_hidden)
    d_projected = d_projected.astype(bf16)
    qw = qcount * width
    each, few = model // (nseq * heads), width // (nseq * heads)
    if nseq <= 8:
        gains = jnp.concatenate(
            [
                jnp.zeros((1, model), jnp.float32),
                d_gain_two[None],
                d_gain_three[None],
                d_gain_four[None],
                jnp.zeros((4, model), jnp.float32),
            ]
        )
        w_qkv = jnp.concatenate([w_query, w_key, w_value], axis=1)
        blocks = [
            d.astype(bf16).reshape(nseq, model // nseq, hidden_units)
            for d in (d_w_gate, d_w_up, d_w_down)
        ]
        grad_tokens, sum_qkv, sum_out, sum_gate, sum_up, sum_down, sum_gains = tail(
            nseq,
            heads,
            qcount,
            scale,
            9,
            queries,
            keys,
            values,
            starts,
            index,
            log_total,
            attended_t,
            mixed_local.T.reshape(nseq, -1, local_rows),
            d_projected,
            w_out,
            q_linear,
            k_linear,
            cosines,
            sines,
            gain_query[None],
            gain_key[None],
            attn_in.T.reshape(nseq, -1, local_rows),
            w_qkv,
            tokens,
            gain_attn_in[None],
            d_hidden,
            gains,
            *blocks,
        )
        which = seq_index * heads + head_index
        wide = lax.dynamic_slice_in_dim(sum_gains[:4], which * each, each, 1)
        narrow = lax.dynamic_slice_in_dim(sum_gains[4:6], which * few, few, 1)
        return (
            output.astype(bf16),
            grad_tokens,
            sum_qkv[:, :qw],
            sum_qkv[:, qw : qw + width],
            sum_qkv[:, qw + width :],
            sum_out,
            sum_gate,
            sum_up,
            sum_down.T,
            wide[0],
            wide[1],
            wide[2],
            wide[3],
            narrow[0],
            narrow[1],
        )
    d_w_out = contract_first(mixed_local, d_projected)
    d_mixed = contract_last(d_projected, w_out).astype(bf16)
    grad_attended = stacked(d_mixed)
    row_dots = jnp.sum(grad_attended.astype(jnp.float32) * attended, axis=1)[None, :]
    d_queries_t, d_keys, d_values = attend_back(
        queries, keys, values, starts, index, log_total, row_dots, grad_attended
    )
    shape = (nseq, heads, local_rows, width)
    ups, downs = seq_orders(bits)
    d_keys, d_values = scatter_all(
        [d_keys.reshape(shape), d_values.reshape(shape)],
        [True, True],
        [[0] + ups, [0] + downs],
        nseq,
        heads,
        6,
        "scatter_keys",
    )
    d_query_rot = unstacked((d_queries_t.T * scale).astype(bf16)).astype(jnp.float32)
    unused, back_query = jax.vjp(query_path, q_linear, gain_query)
    d_q_linear, d_gain_query = back_query(d_query_rot)
    unused, back_key = jax.vjp(key_path, k_linear, gain_key)
    d_k_linear, d_gain_key = back_key(d_keys)
    d_qkv = jnp.concatenate([d_q_linear, d_k_linear, d_values], axis=1).astype(bf16)
    qw = qcount * width
    d_w_qkv = contract_first(attn_in, d_qkv)
    d_attn_in = (
        contract_last(d_qkv[:, :qw], w_query)
        + contract_last(d_qkv[:, qw : qw + width], w_key)
        + contract_last(d_qkv[:, qw + width :], w_value)
    )
    unused, back_one = jax.vjp(norm_rows, inputs, gain_attn_in)
    d_inputs, d_gain_one = back_one(d_attn_in)
    grad_tokens = (d_hidden + d_inputs).astype(bf16)

    def cut(v):
        return v.reshape(nseq, heads, -1)

    wide = jnp.stack([cut(d_gain_one), cut(d_gain_two), cut(d_gain_three), cut(d_gain_four)], 2)
    narrow = jnp.stack([cut(d_gain_query), cut(d_gain_key)], 2)
    each, few = wide.shape[-1], narrow.shape[-1]
    gains = jnp.concatenate(
        [
            jnp.pad(wide, ((0, 0), (0, 0), (0, 0), (0, 128 - each))),
            jnp.pad(narrow, ((0, 0), (0, 0), (0, 2), (0, 128 - few))),
        ],
        axis=2,
    )
    sum_qkv, sum_out, sum_gains = scatter_all(
        [
            d_w_qkv.astype(bf16).reshape(nseq, heads, -1, d_qkv.shape[1]),
            d_w_out.astype(bf16).reshape(nseq, heads, -1, model),
            gains,
        ],
        [True, True, True],
        [[0] + ups, [0] + downs, [0] + downs],
        nseq,
        heads,
        7,
        "scatter_attn",
    )
    sum_gate, sum_up, sum_down = scatter_all(
        [
            d.astype(bf16).reshape(nseq, model // nseq, hidden_units)
            for d in (d_w_gate, d_w_up, d_w_down)
        ],
        [False, False, False],
        [[0] + ups, [0] + downs, [0] + ups],
        nseq,
        heads,
        8,
        "scatter_ffn",
    )
    return (
        output.astype(bf16),
        grad_tokens,
        sum_qkv[:, :qw],
        sum_qkv[:, qw : qw + width],
        sum_qkv[:, qw + width :],
        sum_out,
        sum_gate,
        sum_up,
        sum_down.T,
        sum_gains[0, :each],
        sum_gains[1, :each],
        sum_gains[2, :each],
        sum_gains[3, :each],
        sum_gains[4, :few],
        sum_gains[5, :few],
    )


def solution(mesh):
    rows = P(("seq", "head"), None)
    in_specs = (
        rows,
        P(),
        P(),
        P(),
        P(),
        P(),
        P(None, "head"),
        P(None, "head"),
        P("head", None),
        P(),
        P(),
        P(),
        P(),
        P(),
        P(),
        rows,
    )
    out_specs = (
        rows,
        rows,
        rows,
        rows,
        rows,
        rows,
        P("seq", "head"),
        P("seq", "head"),
        P("head", "seq"),
    ) + (P(("seq", "head")),) * 6
    return jax.shard_map(local, mesh=mesh, in_specs=in_specs, out_specs=out_specs, check_vma=False)
```

```python
import functools
import math

import jax
import jax.numpy as jnp
from jax import lax
from jax.experimental import pallas as pl
from jax.experimental.pallas import tpu as pltpu
from jax.sharding import PartitionSpec as P

EPS = 1e-06
MESH = pl.DeviceIdType.MESH
VMEM = pltpu.VMEM
LIMIT = 56 * 2**20


def norm_rows(v, gain):
    return v * lax.rsqrt(jnp.mean(v * v, axis=-1, keepdims=True) + EPS) * gain


def rotate(v, cosines, sines):
    half = v.shape[-1] // 2
    first = v[..., :half]
    second = v[..., half:]
    return jnp.concatenate(
        [first * cosines - second * sines, second * cosines + first * sines], axis=-1
    )


def rope_tables(positions, width):
    half = width // 2
    freq = jnp.exp(jnp.arange(half, dtype=jnp.float32) * (-2.0 * math.log(1000000.0) / width))
    angle = positions.astype(jnp.float32)[:, None] * freq[None, :]
    return (jnp.cos(angle), jnp.sin(angle))


def contract_first(left, right):
    return lax.dot_general(
        left, right, (((0,), (0,)), ((), ())), preferred_element_type=jnp.float32
    )


def contract_last(left, right):
    return lax.dot_general(
        left, right, (((1,), (1,)), ((), ())), preferred_element_type=jnp.float32
    )


def place():
    return lax.axis_index("seq"), lax.axis_index("head")


def related(s, mask):
    out = s
    bit = 0
    while mask >> bit:
        if (mask >> bit) & 1:
            step = 1 << bit
            out = out + (1 - 2 * ((s // step) % 2)) * step
        bit += 1
    return out


def subsets(bits):
    out = [0]
    for bit in bits:
        out = out + [m | (1 << bit) for m in out]
    return out


def greet(targets):
    barrier = pltpu.get_barrier_semaphore()
    for target in targets:
        pl.semaphore_signal(barrier, inc=1, device_id=target, device_id_type=MESH)
    pl.semaphore_wait(barrier, len(targets))


def remote(src, dst, send, recv, target):
    return pltpu.make_async_remote_copy(
        src_ref=src,
        dst_ref=dst,
        send_sem=send,
        recv_sem=recv,
        device_id=target,
        device_id_type=MESH,
    )


def seq_orders(bits):
    upper = list(range(1, bits))
    return upper, upper[::-1]


def gather_kernel(nseq, heads, local_refs, out_refs, send, recv):
    bits = nseq.bit_length() - 1
    s, h = place()
    others = [lax.rem(h + d, heads) for d in range(1, heads)]
    greet([(related(s, 1 << b), h) for b in range(bits)] + [(s, o) for o in others])
    count = [0]
    started = []

    def go(src, dst, target):
        k = count[0]
        count[0] += 1
        copy = remote(src, dst, send.at[k], recv.at[k], target)
        copy.start()
        started.append(copy)
        return copy

    first = []
    for a in range(len(out_refs)):
        out_refs[a][s, h] = local_refs[a][...]
        first.append(
            [go(local_refs[a], out_refs[a].at[s, h], (s, o)) for o in others]
        )
    orders = [o + [0] for o in seq_orders(bits)]
    held = [{0: first[a]} for a in range(len(out_refs))]
    for stage in range(bits):
        for a in range(len(out_refs)):
            bit = orders[a % 2][stage]
            target = (related(s, 1 << bit), h)
            arrived = {}
            for mask in list(held[a]):
                for copy in held[a][mask]:
                    copy.wait_recv()
                held[a][mask] = []
                group = related(s, mask)
                copy = go(out_refs[a].at[group], out_refs[a].at[group], target)
                arrived[mask | (1 << bit)] = [copy]
            held[a].update(arrived)
    for a in range(len(out_refs)):
        for mask in held[a]:
            for copy in held[a][mask]:
                copy.wait_recv()
    for copy in started:
        copy.wait_send()


def gather_all(arrays, nseq, heads, cid):
    n = len(arrays)
    total = n * (heads - 1 + nseq - 1)

    def kernel(*refs):
        gather_kernel(nseq, heads, refs[:n], refs[n : 2 * n], refs[2 * n], refs[2 * n + 1])

    return pl.pallas_call(
        kernel,
        out_shape=[jax.ShapeDtypeStruct((nseq, heads) + a.shape, a.dtype) for a in arrays],
        in_specs=[pl.BlockSpec(memory_space=VMEM)] * n,
        out_specs=[pl.BlockSpec(memory_space=VMEM)] * n,
        scratch_shapes=[pltpu.SemaphoreType.DMA((total,)), pltpu.SemaphoreType.DMA((total,))],
        name="gather_all",
        compiler_params=pltpu.CompilerParams(
            collective_id=cid, has_side_effects=True, vmem_limit_bytes=LIMIT
        ),
    )(*arrays)


def line_gather_kernel(heads, x_ref, out_ref, send, recv):
    s, h = place()
    right = (s, lax.rem(h + 1, heads))
    left = (s, lax.rem(h + heads - 1, heads))
    greet([right, left])
    out_ref[h] = x_ref[...]
    for step in range(heads - 1):
        to_right = remote(
            out_ref.at[jnp.maximum(h - step, 0)],
            out_ref.at[jnp.maximum(h - step, 0)],
            send.at[0, step],
            recv.at[0, step],
            right,
        )
        to_left = remote(
            out_ref.at[jnp.minimum(h + step, heads - 1)],
            out_ref.at[jnp.minimum(h + step, heads - 1)],
            send.at[1, step],
            recv.at[1, step],
            left,
        )
        pl.when((h - step >= 0) & (h < heads - 1))(to_right.start)
        pl.when((h + step <= heads - 1) & (h > 0))(to_left.start)
        pl.when(h - 1 - step >= 0)(
            remote(
                out_ref.at[jnp.maximum(h - 1 - step, 0)],
                out_ref.at[jnp.maximum(h - 1 - step, 0)],
                send.at[0, step],
                recv.at[0, step],
                right,
            ).wait_recv
        )
        pl.when(h + 1 + step <= heads - 1)(
            remote(
                out_ref.at[jnp.minimum(h + 1 + step, heads - 1)],
                out_ref.at[jnp.minimum(h + 1 + step, heads - 1)],
                send.at[1, step],
                recv.at[1, step],
                left,
            ).wait_recv
        )
        pl.when((h - step >= 0) & (h < heads - 1))(to_right.wait_send)
        pl.when((h + step <= heads - 1) & (h > 0))(to_left.wait_send)


def line_gather(x, heads, cid):
    return pl.pallas_call(
        functools.partial(line_gather_kernel, heads),
        out_shape=jax.ShapeDtypeStruct((heads,) + x.shape, x.dtype),
        in_specs=[pl.BlockSpec(memory_space=VMEM)],
        out_specs=pl.BlockSpec(memory_space=VMEM),
        scratch_shapes=[
            pltpu.SemaphoreType.DMA((2, heads - 1)),
            pltpu.SemaphoreType.DMA((2, heads - 1)),
        ],
        name="line_gather",
        compiler_params=pltpu.CompilerParams(
            collective_id=cid, has_side_effects=True, vmem_limit_bytes=LIMIT
        ),
    )(x)


def line_scatter_kernel(heads, parts, out_ref, from_left, from_right, send, recv):
    s, h = place()
    last = heads - 1
    right = (s, lax.rem(h + 1, heads))
    left = (s, lax.rem(h + heads - 1, heads))
    greet([right, left])
    f32 = jnp.float32
    for step in range(heads - 1):
        r_dest = jnp.clip(last - (step - h), 0, last)
        l_dest = jnp.clip(step - (last - h), 0, last)
        r_on = (step >= h) & (h < last)
        l_on = (step >= last - h) & (h > 0)
        for on, dest, box, lane, target, first in (
            (r_on, r_dest, from_left, 0, right, step == h),
            (l_on, l_dest, from_right, 1, left, step == last - h),
        ):
            at_end = (h == 0) if lane == 0 else (h == last)
            if step > 0:

                def add(box=box, dest=dest):
                    box[step - 1] = (
                        box[step - 1].astype(f32) + parts[dest].astype(f32)
                    ).astype(box.dtype)

                pl.when(on & jnp.logical_not(at_end))(add)
                pl.when(on & jnp.logical_not(at_end))(
                    remote(
                        box.at[step - 1], box.at[step], send.at[lane, step], recv.at[lane, step], target
                    ).start
                )
            pl.when(on & at_end)(
                remote(
                    parts.at[dest], box.at[step], send.at[lane, step], recv.at[lane, step], target
                ).start
            )
        r_in = (step >= h - 1) & (h > 0)
        l_in = (step >= last - h - 1) & (h < last)
        pl.when(r_in)(
            remote(
                from_left.at[step], from_left.at[step], send.at[0, step], recv.at[0, step], right
            ).wait_recv
        )
        pl.when(l_in)(
            remote(
                from_right.at[step], from_right.at[step], send.at[1, step], recv.at[1, step], left
            ).wait_recv
        )
    for step in range(heads - 1):
        for on, box, lane, target in (
            ((step >= h) & (h < last), from_left, 0, right),
            ((step >= last - h) & (h > 0), from_right, 1, left),
        ):
            pl.when(on)(
                remote(
                    box.at[step], box.at[step], send.at[lane, step], recv.at[lane, step], target
                ).wait_send
            )
    out_ref[...] = parts[h].astype(f32)

    def add_left():
        out_ref[...] += from_left[heads - 2].astype(f32)

    def add_right():
        out_ref[...] += from_right[heads - 2].astype(f32)

    pl.when(h > 0)(add_left)
    pl.when(h < last)(add_right)


def line_scatter(parts, heads, cid):
    block = parts.shape[1:]
    return pl.pallas_call(
        functools.partial(line_scatter_kernel, heads),
        out_shape=jax.ShapeDtypeStruct(block, jnp.float32),
        in_specs=[pl.BlockSpec(memory_space=VMEM)],
        out_specs=pl.BlockSpec(memory_space=VMEM),
        scratch_shapes=[
            VMEM((heads - 1,) + block, parts.dtype),
            VMEM((heads - 1,) + block, parts.dtype),
            pltpu.SemaphoreType.DMA((2, heads - 1)),
            pltpu.SemaphoreType.DMA((2, heads - 1)),
        ],
        name="line_scatter",
        compiler_params=pltpu.CompilerParams(
            collective_id=cid, has_side_effects=True, vmem_limit_bytes=LIMIT
        ),
    )(parts)


def scatter_kernel(nseq, heads, zs, orders, parts, outs, boxes, zboxes, send, recv):
    bits = nseq.bit_length() - 1
    s, h = place()
    f32 = jnp.float32
    others = [lax.rem(h + d, heads) for d in range(1, heads)]
    greet(
        [(related(s, 1 << b), h) for b in range(bits)]
        + ([(s, o) for o in others] if any(zs) else [])
    )
    count = [0]
    started = []

    def go(src, dst, target):
        k = count[0]
        count[0] += 1
        copy = remote(src, dst, send.at[k], recv.at[k], target)
        copy.start()
        started.append(copy)
        return copy

    n = len(parts)
    offsets = [0] * n
    slot = [{} for _ in range(n)]
    waiting = [{} for _ in range(n)]

    def current(a, mask):
        if mask in slot[a]:
            return boxes[a].at[slot[a][mask]]
        return parts[a].at[related(s, mask)]

    def launch(a, stage):
        bit = orders[a][stage]
        rest = orders[a][stage + 1 :]
        target = (related(s, 1 << bit), h)
        after = 1 << rest[0] if rest else 0
        masks = sorted(subsets(rest), key=lambda m: 0 if m & after else 1)
        for mask in masks:
            where = offsets[a]
            offsets[a] += 1
            waiting[a][mask] = (
                go(current(a, mask | (1 << bit)), boxes[a].at[where], target),
                where,
            )

    def settle(a, mask):
        copy, where = waiting[a].pop(mask)
        mine = current(a, mask)
        copy.wait_recv()
        boxes[a][where] = (boxes[a][where].astype(f32) + mine[...].astype(f32)).astype(
            boxes[a].dtype
        )
        slot[a][mask] = where

    for a in range(n):
        launch(a, 0)
    for stage in range(bits):
        for a in range(n):
            for mask in list(waiting[a]):
                settle(a, mask)
            if stage + 1 < bits:
                launch(a, stage + 1)
    arriving = []
    for a in range(n):
        if not zs[a]:
            continue
        mine = current(a, 0)
        arriving.append(
            [
                go(mine.at[o], zboxes[a].at[d], (s, o))
                for d, o in enumerate(others)
            ]
        )
    z = 0
    for a in range(n):
        if zs[a]:
            total = current(a, 0)[h].astype(f32)
            for d, copy in enumerate(arriving[z]):
                copy.wait_recv()
                total = total + zboxes[a][d].astype(f32)
            outs[a][...] = total
            z += 1
        else:
            outs[a][...] = current(a, 0)[...].astype(f32)
    for copy in started:
        copy.wait_send()


def scatter_all(arrays, zs, orders, nseq, heads, cid, name):
    n = len(arrays)
    total = sum((nseq - 1) + (heads - 1 if z else 0) for z in zs)
    blocks = [a.shape[2:] if z else a.shape[1:] for a, z in zip(arrays, zs)]

    def kernel(*refs):
        scatter_kernel(
            nseq,
            heads,
            zs,
            orders,
            refs[:n],
            refs[n : 2 * n],
            refs[2 * n : 3 * n],
            refs[3 * n : 4 * n],
            refs[4 * n],
            refs[4 * n + 1],
        )

    return pl.pallas_call(
        kernel,
        out_shape=[jax.ShapeDtypeStruct(b, jnp.float32) for b in blocks],
        in_specs=[pl.BlockSpec(memory_space=VMEM)] * n,
        out_specs=[pl.BlockSpec(memory_space=VMEM)] * n,
        scratch_shapes=[VMEM((nseq - 1,) + a.shape[1:], a.dtype) for a in arrays]
        + [
            VMEM((heads - 1,) + b, a.dtype) if z else VMEM((8, 128), jnp.float32)
            for a, b, z in zip(arrays, blocks, zs)
        ]
        + [pltpu.SemaphoreType.DMA((total,)), pltpu.SemaphoreType.DMA((total,))],
        name=name,
        compiler_params=pltpu.CompilerParams(
            collective_id=cid, has_side_effects=True, vmem_limit_bytes=LIMIT
        ),
    )(*arrays)


def attend_kernel(q_ref, k_ref, v_ref, start_ref, index_ref, out_ref, log_ref):
    s = lax.axis_index("seq")
    span = k_ref.shape[1]
    start = start_ref[...]
    index = index_ref[...]
    queries = q_ref[...]
    rows = queries.shape[0]
    out_ref[...] = jnp.zeros_like(out_ref)

    def step(g, mass):
        scores = contract_last(k_ref[g], queries)
        key = g * span + lax.broadcasted_iota(jnp.int32, (span, rows), 0)
        terms = jnp.where((key >= start) & (key <= index), jnp.exp(scores), 0.0)
        out_ref[...] += contract_first(v_ref[g], terms.astype(jnp.bfloat16))
        return mass + jnp.sum(terms, axis=0, keepdims=True)

    mass = lax.fori_loop(0, s + 1, step, jnp.zeros((1, rows), jnp.float32))
    out_ref[...] = out_ref[...] / mass
    log_ref[...] = jnp.log(mass)


def attend(q, k, v, start, index):
    rows, width = q.shape
    return pl.pallas_call(
        attend_kernel,
        out_shape=[
            jax.ShapeDtypeStruct((width, rows), jnp.float32),
            jax.ShapeDtypeStruct((1, rows), jnp.float32),
        ],
        in_specs=[pl.BlockSpec(memory_space=VMEM)] * 5,
        out_specs=[pl.BlockSpec(memory_space=VMEM)] * 2,
        name="attend",
        compiler_params=pltpu.CompilerParams(vmem_limit_bytes=LIMIT),
    )(q, k, v, start, index)


def attend_back_kernel(
    q_ref, k_ref, v_ref, start_ref, index_ref, log_ref, dots_ref, d_ref, dq_ref, dk_ref, dv_ref
):
    s = lax.axis_index("seq")
    groups, span = k_ref.shape[:2]
    start = start_ref[...]
    index = index_ref[...]
    log_total = log_ref[...]
    dots = dots_ref[...]
    queries = q_ref[...]
    grads = d_ref[...]
    rows = queries.shape[0]
    dq_ref[...] = jnp.zeros_like(dq_ref)

    def step(g, carry):
        keys = k_ref[g]
        scores = contract_last(keys, queries)
        key = g * span + lax.broadcasted_iota(jnp.int32, (span, rows), 0)
        probs = jnp.where((key >= start) & (key <= index), jnp.exp(scores - log_total), 0.0)
        d_probs = contract_last(v_ref[g], grads)
        d_scores = (probs * (d_probs - dots)).astype(jnp.bfloat16)
        dv_ref[g] = jnp.dot(
            probs.astype(jnp.bfloat16), grads, preferred_element_type=jnp.float32
        ).astype(dv_ref.dtype)
        dk_ref[g] = jnp.dot(d_scores, queries, preferred_element_type=jnp.float32).astype(
            dk_ref.dtype
        )
        dq_ref[...] += contract_first(keys, d_scores)
        return carry

    lax.fori_loop(0, s + 1, step, 0)

    def blank(g, carry):
        dk_ref[g] = jnp.zeros(dk_ref.shape[1:], dk_ref.dtype)
        dv_ref[g] = jnp.zeros(dv_ref.shape[1:], dv_ref.dtype)
        return carry

    lax.fori_loop(s + 1, groups, blank, 0)


def attend_back(q, k, v, start, index, log_total, dots, grads):
    rows, width = q.shape
    return pl.pallas_call(
        attend_back_kernel,
        out_shape=[
            jax.ShapeDtypeStruct((width, rows), jnp.float32),
            jax.ShapeDtypeStruct(k.shape, jnp.bfloat16),
            jax.ShapeDtypeStruct(v.shape, jnp.bfloat16),
        ],
        in_specs=[pl.BlockSpec(memory_space=VMEM)] * 8,
        out_specs=[pl.BlockSpec(memory_space=VMEM)] * 3,
        name="attend_back",
        compiler_params=pltpu.CompilerParams(vmem_limit_bytes=LIMIT),
    )(q, k, v, start, index, log_total, dots, grads)


class Sum:
    def __init__(self, links, part, boxes, order):
        self.links, self.part, self.boxes, self.order = links, part, boxes, order
        self.stage = 0
        self.used = 0
        self.slot = {}
        self.waiting = {}

    def current(self, mask):
        if mask in self.slot:
            return self.boxes.at[self.slot[mask]]
        return self.part(mask)

    def launch(self):
        bit = self.order[self.stage]
        rest = self.order[self.stage + 1 :]
        target = self.links.across(bit)
        after = 1 << rest[0] if rest else 0
        for mask in sorted(subsets(rest), key=lambda m: 0 if m & after else 1):
            where = self.used
            self.used += 1
            copy = self.links.go(self.current(mask | (1 << bit)), self.boxes.at[where], target)
            self.waiting[mask] = (copy, where)
        self.stage += 1

    def settle(self, kept=None):
        for mask in list(self.waiting):
            copy, where = self.waiting.pop(mask)
            mine = kept(mask) if kept is not None else self.current(mask)
            copy.wait_recv()
            self.boxes[where] = self.boxes[where] + mine[...]
            self.slot[mask] = where

    def last(self, kept=None):
        ((mask, (copy, where)),) = self.waiting.items()
        self.waiting = {}
        mine = kept(mask) if kept is not None else self.current(mask)
        copy.wait_recv()
        return self.boxes[where].astype(jnp.float32) + mine[...].astype(jnp.float32)


class Links:
    def __init__(self, nseq, heads, send, recv):
        self.s, self.h = place()
        self.nseq, self.heads = nseq, heads
        self.send, self.recv = send, recv
        self.count = 0
        self.started = []
        self.others = [lax.rem(self.h + d, heads) for d in range(1, heads)]

    def greet(self):
        bits = self.nseq.bit_length() - 1
        greet([self.across(b) for b in range(bits)] + [(self.s, o) for o in self.others])

    def across(self, bit):
        return (related(self.s, 1 << bit), self.h)

    def go(self, src, dst, target):
        k = self.count
        self.count += 1
        copy = remote(src, dst, self.send.at[k], self.recv.at[k], target)
        copy.start()
        self.started.append(copy)
        return copy

    def over_heads(self, src, boxes):
        return [self.go(src.at[o], boxes.at[d], (self.s, o)) for d, o in enumerate(self.others)]

    def finish(self):
        for copy in self.started:
            copy.wait_send()


def back_norm(v, gain, d_out):
    scale = lax.rsqrt(jnp.mean(v * v, axis=-1, keepdims=True) + EPS)
    unit = v * scale
    inner = d_out * gain
    d_v = scale * (inner - unit * jnp.mean(inner * unit, axis=-1, keepdims=True))
    return d_v, jnp.sum(d_out * unit, axis=0, keepdims=True)


def back_rotate(d, cosines, sines):
    half = d.shape[-1] // 2
    first, second = d[:, :half], d[:, half:]
    return jnp.concatenate(
        [first * cosines + second * sines, second * cosines - first * sines], axis=-1
    )


def tail_kernel(
    nseq,
    heads,
    qcount,
    scale,
    q_ref,
    k_ref,
    v_ref,
    start_ref,
    index_ref,
    log_ref,
    att_ref,
    mixed_t_ref,
    d_proj_ref,
    w_out_ref,
    q_lin_ref,
    k_lin_ref,
    cos_ref,
    sin_ref,
    gain_q_ref,
    gain_k_ref,
    attn_t_ref,
    w_qkv_ref,
    x_ref,
    gain_in_ref,
    d_hid_ref,
    gains_ref,
    d_gate_ref,
    d_up_ref,
    d_down_ref,
    o_tokens,
    o_qkv,
    o_out,
    o_gate,
    o_up,
    o_down,
    o_gains,
    dk,
    dv,
    dq_t,
    grads,
    grads_t,
    box_k,
    box_v,
    zbox_k,
    zbox_v,
    dw_out,
    box_out,
    zsrc_out,
    zbox_out,
    dw_a,
    dw_b,
    box_a,
    box_b,
    zsrc_qkv,
    zbox_qkv,
    d_qkv,
    keep_gate,
    keep_up,
    keep_down,
    box_gate,
    box_up,
    box_down,
    gsum,
    gbox,
    gzbox,
    send,
    recv,
    local_sem,
):
    f32, bf16 = jnp.float32, jnp.bfloat16
    bits = nseq.bit_length() - 1
    ups, downs = seq_orders(bits)
    links = Links(nseq, heads, send, recv)
    s, h = links.s, links.h
    rows = d_proj_ref.shape[0]
    width = gain_q_ref.shape[1]
    groups, span = k_ref.shape[:2]
    links.greet()

    ffn = []
    kept_copies = []
    kept_masks = subsets(ups)
    for n, (src, keep, box, order) in enumerate(
        (
            (d_gate_ref, keep_gate, box_gate, ups),
            (d_up_ref, keep_up, box_up, downs),
            (d_down_ref, keep_down, box_down, ups),
        )
    ):
        total = Sum(links, lambda m, src=src: src.at[related(s, m)], box, [0] + order)
        total.launch()
        total.kept = lambda m, keep=keep: keep.at[kept_masks.index(m)]
        ffn.append(total)
        for i, m in enumerate(kept_masks):
            copy = pltpu.make_async_copy(src.at[related(s, m)], keep.at[i], local_sem.at[n, i])
            copy.start()
            kept_copies.append(copy)

    d_proj = d_proj_ref[...]

    def out_block(j, carry):
        dw_out[j] = jnp.dot(mixed_t_ref[j], d_proj, preferred_element_type=f32).astype(bf16)
        return carry

    lax.fori_loop(0, nseq, out_block, 0)
    sum_out = Sum(links, lambda m: dw_out.at[related(s, m)], box_out, [0] + downs)
    sum_out.launch()

    for j in range(qcount):
        part = w_out_ref[pl.ds(j * width, width), :]
        grads[pl.ds(j * rows, rows), :] = contract_last(d_proj, part).astype(bf16)
        grads_t[:, pl.ds(j * rows, rows)] = contract_last(part, d_proj).astype(bf16)
    dots = jnp.sum(grads_t[...].astype(f32) * att_ref[...], axis=0, keepdims=True)
    start = start_ref[...]
    index = index_ref[...]
    log_total = log_ref[...]
    dq_t[...] = jnp.zeros_like(dq_t)

    def step(g, carry):
        keys = k_ref[g]
        queries = q_ref[...]
        scores = contract_last(keys, queries)
        key = g * span + lax.broadcasted_iota(jnp.int32, scores.shape, 0)
        probs = jnp.where((key >= start) & (key <= index), jnp.exp(scores - log_total), 0.0)
        d_probs = jnp.dot(v_ref[g], grads_t[...], preferred_element_type=f32)
        d_scores = (probs * (d_probs - dots)).astype(bf16)
        dv[g] = (
            jnp.dot(probs.astype(bf16), grads[...], preferred_element_type=f32)
            .astype(bf16)
            .reshape(dv.shape[1:])
        )
        dk[g] = (
            jnp.dot(d_scores, queries, preferred_element_type=f32)
            .astype(bf16)
            .reshape(dk.shape[1:])
        )
        dq_t[...] += contract_first(keys, d_scores)
        return carry

    lax.fori_loop(0, s + 1, step, 0)

    def blank(g, carry):
        dk[g] = jnp.zeros(dk.shape[1:], bf16)
        dv[g] = jnp.zeros(dv.shape[1:], bf16)
        return carry

    lax.fori_loop(s + 1, groups, blank, 0)
    sum_k = Sum(links, lambda m: dk.at[related(s, m)], box_k, [0] + ups)
    sum_v = Sum(links, lambda m: dv.at[related(s, m)], box_v, [0] + downs)
    sum_k.launch()
    sum_v.launch()

    for copy in kept_copies:
        copy.wait()
    gate, up, down = ffn
    gate.settle(gate.kept)
    gate.launch()
    up.settle(up.kept)
    up.launch()
    sum_k.settle()
    sum_k.launch()
    sum_v.settle()
    sum_v.launch()
    sum_out.settle()
    sum_out.launch()

    cosines, sines = cos_ref[...], sin_ref[...]
    d_gain_q = jnp.zeros((1, width), f32)
    for j in range(qcount):
        d_rot = dq_t[:, pl.ds(j * rows, rows)].T * scale
        d_lin, terms = back_norm(
            q_lin_ref[:, pl.ds(j * width, width)],
            gain_q_ref[...],
            back_rotate(d_rot, cosines, sines),
        )
        d_qkv[:, pl.ds(j * width, width)] = d_lin.astype(bf16)
        d_gain_q = d_gain_q + terms

    sum_k.settle()
    sum_k.launch()
    sum_v.settle()
    sum_v.launch()
    down.settle(down.kept)
    down.launch()
    heads_shape = dk.shape[2:]

    def over(total, zbox, shape):
        where = total.waiting[0][1]
        total.settle()
        return links.over_heads(total.boxes.at[where], zbox), total.boxes.at[where]

    z_k, own_k = over(sum_k, zbox_k, heads_shape)
    z_v, own_v = over(sum_v, zbox_v, heads_shape)
    sum_out.settle()
    sum_out.launch()

    def gathered(copies, zbox, own):
        total = own[h].astype(f32)
        for d, copy in enumerate(copies):
            copy.wait_recv()
            total = total + zbox[d].astype(f32)
        return total

    d_keys = gathered(z_k, zbox_k, own_k)
    d_values = gathered(z_v, zbox_v, own_v)
    d_lin, d_gain_k = back_norm(
        k_lin_ref[...], gain_k_ref[...], back_rotate(d_keys, cosines, sines)
    )
    qw = qcount * width
    d_qkv[:, pl.ds(qw, width)] = d_lin.astype(bf16)
    d_qkv[:, pl.ds(qw + width, width)] = d_values.astype(bf16)
    cut_at = dw_a.shape[2]

    def qkv_block(j, carry):
        dw_a[j] = jnp.dot(
            attn_t_ref[j], d_qkv[:, :cut_at], preferred_element_type=f32
        ).astype(bf16)
        dw_b[j] = jnp.dot(
            attn_t_ref[j], d_qkv[:, cut_at:], preferred_element_type=f32
        ).astype(bf16)
        return carry

    lax.fori_loop(0, nseq, qkv_block, 0)
    sum_a = Sum(links, lambda m: dw_a.at[related(s, m)], box_a, [0] + ups)
    sum_b = Sum(links, lambda m: dw_b.at[related(s, m)], box_b, [0] + downs)
    sum_a.launch()
    sum_b.launch()

    d_attn_in = contract_last(d_qkv[...], w_qkv_ref[...])
    d_x, d_gain_in = back_norm(x_ref[...].astype(f32), gain_in_ref[...], d_attn_in)
    o_tokens[...] = (d_hid_ref[...] + d_x).astype(o_tokens.dtype)

    gsum[0] = gains_ref[...]
    gsum[0, 0:1, :] = d_gain_in
    gsum[0, 4:5, :width] = d_gain_q
    gsum[0, 5:6, :width] = d_gain_k
    gain_copies = [links.go(gsum.at[0], gbox.at[0], links.across(0))]

    sum_a.settle()
    sum_a.launch()
    sum_b.settle()
    sum_b.launch()
    for bit in range(bits):
        gain_copies[-1].wait_recv()
        gsum[bit + 1] = gsum[bit] + gbox[bit]
        if bit + 1 < bits:
            gain_copies.append(
                links.go(gsum.at[bit + 1], gbox.at[bit + 1], links.across(bit + 1))
            )
    gain_z = [
        links.go(gsum.at[bits], gzbox.at[d], (s, o)) for d, o in enumerate(links.others)
    ]

    def pieces(total, zsrc, col, size):
        value = total.last()
        each = value.shape[0] // heads
        for p in range(heads):
            zsrc[p, :, pl.ds(col, size)] = value[p * each : (p + 1) * each].astype(bf16)

    pieces(sum_out, zsrc_out, 0, dw_out.shape[2])
    z_out = links.over_heads(zsrc_out, zbox_out)
    gate.settle()
    gate.launch()
    up.settle()
    up.launch()
    sum_a.settle()
    sum_a.launch()
    sum_b.settle()
    sum_b.launch()
    pieces(sum_a, zsrc_qkv, 0, cut_at)
    pieces(sum_b, zsrc_qkv, cut_at, dw_b.shape[2])
    z_qkv = links.over_heads(zsrc_qkv, zbox_qkv)
    down.settle()
    down.launch()
    o_gate[...] = gate.last()
    o_up[...] = up.last()
    total = gsum[bits]
    for d, copy in enumerate(gain_z):
        copy.wait_recv()
        total = total + gzbox[d]
    o_gains[...] = total
    o_out[...] = gathered(z_out, zbox_out, zsrc_out)
    o_qkv[...] = gathered(z_qkv, zbox_qkv, zsrc_qkv)
    o_down[...] = down.last()
    links.finish()


def tail(nseq, heads, qcount, scale, cid, *arrays):
    (q, k, v, _, _, _, att, mixed_t, d_proj, w_out, q_lin, k_lin, _, _, gain_q, _) = arrays[:16]
    (attn_t, w_qkv, x, gain_in, d_hid, gains, d_gate, d_up, d_down) = arrays[16:]
    f32, bf16 = jnp.float32, jnp.bfloat16
    rows, model = d_proj.shape
    width = gain_q.shape[1]
    cols = w_qkv.shape[1]
    cut_at = cols // 2
    out_rows, qkv_rows = mixed_t.shape[1], attn_t.shape[1]
    pieces_kv = (heads, rows, width)
    ffn_block = d_gate.shape[1:]
    some, all_but = nseq // 2, nseq - 1
    bits = nseq.bit_length() - 1
    copies = 8 * all_but + 5 * (heads - 1) + bits
    vm = pl.BlockSpec(memory_space=VMEM)
    anywhere = pl.BlockSpec(memory_space=pl.ANY)

    def kernel(*refs):
        tail_kernel(nseq, heads, qcount, scale, *refs)

    return pl.pallas_call(
        kernel,
        out_shape=[
            jax.ShapeDtypeStruct((rows, model), bf16),
            jax.ShapeDtypeStruct((qkv_rows // heads, cols), f32),
            jax.ShapeDtypeStruct((out_rows // heads, model), f32),
            jax.ShapeDtypeStruct(ffn_block, f32),
            jax.ShapeDtypeStruct(ffn_block, f32),
            jax.ShapeDtypeStruct(ffn_block, f32),
            jax.ShapeDtypeStruct(gains.shape, f32),
        ],
        in_specs=[vm] * (len(arrays) - 3) + [anywhere] * 3,
        out_specs=[vm] * 7,
        scratch_shapes=[
            VMEM((nseq,) + pieces_kv, bf16),
            VMEM((nseq,) + pieces_kv, bf16),
            VMEM((width, qcount * rows), f32),
            VMEM((qcount * rows, width), bf16),
            VMEM((width, qcount * rows), bf16),
            VMEM((all_but,) + pieces_kv, bf16),
            VMEM((all_but,) + pieces_kv, bf16),
            VMEM((heads - 1, rows, width), bf16),
            VMEM((heads - 1, rows, width), bf16),
            VMEM((nseq, out_rows, model), bf16),
            VMEM((all_but, out_rows, model), bf16),
            VMEM((heads, out_rows // heads, model), bf16),
            VMEM((heads - 1, out_rows // heads, model), bf16),
            VMEM((nseq, qkv_rows, cut_at), bf16),
            VMEM((nseq, qkv_rows, cols - cut_at), bf16),
            VMEM((all_but, qkv_rows, cut_at), bf16),
            VMEM((all_but, qkv_rows, cols - cut_at), bf16),
            VMEM((heads, qkv_rows // heads, cols), bf16),
            VMEM((heads - 1, qkv_rows // heads, cols), bf16),
            VMEM((rows, cols), bf16),
        ]
        + [VMEM((some,) + ffn_block, bf16)] * 3
        + [VMEM((all_but,) + ffn_block, bf16)] * 3
        + [
            VMEM((bits + 1,) + gains.shape, f32),
            VMEM((bits,) + gains.shape, f32),
            VMEM((heads - 1,) + gains.shape, f32),
            pltpu.SemaphoreType.DMA((copies,)),
            pltpu.SemaphoreType.DMA((copies,)),
            pltpu.SemaphoreType.DMA((3, some)),
        ],
        name="tail",
        compiler_params=pltpu.CompilerParams(
            collective_id=cid, has_side_effects=True, vmem_limit_bytes=62 * 2**20
        ),
    )(*arrays)


BLOCK_US, HOP_US = 3.5, 0.8
WORK_US = {"fa": 2.0, "fb": 1.4, "fc": 2.0, "ga": 0.8, "gb": 0.5, "gc": 2.0, "n": 0.3, "e": 0.4}
WORK_US.update({"wd": 3.3, "wg": 3.3, "wu": 3.3})


def plan(chunks, spans, last, block_us, hop_us, work_us):
    needs = {}
    each = chunks // spans
    for c in range(chunks):
        p = c // each
        for k in range(2):
            for t in range(last):
                needs["ags", k, c, t] = [("agw", k, c, t - 1)] if t else ([("n", c)] if k else [])
                needs["agw", k, c, t] = [("ags", k, c, t)]
                before = ("gc", p) if k else ("fc", p)
                needs["rss", k, c, t] = [("rsw", k, c, t - 1)] if t else [before]
                needs["rsw", k, c, t] = [("rss", k, c, t)]
        needs["n", c] = [("rsw", 0, c, last - 1)]
        needs["e", c] = [("rsw", 1, c, last - 1)]
    for p in range(spans):
        mine = range(p * each, (p + 1) * each)
        needs["fa", p] = [("agw", 0, c, last - 1) for c in mine]
        needs["fb", p] = [("fa", p)]
        needs["fc", p] = [("fb", p)]
        needs["ga", p] = [("agw", 1, c, last - 1) for c in mine]
        needs["gb", p] = [("ga", p)]
        needs["gc", p] = [("gb", p)]
    needs[("wd",)] = [("ga", p) for p in range(spans)]
    needs[("wg",)] = [("gb", p) for p in range(spans)] + [("wd",)]
    needs[("wu",)] = [("wg",)]
    rank = {"ags": 0, "rss": 0, "agw": 1, "rsw": 1, "n": 2, "e": 3}
    rank.update({"ga": 4, "gb": 4, "gc": 4, "fa": 5, "fb": 5, "fc": 5, "wd": 6, "wg": 6, "wu": 6})
    now, link, done, order = 0.0, 0.0, {}, []
    while len(order) < len(needs):
        ready = []
        for event, before in needs.items():
            if event in done or any(b not in done for b in before):
                continue
            at = max([done[b] for b in before], default=0.0)
            start = max(now, at)
            if event[0] in ("agw", "rsw") and start <= now + 0.4:
                start = now
            ready.append((start, rank[event[0]], event[2:3] or event[1:2], event, at))
        start, _, _, event, at = min(ready)
        kind = event[0]
        now = max(start, at)
        order.append(event)
        if kind in ("ags", "rss"):
            link = max(link, now) + block_us * 2 / 3
            done[event] = link + block_us / 3 + hop_us
            now += 0.1
        elif kind in ("agw", "rsw"):
            now += 0.1
            done[event] = now
        else:
            now += work_us[kind]
            done[event] = now
    return order


def ffn_kernel(
    heads,
    chunks,
    spans,
    proj_ref,
    x_ref,
    cot_ref,
    gain_two_ref,
    gain_three_ref,
    gain_four_ref,
    w_gate_ref,
    w_up_ref,
    w_down_ref,
    o_out,
    o_hid,
    o_proj,
    o_gains,
    o_gate,
    o_up,
    o_down,
    hidden,
    w_gate,
    w_up,
    w_down,
    u_all,
    d_all,
    by_gate,
    by_up,
    act,
    d_gate,
    d_up,
    parts,
    from_left,
    from_right,
    flipped,
    dw_gate,
    dw_up,
    dw_down,
    ag_send,
    ag_recv,
    rs_send,
    rs_recv,
    local_sem,
):
    f32, bf16 = jnp.float32, jnp.bfloat16
    s, h = place()
    last = heads - 1
    right = (s, lax.rem(h + 1, heads))
    left = (s, lax.rem(h + last, heads))
    rows, model = x_ref.shape
    units = w_gate.shape[0]
    rc = rows // chunks
    each = chunks // spans
    many = rc * heads * each
    tile = 256
    whole_tiles, rest = units // tile, units % tile

    loads = []
    for n, (src, dst) in enumerate(
        ((w_gate_ref, w_gate), (w_up_ref, w_up), (w_down_ref, w_down))
    ):
        copy = pltpu.make_async_copy(src, dst, local_sem.at[n])
        copy.start()
        loads.append(copy)
    greet([right, left])

    proj = proj_ref[...]
    hid = x_ref[...].astype(f32) + norm_rows(proj, gain_two_ref[...])
    hidden[...] = hid
    u_local = norm_rows(hid, gain_three_ref[...]).astype(bf16)
    for c in range(chunks):
        u_all[c, h] = u_local[c * rc : (c + 1) * rc]
    o_gains[...] = jnp.zeros_like(o_gains)

    def lanes(k, c, t):
        buf = d_all if k else u_all
        return (
            (
                (h - t >= 0) & (h < last),
                buf.at[c, jnp.maximum(h - t, 0)],
                0,
                right,
                h - 1 - t >= 0,
                buf.at[c, jnp.maximum(h - 1 - t, 0)],
            ),
            (
                (h + t <= last) & (h > 0),
                buf.at[c, jnp.minimum(h + t, last)],
                1,
                left,
                h + 1 + t <= last,
                buf.at[c, jnp.minimum(h + 1 + t, last)],
            ),
        )

    def ags(k, c, t):
        for on, block, lane, target, _, _ in lanes(k, c, t):
            i = (k, c, lane, t)
            pl.when(on)(remote(block, block, ag_send.at[i], ag_recv.at[i], target).start)

    def agw(k, c, t):
        for _, _, lane, target, on, block in lanes(k, c, t):
            i = (k, c, lane, t)
            pl.when(on)(remote(block, block, ag_send.at[i], ag_recv.at[i], target).wait_recv)

    def rss(k, c, t):
        for on, dest, box, lane, target, at_end in (
            ((t >= h) & (h < last), last - (t - h), from_left, 0, right, h == 0),
            ((t >= last - h) & (h > 0), t - (last - h), from_right, 1, left, h == last),
        ):
            dest = jnp.clip(dest, 0, last)
            i = (k, c, lane, t)
            if t > 0:

                def forward(box=box, dest=dest, i=i, target=target):
                    box[k, c, t - 1] = box[k, c, t - 1] + parts[k, c, dest]
                    remote(
                        box.at[k, c, t - 1], box.at[k, c, t], rs_send.at[i], rs_recv.at[i], target
                    ).start()

                pl.when(on & jnp.logical_not(at_end))(forward)
            pl.when(on & at_end)(
                remote(
                    parts.at[k, c, dest], box.at[k, c, t], rs_send.at[i], rs_recv.at[i], target
                ).start
            )

    def rsw(k, c, t):
        for on, box, lane, target in (
            ((t >= h - 1) & (h > 0), from_left, 0, right),
            ((t >= last - h - 1) & (h < last), from_right, 1, left),
        ):
            i = (k, c, lane, t)
            block = box.at[k, c, t]
            pl.when(on)(remote(block, block, rs_send.at[i], rs_recv.at[i], target).wait_recv)

    def summed(k, c):
        zero = jnp.zeros((rc, model), f32)
        return (
            parts[k, c, h].astype(f32)
            + jnp.where(h > 0, from_left[k, c, last - 1].astype(f32), zero)
            + jnp.where(h < last, from_right[k, c, last - 1].astype(f32), zero)
        )

    def over_tiles(lo, hi, body):
        def step(i, carry):
            body(pl.ds(pl.multiple_of(i * tile, tile), tile))
            return carry

        lax.fori_loop(lo, hi, step, 0)
        if hi == whole_tiles and rest:
            body(pl.ds(whole_tiles * tile, rest))

    arrived = set()

    def need(n):
        if n not in arrived:
            arrived.add(n)
            loads[n].wait()

    def held(buf, p):
        return buf[pl.ds(p * each, each)].reshape(many, model)

    def place_parts(k, p, cols, value):
        parts[k, pl.ds(p * each, each), :, :, cols] = value.astype(bf16).reshape(
            each, heads, rc, value.shape[1]
        )

    def forward_tiles(c, lo, hi):
        need(0)
        need(1)

        def body(cols):
            u = held(u_all, c)
            gate = contract_last(u, w_gate[cols, :])
            up = contract_last(u, w_up[cols, :])
            root = math.sqrt(2.0 / math.pi)
            square = gate * gate
            curve = jnp.tanh(root * gate * (1.0 + 0.044715 * square))
            half = 0.5 * (1.0 + curve)
            gelu = gate * half
            slope = half + 0.5 * gate * (1.0 - curve * curve) * (
                root * (1.0 + 3 * 0.044715 * square)
            )
            by_gate[pl.ds(c * many, many), cols] = slope * up
            by_up[pl.ds(c * many, many), cols] = gelu
            act[pl.ds(c * many, many), cols] = (gelu * up).astype(bf16)

        over_tiles(lo, hi, body)

    out_tile = model // 3

    def down_rows(c):
        need(2)

        def body(i, carry):
            cols = pl.ds(pl.multiple_of(i * out_tile, out_tile), out_tile)
            part = jnp.dot(
                act[pl.ds(c * many, many), :], w_down[:, cols], preferred_element_type=f32
            )
            place_parts(0, c, cols, part)
            return carry

        lax.fori_loop(0, 3, body, 0)

    def turn(c):
        here = pl.ds(c * rc, rc)
        ffn_out = summed(0, c)
        upstream = cot_ref[here, :].astype(f32)
        o_out[here, :] = (hidden[here, :] + norm_rows(ffn_out, gain_four_ref[...])).astype(
            o_out.dtype
        )
        d_out, terms = back_norm(ffn_out, gain_four_ref[...], upstream)
        d_all[c, h] = d_out.astype(bf16)
        o_gains[3:4, :] += terms

    def back_tiles(c, lo, hi):
        def body(cols):
            d_act = contract_last(held(d_all, c), w_down[cols, :])
            d_gate[pl.ds(c * many, many), cols] = (
                d_act * by_gate[pl.ds(c * many, many), cols]
            ).astype(bf16)
            d_up[pl.ds(c * many, many), cols] = (
                d_act * by_up[pl.ds(c * many, many), cols]
            ).astype(bf16)

        over_tiles(lo, hi, body)

    def back_rows(c):
        def body(i, carry):
            cols = pl.ds(pl.multiple_of(i * out_tile, out_tile), out_tile)
            part = jnp.dot(
                d_gate[pl.ds(c * many, many), :], w_gate[:, cols], preferred_element_type=f32
            )
            part = part + jnp.dot(
                d_up[pl.ds(c * many, many), :], w_up[:, cols], preferred_element_type=f32
            )
            place_parts(1, c, cols, part)
            return carry

        lax.fori_loop(0, 3, body, 0)

    def finish_rows(c):
        here = pl.ds(c * rc, rc)
        d_in, terms = back_norm(hidden[here, :], gain_three_ref[...], summed(1, c))
        o_gains[2:3, :] += terms
        d_hid = cot_ref[here, :].astype(f32) + d_in
        o_hid[here, :] = d_hid
        d_proj, terms = back_norm(proj_ref[here, :], gain_two_ref[...], d_hid)
        o_proj[here, :] = d_proj.astype(o_proj.dtype)
        o_gains[1:2, :] += terms

    stores = []

    def flip(source):
        for p in range(spans):
            flipped[:, pl.ds(p * many, many)] = held(source, p).T

    def weight_grad(right_ref, dst, out, n):
        def body(cols):
            value = jnp.dot(flipped[...], right_ref[:, cols], preferred_element_type=f32)
            dst[:, :, cols] = value.astype(bf16).reshape(dst.shape[:2] + (value.shape[1],))

        over_tiles(0, whole_tiles, body)
        copy = pltpu.make_async_copy(dst, out, local_sem.at[n])
        copy.start()
        stores.append(copy)

    half_tiles = (whole_tiles + 1) // 2
    events = plan(chunks, spans, last, BLOCK_US / chunks, HOP_US, WORK_US)
    for event in events:
        kind, args = event[0], event[1:]
        if kind == "ags":
            ags(*args)
        elif kind == "agw":
            agw(*args)
        elif kind == "rss":
            rss(*args)
        elif kind == "rsw":
            rsw(*args)
        elif kind == "fa":
            forward_tiles(args[0], 0, half_tiles)
        elif kind == "fb":
            forward_tiles(args[0], half_tiles, whole_tiles)
        elif kind == "fc":
            down_rows(args[0])
        elif kind == "n":
            turn(args[0])
        elif kind == "ga":
            back_tiles(args[0], 0, half_tiles)
        elif kind == "gb":
            back_tiles(args[0], half_tiles, whole_tiles)
        elif kind == "gc":
            back_rows(args[0])
        elif kind == "e":
            finish_rows(args[0])
        elif kind == "wd":
            flip(d_all)
            weight_grad(act, dw_down, o_down, 3)
        elif kind == "wg":
            flip(u_all)
            weight_grad(d_gate, dw_gate, o_gate, 4)
        else:
            weight_grad(d_up, dw_up, o_up, 5)

    for event in events:
        if event[0] == "ags":
            k, c, t = event[1:]
            for on, block, lane, target, _, _ in lanes(k, c, t):
                i = (k, c, lane, t)
                pl.when(on)(remote(block, block, ag_send.at[i], ag_recv.at[i], target).wait_send)
        elif event[0] == "rss":
            k, c, t = event[1:]
            for on, box, lane, target in (
                ((t >= h) & (h < last), from_left, 0, right),
                ((t >= last - h) & (h > 0), from_right, 1, left),
            ):
                i = (k, c, lane, t)
                block = box.at[k, c, t]
                pl.when(on)(remote(block, block, rs_send.at[i], rs_recv.at[i], target).wait_send)
    for n in range(3):
        need(n)
    for copy in stores:
        copy.wait()


def feed_forward(nseq, heads, chunks, spans, cid, proj, x, cot, gains, w_gate, w_up, w_down):
    f32, bf16 = jnp.float32, jnp.bfloat16
    rows, model = x.shape
    units = w_gate.shape[0]
    rc = rows // chunks
    group = rows * heads
    vm = pl.BlockSpec(memory_space=VMEM)
    anywhere = pl.BlockSpec(memory_space=pl.ANY)
    grad = jax.ShapeDtypeStruct((nseq, model // nseq, units), bf16)
    hops = (2, chunks, 2, heads - 1)
    return pl.pallas_call(
        functools.partial(ffn_kernel, heads, chunks, spans),
        out_shape=[
            jax.ShapeDtypeStruct((rows, model), bf16),
            jax.ShapeDtypeStruct((rows, model), f32),
            jax.ShapeDtypeStruct((rows, model), bf16),
            jax.ShapeDtypeStruct((8, model), f32),
            grad,
            grad,
            grad,
        ],
        in_specs=[vm] * 6 + [anywhere] * 3,
        out_specs=[vm] * 4 + [anywhere] * 3,
        scratch_shapes=[
            VMEM((rows, model), f32),
            VMEM(w_gate.shape, bf16),
            VMEM(w_up.shape, bf16),
            VMEM(w_down.shape, bf16),
            VMEM((chunks, heads, rc, model), bf16),
            VMEM((chunks, heads, rc, model), bf16),
            VMEM((group, units), f32),
            VMEM((group, units), f32),
            VMEM((group, units), bf16),
            VMEM((group, units), bf16),
            VMEM((group, units), bf16),
            VMEM((2, chunks, heads, rc, model), bf16),
            VMEM((2, chunks, heads - 1, rc, model), bf16),
            VMEM((2, chunks, heads - 1, rc, model), bf16),
            VMEM((model, group), bf16),
            VMEM(grad.shape, bf16),
            VMEM(grad.shape, bf16),
            VMEM(grad.shape, bf16),
            pltpu.SemaphoreType.DMA(hops),
            pltpu.SemaphoreType.DMA(hops),
            pltpu.SemaphoreType.DMA(hops),
            pltpu.SemaphoreType.DMA(hops),
            pltpu.SemaphoreType.DMA((6,)),
        ],
        name="feed_forward",
        compiler_params=pltpu.CompilerParams(
            collective_id=cid, has_side_effects=True, vmem_limit_bytes=62 * 2**20
        ),
    )(proj, x, cot, *[g[None] for g in gains], w_gate, w_up, w_down)


def local(
    tokens,
    segment_ids,
    w_query,
    w_key,
    w_value,
    w_out,
    w_gate,
    w_up,
    w_down,
    gain_attn_in,
    gain_attn_out,
    gain_ffn_in,
    gain_ffn_out,
    gain_query,
    gain_key,
    cotangent,
):
    heads = lax.axis_size("head")
    nseq = lax.axis_size("seq")
    head_index = lax.axis_index("head")
    seq_index = lax.axis_index("seq")
    bits = nseq.bit_length() - 1
    local_rows, model = tokens.shape
    width = gain_query.shape[0]
    qcount = w_query.shape[1] // width
    group = local_rows * heads
    total = segment_ids.shape[0]
    hidden_units = w_gate.shape[1]
    scale = 1.0 / math.sqrt(width)
    bf16 = jnp.bfloat16
    first_row = (seq_index * heads + head_index) * local_rows
    my_index = first_row + jnp.arange(local_rows, dtype=jnp.int32)
    my_ids = lax.dynamic_slice_in_dim(segment_ids, first_row, local_rows)
    my_starts = jnp.min(
        jnp.where(
            my_ids[:, None] == segment_ids[None, :],
            jnp.arange(total, dtype=jnp.int32)[None, :],
            total,
        ),
        axis=1,
    )
    cosines, sines = rope_tables(my_index - my_starts, width)

    def query_path(linear, gain):
        shaped = linear.reshape(local_rows, qcount, width)
        turned = rotate(norm_rows(shaped, gain), cosines[:, None, :], sines[:, None, :])
        return turned.reshape(local_rows, qcount * width)

    def key_path(linear, gain):
        return rotate(norm_rows(linear, gain), cosines, sines)

    def gated(gate, up):
        return jax.nn.gelu(gate, approximate=True) * up

    def stacked(v):
        return v.reshape(local_rows, qcount, width).transpose(1, 0, 2).reshape(-1, width)

    def unstacked(v):
        return v.reshape(qcount, local_rows, width).transpose(1, 0, 2).reshape(local_rows, -1)

    inputs = tokens.astype(jnp.float32)
    attn_in = norm_rows(inputs, gain_attn_in).astype(bf16)
    k_linear = jnp.dot(attn_in, w_key, preferred_element_type=jnp.float32)
    keys_local = key_path(k_linear, gain_key).astype(bf16)
    values_local = jnp.dot(attn_in, w_value, preferred_element_type=jnp.float32).astype(bf16)
    q_linear = jnp.dot(attn_in, w_query, preferred_element_type=jnp.float32)
    queries_local = query_path(q_linear, gain_query).astype(bf16)
    queries = stacked(queries_local) * jnp.asarray(scale, bf16)
    keys, values = gather_all([keys_local, values_local], nseq, heads, 1)
    keys = keys.reshape(nseq, group, width)
    values = values.reshape(nseq, group, width)
    starts = jnp.tile(my_starts, qcount)[None, :]
    index = jnp.tile(my_index, qcount)[None, :]
    attended_t, log_total = attend(queries, keys, values, starts, index)
    attended = attended_t.T
    mixed_local = unstacked(attended.astype(bf16))
    projected = jnp.dot(mixed_local, w_out, preferred_element_type=jnp.float32)
    if nseq <= 8 and (model // nseq) % 16 == 0:
        qw = qcount * width
        each, few = model // (nseq * heads), width // (nseq * heads)
        output, d_hidden, d_projected, gains, *blocks = feed_forward(
            nseq,
            heads,
            4,
            2,
            10,
            projected,
            tokens,
            cotangent,
            (gain_attn_out, gain_ffn_in, gain_ffn_out),
            w_gate.T,
            w_up.T,
            w_down,
        )
        w_qkv = jnp.concatenate([w_query, w_key, w_value], axis=1)
        grad_tokens, sum_qkv, sum_out, sum_gate, sum_up, sum_down, sum_gains = tail(
            nseq,
            heads,
            qcount,
            scale,
            9,
            queries,
            keys,
            values,
            starts,
            index,
            log_total,
            attended_t,
            mixed_local.T.reshape(nseq, -1, local_rows),
            d_projected,
            w_out,
            q_linear,
            k_linear,
            cosines,
            sines,
            gain_query[None],
            gain_key[None],
            attn_in.T.reshape(nseq, -1, local_rows),
            w_qkv,
            tokens,
            gain_attn_in[None],
            d_hidden,
            gains,
            *blocks,
        )
        which = seq_index * heads + head_index
        wide = lax.dynamic_slice_in_dim(sum_gains[:4], which * each, each, 1)
        narrow = lax.dynamic_slice_in_dim(sum_gains[4:6], which * few, few, 1)
        return (
            output,
            grad_tokens,
            sum_qkv[:, :qw],
            sum_qkv[:, qw : qw + width],
            sum_qkv[:, qw + width :],
            sum_out,
            sum_gate,
            sum_up,
            sum_down.T,
            wide[0],
            wide[1],
            wide[2],
            wide[3],
            narrow[0],
            narrow[1],
        )
    hidden = inputs + norm_rows(projected, gain_attn_out)
    ffn_in = norm_rows(hidden, gain_ffn_in).astype(bf16)
    ffn_rows = line_gather(ffn_in, heads, 2).reshape(group, model)
    gate = jnp.dot(ffn_rows, w_gate, preferred_element_type=jnp.float32)
    up = jnp.dot(ffn_rows, w_up, preferred_element_type=jnp.float32)
    activated = gated(gate, up).astype(bf16)
    ffn_out = line_scatter(
        jnp.dot(activated, w_down, preferred_element_type=jnp.float32)
        .astype(bf16)
        .reshape(heads, local_rows, model),
        heads,
        3,
    )
    output = hidden + norm_rows(ffn_out, gain_ffn_out)
    upstream = cotangent.astype(jnp.float32)
    unused, back_four = jax.vjp(norm_rows, ffn_out, gain_ffn_out)
    d_ffn_out, d_gain_four = back_four(upstream)
    d_ffn_rows = line_gather(d_ffn_out.astype(bf16), heads, 4).reshape(group, model)
    d_activated = contract_last(d_ffn_rows, w_down)
    d_w_down = contract_first(d_ffn_rows, activated)
    unused, back_gate = jax.vjp(gated, gate, up)
    d_gate, d_up = back_gate(d_activated)
    d_gate = d_gate.astype(bf16)
    d_up = d_up.astype(bf16)
    d_ffn_in = line_scatter(
        (contract_last(d_gate, w_gate) + contract_last(d_up, w_up))
        .astype(bf16)
        .reshape(heads, local_rows, model),
        heads,
        5,
    )
    d_w_gate = contract_first(ffn_rows, d_gate)
    d_w_up = contract_first(ffn_rows, d_up)
    unused, back_three = jax.vjp(norm_rows, hidden, gain_ffn_in)
    d_hidden_part, d_gain_three = back_three(d_ffn_in)
    d_hidden = upstream + d_hidden_part
    unused, back_two = jax.vjp(norm_rows, projected, gain_attn_out)
    d_projected, d_gain_two = back_two(d_hidden)
    d_projected = d_projected.astype(bf16)
    qw = qcount * width
    d_w_out = contract_first(mixed_local, d_projected)
    d_mixed = contract_last(d_projected, w_out).astype(bf16)
    grad_attended = stacked(d_mixed)
    row_dots = jnp.sum(grad_attended.astype(jnp.float32) * attended, axis=1)[None, :]
    d_queries_t, d_keys, d_values = attend_back(
        queries, keys, values, starts, index, log_total, row_dots, grad_attended
    )
    shape = (nseq, heads, local_rows, width)
    ups, downs = seq_orders(bits)
    d_keys, d_values = scatter_all(
        [d_keys.reshape(shape), d_values.reshape(shape)],
        [True, True],
        [[0] + ups, [0] + downs],
        nseq,
        heads,
        6,
        "scatter_keys",
    )
    d_query_rot = unstacked((d_queries_t.T * scale).astype(bf16)).astype(jnp.float32)
    unused, back_query = jax.vjp(query_path, q_linear, gain_query)
    d_q_linear, d_gain_query = back_query(d_query_rot)
    unused, back_key = jax.vjp(key_path, k_linear, gain_key)
    d_k_linear, d_gain_key = back_key(d_keys)
    d_qkv = jnp.concatenate([d_q_linear, d_k_linear, d_values], axis=1).astype(bf16)
    qw = qcount * width
    d_w_qkv = contract_first(attn_in, d_qkv)
    d_attn_in = (
        contract_last(d_qkv[:, :qw], w_query)
        + contract_last(d_qkv[:, qw : qw + width], w_key)
        + contract_last(d_qkv[:, qw + width :], w_value)
    )
    unused, back_one = jax.vjp(norm_rows, inputs, gain_attn_in)
    d_inputs, d_gain_one = back_one(d_attn_in)
    grad_tokens = (d_hidden + d_inputs).astype(bf16)

    def cut(v):
        return v.reshape(nseq, heads, -1)

    wide = jnp.stack([cut(d_gain_one), cut(d_gain_two), cut(d_gain_three), cut(d_gain_four)], 2)
    narrow = jnp.stack([cut(d_gain_query), cut(d_gain_key)], 2)
    each, few = wide.shape[-1], narrow.shape[-1]
    gains = jnp.concatenate(
        [
            jnp.pad(wide, ((0, 0), (0, 0), (0, 0), (0, 128 - each))),
            jnp.pad(narrow, ((0, 0), (0, 0), (0, 2), (0, 128 - few))),
        ],
        axis=2,
    )
    sum_qkv, sum_out, sum_gains = scatter_all(
        [
            d_w_qkv.astype(bf16).reshape(nseq, heads, -1, d_qkv.shape[1]),
            d_w_out.astype(bf16).reshape(nseq, heads, -1, model),
            gains,
        ],
        [True, True, True],
        [[0] + ups, [0] + downs, [0] + downs],
        nseq,
        heads,
        7,
        "scatter_attn",
    )
    sum_gate, sum_up, sum_down = scatter_all(
        [
            d.astype(bf16).reshape(nseq, model // nseq, hidden_units)
            for d in (d_w_gate, d_w_up, d_w_down)
        ],
        [False, False, False],
        [[0] + ups, [0] + downs, [0] + ups],
        nseq,
        heads,
        8,
        "scatter_ffn",
    )
    return (
        output.astype(bf16),
        grad_tokens,
        sum_qkv[:, :qw],
        sum_qkv[:, qw : qw + width],
        sum_qkv[:, qw + width :],
        sum_out,
        sum_gate,
        sum_up,
        sum_down.T,
        sum_gains[0, :each],
        sum_gains[1, :each],
        sum_gains[2, :each],
        sum_gains[3, :each],
        sum_gains[4, :few],
        sum_gains[5, :few],
    )


def solution(mesh):
    rows = P(("seq", "head"), None)
    in_specs = (
        rows,
        P(),
        P(),
        P(),
        P(),
        P(),
        P(None, "head"),
        P(None, "head"),
        P("head", None),
        P(),
        P(),
        P(),
        P(),
        P(),
        P(),
        rows,
    )
    out_specs = (
        rows,
        rows,
        rows,
        rows,
        rows,
        rows,
        P("seq", "head"),
        P("seq", "head"),
        P("head", "seq"),
    ) + (P(("seq", "head")),) * 6
    return jax.shard_map(local, mesh=mesh, in_specs=in_specs, out_specs=out_specs, check_vma=False)
```

```python
import functools
import itertools
import math

import jax
import jax.numpy as jnp
from jax import lax
from jax.experimental import pallas as pl
from jax.experimental.pallas import tpu as pltpu
from jax.sharding import PartitionSpec as P

EPS = 1e-06
MESH = pl.DeviceIdType.MESH
VMEM = pltpu.VMEM
LIMIT = 56 * 2**20


def norm_rows(v, gain):
    return v * lax.rsqrt(jnp.mean(v * v, axis=-1, keepdims=True) + EPS) * gain


def rotate(v, cosines, sines):
    half = v.shape[-1] // 2
    first = v[..., :half]
    second = v[..., half:]
    return jnp.concatenate(
        [first * cosines - second * sines, second * cosines + first * sines], axis=-1
    )


def rope_tables(positions, width):
    half = width // 2
    freq = jnp.exp(jnp.arange(half, dtype=jnp.float32) * (-2.0 * math.log(1000000.0) / width))
    angle = positions.astype(jnp.float32)[:, None] * freq[None, :]
    return (jnp.cos(angle), jnp.sin(angle))


def contract_first(left, right):
    return lax.dot_general(
        left, right, (((0,), (0,)), ((), ())), preferred_element_type=jnp.float32
    )


def contract_last(left, right):
    return lax.dot_general(
        left, right, (((1,), (1,)), ((), ())), preferred_element_type=jnp.float32
    )


def place():
    return lax.axis_index("seq"), lax.axis_index("head")


def related(s, mask):
    out = s
    bit = 0
    while mask >> bit:
        if (mask >> bit) & 1:
            step = 1 << bit
            out = out + (1 - 2 * ((s // step) % 2)) * step
        bit += 1
    return out


def subsets(bits):
    out = [0]
    for bit in bits:
        out = out + [m | (1 << bit) for m in out]
    return out


def greet(targets):
    barrier = pltpu.get_barrier_semaphore()
    for target in targets:
        pl.semaphore_signal(barrier, inc=1, device_id=target, device_id_type=MESH)
    pl.semaphore_wait(barrier, len(targets))


def remote(src, dst, send, recv, target):
    return pltpu.make_async_remote_copy(
        src_ref=src,
        dst_ref=dst,
        send_sem=send,
        recv_sem=recv,
        device_id=target,
        device_id_type=MESH,
    )


def seq_orders(bits):
    upper = list(range(1, bits))
    return upper, upper[::-1]


def gather_kernel(nseq, heads, local_refs, out_refs, send, recv):
    bits = nseq.bit_length() - 1
    s, h = place()
    others = [lax.rem(h + d, heads) for d in range(1, heads)]
    greet([(related(s, 1 << b), h) for b in range(bits)] + [(s, o) for o in others])
    count = [0]
    started = []

    def go(src, dst, target):
        k = count[0]
        count[0] += 1
        copy = remote(src, dst, send.at[k], recv.at[k], target)
        copy.start()
        started.append(copy)
        return copy

    first = []
    for a in range(len(out_refs)):
        out_refs[a][s, h] = local_refs[a][...]
        first.append(
            [go(local_refs[a], out_refs[a].at[s, h], (s, o)) for o in others]
        )
    orders = [o + [0] for o in seq_orders(bits)]
    held = [{0: first[a]} for a in range(len(out_refs))]
    for stage in range(bits):
        for a in range(len(out_refs)):
            bit = orders[a % 2][stage]
            target = (related(s, 1 << bit), h)
            arrived = {}
            for mask in list(held[a]):
                for copy in held[a][mask]:
                    copy.wait_recv()
                held[a][mask] = []
                group = related(s, mask)
                copy = go(out_refs[a].at[group], out_refs[a].at[group], target)
                arrived[mask | (1 << bit)] = [copy]
            held[a].update(arrived)
    for a in range(len(out_refs)):
        for mask in held[a]:
            for copy in held[a][mask]:
                copy.wait_recv()
    for copy in started:
        copy.wait_send()


def gather_all(arrays, nseq, heads, cid):
    n = len(arrays)
    total = n * (heads - 1 + nseq - 1)

    def kernel(*refs):
        gather_kernel(nseq, heads, refs[:n], refs[n : 2 * n], refs[2 * n], refs[2 * n + 1])

    return pl.pallas_call(
        kernel,
        out_shape=[jax.ShapeDtypeStruct((nseq, heads) + a.shape, a.dtype) for a in arrays],
        in_specs=[pl.BlockSpec(memory_space=VMEM)] * n,
        out_specs=[pl.BlockSpec(memory_space=VMEM)] * n,
        scratch_shapes=[pltpu.SemaphoreType.DMA((total,)), pltpu.SemaphoreType.DMA((total,))],
        name="gather_all",
        compiler_params=pltpu.CompilerParams(
            collective_id=cid, has_side_effects=True, vmem_limit_bytes=LIMIT
        ),
    )(*arrays)


def line_gather_kernel(heads, x_ref, out_ref, send, recv):
    s, h = place()
    right = (s, lax.rem(h + 1, heads))
    left = (s, lax.rem(h + heads - 1, heads))
    greet([right, left])
    out_ref[h] = x_ref[...]
    for step in range(heads - 1):
        to_right = remote(
            out_ref.at[jnp.maximum(h - step, 0)],
            out_ref.at[jnp.maximum(h - step, 0)],
            send.at[0, step],
            recv.at[0, step],
            right,
        )
        to_left = remote(
            out_ref.at[jnp.minimum(h + step, heads - 1)],
            out_ref.at[jnp.minimum(h + step, heads - 1)],
            send.at[1, step],
            recv.at[1, step],
            left,
        )
        pl.when((h - step >= 0) & (h < heads - 1))(to_right.start)
        pl.when((h + step <= heads - 1) & (h > 0))(to_left.start)
        pl.when(h - 1 - step >= 0)(
            remote(
                out_ref.at[jnp.maximum(h - 1 - step, 0)],
                out_ref.at[jnp.maximum(h - 1 - step, 0)],
                send.at[0, step],
                recv.at[0, step],
                right,
            ).wait_recv
        )
        pl.when(h + 1 + step <= heads - 1)(
            remote(
                out_ref.at[jnp.minimum(h + 1 + step, heads - 1)],
                out_ref.at[jnp.minimum(h + 1 + step, heads - 1)],
                send.at[1, step],
                recv.at[1, step],
                left,
            ).wait_recv
        )
        pl.when((h - step >= 0) & (h < heads - 1))(to_right.wait_send)
        pl.when((h + step <= heads - 1) & (h > 0))(to_left.wait_send)


def line_gather(x, heads, cid):
    return pl.pallas_call(
        functools.partial(line_gather_kernel, heads),
        out_shape=jax.ShapeDtypeStruct((heads,) + x.shape, x.dtype),
        in_specs=[pl.BlockSpec(memory_space=VMEM)],
        out_specs=pl.BlockSpec(memory_space=VMEM),
        scratch_shapes=[
            pltpu.SemaphoreType.DMA((2, heads - 1)),
            pltpu.SemaphoreType.DMA((2, heads - 1)),
        ],
        name="line_gather",
        compiler_params=pltpu.CompilerParams(
            collective_id=cid, has_side_effects=True, vmem_limit_bytes=LIMIT
        ),
    )(x)


def line_scatter_kernel(heads, parts, out_ref, from_left, from_right, send, recv):
    s, h = place()
    last = heads - 1
    right = (s, lax.rem(h + 1, heads))
    left = (s, lax.rem(h + heads - 1, heads))
    greet([right, left])
    f32 = jnp.float32
    for step in range(heads - 1):
        r_dest = jnp.clip(last - (step - h), 0, last)
        l_dest = jnp.clip(step - (last - h), 0, last)
        r_on = (step >= h) & (h < last)
        l_on = (step >= last - h) & (h > 0)
        for on, dest, box, lane, target, first in (
            (r_on, r_dest, from_left, 0, right, step == h),
            (l_on, l_dest, from_right, 1, left, step == last - h),
        ):
            at_end = (h == 0) if lane == 0 else (h == last)
            if step > 0:

                def add(box=box, dest=dest):
                    box[step - 1] = (
                        box[step - 1].astype(f32) + parts[dest].astype(f32)
                    ).astype(box.dtype)

                pl.when(on & jnp.logical_not(at_end))(add)
                pl.when(on & jnp.logical_not(at_end))(
                    remote(
                        box.at[step - 1], box.at[step], send.at[lane, step], recv.at[lane, step], target
                    ).start
                )
            pl.when(on & at_end)(
                remote(
                    parts.at[dest], box.at[step], send.at[lane, step], recv.at[lane, step], target
                ).start
            )
        r_in = (step >= h - 1) & (h > 0)
        l_in = (step >= last - h - 1) & (h < last)
        pl.when(r_in)(
            remote(
                from_left.at[step], from_left.at[step], send.at[0, step], recv.at[0, step], right
            ).wait_recv
        )
        pl.when(l_in)(
            remote(
                from_right.at[step], from_right.at[step], send.at[1, step], recv.at[1, step], left
            ).wait_recv
        )
    for step in range(heads - 1):
        for on, box, lane, target in (
            ((step >= h) & (h < last), from_left, 0, right),
            ((step >= last - h) & (h > 0), from_right, 1, left),
        ):
            pl.when(on)(
                remote(
                    box.at[step], box.at[step], send.at[lane, step], recv.at[lane, step], target
                ).wait_send
            )
    out_ref[...] = parts[h].astype(f32)

    def add_left():
        out_ref[...] += from_left[heads - 2].astype(f32)

    def add_right():
        out_ref[...] += from_right[heads - 2].astype(f32)

    pl.when(h > 0)(add_left)
    pl.when(h < last)(add_right)


def line_scatter(parts, heads, cid):
    block = parts.shape[1:]
    return pl.pallas_call(
        functools.partial(line_scatter_kernel, heads),
        out_shape=jax.ShapeDtypeStruct(block, jnp.float32),
        in_specs=[pl.BlockSpec(memory_space=VMEM)],
        out_specs=pl.BlockSpec(memory_space=VMEM),
        scratch_shapes=[
            VMEM((heads - 1,) + block, parts.dtype),
            VMEM((heads - 1,) + block, parts.dtype),
            pltpu.SemaphoreType.DMA((2, heads - 1)),
            pltpu.SemaphoreType.DMA((2, heads - 1)),
        ],
        name="line_scatter",
        compiler_params=pltpu.CompilerParams(
            collective_id=cid, has_side_effects=True, vmem_limit_bytes=LIMIT
        ),
    )(parts)


def scatter_kernel(nseq, heads, zs, orders, parts, outs, boxes, zboxes, send, recv):
    bits = nseq.bit_length() - 1
    s, h = place()
    f32 = jnp.float32
    others = [lax.rem(h + d, heads) for d in range(1, heads)]
    greet(
        [(related(s, 1 << b), h) for b in range(bits)]
        + ([(s, o) for o in others] if any(zs) else [])
    )
    count = [0]
    started = []

    def go(src, dst, target):
        k = count[0]
        count[0] += 1
        copy = remote(src, dst, send.at[k], recv.at[k], target)
        copy.start()
        started.append(copy)
        return copy

    n = len(parts)
    offsets = [0] * n
    slot = [{} for _ in range(n)]
    waiting = [{} for _ in range(n)]

    def current(a, mask):
        if mask in slot[a]:
            return boxes[a].at[slot[a][mask]]
        return parts[a].at[related(s, mask)]

    def launch(a, stage):
        bit = orders[a][stage]
        rest = orders[a][stage + 1 :]
        target = (related(s, 1 << bit), h)
        after = 1 << rest[0] if rest else 0
        masks = sorted(subsets(rest), key=lambda m: 0 if m & after else 1)
        for mask in masks:
            where = offsets[a]
            offsets[a] += 1
            waiting[a][mask] = (
                go(current(a, mask | (1 << bit)), boxes[a].at[where], target),
                where,
            )

    def settle(a, mask):
        copy, where = waiting[a].pop(mask)
        mine = current(a, mask)
        copy.wait_recv()
        boxes[a][where] = (boxes[a][where].astype(f32) + mine[...].astype(f32)).astype(
            boxes[a].dtype
        )
        slot[a][mask] = where

    for a in range(n):
        launch(a, 0)
    for stage in range(bits):
        for a in range(n):
            for mask in list(waiting[a]):
                settle(a, mask)
            if stage + 1 < bits:
                launch(a, stage + 1)
    arriving = []
    for a in range(n):
        if not zs[a]:
            continue
        mine = current(a, 0)
        arriving.append(
            [
                go(mine.at[o], zboxes[a].at[d], (s, o))
                for d, o in enumerate(others)
            ]
        )
    z = 0
    for a in range(n):
        if zs[a]:
            total = current(a, 0)[h].astype(f32)
            for d, copy in enumerate(arriving[z]):
                copy.wait_recv()
                total = total + zboxes[a][d].astype(f32)
            outs[a][...] = total
            z += 1
        else:
            outs[a][...] = current(a, 0)[...].astype(f32)
    for copy in started:
        copy.wait_send()


def scatter_all(arrays, zs, orders, nseq, heads, cid, name):
    n = len(arrays)
    total = sum((nseq - 1) + (heads - 1 if z else 0) for z in zs)
    blocks = [a.shape[2:] if z else a.shape[1:] for a, z in zip(arrays, zs)]

    def kernel(*refs):
        scatter_kernel(
            nseq,
            heads,
            zs,
            orders,
            refs[:n],
            refs[n : 2 * n],
            refs[2 * n : 3 * n],
            refs[3 * n : 4 * n],
            refs[4 * n],
            refs[4 * n + 1],
        )

    return pl.pallas_call(
        kernel,
        out_shape=[jax.ShapeDtypeStruct(b, jnp.float32) for b in blocks],
        in_specs=[pl.BlockSpec(memory_space=VMEM)] * n,
        out_specs=[pl.BlockSpec(memory_space=VMEM)] * n,
        scratch_shapes=[VMEM((nseq - 1,) + a.shape[1:], a.dtype) for a in arrays]
        + [
            VMEM((heads - 1,) + b, a.dtype) if z else VMEM((8, 128), jnp.float32)
            for a, b, z in zip(arrays, blocks, zs)
        ]
        + [pltpu.SemaphoreType.DMA((total,)), pltpu.SemaphoreType.DMA((total,))],
        name=name,
        compiler_params=pltpu.CompilerParams(
            collective_id=cid, has_side_effects=True, vmem_limit_bytes=LIMIT
        ),
    )(*arrays)


def attend_kernel(q_ref, k_ref, v_ref, start_ref, index_ref, out_ref, log_ref):
    s = lax.axis_index("seq")
    span = k_ref.shape[1]
    start = start_ref[...]
    index = index_ref[...]
    queries = q_ref[...]
    rows = queries.shape[0]
    out_ref[...] = jnp.zeros_like(out_ref)

    def step(g, mass):
        scores = contract_last(k_ref[g], queries)
        key = g * span + lax.broadcasted_iota(jnp.int32, (span, rows), 0)
        terms = jnp.where((key >= start) & (key <= index), jnp.exp(scores), 0.0)
        out_ref[...] += contract_first(v_ref[g], terms.astype(jnp.bfloat16))
        return mass + jnp.sum(terms, axis=0, keepdims=True)

    mass = lax.fori_loop(0, s + 1, step, jnp.zeros((1, rows), jnp.float32))
    out_ref[...] = out_ref[...] / mass
    log_ref[...] = jnp.log(mass)


def attend(q, k, v, start, index):
    rows, width = q.shape
    return pl.pallas_call(
        attend_kernel,
        out_shape=[
            jax.ShapeDtypeStruct((width, rows), jnp.float32),
            jax.ShapeDtypeStruct((1, rows), jnp.float32),
        ],
        in_specs=[pl.BlockSpec(memory_space=VMEM)] * 5,
        out_specs=[pl.BlockSpec(memory_space=VMEM)] * 2,
        name="attend",
        compiler_params=pltpu.CompilerParams(vmem_limit_bytes=LIMIT),
    )(q, k, v, start, index)


def attend_back_kernel(
    q_ref, k_ref, v_ref, start_ref, index_ref, log_ref, dots_ref, d_ref, dq_ref, dk_ref, dv_ref
):
    s = lax.axis_index("seq")
    groups, span = k_ref.shape[:2]
    start = start_ref[...]
    index = index_ref[...]
    log_total = log_ref[...]
    dots = dots_ref[...]
    queries = q_ref[...]
    grads = d_ref[...]
    rows = queries.shape[0]
    dq_ref[...] = jnp.zeros_like(dq_ref)

    def step(g, carry):
        keys = k_ref[g]
        scores = contract_last(keys, queries)
        key = g * span + lax.broadcasted_iota(jnp.int32, (span, rows), 0)
        probs = jnp.where((key >= start) & (key <= index), jnp.exp(scores - log_total), 0.0)
        d_probs = contract_last(v_ref[g], grads)
        d_scores = (probs * (d_probs - dots)).astype(jnp.bfloat16)
        dv_ref[g] = jnp.dot(
            probs.astype(jnp.bfloat16), grads, preferred_element_type=jnp.float32
        ).astype(dv_ref.dtype)
        dk_ref[g] = jnp.dot(d_scores, queries, preferred_element_type=jnp.float32).astype(
            dk_ref.dtype
        )
        dq_ref[...] += contract_first(keys, d_scores)
        return carry

    lax.fori_loop(0, s + 1, step, 0)

    def blank(g, carry):
        dk_ref[g] = jnp.zeros(dk_ref.shape[1:], dk_ref.dtype)
        dv_ref[g] = jnp.zeros(dv_ref.shape[1:], dv_ref.dtype)
        return carry

    lax.fori_loop(s + 1, groups, blank, 0)


def attend_back(q, k, v, start, index, log_total, dots, grads):
    rows, width = q.shape
    return pl.pallas_call(
        attend_back_kernel,
        out_shape=[
            jax.ShapeDtypeStruct((width, rows), jnp.float32),
            jax.ShapeDtypeStruct(k.shape, jnp.bfloat16),
            jax.ShapeDtypeStruct(v.shape, jnp.bfloat16),
        ],
        in_specs=[pl.BlockSpec(memory_space=VMEM)] * 8,
        out_specs=[pl.BlockSpec(memory_space=VMEM)] * 3,
        name="attend_back",
        compiler_params=pltpu.CompilerParams(vmem_limit_bytes=LIMIT),
    )(q, k, v, start, index, log_total, dots, grads)


class Sum:
    def __init__(self, links, part, boxes, order):
        self.links, self.part, self.boxes, self.order = links, part, boxes, order
        self.used = 0
        self.slot = {}
        self.waiting = {}

    def current(self, mask):
        if mask in self.slot:
            return self.boxes.at[self.slot[mask]]
        return self.part(mask)

    def masks(self, stage):
        rest = self.order[stage + 1 :]
        weight = lambda m: sum(1 << (len(rest) - i) for i, b in enumerate(rest) if m >> b & 1)
        return sorted(subsets(rest), key=weight, reverse=True)

    def send(self, stage, mask):
        bit = self.order[stage]
        where = self.used
        self.used += 1
        copy = self.links.go(
            self.current(mask | (1 << bit)), self.boxes.at[where], self.links.across(bit)
        )
        self.waiting[stage, mask] = (copy, where)

    def start(self):
        for mask in self.masks(0):
            self.send(0, mask)

    def steps(self, stage, kept=None):
        def step(mask):
            copy, where = self.waiting.pop((stage, mask))
            mine = kept(mask) if kept is not None else self.current(mask)
            copy.wait_recv()
            self.boxes[where] = self.boxes[where] + mine[...]
            self.slot[mask] = where
            if stage + 1 < len(self.order):
                bit = 1 << self.order[stage + 1]
                if mask & bit:
                    self.send(stage + 1, mask & ~bit)

        return [functools.partial(step, mask) for mask in self.masks(stage)]

    def last(self, kept=None):
        copy, where = self.waiting.pop((len(self.order) - 1, 0))
        mine = kept(0) if kept is not None else self.current(0)
        copy.wait_recv()
        return self.boxes[where].astype(jnp.float32) + mine[...].astype(jnp.float32)


def in_turn(*lists):
    for group in itertools.zip_longest(*lists):
        for step in group:
            if step is not None:
                step()


class Links:
    def __init__(self, nseq, heads, send, recv):
        self.s, self.h = place()
        self.nseq, self.heads = nseq, heads
        self.send, self.recv = send, recv
        self.count = 0
        self.started = []
        self.others = [lax.rem(self.h + d, heads) for d in range(1, heads)]

    def greet(self):
        bits = self.nseq.bit_length() - 1
        greet([self.across(b) for b in range(bits)] + [(self.s, o) for o in self.others])

    def across(self, bit):
        return (related(self.s, 1 << bit), self.h)

    def go(self, src, dst, target):
        k = self.count
        self.count += 1
        copy = remote(src, dst, self.send.at[k], self.recv.at[k], target)
        copy.start()
        self.started.append(copy)
        return copy

    def over_heads(self, src, boxes):
        return [self.go(src.at[o], boxes.at[d], (self.s, o)) for d, o in enumerate(self.others)]

    def finish(self):
        for copy in self.started:
            copy.wait_send()


def back_norm(v, gain, d_out):
    scale = lax.rsqrt(jnp.mean(v * v, axis=-1, keepdims=True) + EPS)
    unit = v * scale
    inner = d_out * gain
    d_v = scale * (inner - unit * jnp.mean(inner * unit, axis=-1, keepdims=True))
    return d_v, jnp.sum(d_out * unit, axis=0, keepdims=True)


def back_rotate(d, cosines, sines):
    half = d.shape[-1] // 2
    first, second = d[:, :half], d[:, half:]
    return jnp.concatenate(
        [first * cosines + second * sines, second * cosines - first * sines], axis=-1
    )


def tail_kernel(
    nseq,
    heads,
    qcount,
    scale,
    q_ref,
    start_ref,
    index_ref,
    log_ref,
    att_ref,
    mixed_t_ref,
    d_proj_ref,
    w_out_ref,
    q_lin_ref,
    k_lin_ref,
    cos_ref,
    sin_ref,
    gain_q_ref,
    gain_k_ref,
    attn_t_ref,
    x_ref,
    gain_in_ref,
    d_hid_ref,
    gains_ref,
    k_far,
    v_far,
    w_qkv_far,
    d_gate_ref,
    d_up_ref,
    d_down_ref,
    o_tokens,
    o_qkv,
    o_out,
    o_gate,
    o_up,
    o_down,
    o_gains,
    k_ref,
    v_ref,
    w_qkv_ref,
    dk,
    dv,
    dq_t,
    grads,
    grads_t,
    box_k,
    box_v,
    zbox_k,
    zbox_v,
    dw_out,
    box_out,
    zbox_out,
    mid_out,
    end_out,
    dw_qkv,
    box_qkv,
    zsrc_qkv,
    zbox_qkv,
    d_qkv,
    keep_gate,
    keep_up,
    keep_first,
    keep_second,
    box_gate,
    box_up,
    box_first,
    box_second,
    gsum,
    gbox,
    gzbox,
    send,
    recv,
    local_sem,
):
    f32, bf16 = jnp.float32, jnp.bfloat16
    bits = nseq.bit_length() - 1
    ups, downs = seq_orders(bits)
    links = Links(nseq, heads, send, recv)
    s, h = links.s, links.h
    rows = d_proj_ref.shape[0]
    width = gain_q_ref.shape[1]
    groups, span = k_ref.shape[:2]
    loads = []

    def load(src, dst):
        copy = pltpu.make_async_copy(src, dst, local_sem.at[len(loads)])
        copy.start()
        loads.append(copy)
        return copy

    load_k = load(k_far, k_ref)
    load_v = load(v_far, v_ref)
    links.greet()

    held = subsets(ups)
    ffn = []
    split = keep_first.shape[1]
    for src, keep, box, order, low in (
        (d_gate_ref, keep_gate, box_gate, ups, 0),
        (d_up_ref, keep_up, box_up, [0] + downs, 0),
        (d_down_ref, keep_first, box_first, ups, 0),
        (d_down_ref, keep_second, box_second, downs, split),
    ):
        here = pl.ds(low, keep.shape[1])

        def part(m, src=src, here=here):
            if src is d_up_ref:
                return src.at[related(s, m)]
            return src.at[held.index(m), here]

        total = Sum(links, part, box, order)
        kept = subsets(order[1:])
        total.loads = [load(part(m), keep.at[i]) for i, m in enumerate(kept)]
        total.kept = lambda m, keep=keep, kept=kept: keep.at[kept.index(m)]
        ffn.append(total)
    gate, up, first, second = ffn
    up.start()
    gate.start()
    load_w = load(w_qkv_far, w_qkv_ref)

    d_proj = d_proj_ref[...]

    def out_block(j, carry):
        dw_out[j] = (
            jnp.dot(mixed_t_ref[j], d_proj, preferred_element_type=f32)
            .astype(bf16)
            .reshape(dw_out.shape[1:])
        )
        return carry

    lax.fori_loop(0, nseq, out_block, 0)
    sum_out = Sum(links, lambda m: dw_out.at[related(s, m)], box_out, [0])
    sum_out.masks = lambda stage: held
    sum_out.start()

    for j in range(qcount):
        part = w_out_ref[pl.ds(j * width, width), :]
        grads[pl.ds(j * rows, rows), :] = contract_last(d_proj, part).astype(bf16)
        grads_t[:, pl.ds(j * rows, rows)] = contract_last(part, d_proj).astype(bf16)
    for copy in up.loads:
        copy.wait()
    in_turn(up.steps(0, up.kept))
    dots = jnp.sum(grads_t[...].astype(f32) * att_ref[...], axis=0, keepdims=True)
    start = start_ref[...]
    index = index_ref[...]
    log_total = log_ref[...]
    dq_t[...] = jnp.zeros_like(dq_t)
    load_k.wait()
    load_v.wait()

    def step(g, carry):
        keys = k_ref[g]
        queries = q_ref[...]
        scores = contract_last(keys, queries)
        key = g * span + lax.broadcasted_iota(jnp.int32, scores.shape, 0)
        probs = jnp.where((key >= start) & (key <= index), jnp.exp(scores - log_total), 0.0)
        d_probs = jnp.dot(v_ref[g], grads_t[...], preferred_element_type=f32)
        d_scores = (probs * (d_probs - dots)).astype(bf16)
        dv[g] = (
            jnp.dot(probs.astype(bf16), grads[...], preferred_element_type=f32)
            .astype(bf16)
            .reshape(dv.shape[1:])
        )
        dk[g] = (
            jnp.dot(d_scores, queries, preferred_element_type=f32)
            .astype(bf16)
            .reshape(dk.shape[1:])
        )
        dq_t[...] += contract_first(keys, d_scores)
        return carry

    lax.fori_loop(0, s + 1, step, 0)

    def blank(g, carry):
        dk[g] = jnp.zeros(dk.shape[1:], bf16)
        dv[g] = jnp.zeros(dv.shape[1:], bf16)
        return carry

    lax.fori_loop(s + 1, groups, blank, 0)

    kv = []
    for j in list(range(1, heads)) + [0]:
        owner = lax.rem(h + j, heads)
        for far, box, order in ((dk, box_k, ups), (dv, box_v, downs)):
            kv.append(
                Sum(
                    links,
                    lambda m, far=far, owner=owner: far.at[related(s, m), owner],
                    box.at[j],
                    [0] + order,
                )
            )
    for mask_index in range(len(held)):
        for total in kv:
            total.send(0, total.masks(0)[mask_index])

    for m in sum_out.steps(0):
        m()
    z_out = [
        links.go(box_out.at[:, o], zbox_out.at[d], (s, o)) for d, o in enumerate(links.others)
    ]
    in_turn(*[total.steps(0) for total in kv])

    cosines, sines = cos_ref[...], sin_ref[...]
    d_gain_q = jnp.zeros((1, width), f32)
    for j in range(qcount):
        d_rot = dq_t[:, pl.ds(j * rows, rows)].T * scale
        d_lin, terms = back_norm(
            q_lin_ref[:, pl.ds(j * width, width)],
            gain_q_ref[...],
            back_rotate(d_rot, cosines, sines),
        )
        d_qkv[:, pl.ds(j * width, width)] = d_lin.astype(bf16)
        d_gain_q = d_gain_q + terms

    for stage in range(1, bits - 1):
        in_turn(*[total.steps(stage) for total in kv])
    for total in (gate, first, second):
        for copy in total.loads:
            copy.wait()
    in_turn(gate.steps(0, gate.kept), up.steps(1))
    first.start()
    second.start()

    arriving = {}
    for i, total in enumerate(kv):
        for m in total.steps(bits - 1):
            m()
        j = (i // 2 + 1) % heads
        if j:
            zbox = (zbox_k, zbox_v)[i % 2]
            arriving[i % 2, j] = links.go(
                total.current(0), zbox.at[j - 1], (s, links.others[j - 1])
            )
    for d, copy in enumerate(z_out):
        copy.wait_recv()
    own = box_out[:, h].astype(f32)
    for d in range(heads - 1):
        own = own + zbox_out[d].astype(f32)
    mid_out[...] = own.astype(bf16)
    sum_end = Sum(links, lambda m: mid_out.at[held.index(m)], end_out, downs)
    sum_end.start()

    def whole(i, zbox):
        total = kv[len(kv) - 2 + i].current(0)[...].astype(f32)
        for j in range(1, heads):
            arriving[i, j].wait_recv()
            total = total + zbox[j - 1].astype(f32)
        return total

    d_keys = whole(0, zbox_k)
    d_lin, d_gain_k = back_norm(
        k_lin_ref[...], gain_k_ref[...], back_rotate(d_keys, cosines, sines)
    )
    qw = qcount * width
    d_qkv[:, pl.ds(qw, width)] = d_lin.astype(bf16)
    d_values = whole(1, zbox_v)
    d_qkv[:, pl.ds(qw + width, width)] = d_values.astype(bf16)

    pieces, _, block_rows, cut = dw_qkv.shape
    qkv = []
    for j in range(pieces):
        cols = pl.ds(j * cut, cut)

        def qkv_block(g, carry, j=j, cols=cols):
            dw_qkv[j, g] = jnp.dot(
                attn_t_ref[g], d_qkv[:, cols], preferred_element_type=f32
            ).astype(bf16)
            return carry

        lax.fori_loop(0, nseq, qkv_block, 0)
        total = Sum(
            links,
            lambda m, j=j: dw_qkv.at[j, related(s, m)],
            box_qkv.at[j],
            [0] + (downs if j % 2 else ups),
        )
        total.start()
        qkv.append(total)

    load_w.wait()
    d_attn_in = contract_last(d_qkv[...], w_qkv_ref[...])
    in_turn(*[total.steps(0) for total in qkv])
    d_x, d_gain_in = back_norm(x_ref[...].astype(f32), gain_in_ref[...], d_attn_in)
    o_tokens[...] = (d_hid_ref[...] + d_x).astype(o_tokens.dtype)

    gsum[0] = gains_ref[...]
    gsum[0, 0:1, :] = d_gain_in
    gsum[0, 4:5, :width] = d_gain_q
    gsum[0, 5:6, :width] = d_gain_k
    gain_copy = links.go(gsum.at[0], gbox.at[0], links.across(0))
    for stage in range(1, bits - 1):
        in_turn(*[total.steps(stage) for total in qkv])
    for bit in range(bits):
        gain_copy.wait_recv()
        gsum[bit + 1] = gsum[bit] + gbox[bit]
        if bit + 1 < bits:
            gain_copy = links.go(gsum.at[bit + 1], gbox.at[bit + 1], links.across(bit + 1))
    gain_z = [
        links.go(gsum.at[bits], gzbox.at[d], (s, o)) for d, o in enumerate(links.others)
    ]
    in_turn(sum_end.steps(0))
    in_turn(first.steps(0, first.kept), second.steps(0, second.kept))

    each = block_rows // heads
    z_qkv = []
    for j, total in enumerate(qkv):
        value = total.last()
        for p in range(heads):
            zsrc_qkv[j, p] = value[p * each : (p + 1) * each].astype(bf16)
        z_qkv.append(links.over_heads(zsrc_qkv.at[j], zbox_qkv.at[j]))
    o_gate[...] = gate.last()
    o_up[...] = up.last()
    o_down[pl.ds(0, split), :] = first.last()
    o_down[pl.ds(split, o_down.shape[0] - split), :] = second.last()
    o_out[...] = sum_end.last()
    total = gsum[bits]
    for d, copy in enumerate(gain_z):
        copy.wait_recv()
        total = total + gzbox[d]
    o_gains[...] = total
    for j, copies in enumerate(z_qkv):
        total = zsrc_qkv[j, h].astype(f32)
        for d, copy in enumerate(copies):
            copy.wait_recv()
            total = total + zbox_qkv[j, d].astype(f32)
        o_qkv[:, pl.ds(j * cut, cut)] = total
    links.finish()


def tail(nseq, heads, qcount, scale, cid, *arrays):
    (q, _, _, _, att, mixed_t, d_proj, w_out, q_lin, k_lin, _, _, gain_q, _) = arrays[:14]
    (attn_t, x, gain_in, d_hid, gains, k, v, w_qkv, d_gate, _, _) = arrays[14:]
    f32, bf16 = jnp.float32, jnp.bfloat16
    rows, model = d_proj.shape
    width = gain_q.shape[1]
    cols = w_qkv.shape[1]
    pieces = 4
    cut = cols // pieces
    out_rows, qkv_rows = mixed_t.shape[1], attn_t.shape[1]
    ffn_block = d_gate.shape[1:]
    some, all_but = nseq // 2, nseq - 1
    bits = nseq.bit_length() - 1
    out_block = (heads, out_rows // heads, model)
    split = (ffn_block[0] // 2 + 15) // 16 * 16
    parts = [ffn_block, ffn_block, (split, ffn_block[1]), (ffn_block[0] - split, ffn_block[1])]
    copies = (
        3 * (some - 1)
        + all_but
        + some
        + (heads - 1)
        + (some - 1)
        + 2 * heads * all_but
        + 2 * (heads - 1)
        + pieces * (all_but + heads - 1)
        + bits
        + (heads - 1)
    )
    vm = pl.BlockSpec(memory_space=VMEM)
    anywhere = pl.BlockSpec(memory_space=pl.ANY)

    def kernel(*refs):
        tail_kernel(nseq, heads, qcount, scale, *refs)

    return pl.pallas_call(
        kernel,
        out_shape=[
            jax.ShapeDtypeStruct((rows, model), bf16),
            jax.ShapeDtypeStruct((qkv_rows // heads, cols), f32),
            jax.ShapeDtypeStruct(out_block[1:], f32),
            jax.ShapeDtypeStruct(ffn_block, f32),
            jax.ShapeDtypeStruct(ffn_block, f32),
            jax.ShapeDtypeStruct(ffn_block, f32),
            jax.ShapeDtypeStruct(gains.shape, f32),
        ],
        in_specs=[vm] * (len(arrays) - 6) + [anywhere] * 6,
        out_specs=[vm] * 7,
        scratch_shapes=[
            VMEM(k.shape, bf16),
            VMEM(v.shape, bf16),
            VMEM(w_qkv.shape, bf16),
            VMEM((nseq, heads, rows, width), bf16),
            VMEM((nseq, heads, rows, width), bf16),
            VMEM((width, qcount * rows), f32),
            VMEM((qcount * rows, width), bf16),
            VMEM((width, qcount * rows), bf16),
            VMEM((heads, all_but, rows, width), bf16),
            VMEM((heads, all_but, rows, width), bf16),
            VMEM((heads - 1, rows, width), bf16),
            VMEM((heads - 1, rows, width), bf16),
            VMEM((nseq,) + out_block, bf16),
            VMEM((some,) + out_block, bf16),
            VMEM((heads - 1, some) + out_block[1:], bf16),
            VMEM((some,) + out_block[1:], bf16),
            VMEM((some - 1,) + out_block[1:], bf16),
            VMEM((pieces, nseq, qkv_rows, cut), bf16),
            VMEM((pieces, all_but, qkv_rows, cut), bf16),
            VMEM((pieces, heads, qkv_rows // heads, cut), bf16),
            VMEM((pieces, heads - 1, qkv_rows // heads, cut), bf16),
            VMEM((rows, cols), bf16),
        ]
        + [VMEM((some if i == 1 else some // 2,) + part, bf16) for i, part in enumerate(parts)]
        + [VMEM((all_but if i == 1 else some - 1,) + part, bf16) for i, part in enumerate(parts)]
        + [
            VMEM((bits + 1,) + gains.shape, f32),
            VMEM((bits,) + gains.shape, f32),
            VMEM((heads - 1,) + gains.shape, f32),
            pltpu.SemaphoreType.DMA((copies,)),
            pltpu.SemaphoreType.DMA((copies,)),
            pltpu.SemaphoreType.DMA((3 + 3 * some,)),
        ],
        name="tail",
        compiler_params=pltpu.CompilerParams(
            collective_id=cid, has_side_effects=True, vmem_limit_bytes=62 * 2**20
        ),
    )(*arrays)


CHUNKS, SPANS = 4, 2
ORDER = (
    ("ags", 0, 0, 0), ("ags", 0, 1, 0), ("agw", 0, 0, 0), ("ags", 0, 0, 1), ("agw", 0, 1, 0),
    ("ags", 0, 1, 1), ("ags", 0, 2, 0), ("agw", 0, 0, 1), ("ags", 0, 0, 2), ("agw", 0, 1, 1),
    ("ags", 0, 1, 2), ("ags", 0, 3, 0), ("agw", 0, 0, 2), ("agw", 0, 1, 2), ("fa", 0), ("fb", 0),
    ("agw", 0, 3, 0), ("agw", 0, 2, 0), ("ags", 0, 3, 1), ("ags", 0, 2, 1), ("fc", 0),
    ("agw", 0, 3, 1), ("rss", 0, 0, 0), ("ags", 0, 3, 2), ("agw", 0, 3, 2), ("agw", 0, 2, 1),
    ("rss", 0, 1, 0), ("ags", 0, 2, 2), ("rsw", 0, 0, 0), ("rss", 0, 0, 1), ("rsw", 0, 1, 0),
    ("rss", 0, 1, 1), ("agw", 0, 2, 2), ("fa", 1), ("rsw", 0, 0, 1), ("fb", 1), ("rss", 0, 0, 2),
    ("fc", 1), ("rss", 0, 2, 0), ("rsw", 0, 1, 1), ("rss", 0, 3, 0), ("rss", 0, 1, 2),
    ("rsw", 0, 2, 0), ("rss", 0, 2, 1), ("rsw", 0, 0, 2), ("rsw", 0, 3, 0), ("n", 0),
    ("ags", 1, 0, 0), ("rsw", 0, 1, 2), ("rss", 0, 3, 1), ("rsw", 0, 2, 1), ("rss", 0, 2, 2),
    ("n", 1), ("agw", 1, 0, 0), ("ags", 1, 1, 0), ("ags", 1, 0, 1), ("rsw", 0, 3, 1),
    ("rss", 0, 3, 2), ("agw", 1, 1, 0), ("ags", 1, 1, 1), ("rsw", 0, 2, 2), ("n", 2),
    ("agw", 1, 0, 1), ("ags", 1, 0, 2), ("ags", 1, 2, 0), ("rsw", 0, 3, 2), ("n", 3),
    ("agw", 1, 1, 1), ("ags", 1, 1, 2), ("ags", 1, 3, 0), ("agw", 1, 0, 2), ("agw", 1, 2, 0),
    ("agw", 1, 1, 2), ("ga", 0), ("ags", 1, 2, 1), ("gb", 0), ("agw", 1, 3, 0), ("ags", 1, 3, 1),
    ("gc", 0), ("agw", 1, 2, 1), ("ags", 1, 2, 2), ("rss", 1, 1, 0), ("rss", 1, 0, 0),
    ("agw", 1, 3, 1), ("ags", 1, 3, 2), ("rsw", 1, 1, 0), ("rss", 1, 1, 1), ("agw", 1, 2, 2),
    ("agw", 1, 3, 2), ("ga", 1), ("rsw", 1, 0, 0), ("gb", 1), ("rss", 1, 0, 1), ("gc", 1),
    ("rss", 1, 3, 0), ("wd", 0), ("rsw", 1, 1, 1), ("rss", 1, 2, 0), ("wd", 1), ("rss", 1, 1, 2),
    ("dd", 0), ("rsw", 1, 3, 0), ("rss", 1, 3, 1), ("wg", 0), ("rsw", 1, 2, 0), ("rsw", 1, 0, 1),
    ("rss", 1, 2, 1), ("wg", 1), ("dg", 0), ("rss", 1, 0, 2), ("rsw", 1, 1, 2), ("wu", 0),
    ("rsw", 1, 3, 1), ("e", 1), ("rss", 1, 3, 2), ("rsw", 1, 2, 1), ("rss", 1, 2, 2), ("wu", 1),
    ("rsw", 1, 0, 2), ("Dd", 0), ("Dg", 0), ("e", 0), ("rsw", 1, 3, 2), ("e", 3), ("rsw", 1, 2, 2),
    ("e", 2),
)


def ffn_kernel(
    nseq,
    heads,
    chunks,
    spans,
    proj_ref,
    x_ref,
    cot_ref,
    gain_two_ref,
    gain_three_ref,
    gain_four_ref,
    w_gate_ref,
    w_up_ref,
    w_down_ref,
    o_out,
    o_hid,
    o_proj,
    o_gains,
    o_down,
    o_gate,
    o_up,
    hidden,
    w_gate,
    w_up,
    w_down,
    u_all,
    d_all,
    by_gate,
    by_up,
    act,
    d_gate,
    d_up,
    parts,
    from_left,
    from_right,
    flipped,
    dw_gate,
    dw_up,
    dw_down,
    box_gate,
    box_down,
    sum_send,
    sum_recv,
    ag_send,
    ag_recv,
    rs_send,
    rs_recv,
    local_sem,
):
    f32, bf16 = jnp.float32, jnp.bfloat16
    s, h = place()
    last = heads - 1
    right = (s, lax.rem(h + 1, heads))
    left = (s, lax.rem(h + last, heads))
    rows, model = x_ref.shape
    units = w_gate.shape[0]
    rc = rows // chunks
    each = chunks // spans
    many = rc * heads * each
    tile = 256
    whole_tiles, rest = units // tile, units % tile

    loads = []
    for n, (src, dst) in enumerate(
        ((w_gate_ref, w_gate), (w_up_ref, w_up), (w_down_ref, w_down))
    ):
        copy = pltpu.make_async_copy(src, dst, local_sem.at[n])
        copy.start()
        loads.append(copy)
    bits = nseq.bit_length() - 1
    ups, downs = seq_orders(bits)
    links = Links(nseq, heads, sum_send, sum_recv)
    greet([right, left] + [links.across(b) for b in range(bits)])

    proj = proj_ref[...]
    hid = x_ref[...].astype(f32) + norm_rows(proj, gain_two_ref[...])
    hidden[...] = hid
    u_local = norm_rows(hid, gain_three_ref[...]).astype(bf16)
    for c in range(chunks):
        u_all[c, h] = u_local[c * rc : (c + 1) * rc]
    o_gains[...] = jnp.zeros_like(o_gains)

    def lanes(k, c, t):
        buf = d_all if k else u_all
        return (
            (
                (h - t >= 0) & (h < last),
                buf.at[c, jnp.maximum(h - t, 0)],
                0,
                right,
                h - 1 - t >= 0,
                buf.at[c, jnp.maximum(h - 1 - t, 0)],
            ),
            (
                (h + t <= last) & (h > 0),
                buf.at[c, jnp.minimum(h + t, last)],
                1,
                left,
                h + 1 + t <= last,
                buf.at[c, jnp.minimum(h + 1 + t, last)],
            ),
        )

    def ags(k, c, t):
        for on, block, lane, target, _, _ in lanes(k, c, t):
            i = (k, c, lane, t)
            pl.when(on)(remote(block, block, ag_send.at[i], ag_recv.at[i], target).start)

    def agw(k, c, t):
        for _, _, lane, target, on, block in lanes(k, c, t):
            i = (k, c, lane, t)
            pl.when(on)(remote(block, block, ag_send.at[i], ag_recv.at[i], target).wait_recv)

    def rss(k, c, t):
        for on, dest, box, lane, target, at_end in (
            ((t >= h) & (h < last), last - (t - h), from_left, 0, right, h == 0),
            ((t >= last - h) & (h > 0), t - (last - h), from_right, 1, left, h == last),
        ):
            dest = jnp.clip(dest, 0, last)
            i = (k, c, lane, t)
            if t > 0:

                def forward(box=box, dest=dest, i=i, target=target):
                    box[k, c, t - 1] = box[k, c, t - 1] + parts[k, c, dest]
                    remote(
                        box.at[k, c, t - 1], box.at[k, c, t], rs_send.at[i], rs_recv.at[i], target
                    ).start()

                pl.when(on & jnp.logical_not(at_end))(forward)
            pl.when(on & at_end)(
                remote(
                    parts.at[k, c, dest], box.at[k, c, t], rs_send.at[i], rs_recv.at[i], target
                ).start
            )

    def rsw(k, c, t):
        for on, box, lane, target in (
            ((t >= h - 1) & (h > 0), from_left, 0, right),
            ((t >= last - h - 1) & (h < last), from_right, 1, left),
        ):
            i = (k, c, lane, t)
            block = box.at[k, c, t]
            pl.when(on)(remote(block, block, rs_send.at[i], rs_recv.at[i], target).wait_recv)

    def summed(k, c):
        zero = jnp.zeros((rc, model), f32)
        return (
            parts[k, c, h].astype(f32)
            + jnp.where(h > 0, from_left[k, c, last - 1].astype(f32), zero)
            + jnp.where(h < last, from_right[k, c, last - 1].astype(f32), zero)
        )

    def over_tiles(lo, hi, body):
        def step(i, carry):
            body(pl.ds(pl.multiple_of(i * tile, tile), tile))
            return carry

        lax.fori_loop(lo, hi, step, 0)
        if hi == whole_tiles and rest:
            body(pl.ds(whole_tiles * tile, rest))

    arrived = set()

    def need(n):
        if n not in arrived:
            arrived.add(n)
            loads[n].wait()

    def span_rows(buf, p):
        return buf[pl.ds(p * each, each)].reshape(many, model)

    def place_parts(k, p, cols, value):
        parts[k, pl.ds(p * each, each), :, :, cols] = value.astype(bf16).reshape(
            each, heads, rc, value.shape[1]
        )

    def forward_tiles(c, lo, hi):
        need(0)
        need(1)

        def body(cols):
            u = span_rows(u_all, c)
            gate = contract_last(u, w_gate[cols, :])
            up = contract_last(u, w_up[cols, :])
            root = math.sqrt(2.0 / math.pi)
            square = gate * gate
            curve = jnp.tanh(root * gate * (1.0 + 0.044715 * square))
            half = 0.5 * (1.0 + curve)
            gelu = gate * half
            slope = half + 0.5 * gate * (1.0 - curve * curve) * (
                root * (1.0 + 3 * 0.044715 * square)
            )
            by_gate[pl.ds(c * many, many), cols] = slope * up
            by_up[pl.ds(c * many, many), cols] = gelu
            act[pl.ds(c * many, many), cols] = (gelu * up).astype(bf16)

        over_tiles(lo, hi, body)

    out_tile = model // 3

    def down_rows(c):
        need(2)

        def body(i, carry):
            cols = pl.ds(pl.multiple_of(i * out_tile, out_tile), out_tile)
            part = jnp.dot(
                act[pl.ds(c * many, many), :], w_down[:, cols], preferred_element_type=f32
            )
            place_parts(0, c, cols, part)
            return carry

        lax.fori_loop(0, 3, body, 0)

    def turn(c):
        here = pl.ds(c * rc, rc)
        ffn_out = summed(0, c)
        upstream = cot_ref[here, :].astype(f32)
        o_out[here, :] = (hidden[here, :] + norm_rows(ffn_out, gain_four_ref[...])).astype(
            o_out.dtype
        )
        d_out, terms = back_norm(ffn_out, gain_four_ref[...], upstream)
        d_all[c, h] = d_out.astype(bf16)
        o_gains[3:4, :] += terms

    def back_tiles(c, lo, hi):
        def body(cols):
            d_act = contract_last(span_rows(d_all, c), w_down[cols, :])
            d_gate[pl.ds(c * many, many), cols] = (
                d_act * by_gate[pl.ds(c * many, many), cols]
            ).astype(bf16)
            d_up[pl.ds(c * many, many), cols] = (
                d_act * by_up[pl.ds(c * many, many), cols]
            ).astype(bf16)

        over_tiles(lo, hi, body)

    def back_rows(c):
        def body(i, carry):
            cols = pl.ds(pl.multiple_of(i * out_tile, out_tile), out_tile)
            part = jnp.dot(
                d_gate[pl.ds(c * many, many), :], w_gate[:, cols], preferred_element_type=f32
            )
            part = part + jnp.dot(
                d_up[pl.ds(c * many, many), :], w_up[:, cols], preferred_element_type=f32
            )
            place_parts(1, c, cols, part)
            return carry

        lax.fori_loop(0, 3, body, 0)

    def finish_rows(c):
        here = pl.ds(c * rc, rc)
        d_in, terms = back_norm(hidden[here, :], gain_three_ref[...], summed(1, c))
        o_gains[2:3, :] += terms
        d_hid = cot_ref[here, :].astype(f32) + d_in
        o_hid[here, :] = d_hid
        d_proj, terms = back_norm(proj_ref[here, :], gain_two_ref[...], d_hid)
        o_proj[here, :] = d_proj.astype(o_proj.dtype)
        o_gains[1:2, :] += terms

    stores = []

    def flip(source):
        for p in range(spans):
            flipped[:, pl.ds(p * many, many)] = span_rows(source, p).T

    def weight_grad(right_ref, dst, half):
        def body(cols):
            value = jnp.dot(flipped[...], right_ref[:, cols], preferred_element_type=f32)
            dst[:, :, cols] = value.astype(bf16).reshape(dst.shape[:2] + (value.shape[1],))

        over_tiles(half_tiles if half else 0, whole_tiles if half else half_tiles, body)

    half_tiles = (whole_tiles + 1) // 2
    held = subsets(ups)
    sum_gate = Sum(links, lambda m: dw_gate.at[related(s, m)], box_gate, [0])
    sum_down = Sum(links, lambda m: dw_down.at[related(s, m)], box_down, [0])
    for total in (sum_gate, sum_down):
        total.masks = lambda stage: held
    def keep(total, out, n):
        for i, step in enumerate(total.steps(0)):
            step()
            copy = pltpu.make_async_copy(total.boxes.at[i], out.at[i], local_sem.at[n + i])
            copy.start()
            stores.append(copy)

    for event in ORDER:
        kind, args = event[0], event[1:]
        if kind == "ags":
            ags(*args)
        elif kind == "agw":
            agw(*args)
        elif kind == "rss":
            rss(*args)
        elif kind == "rsw":
            rsw(*args)
        elif kind == "fa":
            forward_tiles(args[0], 0, half_tiles)
        elif kind == "fb":
            forward_tiles(args[0], half_tiles, whole_tiles)
        elif kind == "fc":
            down_rows(args[0])
        elif kind == "n":
            turn(args[0])
        elif kind == "ga":
            back_tiles(args[0], 0, half_tiles)
        elif kind == "gb":
            back_tiles(args[0], half_tiles, whole_tiles)
        elif kind == "gc":
            back_rows(args[0])
        elif kind == "e":
            finish_rows(args[0])
        elif kind == "wd":
            if args[0] == 0:
                flip(d_all)
            weight_grad(act, dw_down, args[0])
        elif kind == "wg":
            if args[0] == 0:
                flip(u_all)
            weight_grad(d_gate, dw_gate, args[0])
        elif kind == "wu":
            weight_grad(d_up, dw_up, args[0])
            if args[0] == 1:
                copy = pltpu.make_async_copy(dw_up, o_up, local_sem.at[3 + 2 * len(held)])
                copy.start()
                stores.append(copy)
        elif kind == "dd":
            sum_down.start()
        elif kind == "dg":
            sum_gate.start()
        elif kind == "Dd":
            keep(sum_down, o_down, 3)
        else:
            keep(sum_gate, o_gate, 3 + len(held))

    for event in ORDER:
        if event[0] == "ags":
            k, c, t = event[1:]
            for on, block, lane, target, _, _ in lanes(k, c, t):
                i = (k, c, lane, t)
                pl.when(on)(remote(block, block, ag_send.at[i], ag_recv.at[i], target).wait_send)
        elif event[0] == "rss":
            k, c, t = event[1:]
            for on, box, lane, target in (
                ((t >= h) & (h < last), from_left, 0, right),
                ((t >= last - h) & (h > 0), from_right, 1, left),
            ):
                i = (k, c, lane, t)
                block = box.at[k, c, t]
                pl.when(on)(remote(block, block, rs_send.at[i], rs_recv.at[i], target).wait_send)
    for n in range(3):
        need(n)
    for copy in stores:
        copy.wait()
    links.finish()


def feed_forward(nseq, heads, cid, proj, x, cot, gains, w_gate, w_up, w_down):
    f32, bf16 = jnp.float32, jnp.bfloat16
    rows, model = x.shape
    units = w_gate.shape[0]
    chunks = CHUNKS
    rc = rows // chunks
    group = rows * heads
    vm = pl.BlockSpec(memory_space=VMEM)
    anywhere = pl.BlockSpec(memory_space=pl.ANY)
    block = (model // nseq, units)
    some = nseq // 2
    half = jax.ShapeDtypeStruct((some,) + block, bf16)
    messages = 2 * some
    hops = (2, chunks, 2, heads - 1)
    return pl.pallas_call(
        functools.partial(ffn_kernel, nseq, heads, CHUNKS, SPANS),
        out_shape=[
            jax.ShapeDtypeStruct((rows, model), bf16),
            jax.ShapeDtypeStruct((rows, model), f32),
            jax.ShapeDtypeStruct((rows, model), bf16),
            jax.ShapeDtypeStruct((8, model), f32),
            half,
            half,
            jax.ShapeDtypeStruct((nseq,) + block, bf16),
        ],
        in_specs=[vm] * 6 + [anywhere] * 3,
        out_specs=[vm] * 4 + [anywhere] * 3,
        scratch_shapes=[
            VMEM((rows, model), f32),
            VMEM(w_gate.shape, bf16),
            VMEM(w_up.shape, bf16),
            VMEM(w_down.shape, bf16),
            VMEM((chunks, heads, rc, model), bf16),
            VMEM((chunks, heads, rc, model), bf16),
            VMEM((group, units), f32),
            VMEM((group, units), f32),
            VMEM((group, units), bf16),
            VMEM((group, units), bf16),
            VMEM((group, units), bf16),
            VMEM((2, chunks, heads, rc, model), bf16),
            VMEM((2, chunks, heads - 1, rc, model), bf16),
            VMEM((2, chunks, heads - 1, rc, model), bf16),
            VMEM((model, group), bf16),
            VMEM((nseq,) + block, bf16),
            VMEM((nseq,) + block, bf16),
            VMEM((nseq,) + block, bf16),
            VMEM((some,) + block, bf16),
            VMEM((some,) + block, bf16),
            pltpu.SemaphoreType.DMA((messages,)),
            pltpu.SemaphoreType.DMA((messages,)),
            pltpu.SemaphoreType.DMA(hops),
            pltpu.SemaphoreType.DMA(hops),
            pltpu.SemaphoreType.DMA(hops),
            pltpu.SemaphoreType.DMA(hops),
            pltpu.SemaphoreType.DMA((4 + 2 * some,)),
        ],
        name="feed_forward",
        compiler_params=pltpu.CompilerParams(
            collective_id=cid, has_side_effects=True, vmem_limit_bytes=62 * 2**20
        ),
    )(proj, x, cot, *[g[None] for g in gains], w_gate, w_up, w_down)


def local(
    tokens,
    segment_ids,
    w_query,
    w_key,
    w_value,
    w_out,
    w_gate,
    w_up,
    w_down,
    gain_attn_in,
    gain_attn_out,
    gain_ffn_in,
    gain_ffn_out,
    gain_query,
    gain_key,
    cotangent,
):
    heads = lax.axis_size("head")
    nseq = lax.axis_size("seq")
    head_index = lax.axis_index("head")
    seq_index = lax.axis_index("seq")
    bits = nseq.bit_length() - 1
    local_rows, model = tokens.shape
    width = gain_query.shape[0]
    qcount = w_query.shape[1] // width
    group = local_rows * heads
    total = segment_ids.shape[0]
    hidden_units = w_gate.shape[1]
    scale = 1.0 / math.sqrt(width)
    bf16 = jnp.bfloat16
    first_row = (seq_index * heads + head_index) * local_rows
    my_index = first_row + jnp.arange(local_rows, dtype=jnp.int32)
    my_ids = lax.dynamic_slice_in_dim(segment_ids, first_row, local_rows)
    my_starts = jnp.min(
        jnp.where(
            my_ids[:, None] == segment_ids[None, :],
            jnp.arange(total, dtype=jnp.int32)[None, :],
            total,
        ),
        axis=1,
    )
    cosines, sines = rope_tables(my_index - my_starts, width)

    def query_path(linear, gain):
        shaped = linear.reshape(local_rows, qcount, width)
        turned = rotate(norm_rows(shaped, gain), cosines[:, None, :], sines[:, None, :])
        return turned.reshape(local_rows, qcount * width)

    def key_path(linear, gain):
        return rotate(norm_rows(linear, gain), cosines, sines)

    def gated(gate, up):
        return jax.nn.gelu(gate, approximate=True) * up

    def stacked(v):
        return v.reshape(local_rows, qcount, width).transpose(1, 0, 2).reshape(-1, width)

    def unstacked(v):
        return v.reshape(qcount, local_rows, width).transpose(1, 0, 2).reshape(local_rows, -1)

    inputs = tokens.astype(jnp.float32)
    attn_in = norm_rows(inputs, gain_attn_in).astype(bf16)
    k_linear = jnp.dot(attn_in, w_key, preferred_element_type=jnp.float32)
    keys_local = key_path(k_linear, gain_key).astype(bf16)
    values_local = jnp.dot(attn_in, w_value, preferred_element_type=jnp.float32).astype(bf16)
    q_linear = jnp.dot(attn_in, w_query, preferred_element_type=jnp.float32)
    queries_local = query_path(q_linear, gain_query).astype(bf16)
    queries = stacked(queries_local) * jnp.asarray(scale, bf16)
    keys, values = gather_all([keys_local, values_local], nseq, heads, 1)
    keys = keys.reshape(nseq, group, width)
    values = values.reshape(nseq, group, width)
    starts = jnp.tile(my_starts, qcount)[None, :]
    index = jnp.tile(my_index, qcount)[None, :]
    attended_t, log_total = attend(queries, keys, values, starts, index)
    attended = attended_t.T
    mixed_local = unstacked(attended.astype(bf16))
    projected = jnp.dot(mixed_local, w_out, preferred_element_type=jnp.float32)
    if (nseq, heads) == (8, 4) and (model // nseq) % 16 == 0:
        qw = qcount * width
        each, few = model // (nseq * heads), width // (nseq * heads)
        output, d_hidden, d_projected, gains, half_down, half_gate, all_up = feed_forward(
            nseq,
            heads,
            10,
            projected,
            tokens,
            cotangent,
            (gain_attn_out, gain_ffn_in, gain_ffn_out),
            w_gate.T,
            w_up.T,
            w_down,
        )
        w_qkv = jnp.concatenate([w_query, w_key, w_value], axis=1)
        grad_tokens, sum_qkv, sum_out, sum_gate, sum_up, sum_down, sum_gains = tail(
            nseq,
            heads,
            qcount,
            scale,
            9,
            queries,
            starts,
            index,
            log_total,
            attended_t,
            mixed_local.T.reshape(nseq, -1, local_rows),
            d_projected,
            w_out,
            q_linear,
            k_linear,
            cosines,
            sines,
            gain_query[None],
            gain_key[None],
            attn_in.T.reshape(nseq, -1, local_rows),
            tokens,
            gain_attn_in[None],
            d_hidden,
            gains,
            keys,
            values,
            w_qkv,
            half_gate,
            all_up,
            half_down,
        )
        which = seq_index * heads + head_index
        wide = lax.dynamic_slice_in_dim(sum_gains[:4], which * each, each, 1)
        narrow = lax.dynamic_slice_in_dim(sum_gains[4:6], which * few, few, 1)
        return (
            output,
            grad_tokens,
            sum_qkv[:, :qw],
            sum_qkv[:, qw : qw + width],
            sum_qkv[:, qw + width :],
            sum_out,
            sum_gate,
            sum_up,
            sum_down.T,
            wide[0],
            wide[1],
            wide[2],
            wide[3],
            narrow[0],
            narrow[1],
        )
    hidden = inputs + norm_rows(projected, gain_attn_out)
    ffn_in = norm_rows(hidden, gain_ffn_in).astype(bf16)
    ffn_rows = line_gather(ffn_in, heads, 2).reshape(group, model)
    gate = jnp.dot(ffn_rows, w_gate, preferred_element_type=jnp.float32)
    up = jnp.dot(ffn_rows, w_up, preferred_element_type=jnp.float32)
    activated = gated(gate, up).astype(bf16)
    ffn_out = line_scatter(
        jnp.dot(activated, w_down, preferred_element_type=jnp.float32)
        .astype(bf16)
        .reshape(heads, local_rows, model),
        heads,
        3,
    )
    output = hidden + norm_rows(ffn_out, gain_ffn_out)
    upstream = cotangent.astype(jnp.float32)
    unused, back_four = jax.vjp(norm_rows, ffn_out, gain_ffn_out)
    d_ffn_out, d_gain_four = back_four(upstream)
    d_ffn_rows = line_gather(d_ffn_out.astype(bf16), heads, 4).reshape(group, model)
    d_activated = contract_last(d_ffn_rows, w_down)
    d_w_down = contract_first(d_ffn_rows, activated)
    unused, back_gate = jax.vjp(gated, gate, up)
    d_gate, d_up = back_gate(d_activated)
    d_gate = d_gate.astype(bf16)
    d_up = d_up.astype(bf16)
    d_ffn_in = line_scatter(
        (contract_last(d_gate, w_gate) + contract_last(d_up, w_up))
        .astype(bf16)
        .reshape(heads, local_rows, model),
        heads,
        5,
    )
    d_w_gate = contract_first(ffn_rows, d_gate)
    d_w_up = contract_first(ffn_rows, d_up)
    unused, back_three = jax.vjp(norm_rows, hidden, gain_ffn_in)
    d_hidden_part, d_gain_three = back_three(d_ffn_in)
    d_hidden = upstream + d_hidden_part
    unused, back_two = jax.vjp(norm_rows, projected, gain_attn_out)
    d_projected, d_gain_two = back_two(d_hidden)
    d_projected = d_projected.astype(bf16)
    qw = qcount * width
    d_w_out = contract_first(mixed_local, d_projected)
    d_mixed = contract_last(d_projected, w_out).astype(bf16)
    grad_attended = stacked(d_mixed)
    row_dots = jnp.sum(grad_attended.astype(jnp.float32) * attended, axis=1)[None, :]
    d_queries_t, d_keys, d_values = attend_back(
        queries, keys, values, starts, index, log_total, row_dots, grad_attended
    )
    shape = (nseq, heads, local_rows, width)
    ups, downs = seq_orders(bits)
    d_keys, d_values = scatter_all(
        [d_keys.reshape(shape), d_values.reshape(shape)],
        [True, True],
        [[0] + ups, [0] + downs],
        nseq,
        heads,
        6,
        "scatter_keys",
    )
    d_query_rot = unstacked((d_queries_t.T * scale).astype(bf16)).astype(jnp.float32)
    unused, back_query = jax.vjp(query_path, q_linear, gain_query)
    d_q_linear, d_gain_query = back_query(d_query_rot)
    unused, back_key = jax.vjp(key_path, k_linear, gain_key)
    d_k_linear, d_gain_key = back_key(d_keys)
    d_qkv = jnp.concatenate([d_q_linear, d_k_linear, d_values], axis=1).astype(bf16)
    qw = qcount * width
    d_w_qkv = contract_first(attn_in, d_qkv)
    d_attn_in = (
        contract_last(d_qkv[:, :qw], w_query)
        + contract_last(d_qkv[:, qw : qw + width], w_key)
        + contract_last(d_qkv[:, qw + width :], w_value)
    )
    unused, back_one = jax.vjp(norm_rows, inputs, gain_attn_in)
    d_inputs, d_gain_one = back_one(d_attn_in)
    grad_tokens = (d_hidden + d_inputs).astype(bf16)

    def cut(v):
        return v.reshape(nseq, heads, -1)

    wide = jnp.stack([cut(d_gain_one), cut(d_gain_two), cut(d_gain_three), cut(d_gain_four)], 2)
    narrow = jnp.stack([cut(d_gain_query), cut(d_gain_key)], 2)
    each, few = wide.shape[-1], narrow.shape[-1]
    gains = jnp.concatenate(
        [
            jnp.pad(wide, ((0, 0), (0, 0), (0, 0), (0, 128 - each))),
            jnp.pad(narrow, ((0, 0), (0, 0), (0, 2), (0, 128 - few))),
        ],
        axis=2,
    )
    sum_qkv, sum_out, sum_gains = scatter_all(
        [
            d_w_qkv.astype(bf16).reshape(nseq, heads, -1, d_qkv.shape[1]),
            d_w_out.astype(bf16).reshape(nseq, heads, -1, model),
            gains,
        ],
        [True, True, True],
        [[0] + ups, [0] + downs, [0] + downs],
        nseq,
        heads,
        7,
        "scatter_attn",
    )
    sum_gate, sum_up, sum_down = scatter_all(
        [
            d.astype(bf16).reshape(nseq, model // nseq, hidden_units)
            for d in (d_w_gate, d_w_up, d_w_down)
        ],
        [False, False, False],
        [[0] + ups, [0] + downs, [0] + ups],
        nseq,
        heads,
        8,
        "scatter_ffn",
    )
    return (
        output.astype(bf16),
        grad_tokens,
        sum_qkv[:, :qw],
        sum_qkv[:, qw : qw + width],
        sum_qkv[:, qw + width :],
        sum_out,
        sum_gate,
        sum_up,
        sum_down.T,
        sum_gains[0, :each],
        sum_gains[1, :each],
        sum_gains[2, :each],
        sum_gains[3, :each],
        sum_gains[4, :few],
        sum_gains[5, :few],
    )


def solution(mesh):
    rows = P(("seq", "head"), None)
    in_specs = (
        rows,
        P(),
        P(),
        P(),
        P(),
        P(),
        P(None, "head"),
        P(None, "head"),
        P("head", None),
        P(),
        P(),
        P(),
        P(),
        P(),
        P(),
        rows,
    )
    out_specs = (
        rows,
        rows,
        rows,
        rows,
        rows,
        rows,
        P("seq", "head"),
        P("seq", "head"),
        P("head", "seq"),
    ) + (P(("seq", "head")),) * 6
    return jax.shard_map(local, mesh=mesh, in_specs=in_specs, out_specs=out_specs, check_vma=False)
```

```python
import functools
import itertools
import math

import jax
import jax.numpy as jnp
from jax import lax
from jax.experimental import pallas as pl
from jax.experimental.pallas import tpu as pltpu
from jax.sharding import PartitionSpec as P

EPS = 1e-06
MESH = pl.DeviceIdType.MESH
VMEM = pltpu.VMEM
LIMIT = 56 * 2**20


def norm_rows(v, gain):
    return v * lax.rsqrt(jnp.mean(v * v, axis=-1, keepdims=True) + EPS) * gain


def rotate(v, cosines, sines):
    half = v.shape[-1] // 2
    first = v[..., :half]
    second = v[..., half:]
    return jnp.concatenate(
        [first * cosines - second * sines, second * cosines + first * sines], axis=-1
    )


def rope_tables(positions, width):
    half = width // 2
    freq = jnp.exp(jnp.arange(half, dtype=jnp.float32) * (-2.0 * math.log(1000000.0) / width))
    angle = positions.astype(jnp.float32)[:, None] * freq[None, :]
    return (jnp.cos(angle), jnp.sin(angle))


def contract_first(left, right):
    return lax.dot_general(
        left, right, (((0,), (0,)), ((), ())), preferred_element_type=jnp.float32
    )


def contract_last(left, right):
    return lax.dot_general(
        left, right, (((1,), (1,)), ((), ())), preferred_element_type=jnp.float32
    )


def place():
    return lax.axis_index("seq"), lax.axis_index("head")


def related(s, mask):
    out = s
    bit = 0
    while mask >> bit:
        if (mask >> bit) & 1:
            step = 1 << bit
            out = out + (1 - 2 * ((s // step) % 2)) * step
        bit += 1
    return out


def subsets(bits):
    out = [0]
    for bit in bits:
        out = out + [m | (1 << bit) for m in out]
    return out


def greet(targets):
    barrier = pltpu.get_barrier_semaphore()
    for target in targets:
        pl.semaphore_signal(barrier, inc=1, device_id=target, device_id_type=MESH)
    pl.semaphore_wait(barrier, len(targets))


def remote(src, dst, send, recv, target):
    return pltpu.make_async_remote_copy(
        src_ref=src,
        dst_ref=dst,
        send_sem=send,
        recv_sem=recv,
        device_id=target,
        device_id_type=MESH,
    )


def seq_orders(bits):
    upper = list(range(1, bits))
    return upper, upper[::-1]


def gather_kernel(nseq, heads, local_refs, out_refs, send, recv):
    bits = nseq.bit_length() - 1
    s, h = place()
    others = [lax.rem(h + d, heads) for d in range(1, heads)]
    greet([(related(s, 1 << b), h) for b in range(bits)] + [(s, o) for o in others])
    count = [0]
    started = []

    def go(src, dst, target):
        k = count[0]
        count[0] += 1
        copy = remote(src, dst, send.at[k], recv.at[k], target)
        copy.start()
        started.append(copy)
        return copy

    first = []
    for a in range(len(out_refs)):
        out_refs[a][s, h] = local_refs[a][...]
        first.append(
            [go(local_refs[a], out_refs[a].at[s, h], (s, o)) for o in others]
        )
    orders = [o + [0] for o in seq_orders(bits)]
    held = [{0: first[a]} for a in range(len(out_refs))]
    for stage in range(bits):
        for a in range(len(out_refs)):
            bit = orders[a % 2][stage]
            target = (related(s, 1 << bit), h)
            arrived = {}
            for mask in list(held[a]):
                for copy in held[a][mask]:
                    copy.wait_recv()
                held[a][mask] = []
                group = related(s, mask)
                copy = go(out_refs[a].at[group], out_refs[a].at[group], target)
                arrived[mask | (1 << bit)] = [copy]
            held[a].update(arrived)
    for a in range(len(out_refs)):
        for mask in held[a]:
            for copy in held[a][mask]:
                copy.wait_recv()
    for copy in started:
        copy.wait_send()


def gather_all(arrays, nseq, heads, cid):
    n = len(arrays)
    total = n * (heads - 1 + nseq - 1)

    def kernel(*refs):
        gather_kernel(nseq, heads, refs[:n], refs[n : 2 * n], refs[2 * n], refs[2 * n + 1])

    return pl.pallas_call(
        kernel,
        out_shape=[jax.ShapeDtypeStruct((nseq, heads) + a.shape, a.dtype) for a in arrays],
        in_specs=[pl.BlockSpec(memory_space=VMEM)] * n,
        out_specs=[pl.BlockSpec(memory_space=VMEM)] * n,
        scratch_shapes=[pltpu.SemaphoreType.DMA((total,)), pltpu.SemaphoreType.DMA((total,))],
        name="gather_all",
        compiler_params=pltpu.CompilerParams(
            collective_id=cid, has_side_effects=True, vmem_limit_bytes=LIMIT
        ),
    )(*arrays)


def line_gather_kernel(heads, x_ref, out_ref, send, recv):
    s, h = place()
    right = (s, lax.rem(h + 1, heads))
    left = (s, lax.rem(h + heads - 1, heads))
    greet([right, left])
    out_ref[h] = x_ref[...]
    for step in range(heads - 1):
        to_right = remote(
            out_ref.at[jnp.maximum(h - step, 0)],
            out_ref.at[jnp.maximum(h - step, 0)],
            send.at[0, step],
            recv.at[0, step],
            right,
        )
        to_left = remote(
            out_ref.at[jnp.minimum(h + step, heads - 1)],
            out_ref.at[jnp.minimum(h + step, heads - 1)],
            send.at[1, step],
            recv.at[1, step],
            left,
        )
        pl.when((h - step >= 0) & (h < heads - 1))(to_right.start)
        pl.when((h + step <= heads - 1) & (h > 0))(to_left.start)
        pl.when(h - 1 - step >= 0)(
            remote(
                out_ref.at[jnp.maximum(h - 1 - step, 0)],
                out_ref.at[jnp.maximum(h - 1 - step, 0)],
                send.at[0, step],
                recv.at[0, step],
                right,
            ).wait_recv
        )
        pl.when(h + 1 + step <= heads - 1)(
            remote(
                out_ref.at[jnp.minimum(h + 1 + step, heads - 1)],
                out_ref.at[jnp.minimum(h + 1 + step, heads - 1)],
                send.at[1, step],
                recv.at[1, step],
                left,
            ).wait_recv
        )
        pl.when((h - step >= 0) & (h < heads - 1))(to_right.wait_send)
        pl.when((h + step <= heads - 1) & (h > 0))(to_left.wait_send)


def line_gather(x, heads, cid):
    return pl.pallas_call(
        functools.partial(line_gather_kernel, heads),
        out_shape=jax.ShapeDtypeStruct((heads,) + x.shape, x.dtype),
        in_specs=[pl.BlockSpec(memory_space=VMEM)],
        out_specs=pl.BlockSpec(memory_space=VMEM),
        scratch_shapes=[
            pltpu.SemaphoreType.DMA((2, heads - 1)),
            pltpu.SemaphoreType.DMA((2, heads - 1)),
        ],
        name="line_gather",
        compiler_params=pltpu.CompilerParams(
            collective_id=cid, has_side_effects=True, vmem_limit_bytes=LIMIT
        ),
    )(x)


def line_scatter_kernel(heads, parts, out_ref, from_left, from_right, send, recv):
    s, h = place()
    last = heads - 1
    right = (s, lax.rem(h + 1, heads))
    left = (s, lax.rem(h + heads - 1, heads))
    greet([right, left])
    f32 = jnp.float32
    for step in range(heads - 1):
        r_dest = jnp.clip(last - (step - h), 0, last)
        l_dest = jnp.clip(step - (last - h), 0, last)
        r_on = (step >= h) & (h < last)
        l_on = (step >= last - h) & (h > 0)
        for on, dest, box, lane, target, first in (
            (r_on, r_dest, from_left, 0, right, step == h),
            (l_on, l_dest, from_right, 1, left, step == last - h),
        ):
            at_end = (h == 0) if lane == 0 else (h == last)
            if step > 0:

                def add(box=box, dest=dest):
                    box[step - 1] = (
                        box[step - 1].astype(f32) + parts[dest].astype(f32)
                    ).astype(box.dtype)

                pl.when(on & jnp.logical_not(at_end))(add)
                pl.when(on & jnp.logical_not(at_end))(
                    remote(
                        box.at[step - 1], box.at[step], send.at[lane, step], recv.at[lane, step], target
                    ).start
                )
            pl.when(on & at_end)(
                remote(
                    parts.at[dest], box.at[step], send.at[lane, step], recv.at[lane, step], target
                ).start
            )
        r_in = (step >= h - 1) & (h > 0)
        l_in = (step >= last - h - 1) & (h < last)
        pl.when(r_in)(
            remote(
                from_left.at[step], from_left.at[step], send.at[0, step], recv.at[0, step], right
            ).wait_recv
        )
        pl.when(l_in)(
            remote(
                from_right.at[step], from_right.at[step], send.at[1, step], recv.at[1, step], left
            ).wait_recv
        )
    for step in range(heads - 1):
        for on, box, lane, target in (
            ((step >= h) & (h < last), from_left, 0, right),
            ((step >= last - h) & (h > 0), from_right, 1, left),
        ):
            pl.when(on)(
                remote(
                    box.at[step], box.at[step], send.at[lane, step], recv.at[lane, step], target
                ).wait_send
            )
    out_ref[...] = parts[h].astype(f32)

    def add_left():
        out_ref[...] += from_left[heads - 2].astype(f32)

    def add_right():
        out_ref[...] += from_right[heads - 2].astype(f32)

    pl.when(h > 0)(add_left)
    pl.when(h < last)(add_right)


def line_scatter(parts, heads, cid):
    block = parts.shape[1:]
    return pl.pallas_call(
        functools.partial(line_scatter_kernel, heads),
        out_shape=jax.ShapeDtypeStruct(block, jnp.float32),
        in_specs=[pl.BlockSpec(memory_space=VMEM)],
        out_specs=pl.BlockSpec(memory_space=VMEM),
        scratch_shapes=[
            VMEM((heads - 1,) + block, parts.dtype),
            VMEM((heads - 1,) + block, parts.dtype),
            pltpu.SemaphoreType.DMA((2, heads - 1)),
            pltpu.SemaphoreType.DMA((2, heads - 1)),
        ],
        name="line_scatter",
        compiler_params=pltpu.CompilerParams(
            collective_id=cid, has_side_effects=True, vmem_limit_bytes=LIMIT
        ),
    )(parts)


def scatter_kernel(nseq, heads, zs, orders, parts, outs, boxes, zboxes, send, recv):
    bits = nseq.bit_length() - 1
    s, h = place()
    f32 = jnp.float32
    others = [lax.rem(h + d, heads) for d in range(1, heads)]
    greet(
        [(related(s, 1 << b), h) for b in range(bits)]
        + ([(s, o) for o in others] if any(zs) else [])
    )
    count = [0]
    started = []

    def go(src, dst, target):
        k = count[0]
        count[0] += 1
        copy = remote(src, dst, send.at[k], recv.at[k], target)
        copy.start()
        started.append(copy)
        return copy

    n = len(parts)
    offsets = [0] * n
    slot = [{} for _ in range(n)]
    waiting = [{} for _ in range(n)]

    def current(a, mask):
        if mask in slot[a]:
            return boxes[a].at[slot[a][mask]]
        return parts[a].at[related(s, mask)]

    def launch(a, stage):
        bit = orders[a][stage]
        rest = orders[a][stage + 1 :]
        target = (related(s, 1 << bit), h)
        after = 1 << rest[0] if rest else 0
        masks = sorted(subsets(rest), key=lambda m: 0 if m & after else 1)
        for mask in masks:
            where = offsets[a]
            offsets[a] += 1
            waiting[a][mask] = (
                go(current(a, mask | (1 << bit)), boxes[a].at[where], target),
                where,
            )

    def settle(a, mask):
        copy, where = waiting[a].pop(mask)
        mine = current(a, mask)
        copy.wait_recv()
        boxes[a][where] = (boxes[a][where].astype(f32) + mine[...].astype(f32)).astype(
            boxes[a].dtype
        )
        slot[a][mask] = where

    for a in range(n):
        launch(a, 0)
    for stage in range(bits):
        for a in range(n):
            for mask in list(waiting[a]):
                settle(a, mask)
            if stage + 1 < bits:
                launch(a, stage + 1)
    arriving = []
    for a in range(n):
        if not zs[a]:
            continue
        mine = current(a, 0)
        arriving.append(
            [
                go(mine.at[o], zboxes[a].at[d], (s, o))
                for d, o in enumerate(others)
            ]
        )
    z = 0
    for a in range(n):
        if zs[a]:
            total = current(a, 0)[h].astype(f32)
            for d, copy in enumerate(arriving[z]):
                copy.wait_recv()
                total = total + zboxes[a][d].astype(f32)
            outs[a][...] = total
            z += 1
        else:
            outs[a][...] = current(a, 0)[...].astype(f32)
    for copy in started:
        copy.wait_send()


def scatter_all(arrays, zs, orders, nseq, heads, cid, name):
    n = len(arrays)
    total = sum((nseq - 1) + (heads - 1 if z else 0) for z in zs)
    blocks = [a.shape[2:] if z else a.shape[1:] for a, z in zip(arrays, zs)]

    def kernel(*refs):
        scatter_kernel(
            nseq,
            heads,
            zs,
            orders,
            refs[:n],
            refs[n : 2 * n],
            refs[2 * n : 3 * n],
            refs[3 * n : 4 * n],
            refs[4 * n],
            refs[4 * n + 1],
        )

    return pl.pallas_call(
        kernel,
        out_shape=[jax.ShapeDtypeStruct(b, jnp.float32) for b in blocks],
        in_specs=[pl.BlockSpec(memory_space=VMEM)] * n,
        out_specs=[pl.BlockSpec(memory_space=VMEM)] * n,
        scratch_shapes=[VMEM((nseq - 1,) + a.shape[1:], a.dtype) for a in arrays]
        + [
            VMEM((heads - 1,) + b, a.dtype) if z else VMEM((8, 128), jnp.float32)
            for a, b, z in zip(arrays, blocks, zs)
        ]
        + [pltpu.SemaphoreType.DMA((total,)), pltpu.SemaphoreType.DMA((total,))],
        name=name,
        compiler_params=pltpu.CompilerParams(
            collective_id=cid, has_side_effects=True, vmem_limit_bytes=LIMIT
        ),
    )(*arrays)


def attend_kernel(q_ref, k_ref, v_ref, start_ref, index_ref, out_ref, log_ref):
    s = lax.axis_index("seq")
    span = k_ref.shape[1]
    start = start_ref[...]
    index = index_ref[...]
    queries = q_ref[...]
    rows = queries.shape[0]
    out_ref[...] = jnp.zeros_like(out_ref)

    def step(g, mass):
        scores = contract_last(k_ref[g], queries)
        key = g * span + lax.broadcasted_iota(jnp.int32, (span, rows), 0)
        terms = jnp.where((key >= start) & (key <= index), jnp.exp(scores), 0.0)
        out_ref[...] += contract_first(v_ref[g], terms.astype(jnp.bfloat16))
        return mass + jnp.sum(terms, axis=0, keepdims=True)

    mass = lax.fori_loop(0, s + 1, step, jnp.zeros((1, rows), jnp.float32))
    out_ref[...] = out_ref[...] / mass
    log_ref[...] = jnp.log(mass)


def attend(q, k, v, start, index):
    rows, width = q.shape
    return pl.pallas_call(
        attend_kernel,
        out_shape=[
            jax.ShapeDtypeStruct((width, rows), jnp.float32),
            jax.ShapeDtypeStruct((1, rows), jnp.float32),
        ],
        in_specs=[pl.BlockSpec(memory_space=VMEM)] * 5,
        out_specs=[pl.BlockSpec(memory_space=VMEM)] * 2,
        name="attend",
        compiler_params=pltpu.CompilerParams(vmem_limit_bytes=LIMIT),
    )(q, k, v, start, index)


def attend_back_kernel(
    q_ref, k_ref, v_ref, start_ref, index_ref, log_ref, dots_ref, d_ref, dq_ref, dk_ref, dv_ref
):
    s = lax.axis_index("seq")
    groups, span = k_ref.shape[:2]
    start = start_ref[...]
    index = index_ref[...]
    log_total = log_ref[...]
    dots = dots_ref[...]
    queries = q_ref[...]
    grads = d_ref[...]
    rows = queries.shape[0]
    dq_ref[...] = jnp.zeros_like(dq_ref)

    def step(g, carry):
        keys = k_ref[g]
        scores = contract_last(keys, queries)
        key = g * span + lax.broadcasted_iota(jnp.int32, (span, rows), 0)
        probs = jnp.where((key >= start) & (key <= index), jnp.exp(scores - log_total), 0.0)
        d_probs = contract_last(v_ref[g], grads)
        d_scores = (probs * (d_probs - dots)).astype(jnp.bfloat16)
        dv_ref[g] = jnp.dot(
            probs.astype(jnp.bfloat16), grads, preferred_element_type=jnp.float32
        ).astype(dv_ref.dtype)
        dk_ref[g] = jnp.dot(d_scores, queries, preferred_element_type=jnp.float32).astype(
            dk_ref.dtype
        )
        dq_ref[...] += contract_first(keys, d_scores)
        return carry

    lax.fori_loop(0, s + 1, step, 0)

    def blank(g, carry):
        dk_ref[g] = jnp.zeros(dk_ref.shape[1:], dk_ref.dtype)
        dv_ref[g] = jnp.zeros(dv_ref.shape[1:], dv_ref.dtype)
        return carry

    lax.fori_loop(s + 1, groups, blank, 0)


def attend_back(q, k, v, start, index, log_total, dots, grads):
    rows, width = q.shape
    return pl.pallas_call(
        attend_back_kernel,
        out_shape=[
            jax.ShapeDtypeStruct((width, rows), jnp.float32),
            jax.ShapeDtypeStruct(k.shape, jnp.bfloat16),
            jax.ShapeDtypeStruct(v.shape, jnp.bfloat16),
        ],
        in_specs=[pl.BlockSpec(memory_space=VMEM)] * 8,
        out_specs=[pl.BlockSpec(memory_space=VMEM)] * 3,
        name="attend_back",
        compiler_params=pltpu.CompilerParams(vmem_limit_bytes=LIMIT),
    )(q, k, v, start, index, log_total, dots, grads)


def flat(ref):
    return ref[...].reshape(1, ref.shape[0])


def front_kernel(
    nseq,
    heads,
    qcount,
    scale,
    x_ref,
    ids_ref,
    w_key_ref,
    w_value_ref,
    gain_in_ref,
    gain_q_ref,
    gain_k_ref,
    w_query_far,
    w_out_far,
    o_proj,
    o_q,
    o_k,
    o_v,
    o_start,
    o_index,
    o_log,
    o_att,
    o_q_lin,
    o_k_lin,
    o_cos,
    o_sin,
    o_attn_t,
    w_query,
    w_out,
    k_all,
    v_all,
    send,
    recv,
    local_sem,
):
    f32, bf16 = jnp.float32, jnp.bfloat16
    bits = nseq.bit_length() - 1
    ups, downs = seq_orders(bits)
    links = Links(nseq, heads, send, recv)
    s, h = links.s, links.h
    rows, model = x_ref.shape
    width = w_key_ref.shape[1]
    gain_q, gain_k = flat(gain_q_ref), flat(gain_k_ref)
    half = width // 2
    total = ids_ref.shape[0] * ids_ref.shape[1]
    load_q = pltpu.make_async_copy(w_query_far, w_query, local_sem.at[0])
    load_q.start()
    load_o = pltpu.make_async_copy(w_out_far, w_out, local_sem.at[1])
    load_o.start()
    partners = [related(h, j) for j in range(1, heads)]
    greet([links.across(b) for b in range(bits)] + [(s, o) for o in partners])

    which = s * heads + h
    mine = ids_ref[pl.ds(which, 1), :].astype(f32)
    column = jnp.broadcast_to(mine, (rows, rows)).T[:, 0:1]
    first = jnp.full((rows, rows), float(total), f32)
    for r in range(ids_ref.shape[0]):
        here = ids_ref[r : r + 1, :].astype(f32)
        at = (r * rows + lax.broadcasted_iota(jnp.int32, (1, rows), 1)).astype(f32)
        first = jnp.minimum(first, jnp.where(column == here, at, float(total)))
    start = jnp.min(first, axis=1, keepdims=True)
    index = (which * rows + lax.broadcasted_iota(jnp.int32, (rows, 1), 0)).astype(f32)
    freq = jnp.exp(
        lax.broadcasted_iota(jnp.int32, (1, half), 1).astype(f32)
        * (-2.0 * math.log(1000000.0) / width)
    )
    angle = (index - start) * freq
    turns = jnp.round(angle * (1.0 / (2.0 * math.pi)))
    angle = (angle - turns * 6.28125) - turns * (2.0 * math.pi - 6.28125)
    cosines, sines = jnp.cos(angle), jnp.sin(angle)
    o_cos[...] = cosines
    o_sin[...] = sines
    start_row = jnp.broadcast_to(start, (rows, rows)).T[0:1, :].astype(jnp.int32)
    index_row = which * rows + lax.broadcasted_iota(jnp.int32, (1, rows), 1)
    for j in range(qcount):
        o_start[:, pl.ds(j * rows, rows)] = start_row
        o_index[:, pl.ds(j * rows, rows)] = index_row

    attn_in = norm_rows(x_ref[...].astype(f32), flat(gain_in_ref)).astype(bf16)
    k_lin = jnp.dot(attn_in, w_key_ref[...], preferred_element_type=f32)
    k_all[s, h] = rotate(norm_rows(k_lin, gain_k), cosines, sines).astype(bf16)
    o_k_lin[...] = k_lin
    v_all[s, h] = jnp.dot(attn_in, w_value_ref[...], preferred_element_type=f32).astype(bf16)

    both = ((k_all, ups), (v_all, downs))

    def pass_on(a, mask, j, bit):
        buf = both[a][0]
        block = buf.at[related(s, mask), related(h, j)]
        return links.go(block, block, links.across(bit))

    over_head = {}
    for j in range(1, heads):
        for a in range(2):
            block = both[a][0].at[s, h]
            over_head[a, j] = links.go(block, block, (s, partners[j - 1]))
    arriving = {}

    def spread(a, mask, j, stage):
        order = both[a][1]
        for later in range(stage, len(order)):
            bit = order[later]
            arriving[a, mask | (1 << bit), j] = pass_on(a, mask, j, bit)

    for a in range(2):
        spread(a, 0, 0, 0)

    load_q.wait()
    q_lin = jnp.dot(attn_in, w_query[...], preferred_element_type=f32)
    o_q_lin[...] = q_lin
    for j in range(1, heads):
        for a in range(2):
            over_head[a, j].wait_recv()
            spread(a, 0, j, 0)
    for j in range(qcount):
        part = norm_rows(q_lin[:, j * width : (j + 1) * width], gain_q)
        o_q[pl.ds(j * rows, rows), :] = (rotate(part, cosines, sines) * scale).astype(bf16)

    pairs = []

    def to_pair(a, mask):
        block = both[a][0].at[related(s, mask)]
        pairs.append(links.go(block, block, links.across(0)))

    for a in range(2):
        to_pair(a, 0)
    for stage in range(len(ups)):
        for lower in subsets(range(stage)):
            masks = []
            for a in range(2):
                order = both[a][1]
                mask = sum(1 << order[i] for i in range(stage) if lower >> i & 1)
                masks.append(mask | (1 << order[stage]))
            for j in range(heads):
                for a in range(2):
                    arriving[a, masks[a], j].wait_recv()
                    spread(a, masks[a], j, stage + 1)
            for a in range(2):
                to_pair(a, masks[a])
    for j in range(1):
        o_attn_t[...] = attn_in.T.reshape(o_attn_t.shape)

    queries = o_q[...]
    starts = o_start[...]
    indices = o_index[...]
    o_att[...] = jnp.zeros_like(o_att)
    span = heads * rows
    low = lax.rem(s, 2)

    def attend_group(g, mass):
        scores = contract_last(k_all[g].reshape(span, width), queries)
        key = g * span + lax.broadcasted_iota(jnp.int32, scores.shape, 0)
        terms = jnp.where((key >= starts) & (key <= indices), jnp.exp(scores), 0.0)
        o_att[...] += contract_first(v_all[g].reshape(span, width), terms.astype(bf16))
        return mass + jnp.sum(terms, axis=0, keepdims=True)

    mass = lax.fori_loop(
        0,
        s // 2 + 1,
        lambda i, m: attend_group(2 * i + low, m),
        jnp.zeros((1, qcount * rows), f32),
    )
    for copy in pairs:
        copy.wait_recv()
    mass = lax.fori_loop(
        0, s // 2 + low, lambda i, m: attend_group(2 * i + 1 - low, m), mass
    )
    keep_k = pltpu.make_async_copy(k_all, o_k, local_sem.at[2])
    keep_v = pltpu.make_async_copy(v_all, o_v, local_sem.at[3])
    keep_k.start()
    keep_v.start()
    o_log[...] = jnp.log(mass)
    attended = o_att[...] / mass
    o_att[...] = attended
    load_o.wait()
    proj = jnp.zeros((rows, model), f32)
    for j in range(qcount):
        part = attended[:, j * rows : (j + 1) * rows].T.astype(bf16)
        proj = proj + jnp.dot(
            part, w_out[pl.ds(j * width, width), :], preferred_element_type=f32
        )
    o_proj[...] = proj
    keep_k.wait()
    keep_v.wait()
    links.finish()


def front(nseq, heads, qcount, scale, cid, x, ids, w_key, w_value, gain_in, gain_q, gain_k, w_query, w_out):
    f32, bf16, i32 = jnp.float32, jnp.bfloat16, jnp.int32
    rows, model = x.shape
    width = w_key.shape[1]
    stacked = qcount * rows
    some = nseq // 2
    messages = 2 * (heads - 1) + 2 * heads * (some - 1) + 2 * some
    vm = pl.BlockSpec(memory_space=VMEM)
    anywhere = pl.BlockSpec(memory_space=pl.ANY)
    everyone = (nseq, heads, rows, width)

    def kernel(*refs):
        front_kernel(nseq, heads, qcount, scale, *refs)

    shape = jax.ShapeDtypeStruct
    return pl.pallas_call(
        kernel,
        out_shape=[
            shape((rows, model), f32),
            shape((stacked, width), bf16),
            shape(everyone, bf16),
            shape(everyone, bf16),
            shape((1, stacked), i32),
            shape((1, stacked), i32),
            shape((1, stacked), f32),
            shape((width, stacked), f32),
            shape((rows, qcount * width), f32),
            shape((rows, width), f32),
            shape((rows, width // 2), f32),
            shape((rows, width // 2), f32),
            shape((nseq, model // nseq, rows), bf16),
        ],
        in_specs=[vm] * 7 + [anywhere] * 2,
        out_specs=[vm] * 2 + [anywhere] * 2 + [vm] * 9,
        scratch_shapes=[
            VMEM(w_query.shape, bf16),
            VMEM(w_out.shape, bf16),
            VMEM(everyone, bf16),
            VMEM(everyone, bf16),
            pltpu.SemaphoreType.DMA((messages,)),
            pltpu.SemaphoreType.DMA((messages,)),
            pltpu.SemaphoreType.DMA((4,)),
        ],
        name="front",
        compiler_params=pltpu.CompilerParams(
            collective_id=cid, has_side_effects=True, vmem_limit_bytes=LIMIT
        ),
    )(
        x,
        ids.reshape(nseq * heads, rows),
        w_key,
        w_value,
        gain_in,
        gain_q,
        gain_k,
        w_query,
        w_out,
    )


class Sum:
    def __init__(self, links, part, boxes, order):
        self.links, self.part, self.boxes, self.order = links, part, boxes, order
        self.used = 0
        self.slot = {}
        self.waiting = {}

    def current(self, mask):
        if mask in self.slot:
            return self.boxes.at[self.slot[mask]]
        return self.part(mask)

    def masks(self, stage):
        rest = self.order[stage + 1 :]
        weight = lambda m: sum(1 << (len(rest) - i) for i, b in enumerate(rest) if m >> b & 1)
        return sorted(subsets(rest), key=weight, reverse=True)

    def send(self, stage, mask):
        bit = self.order[stage]
        where = self.used
        self.used += 1
        copy = self.links.go(
            self.current(mask | (1 << bit)), self.boxes.at[where], self.links.across(bit)
        )
        self.waiting[stage, mask] = (copy, where)

    def start(self):
        for mask in self.masks(0):
            self.send(0, mask)

    def steps(self, stage, kept=None):
        def step(mask):
            copy, where = self.waiting.pop((stage, mask))
            mine = kept(mask) if kept is not None else self.current(mask)
            copy.wait_recv()
            self.boxes[where] = self.boxes[where] + mine[...]
            self.slot[mask] = where
            if stage + 1 < len(self.order):
                bit = 1 << self.order[stage + 1]
                if mask & bit:
                    self.send(stage + 1, mask & ~bit)

        return [functools.partial(step, mask) for mask in self.masks(stage)]

    def last(self, kept=None):
        copy, where = self.waiting.pop((len(self.order) - 1, 0))
        mine = kept(0) if kept is not None else self.current(0)
        copy.wait_recv()
        return self.boxes[where].astype(jnp.float32) + mine[...].astype(jnp.float32)


def in_turn(*lists):
    for group in itertools.zip_longest(*lists):
        for step in group:
            if step is not None:
                step()


class Links:
    def __init__(self, nseq, heads, send, recv):
        self.s, self.h = place()
        self.nseq, self.heads = nseq, heads
        self.send, self.recv = send, recv
        self.count = 0
        self.started = []
        self.others = [lax.rem(self.h + d, heads) for d in range(1, heads)]

    def greet(self):
        bits = self.nseq.bit_length() - 1
        greet([self.across(b) for b in range(bits)] + [(self.s, o) for o in self.others])

    def across(self, bit):
        return (related(self.s, 1 << bit), self.h)

    def go(self, src, dst, target):
        k = self.count
        self.count += 1
        copy = remote(src, dst, self.send.at[k], self.recv.at[k], target)
        copy.start()
        self.started.append(copy)
        return copy

    def over_heads(self, src, boxes):
        return [self.go(src.at[o], boxes.at[d], (self.s, o)) for d, o in enumerate(self.others)]

    def finish(self):
        for copy in self.started:
            copy.wait_send()


def back_norm(v, gain, d_out):
    scale = lax.rsqrt(jnp.mean(v * v, axis=-1, keepdims=True) + EPS)
    unit = v * scale
    inner = d_out * gain
    d_v = scale * (inner - unit * jnp.mean(inner * unit, axis=-1, keepdims=True))
    return d_v, jnp.sum(d_out * unit, axis=0, keepdims=True)


def back_rotate(d, cosines, sines):
    half = d.shape[-1] // 2
    first, second = d[:, :half], d[:, half:]
    return jnp.concatenate(
        [first * cosines + second * sines, second * cosines - first * sines], axis=-1
    )


def tail_kernel(
    nseq,
    heads,
    qcount,
    scale,
    q_ref,
    start_ref,
    index_ref,
    log_ref,
    att_ref,
    d_proj_ref,
    w_out_ref,
    q_lin_ref,
    k_lin_ref,
    cos_ref,
    sin_ref,
    gain_q_ref,
    gain_k_ref,
    gain_in_ref,
    attn_t_ref,
    x_ref,
    d_hid_ref,
    gains_ref,
    k_far,
    v_far,
    w_query_far,
    w_key_far,
    w_value_far,
    d_gate_ref,
    d_up_ref,
    d_down_ref,
    o_tokens,
    o_qkv,
    o_out,
    o_gate,
    o_up,
    o_down,
    o_gains,
    k_ref,
    v_ref,
    w_qkv_ref,
    dk,
    dv,
    dq_t,
    grads,
    grads_t,
    box_k,
    box_v,
    zbox_k,
    zbox_v,
    dw_out,
    box_out,
    zbox_out,
    mid_out,
    end_out,
    dw_qkv,
    box_qkv,
    zsrc_qkv,
    zbox_qkv,
    d_qkv,
    keep_gate,
    keep_up,
    keep_first,
    keep_second,
    box_gate,
    box_up,
    box_first,
    box_second,
    gsum,
    gbox,
    gzbox,
    send,
    recv,
    local_sem,
):
    f32, bf16 = jnp.float32, jnp.bfloat16
    bits = nseq.bit_length() - 1
    ups, downs = seq_orders(bits)
    links = Links(nseq, heads, send, recv)
    s, h = links.s, links.h
    rows, model = d_proj_ref.shape
    width = k_lin_ref.shape[1]
    gain_q, gain_k = flat(gain_q_ref), flat(gain_k_ref)
    groups, span = k_ref.shape[:2]
    loads = []

    def load(src, dst):
        copy = pltpu.make_async_copy(src, dst, local_sem.at[len(loads)])
        copy.start()
        loads.append(copy)
        return copy

    load_k = load(k_far, k_ref)
    load_v = load(v_far, v_ref)
    links.greet()

    held = subsets(ups)
    ffn = []
    split = keep_first.shape[1]
    for src, keep, box, order, low in (
        (d_gate_ref, keep_gate, box_gate, ups, 0),
        (d_up_ref, keep_up, box_up, [0] + downs, 0),
        (d_down_ref, keep_first, box_first, ups, 0),
        (d_down_ref, keep_second, box_second, downs, split),
    ):
        here = pl.ds(low, keep.shape[1])

        def part(m, src=src, here=here):
            if src is d_up_ref:
                return src.at[related(s, m)]
            return src.at[held.index(m), here]

        total = Sum(links, part, box, order)
        kept = subsets(order[1:])
        total.loads = [load(part(m), keep.at[i]) for i, m in enumerate(kept)]
        total.kept = lambda m, keep=keep, kept=kept: keep.at[kept.index(m)]
        ffn.append(total)
    gate, up, first, second = ffn
    up.start()
    gate.start()
    load_w = []
    at = 0
    for far in (w_query_far, w_key_far, w_value_far):
        load_w.append(load(far, w_qkv_ref.at[:, pl.ds(at, far.shape[1])]))
        at += far.shape[1]

    d_proj = d_proj_ref[...]

    out_rows = dw_out.shape[1] * dw_out.shape[2]
    for j in range(nseq):
        head, low = divmod(j * out_rows, width)
        mixed_t = att_ref[low : low + out_rows, pl.ds(head * rows, rows)].astype(bf16)
        dw_out[j] = (
            jnp.dot(mixed_t, d_proj, preferred_element_type=f32)
            .astype(bf16)
            .reshape(dw_out.shape[1:])
        )

    sum_out = Sum(links, lambda m: dw_out.at[related(s, m)], box_out, [0])
    sum_out.masks = lambda stage: held
    sum_out.start()

    for j in range(qcount):
        part = w_out_ref[pl.ds(j * width, width), :]
        grads[pl.ds(j * rows, rows), :] = contract_last(d_proj, part).astype(bf16)
        grads_t[:, pl.ds(j * rows, rows)] = contract_last(part, d_proj).astype(bf16)
    for copy in up.loads:
        copy.wait()
    in_turn(up.steps(0, up.kept))
    dots = jnp.sum(grads_t[...].astype(f32) * att_ref[...], axis=0, keepdims=True)
    start = start_ref[...]
    index = index_ref[...]
    log_total = log_ref[...]
    dq_t[...] = jnp.zeros_like(dq_t)
    load_k.wait()
    load_v.wait()

    def step(g, carry):
        keys = k_ref[g]
        queries = q_ref[...]
        scores = contract_last(keys, queries)
        key = g * span + lax.broadcasted_iota(jnp.int32, scores.shape, 0)
        probs = jnp.where((key >= start) & (key <= index), jnp.exp(scores - log_total), 0.0)
        d_probs = jnp.dot(v_ref[g], grads_t[...], preferred_element_type=f32)
        d_scores = (probs * (d_probs - dots)).astype(bf16)
        dv[g] = (
            jnp.dot(probs.astype(bf16), grads[...], preferred_element_type=f32)
            .astype(bf16)
            .reshape(dv.shape[1:])
        )
        dk[g] = (
            jnp.dot(d_scores, queries, preferred_element_type=f32)
            .astype(bf16)
            .reshape(dk.shape[1:])
        )
        dq_t[...] += contract_first(keys, d_scores)
        return carry

    lax.fori_loop(0, s + 1, step, 0)

    def blank(g, carry):
        dk[g] = jnp.zeros(dk.shape[1:], bf16)
        dv[g] = jnp.zeros(dv.shape[1:], bf16)
        return carry

    lax.fori_loop(s + 1, groups, blank, 0)

    kv = []
    for j in list(range(1, heads)) + [0]:
        owner = lax.rem(h + j, heads)
        for far, box, order in ((dk, box_k, ups), (dv, box_v, downs)):
            kv.append(
                Sum(
                    links,
                    lambda m, far=far, owner=owner: far.at[related(s, m), owner],
                    box.at[j],
                    [0] + order,
                )
            )
    for mask_index in range(len(held)):
        for total in kv:
            total.send(0, total.masks(0)[mask_index])

    for m in sum_out.steps(0):
        m()
    z_out = [
        links.go(box_out.at[:, o], zbox_out.at[d], (s, o)) for d, o in enumerate(links.others)
    ]
    in_turn(*[total.steps(0) for total in kv])

    cosines, sines = cos_ref[...], sin_ref[...]
    d_gain_q = jnp.zeros((1, width), f32)
    for j in range(qcount):
        d_rot = dq_t[:, pl.ds(j * rows, rows)].T * scale
        d_lin, terms = back_norm(
            q_lin_ref[:, pl.ds(j * width, width)],
            gain_q,
            back_rotate(d_rot, cosines, sines),
        )
        d_qkv[:, pl.ds(j * width, width)] = d_lin.astype(bf16)
        d_gain_q = d_gain_q + terms

    for stage in range(1, bits - 1):
        in_turn(*[total.steps(stage) for total in kv])
    for total in (gate, first, second):
        for copy in total.loads:
            copy.wait()
    in_turn(gate.steps(0, gate.kept), up.steps(1))
    first.start()
    second.start()

    arriving = {}
    for i, total in enumerate(kv):
        for m in total.steps(bits - 1):
            m()
        j = (i // 2 + 1) % heads
        if j:
            zbox = (zbox_k, zbox_v)[i % 2]
            arriving[i % 2, j] = links.go(
                total.current(0), zbox.at[j - 1], (s, links.others[j - 1])
            )
    for d, copy in enumerate(z_out):
        copy.wait_recv()
    own = box_out[:, h].astype(f32)
    for d in range(heads - 1):
        own = own + zbox_out[d].astype(f32)
    mid_out[...] = own.astype(bf16)
    sum_end = Sum(links, lambda m: mid_out.at[held.index(m)], end_out, downs)
    sum_end.start()

    def whole(i, zbox):
        total = kv[len(kv) - 2 + i].current(0)[...].astype(f32)
        for j in range(1, heads):
            arriving[i, j].wait_recv()
            total = total + zbox[j - 1].astype(f32)
        return total

    d_keys = whole(0, zbox_k)
    d_lin, d_gain_k = back_norm(
        k_lin_ref[...], gain_k, back_rotate(d_keys, cosines, sines)
    )
    qw = qcount * width
    d_qkv[:, pl.ds(qw, width)] = d_lin.astype(bf16)
    d_values = whole(1, zbox_v)
    d_qkv[:, pl.ds(qw + width, width)] = d_values.astype(bf16)

    pieces, _, block_rows, cut = dw_qkv.shape
    qkv = []
    for j in range(pieces):
        cols = pl.ds(j * cut, cut)

        def qkv_block(g, carry, j=j, cols=cols):
            dw_qkv[j, g] = jnp.dot(
                attn_t_ref[g], d_qkv[:, cols], preferred_element_type=f32
            ).astype(bf16)
            return carry

        lax.fori_loop(0, nseq, qkv_block, 0)
        total = Sum(
            links,
            lambda m, j=j: dw_qkv.at[j, related(s, m)],
            box_qkv.at[j],
            [0] + (downs if j % 2 else ups),
        )
        total.start()
        qkv.append(total)

    for copy in load_w:
        copy.wait()
    d_attn_in = contract_last(d_qkv[...], w_qkv_ref[...])
    in_turn(*[total.steps(0) for total in qkv])
    d_x, d_gain_in = back_norm(x_ref[...].astype(f32), flat(gain_in_ref), d_attn_in)
    o_tokens[...] = (d_hid_ref[...] + d_x).astype(o_tokens.dtype)

    gsum[0] = gains_ref[...]
    gsum[0, 0:1, :] = d_gain_in
    gsum[0, 4:5, :width] = d_gain_q
    gsum[0, 5:6, :width] = d_gain_k
    gain_copy = links.go(gsum.at[0], gbox.at[0], links.across(0))
    for stage in range(1, bits - 1):
        in_turn(*[total.steps(stage) for total in qkv])
    for bit in range(bits):
        gain_copy.wait_recv()
        gsum[bit + 1] = gsum[bit] + gbox[bit]
        if bit + 1 < bits:
            gain_copy = links.go(gsum.at[bit + 1], gbox.at[bit + 1], links.across(bit + 1))
    gain_z = [
        links.go(gsum.at[bits], gzbox.at[d], (s, o)) for d, o in enumerate(links.others)
    ]
    in_turn(sum_end.steps(0))
    in_turn(first.steps(0, first.kept), second.steps(0, second.kept))

    each = block_rows // heads
    z_qkv = []
    for j, total in enumerate(qkv):
        value = total.last()
        for p in range(heads):
            zsrc_qkv[j, p] = value[p * each : (p + 1) * each].astype(bf16)
        z_qkv.append(links.over_heads(zsrc_qkv.at[j], zbox_qkv.at[j]))
    o_gate[...] = gate.last()
    o_up[...] = up.last()
    o_down[pl.ds(0, split), :] = first.last()
    o_down[pl.ds(split, o_down.shape[0] - split), :] = second.last()
    o_out[...] = sum_end.last()
    total = gsum[bits]
    for d, copy in enumerate(gain_z):
        copy.wait_recv()
        total = total + gzbox[d]
    o_gains[...] = total
    for j, copies in enumerate(z_qkv):
        total = zsrc_qkv[j, h].astype(f32)
        for d, copy in enumerate(copies):
            copy.wait_recv()
            total = total + zbox_qkv[j, d].astype(f32)
        o_qkv[:, pl.ds(j * cut, cut)] = total
    links.finish()


def tail(nseq, heads, qcount, scale, cid, *arrays):
    (q, _, _, _, att, d_proj, w_out, q_lin, k_lin, _, _, _, _, _) = arrays[:14]
    (attn_t, x, d_hid, gains, k, v, w_query, w_key, w_value, d_gate, _, _) = arrays[14:]
    f32, bf16 = jnp.float32, jnp.bfloat16
    rows, model = d_proj.shape
    width = k_lin.shape[1]
    cols = w_query.shape[1] + w_key.shape[1] + w_value.shape[1]
    pieces = 4
    cut = cols // pieces
    out_rows, qkv_rows = w_out.shape[0] // nseq, attn_t.shape[1]
    ffn_block = d_gate.shape[1:]
    some, all_but = nseq // 2, nseq - 1
    bits = nseq.bit_length() - 1
    out_block = (heads, out_rows // heads, model)
    split = (ffn_block[0] // 2 + 15) // 16 * 16
    parts = [ffn_block, ffn_block, (split, ffn_block[1]), (ffn_block[0] - split, ffn_block[1])]
    copies = (
        3 * (some - 1)
        + all_but
        + some
        + (heads - 1)
        + (some - 1)
        + 2 * heads * all_but
        + 2 * (heads - 1)
        + pieces * (all_but + heads - 1)
        + bits
        + (heads - 1)
    )
    vm = pl.BlockSpec(memory_space=VMEM)
    anywhere = pl.BlockSpec(memory_space=pl.ANY)

    def kernel(*refs):
        tail_kernel(nseq, heads, qcount, scale, *refs)

    return pl.pallas_call(
        kernel,
        out_shape=[
            jax.ShapeDtypeStruct((rows, model), bf16),
            jax.ShapeDtypeStruct((qkv_rows // heads, cols), f32),
            jax.ShapeDtypeStruct(out_block[1:], f32),
            jax.ShapeDtypeStruct(ffn_block, f32),
            jax.ShapeDtypeStruct(ffn_block, f32),
            jax.ShapeDtypeStruct(ffn_block, f32),
            jax.ShapeDtypeStruct(gains.shape, f32),
        ],
        in_specs=[vm] * (len(arrays) - 8) + [anywhere] * 8,
        out_specs=[vm] * 7,
        scratch_shapes=[
            VMEM(k.shape, bf16),
            VMEM(v.shape, bf16),
            VMEM((model, cols), bf16),
            VMEM((nseq, heads, rows, width), bf16),
            VMEM((nseq, heads, rows, width), bf16),
            VMEM((width, qcount * rows), f32),
            VMEM((qcount * rows, width), bf16),
            VMEM((width, qcount * rows), bf16),
            VMEM((heads, all_but, rows, width), bf16),
            VMEM((heads, all_but, rows, width), bf16),
            VMEM((heads - 1, rows, width), bf16),
            VMEM((heads - 1, rows, width), bf16),
            VMEM((nseq,) + out_block, bf16),
            VMEM((some,) + out_block, bf16),
            VMEM((heads - 1, some) + out_block[1:], bf16),
            VMEM((some,) + out_block[1:], bf16),
            VMEM((some - 1,) + out_block[1:], bf16),
            VMEM((pieces, nseq, qkv_rows, cut), bf16),
            VMEM((pieces, all_but, qkv_rows, cut), bf16),
            VMEM((pieces, heads, qkv_rows // heads, cut), bf16),
            VMEM((pieces, heads - 1, qkv_rows // heads, cut), bf16),
            VMEM((rows, cols), bf16),
        ]
        + [VMEM((some if i == 1 else some // 2,) + part, bf16) for i, part in enumerate(parts)]
        + [VMEM((all_but if i == 1 else some - 1,) + part, bf16) for i, part in enumerate(parts)]
        + [
            VMEM((bits + 1,) + gains.shape, f32),
            VMEM((bits,) + gains.shape, f32),
            VMEM((heads - 1,) + gains.shape, f32),
            pltpu.SemaphoreType.DMA((copies,)),
            pltpu.SemaphoreType.DMA((copies,)),
            pltpu.SemaphoreType.DMA((5 + 3 * some,)),
        ],
        name="tail",
        compiler_params=pltpu.CompilerParams(
            collective_id=cid, has_side_effects=True, vmem_limit_bytes=62 * 2**20
        ),
    )(*arrays)


CHUNKS, SPANS = 4, 2
ORDER = (
    ("ags", 0, 0, 0), ("ags", 0, 1, 0), ("agw", 0, 0, 0), ("ags", 0, 0, 1), ("agw", 0, 1, 0),
    ("ags", 0, 1, 1), ("ags", 0, 2, 0), ("agw", 0, 0, 1), ("ags", 0, 0, 2), ("agw", 0, 1, 1),
    ("ags", 0, 1, 2), ("ags", 0, 3, 0), ("agw", 0, 0, 2), ("agw", 0, 1, 2), ("fa", 0), ("fb", 0),
    ("agw", 0, 3, 0), ("agw", 0, 2, 0), ("ags", 0, 3, 1), ("ags", 0, 2, 1), ("fc", 0),
    ("agw", 0, 3, 1), ("rss", 0, 0, 0), ("ags", 0, 3, 2), ("agw", 0, 3, 2), ("agw", 0, 2, 1),
    ("rss", 0, 1, 0), ("ags", 0, 2, 2), ("rsw", 0, 0, 0), ("rss", 0, 0, 1), ("rsw", 0, 1, 0),
    ("rss", 0, 1, 1), ("agw", 0, 2, 2), ("fa", 1), ("rsw", 0, 0, 1), ("fb", 1), ("rss", 0, 0, 2),
    ("fc", 1), ("rss", 0, 2, 0), ("rsw", 0, 1, 1), ("rss", 0, 3, 0), ("rss", 0, 1, 2),
    ("rsw", 0, 2, 0), ("rss", 0, 2, 1), ("rsw", 0, 0, 2), ("rsw", 0, 3, 0), ("n", 0),
    ("ags", 1, 0, 0), ("rsw", 0, 1, 2), ("rss", 0, 3, 1), ("rsw", 0, 2, 1), ("rss", 0, 2, 2),
    ("n", 1), ("agw", 1, 0, 0), ("ags", 1, 1, 0), ("ags", 1, 0, 1), ("rsw", 0, 3, 1),
    ("rss", 0, 3, 2), ("agw", 1, 1, 0), ("ags", 1, 1, 1), ("rsw", 0, 2, 2), ("n", 2),
    ("agw", 1, 0, 1), ("ags", 1, 0, 2), ("ags", 1, 2, 0), ("rsw", 0, 3, 2), ("n", 3),
    ("agw", 1, 1, 1), ("ags", 1, 1, 2), ("ags", 1, 3, 0), ("agw", 1, 0, 2), ("agw", 1, 2, 0),
    ("agw", 1, 1, 2), ("ga", 0), ("ags", 1, 2, 1), ("gb", 0), ("agw", 1, 3, 0), ("ags", 1, 3, 1),
    ("gc", 0), ("agw", 1, 2, 1), ("ags", 1, 2, 2), ("rss", 1, 1, 0), ("rss", 1, 0, 0),
    ("agw", 1, 3, 1), ("ags", 1, 3, 2), ("rsw", 1, 1, 0), ("rss", 1, 1, 1), ("agw", 1, 2, 2),
    ("agw", 1, 3, 2), ("ga", 1), ("rsw", 1, 0, 0), ("gb", 1), ("rss", 1, 0, 1), ("gc", 1),
    ("rss", 1, 3, 0), ("wd", 0), ("rsw", 1, 1, 1), ("rss", 1, 2, 0), ("wd", 1), ("rss", 1, 1, 2),
    ("dd", 0), ("rsw", 1, 3, 0), ("rss", 1, 3, 1), ("wg", 0), ("rsw", 1, 2, 0), ("rsw", 1, 0, 1),
    ("rss", 1, 2, 1), ("wg", 1), ("dg", 0), ("rss", 1, 0, 2), ("rsw", 1, 1, 2), ("wu", 0),
    ("rsw", 1, 3, 1), ("e", 1), ("rss", 1, 3, 2), ("rsw", 1, 2, 1), ("rss", 1, 2, 2), ("wu", 1),
    ("rsw", 1, 0, 2), ("Dd", 0), ("Dg", 0), ("e", 0), ("rsw", 1, 3, 2), ("e", 3), ("rsw", 1, 2, 2),
    ("e", 2),
)


def ffn_kernel(
    nseq,
    heads,
    chunks,
    spans,
    proj_ref,
    x_ref,
    cot_ref,
    gain_two_ref,
    gain_three_ref,
    gain_four_ref,
    w_gate_ref,
    w_up_ref,
    w_down_ref,
    o_out,
    o_hid,
    o_proj,
    o_gains,
    o_down,
    o_gate,
    o_up,
    hidden,
    w_gate,
    w_up,
    w_down,
    u_all,
    d_all,
    by_gate,
    by_up,
    act,
    d_gate,
    d_up,
    parts,
    from_left,
    from_right,
    flipped,
    dw_gate,
    dw_up,
    dw_down,
    box_gate,
    box_down,
    sum_send,
    sum_recv,
    ag_send,
    ag_recv,
    rs_send,
    rs_recv,
    local_sem,
):
    f32, bf16 = jnp.float32, jnp.bfloat16
    s, h = place()
    last = heads - 1
    right = (s, lax.rem(h + 1, heads))
    left = (s, lax.rem(h + last, heads))
    rows, model = x_ref.shape
    units = w_gate.shape[0]
    rc = rows // chunks
    each = chunks // spans
    many = rc * heads * each
    tile = 256
    whole_tiles, rest = units // tile, units % tile

    loads = []
    for n, (src, dst) in enumerate(
        ((w_gate_ref, w_gate), (w_up_ref, w_up), (w_down_ref, w_down))
    ):
        copy = pltpu.make_async_copy(src, dst, local_sem.at[n])
        copy.start()
        loads.append(copy)
    bits = nseq.bit_length() - 1
    ups, downs = seq_orders(bits)
    links = Links(nseq, heads, sum_send, sum_recv)
    greet([right, left] + [links.across(b) for b in range(bits)])

    proj = proj_ref[...]
    hid = x_ref[...].astype(f32) + norm_rows(proj, flat(gain_two_ref))
    hidden[...] = hid
    u_local = norm_rows(hid, flat(gain_three_ref)).astype(bf16)
    for c in range(chunks):
        u_all[c, h] = u_local[c * rc : (c + 1) * rc]
    o_gains[...] = jnp.zeros_like(o_gains)

    def lanes(k, c, t):
        buf = d_all if k else u_all
        return (
            (
                (h - t >= 0) & (h < last),
                buf.at[c, jnp.maximum(h - t, 0)],
                0,
                right,
                h - 1 - t >= 0,
                buf.at[c, jnp.maximum(h - 1 - t, 0)],
            ),
            (
                (h + t <= last) & (h > 0),
                buf.at[c, jnp.minimum(h + t, last)],
                1,
                left,
                h + 1 + t <= last,
                buf.at[c, jnp.minimum(h + 1 + t, last)],
            ),
        )

    def ags(k, c, t):
        for on, block, lane, target, _, _ in lanes(k, c, t):
            i = (k, c, lane, t)
            pl.when(on)(remote(block, block, ag_send.at[i], ag_recv.at[i], target).start)

    def agw(k, c, t):
        for _, _, lane, target, on, block in lanes(k, c, t):
            i = (k, c, lane, t)
            pl.when(on)(remote(block, block, ag_send.at[i], ag_recv.at[i], target).wait_recv)

    def rss(k, c, t):
        for on, dest, box, lane, target, at_end in (
            ((t >= h) & (h < last), last - (t - h), from_left, 0, right, h == 0),
            ((t >= last - h) & (h > 0), t - (last - h), from_right, 1, left, h == last),
        ):
            dest = jnp.clip(dest, 0, last)
            i = (k, c, lane, t)
            if t > 0:

                def forward(box=box, dest=dest, i=i, target=target):
                    box[k, c, t - 1] = box[k, c, t - 1] + parts[k, c, dest]
                    remote(
                        box.at[k, c, t - 1], box.at[k, c, t], rs_send.at[i], rs_recv.at[i], target
                    ).start()

                pl.when(on & jnp.logical_not(at_end))(forward)
            pl.when(on & at_end)(
                remote(
                    parts.at[k, c, dest], box.at[k, c, t], rs_send.at[i], rs_recv.at[i], target
                ).start
            )

    def rsw(k, c, t):
        for on, box, lane, target in (
            ((t >= h - 1) & (h > 0), from_left, 0, right),
            ((t >= last - h - 1) & (h < last), from_right, 1, left),
        ):
            i = (k, c, lane, t)
            block = box.at[k, c, t]
            pl.when(on)(remote(block, block, rs_send.at[i], rs_recv.at[i], target).wait_recv)

    def summed(k, c):
        zero = jnp.zeros((rc, model), f32)
        return (
            parts[k, c, h].astype(f32)
            + jnp.where(h > 0, from_left[k, c, last - 1].astype(f32), zero)
            + jnp.where(h < last, from_right[k, c, last - 1].astype(f32), zero)
        )

    def over_tiles(lo, hi, body):
        def step(i, carry):
            body(pl.ds(pl.multiple_of(i * tile, tile), tile))
            return carry

        lax.fori_loop(lo, hi, step, 0)
        if hi == whole_tiles and rest:
            body(pl.ds(whole_tiles * tile, rest))

    arrived = set()

    def need(n):
        if n not in arrived:
            arrived.add(n)
            loads[n].wait()

    def span_rows(buf, p):
        return buf[pl.ds(p * each, each)].reshape(many, model)

    def place_parts(k, p, cols, value):
        parts[k, pl.ds(p * each, each), :, :, cols] = value.astype(bf16).reshape(
            each, heads, rc, value.shape[1]
        )

    def forward_tiles(c, lo, hi):
        need(0)
        need(1)

        def body(cols):
            u = span_rows(u_all, c)
            gate = contract_last(u, w_gate[cols, :])
            up = contract_last(u, w_up[cols, :])
            root = math.sqrt(2.0 / math.pi)
            square = gate * gate
            curve = jnp.tanh(root * gate * (1.0 + 0.044715 * square))
            half = 0.5 * (1.0 + curve)
            gelu = gate * half
            slope = half + 0.5 * gate * (1.0 - curve * curve) * (
                root * (1.0 + 3 * 0.044715 * square)
            )
            by_gate[pl.ds(c * many, many), cols] = slope * up
            by_up[pl.ds(c * many, many), cols] = gelu
            act[pl.ds(c * many, many), cols] = (gelu * up).astype(bf16)

        over_tiles(lo, hi, body)

    out_tile = model // 3

    def down_rows(c):
        need(2)

        def body(i, carry):
            cols = pl.ds(pl.multiple_of(i * out_tile, out_tile), out_tile)
            part = jnp.dot(
                act[pl.ds(c * many, many), :], w_down[:, cols], preferred_element_type=f32
            )
            place_parts(0, c, cols, part)
            return carry

        lax.fori_loop(0, 3, body, 0)

    def turn(c):
        here = pl.ds(c * rc, rc)
        ffn_out = summed(0, c)
        upstream = cot_ref[here, :].astype(f32)
        o_out[here, :] = (hidden[here, :] + norm_rows(ffn_out, flat(gain_four_ref))).astype(
            o_out.dtype
        )
        d_out, terms = back_norm(ffn_out, flat(gain_four_ref), upstream)
        d_all[c, h] = d_out.astype(bf16)
        o_gains[3:4, :] += terms

    def back_tiles(c, lo, hi):
        def body(cols):
            d_act = contract_last(span_rows(d_all, c), w_down[cols, :])
            d_gate[pl.ds(c * many, many), cols] = (
                d_act * by_gate[pl.ds(c * many, many), cols]
            ).astype(bf16)
            d_up[pl.ds(c * many, many), cols] = (
                d_act * by_up[pl.ds(c * many, many), cols]
            ).astype(bf16)

        over_tiles(lo, hi, body)

    def back_rows(c):
        def body(i, carry):
            cols = pl.ds(pl.multiple_of(i * out_tile, out_tile), out_tile)
            part = jnp.dot(
                d_gate[pl.ds(c * many, many), :], w_gate[:, cols], preferred_element_type=f32
            )
            part = part + jnp.dot(
                d_up[pl.ds(c * many, many), :], w_up[:, cols], preferred_element_type=f32
            )
            place_parts(1, c, cols, part)
            return carry

        lax.fori_loop(0, 3, body, 0)

    def finish_rows(c):
        here = pl.ds(c * rc, rc)
        d_in, terms = back_norm(hidden[here, :], flat(gain_three_ref), summed(1, c))
        o_gains[2:3, :] += terms
        d_hid = cot_ref[here, :].astype(f32) + d_in
        o_hid[here, :] = d_hid
        d_proj, terms = back_norm(proj_ref[here, :], flat(gain_two_ref), d_hid)
        o_proj[here, :] = d_proj.astype(o_proj.dtype)
        o_gains[1:2, :] += terms

    stores = []

    def flip(source):
        for p in range(spans):
            flipped[:, pl.ds(p * many, many)] = span_rows(source, p).T

    def weight_grad(right_ref, dst, half):
        def body(cols):
            value = jnp.dot(flipped[...], right_ref[:, cols], preferred_element_type=f32)
            dst[:, :, cols] = value.astype(bf16).reshape(dst.shape[:2] + (value.shape[1],))

        over_tiles(half_tiles if half else 0, whole_tiles if half else half_tiles, body)

    half_tiles = (whole_tiles + 1) // 2
    held = subsets(ups)
    sum_gate = Sum(links, lambda m: dw_gate.at[related(s, m)], box_gate, [0])
    sum_down = Sum(links, lambda m: dw_down.at[related(s, m)], box_down, [0])
    for total in (sum_gate, sum_down):
        total.masks = lambda stage: held
    def keep(total, out, n):
        for i, step in enumerate(total.steps(0)):
            step()
            copy = pltpu.make_async_copy(total.boxes.at[i], out.at[i], local_sem.at[n + i])
            copy.start()
            stores.append(copy)

    for event in ORDER:
        kind, args = event[0], event[1:]
        if kind == "ags":
            ags(*args)
        elif kind == "agw":
            agw(*args)
        elif kind == "rss":
            rss(*args)
        elif kind == "rsw":
            rsw(*args)
        elif kind == "fa":
            forward_tiles(args[0], 0, half_tiles)
        elif kind == "fb":
            forward_tiles(args[0], half_tiles, whole_tiles)
        elif kind == "fc":
            down_rows(args[0])
        elif kind == "n":
            turn(args[0])
        elif kind == "ga":
            back_tiles(args[0], 0, half_tiles)
        elif kind == "gb":
            back_tiles(args[0], half_tiles, whole_tiles)
        elif kind == "gc":
            back_rows(args[0])
        elif kind == "e":
            finish_rows(args[0])
        elif kind == "wd":
            if args[0] == 0:
                flip(d_all)
            weight_grad(act, dw_down, args[0])
        elif kind == "wg":
            if args[0] == 0:
                flip(u_all)
            weight_grad(d_gate, dw_gate, args[0])
        elif kind == "wu":
            weight_grad(d_up, dw_up, args[0])
            if args[0] == 1:
                copy = pltpu.make_async_copy(dw_up, o_up, local_sem.at[3 + 2 * len(held)])
                copy.start()
                stores.append(copy)
        elif kind == "dd":
            sum_down.start()
        elif kind == "dg":
            sum_gate.start()
        elif kind == "Dd":
            keep(sum_down, o_down, 3)
        else:
            keep(sum_gate, o_gate, 3 + len(held))

    for event in ORDER:
        if event[0] == "ags":
            k, c, t = event[1:]
            for on, block, lane, target, _, _ in lanes(k, c, t):
                i = (k, c, lane, t)
                pl.when(on)(remote(block, block, ag_send.at[i], ag_recv.at[i], target).wait_send)
        elif event[0] == "rss":
            k, c, t = event[1:]
            for on, box, lane, target in (
                ((t >= h) & (h < last), from_left, 0, right),
                ((t >= last - h) & (h > 0), from_right, 1, left),
            ):
                i = (k, c, lane, t)
                block = box.at[k, c, t]
                pl.when(on)(remote(block, block, rs_send.at[i], rs_recv.at[i], target).wait_send)
    for n in range(3):
        need(n)
    for copy in stores:
        copy.wait()
    links.finish()


def feed_forward(nseq, heads, cid, *arrays):
    _, x, _, _, _, _, w_gate, w_up, w_down = arrays
    f32, bf16 = jnp.float32, jnp.bfloat16
    rows, model = x.shape
    units = w_gate.shape[0]
    chunks = CHUNKS
    rc = rows // chunks
    group = rows * heads
    vm = pl.BlockSpec(memory_space=VMEM)
    anywhere = pl.BlockSpec(memory_space=pl.ANY)
    block = (model // nseq, units)
    some = nseq // 2
    half = jax.ShapeDtypeStruct((some,) + block, bf16)
    messages = 2 * some
    hops = (2, chunks, 2, heads - 1)
    return pl.pallas_call(
        functools.partial(ffn_kernel, nseq, heads, CHUNKS, SPANS),
        out_shape=[
            jax.ShapeDtypeStruct((rows, model), bf16),
            jax.ShapeDtypeStruct((rows, model), f32),
            jax.ShapeDtypeStruct((rows, model), bf16),
            jax.ShapeDtypeStruct((8, model), f32),
            half,
            half,
            jax.ShapeDtypeStruct((nseq,) + block, bf16),
        ],
        in_specs=[vm] * 6 + [anywhere] * 3,
        out_specs=[vm] * 4 + [anywhere] * 3,
        scratch_shapes=[
            VMEM((rows, model), f32),
            VMEM(w_gate.shape, bf16),
            VMEM(w_up.shape, bf16),
            VMEM(w_down.shape, bf16),
            VMEM((chunks, heads, rc, model), bf16),
            VMEM((chunks, heads, rc, model), bf16),
            VMEM((group, units), f32),
            VMEM((group, units), f32),
            VMEM((group, units), bf16),
            VMEM((group, units), bf16),
            VMEM((group, units), bf16),
            VMEM((2, chunks, heads, rc, model), bf16),
            VMEM((2, chunks, heads - 1, rc, model), bf16),
            VMEM((2, chunks, heads - 1, rc, model), bf16),
            VMEM((model, group), bf16),
            VMEM((nseq,) + block, bf16),
            VMEM((nseq,) + block, bf16),
            VMEM((nseq,) + block, bf16),
            VMEM((some,) + block, bf16),
            VMEM((some,) + block, bf16),
            pltpu.SemaphoreType.DMA((messages,)),
            pltpu.SemaphoreType.DMA((messages,)),
            pltpu.SemaphoreType.DMA(hops),
            pltpu.SemaphoreType.DMA(hops),
            pltpu.SemaphoreType.DMA(hops),
            pltpu.SemaphoreType.DMA(hops),
            pltpu.SemaphoreType.DMA((4 + 2 * some,)),
        ],
        name="feed_forward",
        compiler_params=pltpu.CompilerParams(
            collective_id=cid, has_side_effects=True, vmem_limit_bytes=62 * 2**20
        ),
    )(*arrays)


def finish_kernel(nseq, qw, width, each, few, *refs):
    out, tokens, qkv, w_out, gate, up, down, gains = refs[:8]
    o_out, o_tokens, o_query, o_key, o_value, o_w_out, o_gate, o_up, o_down = refs[8:17]
    o_gains = refs[17:]
    s, h = place()
    which = s * lax.axis_size("head") + h
    o_out[...] = out[...]
    o_tokens[...] = tokens[...]
    o_query[...] = qkv[:, :qw]
    o_key[...] = qkv[:, qw : qw + width]
    o_value[...] = qkv[:, qw + width :]
    o_w_out[...] = w_out[...]
    o_gate[...] = gate[...]
    o_up[...] = up[...]
    o_down[...] = down[...]
    model = gains.shape[1]
    wide = pltpu.roll(gains[...], lax.rem(model - which * each, model), 1)
    narrow = pltpu.roll(gains[...], lax.rem(model - which * few, model), 1)
    for i in range(4):
        o_gains[i][...] = wide[i : i + 1, :each]
    for i in range(4, 6):
        o_gains[i][...] = narrow[i : i + 1, :few]


def finish(nseq, qw, width, each, few, *arrays):
    out, tokens, qkv, w_out, gate, up, down, gains = arrays
    vm = pl.BlockSpec(memory_space=VMEM)
    shape = lambda a: jax.ShapeDtypeStruct(a.shape, a.dtype)
    f32 = jnp.float32
    rows = qkv.shape[0]
    wide, narrow = jax.ShapeDtypeStruct((1, each), f32), jax.ShapeDtypeStruct((1, few), f32)
    return pl.pallas_call(
        functools.partial(finish_kernel, nseq, qw, width, each, few),
        out_shape=[shape(out), shape(tokens)]
        + [jax.ShapeDtypeStruct((rows, n), f32) for n in (qw, width, width)]
        + [shape(w_out), shape(gate), shape(up), shape(down)]
        + [wide] * 4
        + [narrow] * 2,
        in_specs=[vm] * 8,
        out_specs=[vm] * 15,
        name="finish",
        compiler_params=pltpu.CompilerParams(vmem_limit_bytes=LIMIT),
    )(*arrays)


def local(
    tokens,
    segment_ids,
    w_query,
    w_key,
    w_value,
    w_out,
    w_gate,
    w_up,
    w_down,
    gain_attn_in,
    gain_attn_out,
    gain_ffn_in,
    gain_ffn_out,
    gain_query,
    gain_key,
    cotangent,
):
    heads = lax.axis_size("head")
    nseq = lax.axis_size("seq")
    head_index = lax.axis_index("head")
    seq_index = lax.axis_index("seq")
    bits = nseq.bit_length() - 1
    local_rows, model = tokens.shape
    width = gain_query.shape[0]
    qcount = w_query.shape[1] // width
    group = local_rows * heads
    total = segment_ids.shape[0]
    hidden_units = w_gate.shape[1]
    scale = 1.0 / math.sqrt(width)
    bf16 = jnp.bfloat16
    if (nseq, heads) == (8, 4) and (model // nseq) % 16 == 0:
        qw = qcount * width
        each, few = model // (nseq * heads), width // (nseq * heads)
        (
            projected,
            queries,
            keys,
            values,
            starts,
            index,
            log_total,
            attended_t,
            q_linear,
            k_linear,
            cosines,
            sines,
            attn_t,
        ) = front(
            nseq,
            heads,
            qcount,
            scale,
            11,
            tokens,
            segment_ids,
            w_key,
            w_value,
            gain_attn_in,
            gain_query,
            gain_key,
            w_query,
            w_out,
        )
        output, d_hidden, d_projected, gains, half_down, half_gate, all_up = feed_forward(
            nseq,
            heads,
            10,
            projected,
            tokens,
            cotangent,
            gain_attn_out,
            gain_ffn_in,
            gain_ffn_out,
            w_gate.T,
            w_up.T,
            w_down,
        )
        grad_tokens, sum_qkv, sum_out, sum_gate, sum_up, sum_down, sum_gains = tail(
            nseq,
            heads,
            qcount,
            scale,
            9,
            queries,
            starts,
            index,
            log_total,
            attended_t,
            d_projected,
            w_out,
            q_linear,
            k_linear,
            cosines,
            sines,
            gain_query,
            gain_key,
            gain_attn_in,
            attn_t,
            tokens,
            d_hidden,
            gains,
            keys.reshape(nseq, group, width),
            values.reshape(nseq, group, width),
            w_query,
            w_key,
            w_value,
            half_gate,
            all_up,
            half_down,
        )
        (
            output,
            grad_tokens,
            sum_query,
            sum_key,
            sum_value,
            sum_out,
            sum_gate,
            sum_up,
            sum_down,
            *sum_gains,
        ) = finish(
            nseq,
            qw,
            width,
            each,
            few,
            output,
            grad_tokens,
            sum_qkv,
            sum_out,
            sum_gate,
            sum_up,
            sum_down,
            sum_gains,
        )
        return (
            output,
            grad_tokens,
            sum_query,
            sum_key,
            sum_value,
            sum_out,
            sum_gate,
            sum_up,
            sum_down.T,
            *[g[0] for g in sum_gains],
        )
    first_row = (seq_index * heads + head_index) * local_rows
    my_index = first_row + jnp.arange(local_rows, dtype=jnp.int32)
    my_ids = lax.dynamic_slice_in_dim(segment_ids, first_row, local_rows)
    my_starts = jnp.min(
        jnp.where(
            my_ids[:, None] == segment_ids[None, :],
            jnp.arange(total, dtype=jnp.int32)[None, :],
            total,
        ),
        axis=1,
    )
    cosines, sines = rope_tables(my_index - my_starts, width)

    def query_path(linear, gain):
        shaped = linear.reshape(local_rows, qcount, width)
        turned = rotate(norm_rows(shaped, gain), cosines[:, None, :], sines[:, None, :])
        return turned.reshape(local_rows, qcount * width)

    def key_path(linear, gain):
        return rotate(norm_rows(linear, gain), cosines, sines)

    def gated(gate, up):
        return jax.nn.gelu(gate, approximate=True) * up

    def stacked(v):
        return v.reshape(local_rows, qcount, width).transpose(1, 0, 2).reshape(-1, width)

    def unstacked(v):
        return v.reshape(qcount, local_rows, width).transpose(1, 0, 2).reshape(local_rows, -1)

    inputs = tokens.astype(jnp.float32)
    attn_in = norm_rows(inputs, gain_attn_in).astype(bf16)
    k_linear = jnp.dot(attn_in, w_key, preferred_element_type=jnp.float32)
    keys_local = key_path(k_linear, gain_key).astype(bf16)
    values_local = jnp.dot(attn_in, w_value, preferred_element_type=jnp.float32).astype(bf16)
    q_linear = jnp.dot(attn_in, w_query, preferred_element_type=jnp.float32)
    queries_local = query_path(q_linear, gain_query).astype(bf16)
    queries = stacked(queries_local) * jnp.asarray(scale, bf16)
    keys, values = gather_all([keys_local, values_local], nseq, heads, 1)
    keys = keys.reshape(nseq, group, width)
    values = values.reshape(nseq, group, width)
    starts = jnp.tile(my_starts, qcount)[None, :]
    index = jnp.tile(my_index, qcount)[None, :]
    attended_t, log_total = attend(queries, keys, values, starts, index)
    attended = attended_t.T
    mixed_local = unstacked(attended.astype(bf16))
    projected = jnp.dot(mixed_local, w_out, preferred_element_type=jnp.float32)
    hidden = inputs + norm_rows(projected, gain_attn_out)
    ffn_in = norm_rows(hidden, gain_ffn_in).astype(bf16)
    ffn_rows = line_gather(ffn_in, heads, 2).reshape(group, model)
    gate = jnp.dot(ffn_rows, w_gate, preferred_element_type=jnp.float32)
    up = jnp.dot(ffn_rows, w_up, preferred_element_type=jnp.float32)
    activated = gated(gate, up).astype(bf16)
    ffn_out = line_scatter(
        jnp.dot(activated, w_down, preferred_element_type=jnp.float32)
        .astype(bf16)
        .reshape(heads, local_rows, model),
        heads,
        3,
    )
    output = hidden + norm_rows(ffn_out, gain_ffn_out)
    upstream = cotangent.astype(jnp.float32)
    unused, back_four = jax.vjp(norm_rows, ffn_out, gain_ffn_out)
    d_ffn_out, d_gain_four = back_four(upstream)
    d_ffn_rows = line_gather(d_ffn_out.astype(bf16), heads, 4).reshape(group, model)
    d_activated = contract_last(d_ffn_rows, w_down)
    d_w_down = contract_first(d_ffn_rows, activated)
    unused, back_gate = jax.vjp(gated, gate, up)
    d_gate, d_up = back_gate(d_activated)
    d_gate = d_gate.astype(bf16)
    d_up = d_up.astype(bf16)
    d_ffn_in = line_scatter(
        (contract_last(d_gate, w_gate) + contract_last(d_up, w_up))
        .astype(bf16)
        .reshape(heads, local_rows, model),
        heads,
        5,
    )
    d_w_gate = contract_first(ffn_rows, d_gate)
    d_w_up = contract_first(ffn_rows, d_up)
    unused, back_three = jax.vjp(norm_rows, hidden, gain_ffn_in)
    d_hidden_part, d_gain_three = back_three(d_ffn_in)
    d_hidden = upstream + d_hidden_part
    unused, back_two = jax.vjp(norm_rows, projected, gain_attn_out)
    d_projected, d_gain_two = back_two(d_hidden)
    d_projected = d_projected.astype(bf16)
    qw = qcount * width
    d_w_out = contract_first(mixed_local, d_projected)
    d_mixed = contract_last(d_projected, w_out).astype(bf16)
    grad_attended = stacked(d_mixed)
    row_dots = jnp.sum(grad_attended.astype(jnp.float32) * attended, axis=1)[None, :]
    d_queries_t, d_keys, d_values = attend_back(
        queries, keys, values, starts, index, log_total, row_dots, grad_attended
    )
    shape = (nseq, heads, local_rows, width)
    ups, downs = seq_orders(bits)
    d_keys, d_values = scatter_all(
        [d_keys.reshape(shape), d_values.reshape(shape)],
        [True, True],
        [[0] + ups, [0] + downs],
        nseq,
        heads,
        6,
        "scatter_keys",
    )
    d_query_rot = unstacked((d_queries_t.T * scale).astype(bf16)).astype(jnp.float32)
    unused, back_query = jax.vjp(query_path, q_linear, gain_query)
    d_q_linear, d_gain_query = back_query(d_query_rot)
    unused, back_key = jax.vjp(key_path, k_linear, gain_key)
    d_k_linear, d_gain_key = back_key(d_keys)
    d_qkv = jnp.concatenate([d_q_linear, d_k_linear, d_values], axis=1).astype(bf16)
    qw = qcount * width
    d_w_qkv = contract_first(attn_in, d_qkv)
    d_attn_in = (
        contract_last(d_qkv[:, :qw], w_query)
        + contract_last(d_qkv[:, qw : qw + width], w_key)
        + contract_last(d_qkv[:, qw + width :], w_value)
    )
    unused, back_one = jax.vjp(norm_rows, inputs, gain_attn_in)
    d_inputs, d_gain_one = back_one(d_attn_in)
    grad_tokens = (d_hidden + d_inputs).astype(bf16)

    def cut(v):
        return v.reshape(nseq, heads, -1)

    wide = jnp.stack([cut(d_gain_one), cut(d_gain_two), cut(d_gain_three), cut(d_gain_four)], 2)
    narrow = jnp.stack([cut(d_gain_query), cut(d_gain_key)], 2)
    each, few = wide.shape[-1], narrow.shape[-1]
    gains = jnp.concatenate(
        [
            jnp.pad(wide, ((0, 0), (0, 0), (0, 0), (0, 128 - each))),
            jnp.pad(narrow, ((0, 0), (0, 0), (0, 2), (0, 128 - few))),
        ],
        axis=2,
    )
    sum_qkv, sum_out, sum_gains = scatter_all(
        [
            d_w_qkv.astype(bf16).reshape(nseq, heads, -1, d_qkv.shape[1]),
            d_w_out.astype(bf16).reshape(nseq, heads, -1, model),
            gains,
        ],
        [True, True, True],
        [[0] + ups, [0] + downs, [0] + downs],
        nseq,
        heads,
        7,
        "scatter_attn",
    )
    sum_gate, sum_up, sum_down = scatter_all(
        [
            d.astype(bf16).reshape(nseq, model // nseq, hidden_units)
            for d in (d_w_gate, d_w_up, d_w_down)
        ],
        [False, False, False],
        [[0] + ups, [0] + downs, [0] + ups],
        nseq,
        heads,
        8,
        "scatter_ffn",
    )
    return (
        output.astype(bf16),
        grad_tokens,
        sum_qkv[:, :qw],
        sum_qkv[:, qw : qw + width],
        sum_qkv[:, qw + width :],
        sum_out,
        sum_gate,
        sum_up,
        sum_down.T,
        sum_gains[0, :each],
        sum_gains[1, :each],
        sum_gains[2, :each],
        sum_gains[3, :each],
        sum_gains[4, :few],
        sum_gains[5, :few],
    )


def solution(mesh):
    rows = P(("seq", "head"), None)
    in_specs = (
        rows,
        P(),
        P(),
        P(),
        P(),
        P(),
        P(None, "head"),
        P(None, "head"),
        P("head", None),
        P(),
        P(),
        P(),
        P(),
        P(),
        P(),
        rows,
    )
    out_specs = (
        rows,
        rows,
        rows,
        rows,
        rows,
        rows,
        P("seq", "head"),
        P("seq", "head"),
        P("head", "seq"),
    ) + (P(("seq", "head")),) * 6
    return jax.shard_map(local, mesh=mesh, in_specs=in_specs, out_specs=out_specs, check_vma=False)
```

```python
import functools
import itertools
import math

import jax
import jax.numpy as jnp
from jax import lax
from jax.experimental import pallas as pl
from jax.experimental.pallas import tpu as pltpu
from jax.sharding import PartitionSpec as P

EPS = 1e-06
MESH = pl.DeviceIdType.MESH
VMEM = pltpu.VMEM
LIMIT = 56 * 2**20


def norm_rows(v, gain):
    return v * lax.rsqrt(jnp.mean(v * v, axis=-1, keepdims=True) + EPS) * gain


def rotate(v, cosines, sines):
    half = v.shape[-1] // 2
    first = v[..., :half]
    second = v[..., half:]
    return jnp.concatenate(
        [first * cosines - second * sines, second * cosines + first * sines], axis=-1
    )


def rope_tables(positions, width):
    half = width // 2
    freq = jnp.exp(jnp.arange(half, dtype=jnp.float32) * (-2.0 * math.log(1000000.0) / width))
    angle = positions.astype(jnp.float32)[:, None] * freq[None, :]
    return (jnp.cos(angle), jnp.sin(angle))


def contract_first(left, right):
    return lax.dot_general(
        left, right, (((0,), (0,)), ((), ())), preferred_element_type=jnp.float32
    )


def contract_last(left, right):
    return lax.dot_general(
        left, right, (((1,), (1,)), ((), ())), preferred_element_type=jnp.float32
    )


def place():
    return lax.axis_index("seq"), lax.axis_index("head")


def related(s, mask):
    out = s
    bit = 0
    while mask >> bit:
        if (mask >> bit) & 1:
            step = 1 << bit
            out = out + (1 - 2 * ((s // step) % 2)) * step
        bit += 1
    return out


def subsets(bits):
    out = [0]
    for bit in bits:
        out = out + [m | (1 << bit) for m in out]
    return out


def greet(targets):
    barrier = pltpu.get_barrier_semaphore()
    for target in targets:
        pl.semaphore_signal(barrier, inc=1, device_id=target, device_id_type=MESH)
    pl.semaphore_wait(barrier, len(targets))


def remote(src, dst, send, recv, target):
    return pltpu.make_async_remote_copy(
        src_ref=src,
        dst_ref=dst,
        send_sem=send,
        recv_sem=recv,
        device_id=target,
        device_id_type=MESH,
    )


def seq_orders(bits):
    upper = list(range(1, bits))
    return upper, upper[::-1]


def gather_kernel(nseq, heads, local_refs, out_refs, send, recv):
    bits = nseq.bit_length() - 1
    s, h = place()
    others = [lax.rem(h + d, heads) for d in range(1, heads)]
    greet([(related(s, 1 << b), h) for b in range(bits)] + [(s, o) for o in others])
    count = [0]
    started = []

    def go(src, dst, target):
        k = count[0]
        count[0] += 1
        copy = remote(src, dst, send.at[k], recv.at[k], target)
        copy.start()
        started.append(copy)
        return copy

    first = []
    for a in range(len(out_refs)):
        out_refs[a][s, h] = local_refs[a][...]
        first.append(
            [go(local_refs[a], out_refs[a].at[s, h], (s, o)) for o in others]
        )
    orders = [o + [0] for o in seq_orders(bits)]
    held = [{0: first[a]} for a in range(len(out_refs))]
    for stage in range(bits):
        for a in range(len(out_refs)):
            bit = orders[a % 2][stage]
            target = (related(s, 1 << bit), h)
            arrived = {}
            for mask in list(held[a]):
                for copy in held[a][mask]:
                    copy.wait_recv()
                held[a][mask] = []
                group = related(s, mask)
                copy = go(out_refs[a].at[group], out_refs[a].at[group], target)
                arrived[mask | (1 << bit)] = [copy]
            held[a].update(arrived)
    for a in range(len(out_refs)):
        for mask in held[a]:
            for copy in held[a][mask]:
                copy.wait_recv()
    for copy in started:
        copy.wait_send()


def gather_all(arrays, nseq, heads, cid):
    n = len(arrays)
    total = n * (heads - 1 + nseq - 1)

    def kernel(*refs):
        gather_kernel(nseq, heads, refs[:n], refs[n : 2 * n], refs[2 * n], refs[2 * n + 1])

    return pl.pallas_call(
        kernel,
        out_shape=[jax.ShapeDtypeStruct((nseq, heads) + a.shape, a.dtype) for a in arrays],
        in_specs=[pl.BlockSpec(memory_space=VMEM)] * n,
        out_specs=[pl.BlockSpec(memory_space=VMEM)] * n,
        scratch_shapes=[pltpu.SemaphoreType.DMA((total,)), pltpu.SemaphoreType.DMA((total,))],
        name="gather_all",
        compiler_params=pltpu.CompilerParams(
            collective_id=cid, has_side_effects=True, vmem_limit_bytes=LIMIT
        ),
    )(*arrays)


def line_gather_kernel(heads, x_ref, out_ref, send, recv):
    s, h = place()
    right = (s, lax.rem(h + 1, heads))
    left = (s, lax.rem(h + heads - 1, heads))
    greet([right, left])
    out_ref[h] = x_ref[...]
    for step in range(heads - 1):
        to_right = remote(
            out_ref.at[jnp.maximum(h - step, 0)],
            out_ref.at[jnp.maximum(h - step, 0)],
            send.at[0, step],
            recv.at[0, step],
            right,
        )
        to_left = remote(
            out_ref.at[jnp.minimum(h + step, heads - 1)],
            out_ref.at[jnp.minimum(h + step, heads - 1)],
            send.at[1, step],
            recv.at[1, step],
            left,
        )
        pl.when((h - step >= 0) & (h < heads - 1))(to_right.start)
        pl.when((h + step <= heads - 1) & (h > 0))(to_left.start)
        pl.when(h - 1 - step >= 0)(
            remote(
                out_ref.at[jnp.maximum(h - 1 - step, 0)],
                out_ref.at[jnp.maximum(h - 1 - step, 0)],
                send.at[0, step],
                recv.at[0, step],
                right,
            ).wait_recv
        )
        pl.when(h + 1 + step <= heads - 1)(
            remote(
                out_ref.at[jnp.minimum(h + 1 + step, heads - 1)],
                out_ref.at[jnp.minimum(h + 1 + step, heads - 1)],
                send.at[1, step],
                recv.at[1, step],
                left,
            ).wait_recv
        )
        pl.when((h - step >= 0) & (h < heads - 1))(to_right.wait_send)
        pl.when((h + step <= heads - 1) & (h > 0))(to_left.wait_send)


def line_gather(x, heads, cid):
    return pl.pallas_call(
        functools.partial(line_gather_kernel, heads),
        out_shape=jax.ShapeDtypeStruct((heads,) + x.shape, x.dtype),
        in_specs=[pl.BlockSpec(memory_space=VMEM)],
        out_specs=pl.BlockSpec(memory_space=VMEM),
        scratch_shapes=[
            pltpu.SemaphoreType.DMA((2, heads - 1)),
            pltpu.SemaphoreType.DMA((2, heads - 1)),
        ],
        name="line_gather",
        compiler_params=pltpu.CompilerParams(
            collective_id=cid, has_side_effects=True, vmem_limit_bytes=LIMIT
        ),
    )(x)


def line_scatter_kernel(heads, parts, out_ref, from_left, from_right, send, recv):
    s, h = place()
    last = heads - 1
    right = (s, lax.rem(h + 1, heads))
    left = (s, lax.rem(h + heads - 1, heads))
    greet([right, left])
    f32 = jnp.float32
    for step in range(heads - 1):
        r_dest = jnp.clip(last - (step - h), 0, last)
        l_dest = jnp.clip(step - (last - h), 0, last)
        r_on = (step >= h) & (h < last)
        l_on = (step >= last - h) & (h > 0)
        for on, dest, box, lane, target, first in (
            (r_on, r_dest, from_left, 0, right, step == h),
            (l_on, l_dest, from_right, 1, left, step == last - h),
        ):
            at_end = (h == 0) if lane == 0 else (h == last)
            if step > 0:

                def add(box=box, dest=dest):
                    box[step - 1] = (
                        box[step - 1].astype(f32) + parts[dest].astype(f32)
                    ).astype(box.dtype)

                pl.when(on & jnp.logical_not(at_end))(add)
                pl.when(on & jnp.logical_not(at_end))(
                    remote(
                        box.at[step - 1], box.at[step], send.at[lane, step], recv.at[lane, step], target
                    ).start
                )
            pl.when(on & at_end)(
                remote(
                    parts.at[dest], box.at[step], send.at[lane, step], recv.at[lane, step], target
                ).start
            )
        r_in = (step >= h - 1) & (h > 0)
        l_in = (step >= last - h - 1) & (h < last)
        pl.when(r_in)(
            remote(
                from_left.at[step], from_left.at[step], send.at[0, step], recv.at[0, step], right
            ).wait_recv
        )
        pl.when(l_in)(
            remote(
                from_right.at[step], from_right.at[step], send.at[1, step], recv.at[1, step], left
            ).wait_recv
        )
    for step in range(heads - 1):
        for on, box, lane, target in (
            ((step >= h) & (h < last), from_left, 0, right),
            ((step >= last - h) & (h > 0), from_right, 1, left),
        ):
            pl.when(on)(
                remote(
                    box.at[step], box.at[step], send.at[lane, step], recv.at[lane, step], target
                ).wait_send
            )
    out_ref[...] = parts[h].astype(f32)

    def add_left():
        out_ref[...] += from_left[heads - 2].astype(f32)

    def add_right():
        out_ref[...] += from_right[heads - 2].astype(f32)

    pl.when(h > 0)(add_left)
    pl.when(h < last)(add_right)


def line_scatter(parts, heads, cid):
    block = parts.shape[1:]
    return pl.pallas_call(
        functools.partial(line_scatter_kernel, heads),
        out_shape=jax.ShapeDtypeStruct(block, jnp.float32),
        in_specs=[pl.BlockSpec(memory_space=VMEM)],
        out_specs=pl.BlockSpec(memory_space=VMEM),
        scratch_shapes=[
            VMEM((heads - 1,) + block, parts.dtype),
            VMEM((heads - 1,) + block, parts.dtype),
            pltpu.SemaphoreType.DMA((2, heads - 1)),
            pltpu.SemaphoreType.DMA((2, heads - 1)),
        ],
        name="line_scatter",
        compiler_params=pltpu.CompilerParams(
            collective_id=cid, has_side_effects=True, vmem_limit_bytes=LIMIT
        ),
    )(parts)


def scatter_kernel(nseq, heads, zs, orders, parts, outs, boxes, zboxes, send, recv):
    bits = nseq.bit_length() - 1
    s, h = place()
    f32 = jnp.float32
    others = [lax.rem(h + d, heads) for d in range(1, heads)]
    greet(
        [(related(s, 1 << b), h) for b in range(bits)]
        + ([(s, o) for o in others] if any(zs) else [])
    )
    count = [0]
    started = []

    def go(src, dst, target):
        k = count[0]
        count[0] += 1
        copy = remote(src, dst, send.at[k], recv.at[k], target)
        copy.start()
        started.append(copy)
        return copy

    n = len(parts)
    offsets = [0] * n
    slot = [{} for _ in range(n)]
    waiting = [{} for _ in range(n)]

    def current(a, mask):
        if mask in slot[a]:
            return boxes[a].at[slot[a][mask]]
        return parts[a].at[related(s, mask)]

    def launch(a, stage):
        bit = orders[a][stage]
        rest = orders[a][stage + 1 :]
        target = (related(s, 1 << bit), h)
        after = 1 << rest[0] if rest else 0
        masks = sorted(subsets(rest), key=lambda m: 0 if m & after else 1)
        for mask in masks:
            where = offsets[a]
            offsets[a] += 1
            waiting[a][mask] = (
                go(current(a, mask | (1 << bit)), boxes[a].at[where], target),
                where,
            )

    def settle(a, mask):
        copy, where = waiting[a].pop(mask)
        mine = current(a, mask)
        copy.wait_recv()
        boxes[a][where] = (boxes[a][where].astype(f32) + mine[...].astype(f32)).astype(
            boxes[a].dtype
        )
        slot[a][mask] = where

    for a in range(n):
        launch(a, 0)
    for stage in range(bits):
        for a in range(n):
            for mask in list(waiting[a]):
                settle(a, mask)
            if stage + 1 < bits:
                launch(a, stage + 1)
    arriving = []
    for a in range(n):
        if not zs[a]:
            continue
        mine = current(a, 0)
        arriving.append(
            [
                go(mine.at[o], zboxes[a].at[d], (s, o))
                for d, o in enumerate(others)
            ]
        )
    z = 0
    for a in range(n):
        if zs[a]:
            total = current(a, 0)[h].astype(f32)
            for d, copy in enumerate(arriving[z]):
                copy.wait_recv()
                total = total + zboxes[a][d].astype(f32)
            outs[a][...] = total
            z += 1
        else:
            outs[a][...] = current(a, 0)[...].astype(f32)
    for copy in started:
        copy.wait_send()


def scatter_all(arrays, zs, orders, nseq, heads, cid, name):
    n = len(arrays)
    total = sum((nseq - 1) + (heads - 1 if z else 0) for z in zs)
    blocks = [a.shape[2:] if z else a.shape[1:] for a, z in zip(arrays, zs)]

    def kernel(*refs):
        scatter_kernel(
            nseq,
            heads,
            zs,
            orders,
            refs[:n],
            refs[n : 2 * n],
            refs[2 * n : 3 * n],
            refs[3 * n : 4 * n],
            refs[4 * n],
            refs[4 * n + 1],
        )

    return pl.pallas_call(
        kernel,
        out_shape=[jax.ShapeDtypeStruct(b, jnp.float32) for b in blocks],
        in_specs=[pl.BlockSpec(memory_space=VMEM)] * n,
        out_specs=[pl.BlockSpec(memory_space=VMEM)] * n,
        scratch_shapes=[VMEM((nseq - 1,) + a.shape[1:], a.dtype) for a in arrays]
        + [
            VMEM((heads - 1,) + b, a.dtype) if z else VMEM((8, 128), jnp.float32)
            for a, b, z in zip(arrays, blocks, zs)
        ]
        + [pltpu.SemaphoreType.DMA((total,)), pltpu.SemaphoreType.DMA((total,))],
        name=name,
        compiler_params=pltpu.CompilerParams(
            collective_id=cid, has_side_effects=True, vmem_limit_bytes=LIMIT
        ),
    )(*arrays)


def attend_kernel(q_ref, k_ref, v_ref, start_ref, index_ref, out_ref, log_ref):
    s = lax.axis_index("seq")
    span = k_ref.shape[1]
    start = start_ref[...]
    index = index_ref[...]
    queries = q_ref[...]
    rows = queries.shape[0]
    out_ref[...] = jnp.zeros_like(out_ref)

    def step(g, mass):
        scores = contract_last(k_ref[g], queries)
        key = g * span + lax.broadcasted_iota(jnp.int32, (span, rows), 0)
        terms = jnp.where((key >= start) & (key <= index), jnp.exp(scores), 0.0)
        out_ref[...] += contract_first(v_ref[g], terms.astype(jnp.bfloat16))
        return mass + jnp.sum(terms, axis=0, keepdims=True)

    mass = lax.fori_loop(0, s + 1, step, jnp.zeros((1, rows), jnp.float32))
    out_ref[...] = out_ref[...] / mass
    log_ref[...] = jnp.log(mass)


def attend(q, k, v, start, index):
    rows, width = q.shape
    return pl.pallas_call(
        attend_kernel,
        out_shape=[
            jax.ShapeDtypeStruct((width, rows), jnp.float32),
            jax.ShapeDtypeStruct((1, rows), jnp.float32),
        ],
        in_specs=[pl.BlockSpec(memory_space=VMEM)] * 5,
        out_specs=[pl.BlockSpec(memory_space=VMEM)] * 2,
        name="attend",
        compiler_params=pltpu.CompilerParams(vmem_limit_bytes=LIMIT),
    )(q, k, v, start, index)


def attend_back_kernel(
    q_ref, k_ref, v_ref, start_ref, index_ref, log_ref, dots_ref, d_ref, dq_ref, dk_ref, dv_ref
):
    s = lax.axis_index("seq")
    groups, span = k_ref.shape[:2]
    start = start_ref[...]
    index = index_ref[...]
    log_total = log_ref[...]
    dots = dots_ref[...]
    queries = q_ref[...]
    grads = d_ref[...]
    rows = queries.shape[0]
    dq_ref[...] = jnp.zeros_like(dq_ref)

    def step(g, carry):
        keys = k_ref[g]
        scores = contract_last(keys, queries)
        key = g * span + lax.broadcasted_iota(jnp.int32, (span, rows), 0)
        probs = jnp.where((key >= start) & (key <= index), jnp.exp(scores - log_total), 0.0)
        d_probs = contract_last(v_ref[g], grads)
        d_scores = (probs * (d_probs - dots)).astype(jnp.bfloat16)
        dv_ref[g] = jnp.dot(
            probs.astype(jnp.bfloat16), grads, preferred_element_type=jnp.float32
        ).astype(dv_ref.dtype)
        dk_ref[g] = jnp.dot(d_scores, queries, preferred_element_type=jnp.float32).astype(
            dk_ref.dtype
        )
        dq_ref[...] += contract_first(keys, d_scores)
        return carry

    lax.fori_loop(0, s + 1, step, 0)

    def blank(g, carry):
        dk_ref[g] = jnp.zeros(dk_ref.shape[1:], dk_ref.dtype)
        dv_ref[g] = jnp.zeros(dv_ref.shape[1:], dv_ref.dtype)
        return carry

    lax.fori_loop(s + 1, groups, blank, 0)


def attend_back(q, k, v, start, index, log_total, dots, grads):
    rows, width = q.shape
    return pl.pallas_call(
        attend_back_kernel,
        out_shape=[
            jax.ShapeDtypeStruct((width, rows), jnp.float32),
            jax.ShapeDtypeStruct(k.shape, jnp.bfloat16),
            jax.ShapeDtypeStruct(v.shape, jnp.bfloat16),
        ],
        in_specs=[pl.BlockSpec(memory_space=VMEM)] * 8,
        out_specs=[pl.BlockSpec(memory_space=VMEM)] * 3,
        name="attend_back",
        compiler_params=pltpu.CompilerParams(vmem_limit_bytes=LIMIT),
    )(q, k, v, start, index, log_total, dots, grads)


def flat(ref):
    return ref[...].reshape(1, ref.shape[0])


def front_kernel(
    nseq,
    heads,
    qcount,
    scale,
    x_ref,
    ids_ref,
    w_key_ref,
    w_value_ref,
    gain_in_ref,
    gain_q_ref,
    gain_k_ref,
    w_query_far,
    w_out_far,
    o_proj,
    o_q,
    o_k,
    o_v,
    o_start,
    o_index,
    o_log,
    o_att,
    o_q_lin,
    o_k_lin,
    o_cos,
    o_sin,
    o_attn_t,
    w_query,
    w_out,
    k_all,
    v_all,
    send,
    recv,
    local_sem,
):
    f32, bf16 = jnp.float32, jnp.bfloat16
    bits = nseq.bit_length() - 1
    ups, downs = seq_orders(bits)
    links = Links(nseq, heads, send, recv)
    s, h = links.s, links.h
    rows, model = x_ref.shape
    width = w_key_ref.shape[1]
    gain_q, gain_k = flat(gain_q_ref), flat(gain_k_ref)
    half = width // 2
    total = ids_ref.shape[0] * ids_ref.shape[1]
    load_q = pltpu.make_async_copy(w_query_far, w_query, local_sem.at[0])
    load_q.start()
    load_o = pltpu.make_async_copy(w_out_far, w_out, local_sem.at[1])
    load_o.start()
    partners = [related(h, j) for j in range(1, heads)]
    greet([links.across(b) for b in range(bits)] + [(s, o) for o in partners])

    which = s * heads + h
    mine = ids_ref[pl.ds(which, 1), :].astype(f32)
    column = jnp.broadcast_to(mine, (rows, rows)).T[:, 0:1]
    first = jnp.full((rows, rows), float(total), f32)
    for r in range(ids_ref.shape[0]):
        here = ids_ref[r : r + 1, :].astype(f32)
        at = (r * rows + lax.broadcasted_iota(jnp.int32, (1, rows), 1)).astype(f32)
        first = jnp.minimum(first, jnp.where(column == here, at, float(total)))
    start = jnp.min(first, axis=1, keepdims=True)
    index = (which * rows + lax.broadcasted_iota(jnp.int32, (rows, 1), 0)).astype(f32)
    freq = jnp.exp(
        lax.broadcasted_iota(jnp.int32, (1, half), 1).astype(f32)
        * (-2.0 * math.log(1000000.0) / width)
    )
    angle = (index - start) * freq
    turns = jnp.round(angle * (1.0 / (2.0 * math.pi)))
    angle = (angle - turns * 6.28125) - turns * (2.0 * math.pi - 6.28125)
    cosines, sines = jnp.cos(angle), jnp.sin(angle)
    o_cos[...] = cosines
    o_sin[...] = sines
    start_row = jnp.broadcast_to(start, (rows, rows)).T[0:1, :].astype(jnp.int32)
    index_row = which * rows + lax.broadcasted_iota(jnp.int32, (1, rows), 1)
    for j in range(qcount):
        o_start[:, pl.ds(j * rows, rows)] = start_row
        o_index[:, pl.ds(j * rows, rows)] = index_row

    attn_in = norm_rows(x_ref[...].astype(f32), flat(gain_in_ref)).astype(bf16)
    k_lin = jnp.dot(attn_in, w_key_ref[...], preferred_element_type=f32)
    k_all[s, h] = rotate(norm_rows(k_lin, gain_k), cosines, sines).astype(bf16)
    o_k_lin[...] = k_lin
    v_all[s, h] = jnp.dot(attn_in, w_value_ref[...], preferred_element_type=f32).astype(bf16)

    both = ((k_all, ups), (v_all, downs))

    def pass_on(a, mask, j, bit):
        buf = both[a][0]
        block = buf.at[related(s, mask), related(h, j)]
        return links.go(block, block, links.across(bit))

    over_head = {}
    for j in range(1, heads):
        for a in range(2):
            block = both[a][0].at[s, h]
            over_head[a, j] = links.go(block, block, (s, partners[j - 1]))
    arriving = {}

    def spread(a, mask, j, stage):
        order = both[a][1]
        for later in range(stage, len(order)):
            bit = order[later]
            arriving[a, mask | (1 << bit), j] = pass_on(a, mask, j, bit)

    for a in range(2):
        spread(a, 0, 0, 0)

    load_q.wait()
    q_lin = jnp.dot(attn_in, w_query[...], preferred_element_type=f32)
    o_q_lin[...] = q_lin
    for j in range(1, heads):
        for a in range(2):
            over_head[a, j].wait_recv()
            spread(a, 0, j, 0)
    for j in range(qcount):
        part = norm_rows(q_lin[:, j * width : (j + 1) * width], gain_q)
        o_q[pl.ds(j * rows, rows), :] = (rotate(part, cosines, sines) * scale).astype(bf16)

    pairs = []

    def to_pair(a, mask):
        block = both[a][0].at[related(s, mask)]
        pairs.append(links.go(block, block, links.across(0)))

    for a in range(2):
        to_pair(a, 0)
    for stage in range(len(ups)):
        for lower in subsets(range(stage)):
            masks = []
            for a in range(2):
                order = both[a][1]
                mask = sum(1 << order[i] for i in range(stage) if lower >> i & 1)
                masks.append(mask | (1 << order[stage]))
            for j in range(heads):
                for a in range(2):
                    arriving[a, masks[a], j].wait_recv()
                    spread(a, masks[a], j, stage + 1)
            for a in range(2):
                to_pair(a, masks[a])
    for j in range(1):
        o_attn_t[...] = attn_in.T.reshape(o_attn_t.shape)

    queries = o_q[...]
    starts = o_start[...]
    indices = o_index[...]
    o_att[...] = jnp.zeros_like(o_att)
    span = heads * rows
    low = lax.rem(s, 2)

    def attend_group(g, mass):
        scores = contract_last(k_all[g].reshape(span, width), queries)
        key = g * span + lax.broadcasted_iota(jnp.int32, scores.shape, 0)
        terms = jnp.where((key >= starts) & (key <= indices), jnp.exp(scores), 0.0)
        o_att[...] += contract_first(v_all[g].reshape(span, width), terms.astype(bf16))
        return mass + jnp.sum(terms, axis=0, keepdims=True)

    mass = lax.fori_loop(
        0,
        s // 2 + 1,
        lambda i, m: attend_group(2 * i + low, m),
        jnp.zeros((1, qcount * rows), f32),
    )
    for copy in pairs:
        copy.wait_recv()
    mass = lax.fori_loop(
        0, s // 2 + low, lambda i, m: attend_group(2 * i + 1 - low, m), mass
    )
    keep_k = pltpu.make_async_copy(k_all, o_k, local_sem.at[2])
    keep_v = pltpu.make_async_copy(v_all, o_v, local_sem.at[3])
    keep_k.start()
    keep_v.start()
    o_log[...] = jnp.log(mass)
    attended = o_att[...] / mass
    o_att[...] = attended
    load_o.wait()
    proj = jnp.zeros((rows, model), f32)
    for j in range(qcount):
        part = attended[:, j * rows : (j + 1) * rows].T.astype(bf16)
        proj = proj + jnp.dot(
            part, w_out[pl.ds(j * width, width), :], preferred_element_type=f32
        )
    o_proj[...] = proj
    keep_k.wait()
    keep_v.wait()
    links.finish()


def front(nseq, heads, qcount, scale, cid, x, ids, w_key, w_value, gain_in, gain_q, gain_k, w_query, w_out):
    f32, bf16, i32 = jnp.float32, jnp.bfloat16, jnp.int32
    rows, model = x.shape
    width = w_key.shape[1]
    stacked = qcount * rows
    some = nseq // 2
    messages = 2 * (heads - 1) + 2 * heads * (some - 1) + 2 * some
    vm = pl.BlockSpec(memory_space=VMEM)
    anywhere = pl.BlockSpec(memory_space=pl.ANY)
    everyone = (nseq, heads, rows, width)

    def kernel(*refs):
        front_kernel(nseq, heads, qcount, scale, *refs)

    shape = jax.ShapeDtypeStruct
    return pl.pallas_call(
        kernel,
        out_shape=[
            shape((rows, model), f32),
            shape((stacked, width), bf16),
            shape(everyone, bf16),
            shape(everyone, bf16),
            shape((1, stacked), i32),
            shape((1, stacked), i32),
            shape((1, stacked), f32),
            shape((width, stacked), f32),
            shape((rows, qcount * width), f32),
            shape((rows, width), f32),
            shape((rows, width // 2), f32),
            shape((rows, width // 2), f32),
            shape((nseq, model // nseq, rows), bf16),
        ],
        in_specs=[vm] * 7 + [anywhere] * 2,
        out_specs=[vm] * 2 + [anywhere] * 2 + [vm] * 9,
        scratch_shapes=[
            VMEM(w_query.shape, bf16),
            VMEM(w_out.shape, bf16),
            VMEM(everyone, bf16),
            VMEM(everyone, bf16),
            pltpu.SemaphoreType.DMA((messages,)),
            pltpu.SemaphoreType.DMA((messages,)),
            pltpu.SemaphoreType.DMA((4,)),
        ],
        name="front",
        compiler_params=pltpu.CompilerParams(
            collective_id=cid, has_side_effects=True, vmem_limit_bytes=LIMIT
        ),
    )(
        x,
        ids.reshape(nseq * heads, rows),
        w_key,
        w_value,
        gain_in,
        gain_q,
        gain_k,
        w_query,
        w_out,
    )


class Sum:
    def __init__(self, links, part, boxes, order):
        self.links, self.part, self.boxes, self.order = links, part, boxes, order
        self.used = 0
        self.slot = {}
        self.waiting = {}

    def current(self, mask):
        if mask in self.slot:
            return self.boxes.at[self.slot[mask]]
        return self.part(mask)

    def masks(self, stage):
        rest = self.order[stage + 1 :]
        weight = lambda m: sum(1 << (len(rest) - i) for i, b in enumerate(rest) if m >> b & 1)
        return sorted(subsets(rest), key=weight, reverse=True)

    def send(self, stage, mask):
        bit = self.order[stage]
        where = self.used
        self.used += 1
        copy = self.links.go(
            self.current(mask | (1 << bit)), self.boxes.at[where], self.links.across(bit)
        )
        self.waiting[stage, mask] = (copy, where)

    def start(self):
        for mask in self.masks(0):
            self.send(0, mask)

    def steps(self, stage, kept=None):
        def step(mask):
            copy, where = self.waiting.pop((stage, mask))
            mine = kept(mask) if kept is not None else self.current(mask)
            copy.wait_recv()
            self.boxes[where] = self.boxes[where] + mine[...]
            self.slot[mask] = where
            if stage + 1 < len(self.order):
                bit = 1 << self.order[stage + 1]
                if mask & bit:
                    self.send(stage + 1, mask & ~bit)

        return [functools.partial(step, mask) for mask in self.masks(stage)]

    def last(self, kept=None):
        copy, where = self.waiting.pop((len(self.order) - 1, 0))
        mine = kept(0) if kept is not None else self.current(0)
        copy.wait_recv()
        return self.boxes[where].astype(jnp.float32) + mine[...].astype(jnp.float32)


def in_turn(*lists):
    for group in itertools.zip_longest(*lists):
        for step in group:
            if step is not None:
                step()


def split_rows(rows):
    return (rows // 2 + 15) // 16 * 16


class Links:
    def __init__(self, nseq, heads, send, recv):
        self.s, self.h = place()
        self.nseq, self.heads = nseq, heads
        self.send, self.recv = send, recv
        self.count = 0
        self.started = []
        self.others = [lax.rem(self.h + d, heads) for d in range(1, heads)]

    def greet(self, more=()):
        bits = self.nseq.bit_length() - 1
        near = [self.across(b) for b in range(bits)]
        greet(near + [(self.s, o) for o in self.others] + list(more))

    def across(self, bit):
        return (related(self.s, 1 << bit), self.h)

    def go(self, src, dst, target):
        k = self.count
        self.count += 1
        copy = remote(src, dst, self.send.at[k], self.recv.at[k], target)
        copy.start()
        self.started.append(copy)
        return copy

    def over_heads(self, src, boxes):
        return [self.go(src.at[o], boxes.at[d], (self.s, o)) for d, o in enumerate(self.others)]

    def finish(self):
        for copy in self.started:
            copy.wait_send()


def back_norm(v, gain, d_out):
    scale = lax.rsqrt(jnp.mean(v * v, axis=-1, keepdims=True) + EPS)
    unit = v * scale
    inner = d_out * gain
    d_v = scale * (inner - unit * jnp.mean(inner * unit, axis=-1, keepdims=True))
    return d_v, jnp.sum(d_out * unit, axis=0, keepdims=True)


def back_rotate(d, cosines, sines):
    half = d.shape[-1] // 2
    first, second = d[:, :half], d[:, half:]
    return jnp.concatenate(
        [first * cosines + second * sines, second * cosines - first * sines], axis=-1
    )


def tail_kernel(
    nseq,
    heads,
    qcount,
    scale,
    q_ref,
    start_ref,
    index_ref,
    log_ref,
    att_ref,
    d_proj_ref,
    w_out_ref,
    q_lin_ref,
    k_lin_ref,
    cos_ref,
    sin_ref,
    gain_q_ref,
    gain_k_ref,
    gain_in_ref,
    attn_t_ref,
    x_ref,
    d_hid_ref,
    gains_ref,
    k_far,
    v_far,
    w_query_far,
    w_key_far,
    w_value_far,
    d_gate_ref,
    d_up_ref,
    d_down_first,
    d_down_second,
    o_tokens,
    o_qkv,
    o_out,
    o_gate,
    o_up,
    o_down,
    o_gains,
    k_ref,
    v_ref,
    w_qkv_ref,
    dk,
    dv,
    dq_t,
    grads,
    grads_t,
    box_k,
    box_v,
    zbox_k,
    zbox_v,
    dw_out,
    box_out,
    zbox_out,
    mid_out,
    end_out,
    dw_qkv,
    box_qkv,
    zsrc_qkv,
    zbox_qkv,
    d_qkv,
    keep_gate_first,
    keep_gate_second,
    keep_up_first,
    keep_up_second,
    keep_down_first,
    keep_down_second,
    box_gate_first,
    box_gate_second,
    box_up_first,
    box_up_second,
    box_down_first,
    box_down_second,
    gsum,
    gbox,
    gzbox,
    send,
    recv,
    local_sem,
):
    f32, bf16 = jnp.float32, jnp.bfloat16
    bits = nseq.bit_length() - 1
    ups, downs = seq_orders(bits)
    links = Links(nseq, heads, send, recv)
    s, h = links.s, links.h
    rows, model = d_proj_ref.shape
    width = k_lin_ref.shape[1]
    gain_q, gain_k = flat(gain_q_ref), flat(gain_k_ref)
    groups, span = k_ref.shape[:2]
    loads = []

    def load(src, dst):
        copy = pltpu.make_async_copy(src, dst, local_sem.at[len(loads)])
        copy.start()
        loads.append(copy)
        return copy

    load_k = load(k_far, k_ref)
    load_v = load(v_far, v_ref)
    plane = subsets(ups)[1:]
    links.greet([(related(s, m), links.h) for m in plane if m & (m - 1)])

    held = subsets(ups)
    ffn = []
    split = keep_gate_first.shape[1]
    for src, keep, box, order, low, past in (
        (d_gate_ref, keep_gate_first, box_gate_first, ups, 0, 1),
        (d_gate_ref, keep_gate_second, box_gate_second, downs, split, 1),
        (d_up_ref, keep_up_first, box_up_first, [0] + ups, 0, 0),
        (d_up_ref, keep_up_second, box_up_second, [0] + downs, split, 0),
        (d_down_first, keep_down_first, box_down_first, ups[1:], 0, 2),
        (d_down_second, keep_down_second, box_down_second, downs[1:], 0, 2),
    ):
        here = pl.ds(low, keep.shape[1])

        def part(m, src=src, here=here, past=past, order=order):
            if past == 0:
                return src.at[related(s, m), here]
            if past == 1:
                return src.at[held.index(m), here]
            return src.at[0 if m else 1, here]

        total = Sum(links, part, box, order)
        kept = subsets(order[1:])
        total.loads = [load(part(m), keep.at[i]) for i, m in enumerate(kept)]
        total.kept = lambda m, keep=keep, kept=kept: keep.at[kept.index(m)]
        ffn.append(total)
    gate, up, down = ffn[0:2], ffn[2:4], ffn[4:6]
    for total in up + gate + down:
        total.start()

    def settle(pair, stage, first=False):
        if first:
            for total in pair:
                for copy in total.loads:
                    copy.wait()
        in_turn(*[total.steps(stage, total.kept if first else None) for total in pair])

    def put(pair, out, first=False):
        at = 0
        for total in pair:
            value = total.last(total.kept if first else None)
            out[pl.ds(at, value.shape[0]), :] = value
            at += value.shape[0]

    load_w = []
    at = 0
    for far in (w_query_far, w_key_far, w_value_far):
        load_w.append(load(far, w_qkv_ref.at[:, pl.ds(at, far.shape[1])]))
        at += far.shape[1]

    d_proj = d_proj_ref[...]

    out_rows = dw_out.shape[1] * dw_out.shape[2]
    for j in range(nseq):
        head, low = divmod(j * out_rows, width)
        mixed_t = att_ref[low : low + out_rows, pl.ds(head * rows, rows)].astype(bf16)
        dw_out[j] = (
            jnp.dot(mixed_t, d_proj, preferred_element_type=f32)
            .astype(bf16)
            .reshape(dw_out.shape[1:])
        )

    sum_out = Sum(links, lambda m: dw_out.at[related(s, m)], box_out, [0])
    sum_out.masks = lambda stage: held
    sum_out.start()

    for j in range(qcount):
        part = w_out_ref[pl.ds(j * width, width), :]
        grads[pl.ds(j * rows, rows), :] = contract_last(d_proj, part).astype(bf16)
        grads_t[:, pl.ds(j * rows, rows)] = contract_last(part, d_proj).astype(bf16)
    in_turn(sum_out.steps(0))
    z_out = [
        links.go(box_out.at[:, o], zbox_out.at[d], (s, o)) for d, o in enumerate(links.others)
    ]
    dots = jnp.sum(grads_t[...].astype(f32) * att_ref[...], axis=0, keepdims=True)
    start = start_ref[...]
    index = index_ref[...]
    log_total = log_ref[...]
    dq_t[...] = jnp.zeros_like(dq_t)
    load_k.wait()
    load_v.wait()

    def step(g, carry):
        keys = k_ref[g]
        queries = q_ref[...]
        scores = contract_last(keys, queries)
        key = g * span + lax.broadcasted_iota(jnp.int32, scores.shape, 0)
        probs = jnp.where((key >= start) & (key <= index), jnp.exp(scores - log_total), 0.0)
        d_probs = jnp.dot(v_ref[g], grads_t[...], preferred_element_type=f32)
        d_scores = (probs * (d_probs - dots)).astype(bf16)
        dv[g] = (
            jnp.dot(probs.astype(bf16), grads[...], preferred_element_type=f32)
            .astype(bf16)
            .reshape(dv.shape[1:])
        )
        dk[g] = (
            jnp.dot(d_scores, queries, preferred_element_type=f32)
            .astype(bf16)
            .reshape(dk.shape[1:])
        )
        dq_t[...] += contract_first(keys, d_scores)
        return carry

    lax.fori_loop(0, s + 1, step, 0)

    def blank(g, carry):
        dk[g] = jnp.zeros(dk.shape[1:], bf16)
        dv[g] = jnp.zeros(dv.shape[1:], bf16)
        return carry

    lax.fori_loop(s + 1, groups, blank, 0)

    kv = []
    for j in list(range(1, heads)) + [0]:
        owner = lax.rem(h + j, heads)
        for far, box, order in ((dk, box_k, ups), (dv, box_v, downs)):
            kv.append(
                Sum(
                    links,
                    lambda m, far=far, owner=owner: far.at[related(s, m), owner],
                    box.at[j],
                    [0] + order,
                )
            )
    for mask_index in range(len(held)):
        for total in kv:
            total.send(0, total.masks(0)[mask_index])

    in_turn(*[total.steps(0) for total in kv])

    cosines, sines = cos_ref[...], sin_ref[...]
    d_gain_q = jnp.zeros((1, width), f32)
    for j in range(qcount):
        d_rot = dq_t[:, pl.ds(j * rows, rows)].T * scale
        d_lin, terms = back_norm(
            q_lin_ref[:, pl.ds(j * width, width)],
            gain_q,
            back_rotate(d_rot, cosines, sines),
        )
        d_qkv[:, pl.ds(j * width, width)] = d_lin.astype(bf16)
        d_gain_q = d_gain_q + terms

    for stage in range(1, bits - 1):
        in_turn(*[total.steps(stage) for total in kv])
    settle(gate, 0, True)

    arriving = {}
    for i, total in enumerate(kv):
        for m in total.steps(bits - 1):
            m()
        j = (i // 2 + 1) % heads
        if j:
            zbox = (zbox_k, zbox_v)[i % 2]
            arriving[i % 2, j] = links.go(
                total.current(0), zbox.at[j - 1], (s, links.others[j - 1])
            )
    for d, copy in enumerate(z_out):
        copy.wait_recv()
    own = box_out[:, h].astype(f32)
    for d in range(heads - 1):
        own = own + zbox_out[d].astype(f32)
    mid_out[...] = own.astype(bf16)
    sum_end = Sum(links, lambda m: mid_out.at[held.index(m)], end_out, downs)
    sum_end.start()


    settle(up, 0, True)

    def whole(i, zbox):
        total = kv[len(kv) - 2 + i].current(0)[...].astype(f32)
        for j in range(1, heads):
            arriving[i, j].wait_recv()
            total = total + zbox[j - 1].astype(f32)
        return total

    d_keys = whole(0, zbox_k)
    d_lin, d_gain_k = back_norm(
        k_lin_ref[...], gain_k, back_rotate(d_keys, cosines, sines)
    )
    qw = qcount * width
    d_qkv[:, pl.ds(qw, width)] = d_lin.astype(bf16)
    d_values = whole(1, zbox_v)
    d_qkv[:, pl.ds(qw + width, width)] = d_values.astype(bf16)

    pieces, _, block_rows, cut = dw_qkv.shape
    qkv = []
    for j in range(pieces):
        cols = pl.ds(j * cut, cut)

        def qkv_block(g, carry, j=j, cols=cols):
            dw_qkv[j, g] = jnp.dot(
                attn_t_ref[g], d_qkv[:, cols], preferred_element_type=f32
            ).astype(bf16)
            return carry

        lax.fori_loop(0, nseq, qkv_block, 0)
        total = Sum(
            links,
            lambda m, j=j: dw_qkv.at[j, related(s, m)],
            box_qkv.at[j],
            [0] + (downs if j % 2 else ups),
        )
        total.start()
        qkv.append(total)

    for copy in load_w:
        copy.wait()
    d_attn_in = contract_last(d_qkv[...], w_qkv_ref[...])
    in_turn(*[total.steps(0) for total in qkv])
    d_x, d_gain_in = back_norm(x_ref[...].astype(f32), flat(gain_in_ref), d_attn_in)
    o_tokens[...] = (d_hid_ref[...] + d_x).astype(o_tokens.dtype)

    gsum[0] = gains_ref[...]
    gsum[0, 0:1, :] = d_gain_in
    gsum[0, 4:5, :width] = d_gain_q
    gsum[0, 5:6, :width] = d_gain_k
    gain_copy = links.go(gsum.at[0], gbox.at[0], links.across(0))
    for stage in range(1, bits - 1):
        in_turn(*[total.steps(stage) for total in qkv])
    settle(up, 1)
    each = block_rows // heads
    z_qkv = []

    gain_copy.wait_recv()
    gsum[1] = gsum[0] + gbox[0]
    gain_plane = [
        links.go(gsum.at[1], gbox.at[1 + i], (related(s, m), h)) for i, m in enumerate(plane)
    ]
    for j, total in enumerate(qkv):
        if j == 2:
            total_gains = gsum[1]
            for i, copy in enumerate(gain_plane):
                copy.wait_recv()
                total_gains = total_gains + gbox[1 + i]
            gsum[2] = total_gains
            gain_z = [
                links.go(gsum.at[2], gzbox.at[d], (s, o)) for d, o in enumerate(links.others)
            ]
        value = total.last()
        for p in range(heads):
            zsrc_qkv[j, p] = value[p * each : (p + 1) * each].astype(bf16)
        z_qkv.append(links.over_heads(zsrc_qkv.at[j], zbox_qkv.at[j]))
    for total in down:
        for copy in total.loads:
            copy.wait()
    put(down, o_down, True)
    put(gate, o_gate)
    put(up, o_up)
    in_turn(sum_end.steps(0))
    o_out[...] = sum_end.last()
    total = gsum[2]
    for d, copy in enumerate(gain_z):
        copy.wait_recv()
        total = total + gzbox[d]
    o_gains[...] = total
    for j, copies in enumerate(z_qkv):
        total = zsrc_qkv[j, h].astype(f32)
        for d, copy in enumerate(copies):
            copy.wait_recv()
            total = total + zbox_qkv[j, d].astype(f32)
        o_qkv[:, pl.ds(j * cut, cut)] = total
    links.finish()


def tail(nseq, heads, qcount, scale, cid, *arrays):
    (q, _, _, _, att, d_proj, w_out, q_lin, k_lin, _, _, _, _, _) = arrays[:14]
    (attn_t, x, d_hid, gains, k, v, w_query, w_key, w_value, d_gate, _, _, _) = arrays[14:]
    f32, bf16 = jnp.float32, jnp.bfloat16
    rows, model = d_proj.shape
    width = k_lin.shape[1]
    cols = w_query.shape[1] + w_key.shape[1] + w_value.shape[1]
    pieces = 4
    cut = cols // pieces
    out_rows, qkv_rows = w_out.shape[0] // nseq, attn_t.shape[1]
    ffn_block = d_gate.shape[1:]
    some, all_but = nseq // 2, nseq - 1
    out_block = (heads, out_rows // heads, model)
    split = split_rows(ffn_block[0])
    low, high = (split, ffn_block[1]), (ffn_block[0] - split, ffn_block[1])
    parts = [(part, *n) for n in ((2, 3), (4, 7), (1, 1)) for part in (low, high)]
    copies = (
        sum(n for _, _, n in parts)
        + some
        + (heads - 1)
        + (some - 1)
        + 2 * heads * all_but
        + 2 * (heads - 1)
        + pieces * (all_but + heads - 1)
        + some
        + (heads - 1)
    )
    vm = pl.BlockSpec(memory_space=VMEM)
    anywhere = pl.BlockSpec(memory_space=pl.ANY)

    def kernel(*refs):
        tail_kernel(nseq, heads, qcount, scale, *refs)

    return pl.pallas_call(
        kernel,
        out_shape=[
            jax.ShapeDtypeStruct((rows, model), bf16),
            jax.ShapeDtypeStruct((qkv_rows // heads, cols), f32),
            jax.ShapeDtypeStruct(out_block[1:], f32),
            jax.ShapeDtypeStruct(ffn_block, f32),
            jax.ShapeDtypeStruct(ffn_block, f32),
            jax.ShapeDtypeStruct(ffn_block, f32),
            jax.ShapeDtypeStruct(gains.shape, f32),
        ],
        in_specs=[vm] * (len(arrays) - 9) + [anywhere] * 9,
        out_specs=[vm] * 7,
        scratch_shapes=[
            VMEM(k.shape, bf16),
            VMEM(v.shape, bf16),
            VMEM((model, cols), bf16),
            VMEM((nseq, heads, rows, width), bf16),
            VMEM((nseq, heads, rows, width), bf16),
            VMEM((width, qcount * rows), f32),
            VMEM((qcount * rows, width), bf16),
            VMEM((width, qcount * rows), bf16),
            VMEM((heads, all_but, rows, width), bf16),
            VMEM((heads, all_but, rows, width), bf16),
            VMEM((heads - 1, rows, width), bf16),
            VMEM((heads - 1, rows, width), bf16),
            VMEM((nseq,) + out_block, bf16),
            VMEM((some,) + out_block, bf16),
            VMEM((heads - 1, some) + out_block[1:], bf16),
            VMEM((some,) + out_block[1:], bf16),
            VMEM((some - 1,) + out_block[1:], bf16),
            VMEM((pieces, nseq, qkv_rows, cut), bf16),
            VMEM((pieces, all_but, qkv_rows, cut), bf16),
            VMEM((pieces, heads, qkv_rows // heads, cut), bf16),
            VMEM((pieces, heads - 1, qkv_rows // heads, cut), bf16),
            VMEM((rows, cols), bf16),
        ]
        + [VMEM((n,) + part, bf16) for part, n, _ in parts]
        + [VMEM((n,) + part, bf16) for part, _, n in parts]
        + [
            VMEM((3,) + gains.shape, f32),
            VMEM((some,) + gains.shape, f32),
            VMEM((heads - 1,) + gains.shape, f32),
            pltpu.SemaphoreType.DMA((copies,)),
            pltpu.SemaphoreType.DMA((copies,)),
            pltpu.SemaphoreType.DMA((5 + sum(n for _, n, _ in parts),)),
        ],
        name="tail",
        compiler_params=pltpu.CompilerParams(
            collective_id=cid, has_side_effects=True, vmem_limit_bytes=62 * 2**20
        ),
    )(*arrays)


CHUNKS, SPANS = 4, 2
ORDER = (
    ("ags", 0, 0, 0), ("ags", 0, 1, 0), ("ags", 0, 3, 0), ("agw", 0, 0, 0), ("ags", 0, 0, 1),
    ("agw", 0, 1, 0), ("ags", 0, 1, 1), ("agw", 0, 0, 1), ("ags", 0, 0, 2), ("agw", 0, 3, 0),
    ("agw", 0, 1, 1), ("ags", 0, 1, 2), ("ags", 0, 2, 0), ("agw", 0, 0, 2), ("agw", 0, 1, 2),
    ("fa", 0), ("fb", 0), ("ags", 0, 3, 1), ("agw", 0, 2, 0), ("ags", 0, 2, 1), ("fc", 0),
    ("rss", 0, 0, 0), ("agw", 0, 3, 1), ("ags", 0, 3, 2), ("agw", 0, 2, 1), ("rss", 0, 1, 0),
    ("ags", 0, 2, 2), ("rsw", 0, 0, 0), ("rss", 0, 0, 1), ("agw", 0, 2, 2), ("agw", 0, 3, 2),
    ("rsw", 0, 1, 0), ("rss", 0, 1, 1), ("fa", 1), ("rsw", 0, 0, 1), ("rss", 0, 0, 2), ("fb", 1),
    ("rsw", 0, 1, 1), ("rss", 0, 1, 2), ("fc", 1), ("rss", 0, 3, 0), ("rsw", 0, 0, 2),
    ("rss", 0, 2, 0), ("n", 0), ("ags", 1, 0, 0), ("rsw", 0, 3, 0), ("rss", 0, 3, 1),
    ("rsw", 0, 2, 0), ("rss", 0, 2, 1), ("rsw", 0, 1, 2), ("n", 1), ("ags", 1, 1, 0),
    ("agw", 1, 0, 0), ("ags", 1, 0, 1), ("rsw", 0, 3, 1), ("rss", 0, 3, 2), ("rsw", 0, 2, 1),
    ("rss", 0, 2, 2), ("agw", 1, 1, 0), ("ags", 1, 1, 1), ("agw", 1, 0, 1), ("ags", 1, 0, 2),
    ("rsw", 0, 3, 2), ("rsw", 0, 2, 2), ("n", 2), ("ags", 1, 2, 0), ("agw", 1, 1, 1), ("n", 3),
    ("ags", 1, 1, 2), ("ags", 1, 3, 0), ("agw", 1, 0, 2), ("agw", 1, 1, 2), ("ga", 0),
    ("agw", 1, 2, 0), ("ags", 1, 2, 1), ("gb", 0), ("agw", 1, 3, 0), ("ags", 1, 3, 1), ("gc", 0),
    ("agw", 1, 2, 1), ("rss", 1, 0, 0), ("ags", 1, 2, 2), ("agw", 1, 2, 2), ("agw", 1, 3, 1),
    ("rss", 1, 1, 0), ("ags", 1, 3, 2), ("rsw", 1, 0, 0), ("rss", 1, 0, 1), ("agw", 1, 3, 2),
    ("wd", 0), ("wd", 1), ("dd", 0), ("rsw", 1, 1, 0), ("ga", 1), ("gb", 1), ("rss", 1, 1, 1),
    ("gc", 1), ("rss", 1, 2, 0), ("Dd", 0), ("rsw", 1, 0, 1), ("rsw", 1, 1, 1), ("rss", 1, 3, 0),
    ("rss", 1, 1, 2), ("wg", 0), ("rsw", 1, 2, 0), ("rss", 1, 2, 1), ("wg", 1), ("rsw", 1, 3, 0),
    ("rss", 1, 3, 1), ("wu", 0), ("rss", 1, 0, 2), ("dg", 0), ("wu", 1), ("rsw", 1, 2, 1),
    ("rss", 1, 2, 2), ("rsw", 1, 3, 1), ("rsw", 1, 1, 2), ("rss", 1, 3, 2), ("Dg", 0),
    ("rsw", 1, 0, 2), ("rsw", 1, 2, 2), ("e", 0), ("e", 2), ("e", 1), ("rsw", 1, 3, 2), ("e", 3),
    ("D2", 0),
)


def ffn_kernel(
    nseq,
    heads,
    chunks,
    spans,
    proj_ref,
    x_ref,
    cot_ref,
    gain_two_ref,
    gain_three_ref,
    gain_four_ref,
    w_gate_ref,
    w_up_ref,
    w_down_ref,
    o_out,
    o_hid,
    o_proj,
    o_gains,
    o_first,
    o_second,
    o_gate,
    o_up,
    hidden,
    w_gate,
    w_up,
    w_down,
    u_all,
    d_all,
    by_gate,
    by_up,
    act,
    d_gate,
    d_up,
    parts,
    from_left,
    from_right,
    flipped,
    dw_gate,
    dw_up,
    dw_down,
    box_gate,
    box_down,
    box_first,
    box_second,
    sum_send,
    sum_recv,
    ag_send,
    ag_recv,
    rs_send,
    rs_recv,
    local_sem,
):
    f32, bf16 = jnp.float32, jnp.bfloat16
    s, h = place()
    last = heads - 1
    right = (s, lax.rem(h + 1, heads))
    left = (s, lax.rem(h + last, heads))
    rows, model = x_ref.shape
    units = w_gate.shape[0]
    rc = rows // chunks
    each = chunks // spans
    many = rc * heads * each
    tile = 256
    whole_tiles, rest = units // tile, units % tile

    loads = []
    for n, (src, dst) in enumerate(
        ((w_gate_ref, w_gate), (w_up_ref, w_up), (w_down_ref, w_down))
    ):
        copy = pltpu.make_async_copy(src, dst, local_sem.at[n])
        copy.start()
        loads.append(copy)
    bits = nseq.bit_length() - 1
    ups, downs = seq_orders(bits)
    links = Links(nseq, heads, sum_send, sum_recv)
    greet([right, left] + [links.across(b) for b in range(bits)])

    proj = proj_ref[...]
    hid = x_ref[...].astype(f32) + norm_rows(proj, flat(gain_two_ref))
    hidden[...] = hid
    u_local = norm_rows(hid, flat(gain_three_ref)).astype(bf16)
    for c in range(chunks):
        u_all[c, h] = u_local[c * rc : (c + 1) * rc]
    o_gains[...] = jnp.zeros_like(o_gains)

    def lanes(k, c, t):
        buf = d_all if k else u_all
        return (
            (
                (h - t >= 0) & (h < last),
                buf.at[c, jnp.maximum(h - t, 0)],
                0,
                right,
                h - 1 - t >= 0,
                buf.at[c, jnp.maximum(h - 1 - t, 0)],
            ),
            (
                (h + t <= last) & (h > 0),
                buf.at[c, jnp.minimum(h + t, last)],
                1,
                left,
                h + 1 + t <= last,
                buf.at[c, jnp.minimum(h + 1 + t, last)],
            ),
        )

    def ags(k, c, t):
        for on, block, lane, target, _, _ in lanes(k, c, t):
            i = (k, c, lane, t)
            pl.when(on)(remote(block, block, ag_send.at[i], ag_recv.at[i], target).start)

    def agw(k, c, t):
        for _, _, lane, target, on, block in lanes(k, c, t):
            i = (k, c, lane, t)
            pl.when(on)(remote(block, block, ag_send.at[i], ag_recv.at[i], target).wait_recv)

    def rss(k, c, t):
        for on, dest, box, lane, target, at_end in (
            ((t >= h) & (h < last), last - (t - h), from_left, 0, right, h == 0),
            ((t >= last - h) & (h > 0), t - (last - h), from_right, 1, left, h == last),
        ):
            dest = jnp.clip(dest, 0, last)
            i = (k, c, lane, t)
            if t > 0:

                def forward(box=box, dest=dest, i=i, target=target):
                    box[k, c, t - 1] = box[k, c, t - 1] + parts[k, c, dest]
                    remote(
                        box.at[k, c, t - 1], box.at[k, c, t], rs_send.at[i], rs_recv.at[i], target
                    ).start()

                pl.when(on & jnp.logical_not(at_end))(forward)
            pl.when(on & at_end)(
                remote(
                    parts.at[k, c, dest], box.at[k, c, t], rs_send.at[i], rs_recv.at[i], target
                ).start
            )

    def rsw(k, c, t):
        for on, box, lane, target in (
            ((t >= h - 1) & (h > 0), from_left, 0, right),
            ((t >= last - h - 1) & (h < last), from_right, 1, left),
        ):
            i = (k, c, lane, t)
            block = box.at[k, c, t]
            pl.when(on)(remote(block, block, rs_send.at[i], rs_recv.at[i], target).wait_recv)

    def summed(k, c):
        zero = jnp.zeros((rc, model), f32)
        return (
            parts[k, c, h].astype(f32)
            + jnp.where(h > 0, from_left[k, c, last - 1].astype(f32), zero)
            + jnp.where(h < last, from_right[k, c, last - 1].astype(f32), zero)
        )

    def over_tiles(lo, hi, body):
        def step(i, carry):
            body(pl.ds(pl.multiple_of(i * tile, tile), tile))
            return carry

        lax.fori_loop(lo, hi, step, 0)
        if hi == whole_tiles and rest:
            body(pl.ds(whole_tiles * tile, rest))

    arrived = set()

    def need(n):
        if n not in arrived:
            arrived.add(n)
            loads[n].wait()

    def span_rows(buf, p):
        return buf[pl.ds(p * each, each)].reshape(many, model)

    def place_parts(k, p, cols, value):
        parts[k, pl.ds(p * each, each), :, :, cols] = value.astype(bf16).reshape(
            each, heads, rc, value.shape[1]
        )

    def forward_tiles(c, lo, hi):
        need(0)
        need(1)

        def body(cols):
            u = span_rows(u_all, c)
            gate = contract_last(u, w_gate[cols, :])
            up = contract_last(u, w_up[cols, :])
            root = math.sqrt(2.0 / math.pi)
            square = gate * gate
            curve = jnp.tanh(root * gate * (1.0 + 0.044715 * square))
            half = 0.5 * (1.0 + curve)
            gelu = gate * half
            slope = half + 0.5 * gate * (1.0 - curve * curve) * (
                root * (1.0 + 3 * 0.044715 * square)
            )
            by_gate[pl.ds(c * many, many), cols] = slope * up
            by_up[pl.ds(c * many, many), cols] = gelu
            act[pl.ds(c * many, many), cols] = (gelu * up).astype(bf16)

        over_tiles(lo, hi, body)

    out_tile = model // 3

    def down_rows(c):
        need(2)

        def body(i, carry):
            cols = pl.ds(pl.multiple_of(i * out_tile, out_tile), out_tile)
            part = jnp.dot(
                act[pl.ds(c * many, many), :], w_down[:, cols], preferred_element_type=f32
            )
            place_parts(0, c, cols, part)
            return carry

        lax.fori_loop(0, 3, body, 0)

    def turn(c):
        here = pl.ds(c * rc, rc)
        ffn_out = summed(0, c)
        upstream = cot_ref[here, :].astype(f32)
        o_out[here, :] = (hidden[here, :] + norm_rows(ffn_out, flat(gain_four_ref))).astype(
            o_out.dtype
        )
        d_out, terms = back_norm(ffn_out, flat(gain_four_ref), upstream)
        d_all[c, h] = d_out.astype(bf16)
        o_gains[3:4, :] += terms

    def back_tiles(c, lo, hi):
        def body(cols):
            d_act = contract_last(span_rows(d_all, c), w_down[cols, :])
            d_gate[pl.ds(c * many, many), cols] = (
                d_act * by_gate[pl.ds(c * many, many), cols]
            ).astype(bf16)
            d_up[pl.ds(c * many, many), cols] = (
                d_act * by_up[pl.ds(c * many, many), cols]
            ).astype(bf16)

        over_tiles(lo, hi, body)

    def back_rows(c):
        def body(i, carry):
            cols = pl.ds(pl.multiple_of(i * out_tile, out_tile), out_tile)
            part = jnp.dot(
                d_gate[pl.ds(c * many, many), :], w_gate[:, cols], preferred_element_type=f32
            )
            part = part + jnp.dot(
                d_up[pl.ds(c * many, many), :], w_up[:, cols], preferred_element_type=f32
            )
            place_parts(1, c, cols, part)
            return carry

        lax.fori_loop(0, 3, body, 0)

    def finish_rows(c):
        here = pl.ds(c * rc, rc)
        d_in, terms = back_norm(hidden[here, :], flat(gain_three_ref), summed(1, c))
        o_gains[2:3, :] += terms
        d_hid = cot_ref[here, :].astype(f32) + d_in
        o_hid[here, :] = d_hid
        d_proj, terms = back_norm(proj_ref[here, :], flat(gain_two_ref), d_hid)
        o_proj[here, :] = d_proj.astype(o_proj.dtype)
        o_gains[1:2, :] += terms

    stores = []

    def flip(source):
        for p in range(spans):
            flipped[:, pl.ds(p * many, many)] = span_rows(source, p).T

    def weight_grad(right_ref, dst, half):
        def body(cols):
            value = jnp.dot(flipped[...], right_ref[:, cols], preferred_element_type=f32)
            dst[:, :, cols] = value.astype(bf16).reshape(dst.shape[:2] + (value.shape[1],))

        over_tiles(half_tiles if half else 0, whole_tiles if half else half_tiles, body)

    half_tiles = (whole_tiles + 1) // 2
    held = subsets(ups)
    sum_gate = Sum(links, lambda m: dw_gate.at[related(s, m)], box_gate, [0])
    sum_down = Sum(links, lambda m: dw_down.at[related(s, m)], box_down, [0])
    for total in (sum_gate, sum_down):
        total.masks = lambda stage: held
    def store(src, dst):
        copy = pltpu.make_async_copy(src, dst, local_sem.at[3 + len(stores)])
        copy.start()
        stores.append(copy)

    split = box_first.shape[1]
    pieces = []
    for box, order, low in ((box_first, ups, 0), (box_second, downs, split)):
        here = pl.ds(low, box.shape[1])
        pieces.append(
            Sum(links, lambda m, here=here: box_down.at[held.index(m), here], box, order)
        )

    for event in ORDER:
        kind, args = event[0], event[1:]
        if kind == "ags":
            ags(*args)
        elif kind == "agw":
            agw(*args)
        elif kind == "rss":
            rss(*args)
        elif kind == "rsw":
            rsw(*args)
        elif kind == "fa":
            forward_tiles(args[0], 0, half_tiles)
        elif kind == "fb":
            forward_tiles(args[0], half_tiles, whole_tiles)
        elif kind == "fc":
            down_rows(args[0])
        elif kind == "n":
            turn(args[0])
        elif kind == "ga":
            back_tiles(args[0], 0, half_tiles)
        elif kind == "gb":
            back_tiles(args[0], half_tiles, whole_tiles)
        elif kind == "gc":
            back_rows(args[0])
        elif kind == "e":
            finish_rows(args[0])
        elif kind == "wd":
            if args[0] == 0:
                flip(d_all)
            weight_grad(act, dw_down, args[0])
        elif kind == "wg":
            if args[0] == 0:
                flip(u_all)
            weight_grad(d_gate, dw_gate, args[0])
        elif kind == "wu":
            weight_grad(d_up, dw_up, args[0])
            if args[0] == 1:
                store(dw_up, o_up)
        elif kind == "dd":
            sum_down.start()
        elif kind == "dg":
            sum_gate.start()
        elif kind == "Dg":
            in_turn(sum_gate.steps(0))
            store(box_gate, o_gate)
        elif kind == "Dd":
            in_turn(sum_down.steps(0))
            for total in pieces:
                for m in total.masks(0):
                    total.send(0, m)
        else:
            for total, out in zip(pieces, (o_first, o_second)):
                for m in total.masks(0):
                    copy, where = total.waiting.pop((0, m))
                    copy.wait_recv()
                    total.boxes[where] = total.boxes[where] + total.current(m)[...]
                store(total.boxes, out)

    for event in ORDER:
        if event[0] == "ags":
            k, c, t = event[1:]
            for on, block, lane, target, _, _ in lanes(k, c, t):
                i = (k, c, lane, t)
                pl.when(on)(remote(block, block, ag_send.at[i], ag_recv.at[i], target).wait_send)
        elif event[0] == "rss":
            k, c, t = event[1:]
            for on, box, lane, target in (
                ((t >= h) & (h < last), from_left, 0, right),
                ((t >= last - h) & (h > 0), from_right, 1, left),
            ):
                i = (k, c, lane, t)
                block = box.at[k, c, t]
                pl.when(on)(remote(block, block, rs_send.at[i], rs_recv.at[i], target).wait_send)
    for n in range(3):
        need(n)
    for copy in stores:
        copy.wait()
    links.finish()


def feed_forward(nseq, heads, cid, *arrays):
    _, x, _, _, _, _, w_gate, w_up, w_down = arrays
    f32, bf16 = jnp.float32, jnp.bfloat16
    rows, model = x.shape
    units = w_gate.shape[0]
    chunks = CHUNKS
    rc = rows // chunks
    group = rows * heads
    vm = pl.BlockSpec(memory_space=VMEM)
    anywhere = pl.BlockSpec(memory_space=pl.ANY)
    block = (model // nseq, units)
    some = nseq // 2
    half = jax.ShapeDtypeStruct((some,) + block, bf16)
    split = split_rows(block[0])
    parts = [(split, units), (block[0] - split, units)]
    messages = 3 * some
    hops = (2, chunks, 2, heads - 1)
    return pl.pallas_call(
        functools.partial(ffn_kernel, nseq, heads, CHUNKS, SPANS),
        out_shape=[
            jax.ShapeDtypeStruct((rows, model), bf16),
            jax.ShapeDtypeStruct((rows, model), f32),
            jax.ShapeDtypeStruct((rows, model), bf16),
            jax.ShapeDtypeStruct((8, model), f32),
            *[jax.ShapeDtypeStruct((some // 2,) + part, bf16) for part in parts],
            half,
            jax.ShapeDtypeStruct((nseq,) + block, bf16),
        ],
        in_specs=[vm] * 6 + [anywhere] * 3,
        out_specs=[vm] * 4 + [anywhere] * 4,
        scratch_shapes=[
            VMEM((rows, model), f32),
            VMEM(w_gate.shape, bf16),
            VMEM(w_up.shape, bf16),
            VMEM(w_down.shape, bf16),
            VMEM((chunks, heads, rc, model), bf16),
            VMEM((chunks, heads, rc, model), bf16),
            VMEM((group, units), f32),
            VMEM((group, units), f32),
            VMEM((group, units), bf16),
            VMEM((group, units), bf16),
            VMEM((group, units), bf16),
            VMEM((2, chunks, heads, rc, model), bf16),
            VMEM((2, chunks, heads - 1, rc, model), bf16),
            VMEM((2, chunks, heads - 1, rc, model), bf16),
            VMEM((model, group), bf16),
            VMEM((nseq,) + block, bf16),
            VMEM((nseq,) + block, bf16),
            VMEM((nseq,) + block, bf16),
            VMEM((some,) + block, bf16),
            VMEM((some,) + block, bf16),
            *[VMEM((some // 2,) + part, bf16) for part in parts],
            pltpu.SemaphoreType.DMA((messages,)),
            pltpu.SemaphoreType.DMA((messages,)),
            pltpu.SemaphoreType.DMA(hops),
            pltpu.SemaphoreType.DMA(hops),
            pltpu.SemaphoreType.DMA(hops),
            pltpu.SemaphoreType.DMA(hops),
            pltpu.SemaphoreType.DMA((7,)),
        ],
        name="feed_forward",
        compiler_params=pltpu.CompilerParams(
            collective_id=cid, has_side_effects=True, vmem_limit_bytes=62 * 2**20
        ),
    )(*arrays)


def finish_kernel(nseq, qw, width, each, few, *refs):
    out, tokens, qkv, w_out, gate, up, down, gains = refs[:8]
    o_out, o_tokens, o_query, o_key, o_value, o_w_out, o_gate, o_up, o_down = refs[8:17]
    o_gains = refs[17:]
    s, h = place()
    which = s * lax.axis_size("head") + h
    o_out[...] = out[...]
    o_tokens[...] = tokens[...]
    o_query[...] = qkv[:, :qw]
    o_key[...] = qkv[:, qw : qw + width]
    o_value[...] = qkv[:, qw + width :]
    o_w_out[...] = w_out[...]
    o_gate[...] = gate[...]
    o_up[...] = up[...]
    o_down[...] = down[...]
    model = gains.shape[1]
    wide = pltpu.roll(gains[...], lax.rem(model - which * each, model), 1)
    narrow = pltpu.roll(gains[...], lax.rem(model - which * few, model), 1)
    for i in range(4):
        o_gains[i][...] = wide[i : i + 1, :each]
    for i in range(4, 6):
        o_gains[i][...] = narrow[i : i + 1, :few]


def finish(nseq, qw, width, each, few, *arrays):
    out, tokens, qkv, w_out, gate, up, down, gains = arrays
    vm = pl.BlockSpec(memory_space=VMEM)
    shape = lambda a: jax.ShapeDtypeStruct(a.shape, a.dtype)
    f32 = jnp.float32
    rows = qkv.shape[0]
    wide, narrow = jax.ShapeDtypeStruct((1, each), f32), jax.ShapeDtypeStruct((1, few), f32)
    return pl.pallas_call(
        functools.partial(finish_kernel, nseq, qw, width, each, few),
        out_shape=[shape(out), shape(tokens)]
        + [jax.ShapeDtypeStruct((rows, n), f32) for n in (qw, width, width)]
        + [shape(w_out), shape(gate), shape(up), shape(down)]
        + [wide] * 4
        + [narrow] * 2,
        in_specs=[vm] * 8,
        out_specs=[vm] * 15,
        name="finish",
        compiler_params=pltpu.CompilerParams(vmem_limit_bytes=LIMIT),
    )(*arrays)


def local(
    tokens,
    segment_ids,
    w_query,
    w_key,
    w_value,
    w_out,
    w_gate,
    w_up,
    w_down,
    gain_attn_in,
    gain_attn_out,
    gain_ffn_in,
    gain_ffn_out,
    gain_query,
    gain_key,
    cotangent,
):
    heads = lax.axis_size("head")
    nseq = lax.axis_size("seq")
    head_index = lax.axis_index("head")
    seq_index = lax.axis_index("seq")
    bits = nseq.bit_length() - 1
    local_rows, model = tokens.shape
    width = gain_query.shape[0]
    qcount = w_query.shape[1] // width
    group = local_rows * heads
    total = segment_ids.shape[0]
    hidden_units = w_gate.shape[1]
    scale = 1.0 / math.sqrt(width)
    bf16 = jnp.bfloat16
    if (nseq, heads) == (8, 4) and (model // nseq) % 16 == 0:
        qw = qcount * width
        each, few = model // (nseq * heads), width // (nseq * heads)
        (
            projected,
            queries,
            keys,
            values,
            starts,
            index,
            log_total,
            attended_t,
            q_linear,
            k_linear,
            cosines,
            sines,
            attn_t,
        ) = front(
            nseq,
            heads,
            qcount,
            scale,
            11,
            tokens,
            segment_ids,
            w_key,
            w_value,
            gain_attn_in,
            gain_query,
            gain_key,
            w_query,
            w_out,
        )
        output, d_hidden, d_projected, gains, down_first, down_second, half_gate, all_up = feed_forward(
            nseq,
            heads,
            10,
            projected,
            tokens,
            cotangent,
            gain_attn_out,
            gain_ffn_in,
            gain_ffn_out,
            w_gate.T,
            w_up.T,
            w_down,
        )
        grad_tokens, sum_qkv, sum_out, sum_gate, sum_up, sum_down, sum_gains = tail(
            nseq,
            heads,
            qcount,
            scale,
            9,
            queries,
            starts,
            index,
            log_total,
            attended_t,
            d_projected,
            w_out,
            q_linear,
            k_linear,
            cosines,
            sines,
            gain_query,
            gain_key,
            gain_attn_in,
            attn_t,
            tokens,
            d_hidden,
            gains,
            keys.reshape(nseq, group, width),
            values.reshape(nseq, group, width),
            w_query,
            w_key,
            w_value,
            half_gate,
            all_up,
            down_first,
            down_second,
        )
        (
            output,
            grad_tokens,
            sum_query,
            sum_key,
            sum_value,
            sum_out,
            sum_gate,
            sum_up,
            sum_down,
            *sum_gains,
        ) = finish(
            nseq,
            qw,
            width,
            each,
            few,
            output,
            grad_tokens,
            sum_qkv,
            sum_out,
            sum_gate,
            sum_up,
            sum_down,
            sum_gains,
        )
        return (
            output,
            grad_tokens,
            sum_query,
            sum_key,
            sum_value,
            sum_out,
            sum_gate,
            sum_up,
            sum_down.T,
            *[g[0] for g in sum_gains],
        )
    first_row = (seq_index * heads + head_index) * local_rows
    my_index = first_row + jnp.arange(local_rows, dtype=jnp.int32)
    my_ids = lax.dynamic_slice_in_dim(segment_ids, first_row, local_rows)
    my_starts = jnp.min(
        jnp.where(
            my_ids[:, None] == segment_ids[None, :],
            jnp.arange(total, dtype=jnp.int32)[None, :],
            total,
        ),
        axis=1,
    )
    cosines, sines = rope_tables(my_index - my_starts, width)

    def query_path(linear, gain):
        shaped = linear.reshape(local_rows, qcount, width)
        turned = rotate(norm_rows(shaped, gain), cosines[:, None, :], sines[:, None, :])
        return turned.reshape(local_rows, qcount * width)

    def key_path(linear, gain):
        return rotate(norm_rows(linear, gain), cosines, sines)

    def gated(gate, up):
        return jax.nn.gelu(gate, approximate=True) * up

    def stacked(v):
        return v.reshape(local_rows, qcount, width).transpose(1, 0, 2).reshape(-1, width)

    def unstacked(v):
        return v.reshape(qcount, local_rows, width).transpose(1, 0, 2).reshape(local_rows, -1)

    inputs = tokens.astype(jnp.float32)
    attn_in = norm_rows(inputs, gain_attn_in).astype(bf16)
    k_linear = jnp.dot(attn_in, w_key, preferred_element_type=jnp.float32)
    keys_local = key_path(k_linear, gain_key).astype(bf16)
    values_local = jnp.dot(attn_in, w_value, preferred_element_type=jnp.float32).astype(bf16)
    q_linear = jnp.dot(attn_in, w_query, preferred_element_type=jnp.float32)
    queries_local = query_path(q_linear, gain_query).astype(bf16)
    queries = stacked(queries_local) * jnp.asarray(scale, bf16)
    keys, values = gather_all([keys_local, values_local], nseq, heads, 1)
    keys = keys.reshape(nseq, group, width)
    values = values.reshape(nseq, group, width)
    starts = jnp.tile(my_starts, qcount)[None, :]
    index = jnp.tile(my_index, qcount)[None, :]
    attended_t, log_total = attend(queries, keys, values, starts, index)
    attended = attended_t.T
    mixed_local = unstacked(attended.astype(bf16))
    projected = jnp.dot(mixed_local, w_out, preferred_element_type=jnp.float32)
    hidden = inputs + norm_rows(projected, gain_attn_out)
    ffn_in = norm_rows(hidden, gain_ffn_in).astype(bf16)
    ffn_rows = line_gather(ffn_in, heads, 2).reshape(group, model)
    gate = jnp.dot(ffn_rows, w_gate, preferred_element_type=jnp.float32)
    up = jnp.dot(ffn_rows, w_up, preferred_element_type=jnp.float32)
    activated = gated(gate, up).astype(bf16)
    ffn_out = line_scatter(
        jnp.dot(activated, w_down, preferred_element_type=jnp.float32)
        .astype(bf16)
        .reshape(heads, local_rows, model),
        heads,
        3,
    )
    output = hidden + norm_rows(ffn_out, gain_ffn_out)
    upstream = cotangent.astype(jnp.float32)
    unused, back_four = jax.vjp(norm_rows, ffn_out, gain_ffn_out)
    d_ffn_out, d_gain_four = back_four(upstream)
    d_ffn_rows = line_gather(d_ffn_out.astype(bf16), heads, 4).reshape(group, model)
    d_activated = contract_last(d_ffn_rows, w_down)
    d_w_down = contract_first(d_ffn_rows, activated)
    unused, back_gate = jax.vjp(gated, gate, up)
    d_gate, d_up = back_gate(d_activated)
    d_gate = d_gate.astype(bf16)
    d_up = d_up.astype(bf16)
    d_ffn_in = line_scatter(
        (contract_last(d_gate, w_gate) + contract_last(d_up, w_up))
        .astype(bf16)
        .reshape(heads, local_rows, model),
        heads,
        5,
    )
    d_w_gate = contract_first(ffn_rows, d_gate)
    d_w_up = contract_first(ffn_rows, d_up)
    unused, back_three = jax.vjp(norm_rows, hidden, gain_ffn_in)
    d_hidden_part, d_gain_three = back_three(d_ffn_in)
    d_hidden = upstream + d_hidden_part
    unused, back_two = jax.vjp(norm_rows, projected, gain_attn_out)
    d_projected, d_gain_two = back_two(d_hidden)
    d_projected = d_projected.astype(bf16)
    qw = qcount * width
    d_w_out = contract_first(mixed_local, d_projected)
    d_mixed = contract_last(d_projected, w_out).astype(bf16)
    grad_attended = stacked(d_mixed)
    row_dots = jnp.sum(grad_attended.astype(jnp.float32) * attended, axis=1)[None, :]
    d_queries_t, d_keys, d_values = attend_back(
        queries, keys, values, starts, index, log_total, row_dots, grad_attended
    )
    shape = (nseq, heads, local_rows, width)
    ups, downs = seq_orders(bits)
    d_keys, d_values = scatter_all(
        [d_keys.reshape(shape), d_values.reshape(shape)],
        [True, True],
        [[0] + ups, [0] + downs],
        nseq,
        heads,
        6,
        "scatter_keys",
    )
    d_query_rot = unstacked((d_queries_t.T * scale).astype(bf16)).astype(jnp.float32)
    unused, back_query = jax.vjp(query_path, q_linear, gain_query)
    d_q_linear, d_gain_query = back_query(d_query_rot)
    unused, back_key = jax.vjp(key_path, k_linear, gain_key)
    d_k_linear, d_gain_key = back_key(d_keys)
    d_qkv = jnp.concatenate([d_q_linear, d_k_linear, d_values], axis=1).astype(bf16)
    qw = qcount * width
    d_w_qkv = contract_first(attn_in, d_qkv)
    d_attn_in = (
        contract_last(d_qkv[:, :qw], w_query)
        + contract_last(d_qkv[:, qw : qw + width], w_key)
        + contract_last(d_qkv[:, qw + width :], w_value)
    )
    unused, back_one = jax.vjp(norm_rows, inputs, gain_attn_in)
    d_inputs, d_gain_one = back_one(d_attn_in)
    grad_tokens = (d_hidden + d_inputs).astype(bf16)

    def cut(v):
        return v.reshape(nseq, heads, -1)

    wide = jnp.stack([cut(d_gain_one), cut(d_gain_two), cut(d_gain_three), cut(d_gain_four)], 2)
    narrow = jnp.stack([cut(d_gain_query), cut(d_gain_key)], 2)
    each, few = wide.shape[-1], narrow.shape[-1]
    gains = jnp.concatenate(
        [
            jnp.pad(wide, ((0, 0), (0, 0), (0, 0), (0, 128 - each))),
            jnp.pad(narrow, ((0, 0), (0, 0), (0, 2), (0, 128 - few))),
        ],
        axis=2,
    )
    sum_qkv, sum_out, sum_gains = scatter_all(
        [
            d_w_qkv.astype(bf16).reshape(nseq, heads, -1, d_qkv.shape[1]),
            d_w_out.astype(bf16).reshape(nseq, heads, -1, model),
            gains,
        ],
        [True, True, True],
        [[0] + ups, [0] + downs, [0] + downs],
        nseq,
        heads,
        7,
        "scatter_attn",
    )
    sum_gate, sum_up, sum_down = scatter_all(
        [
            d.astype(bf16).reshape(nseq, model // nseq, hidden_units)
            for d in (d_w_gate, d_w_up, d_w_down)
        ],
        [False, False, False],
        [[0] + ups, [0] + downs, [0] + ups],
        nseq,
        heads,
        8,
        "scatter_ffn",
    )
    return (
        output.astype(bf16),
        grad_tokens,
        sum_qkv[:, :qw],
        sum_qkv[:, qw : qw + width],
        sum_qkv[:, qw + width :],
        sum_out,
        sum_gate,
        sum_up,
        sum_down.T,
        sum_gains[0, :each],
        sum_gains[1, :each],
        sum_gains[2, :each],
        sum_gains[3, :each],
        sum_gains[4, :few],
        sum_gains[5, :few],
    )


def solution(mesh):
    rows = P(("seq", "head"), None)
    in_specs = (
        rows,
        P(),
        P(),
        P(),
        P(),
        P(),
        P(None, "head"),
        P(None, "head"),
        P("head", None),
        P(),
        P(),
        P(),
        P(),
        P(),
        P(),
        rows,
    )
    out_specs = (
        rows,
        rows,
        rows,
        rows,
        rows,
        rows,
        P("seq", "head"),
        P("seq", "head"),
        P("head", "seq"),
    ) + (P(("seq", "head")),) * 6
    return jax.shard_map(local, mesh=mesh, in_specs=in_specs, out_specs=out_specs, check_vma=False)
```

```python
import functools
import itertools
import math

import jax
import jax.numpy as jnp
from jax import lax
from jax.experimental import pallas as pl
from jax.experimental.pallas import tpu as pltpu
from jax.sharding import PartitionSpec as P

EPS = 1e-06
MESH = pl.DeviceIdType.MESH
VMEM = pltpu.VMEM
LIMIT = 56 * 2**20


def norm_rows(v, gain):
    return v * lax.rsqrt(jnp.mean(v * v, axis=-1, keepdims=True) + EPS) * gain


def rotate(v, cosines, sines):
    half = v.shape[-1] // 2
    first = v[..., :half]
    second = v[..., half:]
    return jnp.concatenate(
        [first * cosines - second * sines, second * cosines + first * sines], axis=-1
    )


def rope_tables(positions, width):
    half = width // 2
    freq = jnp.exp(jnp.arange(half, dtype=jnp.float32) * (-2.0 * math.log(1000000.0) / width))
    angle = positions.astype(jnp.float32)[:, None] * freq[None, :]
    return (jnp.cos(angle), jnp.sin(angle))


def contract_first(left, right):
    return lax.dot_general(
        left, right, (((0,), (0,)), ((), ())), preferred_element_type=jnp.float32
    )


def contract_last(left, right):
    return lax.dot_general(
        left, right, (((1,), (1,)), ((), ())), preferred_element_type=jnp.float32
    )


def place():
    return lax.axis_index("seq"), lax.axis_index("head")


def related(s, mask):
    out = s
    bit = 0
    while mask >> bit:
        if (mask >> bit) & 1:
            step = 1 << bit
            out = out + (1 - 2 * ((s // step) % 2)) * step
        bit += 1
    return out


def subsets(bits):
    out = [0]
    for bit in bits:
        out = out + [m | (1 << bit) for m in out]
    return out


def greet(targets):
    barrier = pltpu.get_barrier_semaphore()
    for target in targets:
        pl.semaphore_signal(barrier, inc=1, device_id=target, device_id_type=MESH)
    pl.semaphore_wait(barrier, len(targets))


def remote(src, dst, send, recv, target):
    return pltpu.make_async_remote_copy(
        src_ref=src,
        dst_ref=dst,
        send_sem=send,
        recv_sem=recv,
        device_id=target,
        device_id_type=MESH,
    )


def seq_orders(bits):
    upper = list(range(1, bits))
    return upper, upper[::-1]


def gather_kernel(nseq, heads, local_refs, out_refs, send, recv):
    bits = nseq.bit_length() - 1
    s, h = place()
    others = [lax.rem(h + d, heads) for d in range(1, heads)]
    greet([(related(s, 1 << b), h) for b in range(bits)] + [(s, o) for o in others])
    count = [0]
    started = []

    def go(src, dst, target):
        k = count[0]
        count[0] += 1
        copy = remote(src, dst, send.at[k], recv.at[k], target)
        copy.start()
        started.append(copy)
        return copy

    first = []
    for a in range(len(out_refs)):
        out_refs[a][s, h] = local_refs[a][...]
        first.append(
            [go(local_refs[a], out_refs[a].at[s, h], (s, o)) for o in others]
        )
    orders = [o + [0] for o in seq_orders(bits)]
    held = [{0: first[a]} for a in range(len(out_refs))]
    for stage in range(bits):
        for a in range(len(out_refs)):
            bit = orders[a % 2][stage]
            target = (related(s, 1 << bit), h)
            arrived = {}
            for mask in list(held[a]):
                for copy in held[a][mask]:
                    copy.wait_recv()
                held[a][mask] = []
                group = related(s, mask)
                copy = go(out_refs[a].at[group], out_refs[a].at[group], target)
                arrived[mask | (1 << bit)] = [copy]
            held[a].update(arrived)
    for a in range(len(out_refs)):
        for mask in held[a]:
            for copy in held[a][mask]:
                copy.wait_recv()
    for copy in started:
        copy.wait_send()


def gather_all(arrays, nseq, heads, cid):
    n = len(arrays)
    total = n * (heads - 1 + nseq - 1)

    def kernel(*refs):
        gather_kernel(nseq, heads, refs[:n], refs[n : 2 * n], refs[2 * n], refs[2 * n + 1])

    return pl.pallas_call(
        kernel,
        out_shape=[jax.ShapeDtypeStruct((nseq, heads) + a.shape, a.dtype) for a in arrays],
        in_specs=[pl.BlockSpec(memory_space=VMEM)] * n,
        out_specs=[pl.BlockSpec(memory_space=VMEM)] * n,
        scratch_shapes=[pltpu.SemaphoreType.DMA((total,)), pltpu.SemaphoreType.DMA((total,))],
        name="gather_all",
        compiler_params=pltpu.CompilerParams(
            collective_id=cid, has_side_effects=True, vmem_limit_bytes=LIMIT
        ),
    )(*arrays)


def line_gather_kernel(heads, x_ref, out_ref, send, recv):
    s, h = place()
    right = (s, lax.rem(h + 1, heads))
    left = (s, lax.rem(h + heads - 1, heads))
    greet([right, left])
    out_ref[h] = x_ref[...]
    for step in range(heads - 1):
        to_right = remote(
            out_ref.at[jnp.maximum(h - step, 0)],
            out_ref.at[jnp.maximum(h - step, 0)],
            send.at[0, step],
            recv.at[0, step],
            right,
        )
        to_left = remote(
            out_ref.at[jnp.minimum(h + step, heads - 1)],
            out_ref.at[jnp.minimum(h + step, heads - 1)],
            send.at[1, step],
            recv.at[1, step],
            left,
        )
        pl.when((h - step >= 0) & (h < heads - 1))(to_right.start)
        pl.when((h + step <= heads - 1) & (h > 0))(to_left.start)
        pl.when(h - 1 - step >= 0)(
            remote(
                out_ref.at[jnp.maximum(h - 1 - step, 0)],
                out_ref.at[jnp.maximum(h - 1 - step, 0)],
                send.at[0, step],
                recv.at[0, step],
                right,
            ).wait_recv
        )
        pl.when(h + 1 + step <= heads - 1)(
            remote(
                out_ref.at[jnp.minimum(h + 1 + step, heads - 1)],
                out_ref.at[jnp.minimum(h + 1 + step, heads - 1)],
                send.at[1, step],
                recv.at[1, step],
                left,
            ).wait_recv
        )
        pl.when((h - step >= 0) & (h < heads - 1))(to_right.wait_send)
        pl.when((h + step <= heads - 1) & (h > 0))(to_left.wait_send)


def line_gather(x, heads, cid):
    return pl.pallas_call(
        functools.partial(line_gather_kernel, heads),
        out_shape=jax.ShapeDtypeStruct((heads,) + x.shape, x.dtype),
        in_specs=[pl.BlockSpec(memory_space=VMEM)],
        out_specs=pl.BlockSpec(memory_space=VMEM),
        scratch_shapes=[
            pltpu.SemaphoreType.DMA((2, heads - 1)),
            pltpu.SemaphoreType.DMA((2, heads - 1)),
        ],
        name="line_gather",
        compiler_params=pltpu.CompilerParams(
            collective_id=cid, has_side_effects=True, vmem_limit_bytes=LIMIT
        ),
    )(x)


def line_scatter_kernel(heads, parts, out_ref, from_left, from_right, send, recv):
    s, h = place()
    last = heads - 1
    right = (s, lax.rem(h + 1, heads))
    left = (s, lax.rem(h + heads - 1, heads))
    greet([right, left])
    f32 = jnp.float32
    for step in range(heads - 1):
        r_dest = jnp.clip(last - (step - h), 0, last)
        l_dest = jnp.clip(step - (last - h), 0, last)
        r_on = (step >= h) & (h < last)
        l_on = (step >= last - h) & (h > 0)
        for on, dest, box, lane, target, first in (
            (r_on, r_dest, from_left, 0, right, step == h),
            (l_on, l_dest, from_right, 1, left, step == last - h),
        ):
            at_end = (h == 0) if lane == 0 else (h == last)
            if step > 0:

                def add(box=box, dest=dest):
                    box[step - 1] = (
                        box[step - 1].astype(f32) + parts[dest].astype(f32)
                    ).astype(box.dtype)

                pl.when(on & jnp.logical_not(at_end))(add)
                pl.when(on & jnp.logical_not(at_end))(
                    remote(
                        box.at[step - 1], box.at[step], send.at[lane, step], recv.at[lane, step], target
                    ).start
                )
            pl.when(on & at_end)(
                remote(
                    parts.at[dest], box.at[step], send.at[lane, step], recv.at[lane, step], target
                ).start
            )
        r_in = (step >= h - 1) & (h > 0)
        l_in = (step >= last - h - 1) & (h < last)
        pl.when(r_in)(
            remote(
                from_left.at[step], from_left.at[step], send.at[0, step], recv.at[0, step], right
            ).wait_recv
        )
        pl.when(l_in)(
            remote(
                from_right.at[step], from_right.at[step], send.at[1, step], recv.at[1, step], left
            ).wait_recv
        )
    for step in range(heads - 1):
        for on, box, lane, target in (
            ((step >= h) & (h < last), from_left, 0, right),
            ((step >= last - h) & (h > 0), from_right, 1, left),
        ):
            pl.when(on)(
                remote(
                    box.at[step], box.at[step], send.at[lane, step], recv.at[lane, step], target
                ).wait_send
            )
    out_ref[...] = parts[h].astype(f32)

    def add_left():
        out_ref[...] += from_left[heads - 2].astype(f32)

    def add_right():
        out_ref[...] += from_right[heads - 2].astype(f32)

    pl.when(h > 0)(add_left)
    pl.when(h < last)(add_right)


def line_scatter(parts, heads, cid):
    block = parts.shape[1:]
    return pl.pallas_call(
        functools.partial(line_scatter_kernel, heads),
        out_shape=jax.ShapeDtypeStruct(block, jnp.float32),
        in_specs=[pl.BlockSpec(memory_space=VMEM)],
        out_specs=pl.BlockSpec(memory_space=VMEM),
        scratch_shapes=[
            VMEM((heads - 1,) + block, parts.dtype),
            VMEM((heads - 1,) + block, parts.dtype),
            pltpu.SemaphoreType.DMA((2, heads - 1)),
            pltpu.SemaphoreType.DMA((2, heads - 1)),
        ],
        name="line_scatter",
        compiler_params=pltpu.CompilerParams(
            collective_id=cid, has_side_effects=True, vmem_limit_bytes=LIMIT
        ),
    )(parts)


def scatter_kernel(nseq, heads, zs, orders, parts, outs, boxes, zboxes, send, recv):
    bits = nseq.bit_length() - 1
    s, h = place()
    f32 = jnp.float32
    others = [lax.rem(h + d, heads) for d in range(1, heads)]
    greet(
        [(related(s, 1 << b), h) for b in range(bits)]
        + ([(s, o) for o in others] if any(zs) else [])
    )
    count = [0]
    started = []

    def go(src, dst, target):
        k = count[0]
        count[0] += 1
        copy = remote(src, dst, send.at[k], recv.at[k], target)
        copy.start()
        started.append(copy)
        return copy

    n = len(parts)
    offsets = [0] * n
    slot = [{} for _ in range(n)]
    waiting = [{} for _ in range(n)]

    def current(a, mask):
        if mask in slot[a]:
            return boxes[a].at[slot[a][mask]]
        return parts[a].at[related(s, mask)]

    def launch(a, stage):
        bit = orders[a][stage]
        rest = orders[a][stage + 1 :]
        target = (related(s, 1 << bit), h)
        after = 1 << rest[0] if rest else 0
        masks = sorted(subsets(rest), key=lambda m: 0 if m & after else 1)
        for mask in masks:
            where = offsets[a]
            offsets[a] += 1
            waiting[a][mask] = (
                go(current(a, mask | (1 << bit)), boxes[a].at[where], target),
                where,
            )

    def settle(a, mask):
        copy, where = waiting[a].pop(mask)
        mine = current(a, mask)
        copy.wait_recv()
        boxes[a][where] = (boxes[a][where].astype(f32) + mine[...].astype(f32)).astype(
            boxes[a].dtype
        )
        slot[a][mask] = where

    for a in range(n):
        launch(a, 0)
    for stage in range(bits):
        for a in range(n):
            for mask in list(waiting[a]):
                settle(a, mask)
            if stage + 1 < bits:
                launch(a, stage + 1)
    arriving = []
    for a in range(n):
        if not zs[a]:
            continue
        mine = current(a, 0)
        arriving.append(
            [
                go(mine.at[o], zboxes[a].at[d], (s, o))
                for d, o in enumerate(others)
            ]
        )
    z = 0
    for a in range(n):
        if zs[a]:
            total = current(a, 0)[h].astype(f32)
            for d, copy in enumerate(arriving[z]):
                copy.wait_recv()
                total = total + zboxes[a][d].astype(f32)
            outs[a][...] = total
            z += 1
        else:
            outs[a][...] = current(a, 0)[...].astype(f32)
    for copy in started:
        copy.wait_send()


def scatter_all(arrays, zs, orders, nseq, heads, cid, name):
    n = len(arrays)
    total = sum((nseq - 1) + (heads - 1 if z else 0) for z in zs)
    blocks = [a.shape[2:] if z else a.shape[1:] for a, z in zip(arrays, zs)]

    def kernel(*refs):
        scatter_kernel(
            nseq,
            heads,
            zs,
            orders,
            refs[:n],
            refs[n : 2 * n],
            refs[2 * n : 3 * n],
            refs[3 * n : 4 * n],
            refs[4 * n],
            refs[4 * n + 1],
        )

    return pl.pallas_call(
        kernel,
        out_shape=[jax.ShapeDtypeStruct(b, jnp.float32) for b in blocks],
        in_specs=[pl.BlockSpec(memory_space=VMEM)] * n,
        out_specs=[pl.BlockSpec(memory_space=VMEM)] * n,
        scratch_shapes=[VMEM((nseq - 1,) + a.shape[1:], a.dtype) for a in arrays]
        + [
            VMEM((heads - 1,) + b, a.dtype) if z else VMEM((8, 128), jnp.float32)
            for a, b, z in zip(arrays, blocks, zs)
        ]
        + [pltpu.SemaphoreType.DMA((total,)), pltpu.SemaphoreType.DMA((total,))],
        name=name,
        compiler_params=pltpu.CompilerParams(
            collective_id=cid, has_side_effects=True, vmem_limit_bytes=LIMIT
        ),
    )(*arrays)


def attend_kernel(q_ref, k_ref, v_ref, start_ref, index_ref, out_ref, log_ref):
    s = lax.axis_index("seq")
    span = k_ref.shape[1]
    start = start_ref[...]
    index = index_ref[...]
    queries = q_ref[...]
    rows = queries.shape[0]
    out_ref[...] = jnp.zeros_like(out_ref)

    def step(g, mass):
        scores = contract_last(k_ref[g], queries)
        key = g * span + lax.broadcasted_iota(jnp.int32, (span, rows), 0)
        terms = jnp.where((key >= start) & (key <= index), jnp.exp(scores), 0.0)
        out_ref[...] += contract_first(v_ref[g], terms.astype(jnp.bfloat16))
        return mass + jnp.sum(terms, axis=0, keepdims=True)

    mass = lax.fori_loop(0, s + 1, step, jnp.zeros((1, rows), jnp.float32))
    out_ref[...] = out_ref[...] / mass
    log_ref[...] = jnp.log(mass)


def attend(q, k, v, start, index):
    rows, width = q.shape
    return pl.pallas_call(
        attend_kernel,
        out_shape=[
            jax.ShapeDtypeStruct((width, rows), jnp.float32),
            jax.ShapeDtypeStruct((1, rows), jnp.float32),
        ],
        in_specs=[pl.BlockSpec(memory_space=VMEM)] * 5,
        out_specs=[pl.BlockSpec(memory_space=VMEM)] * 2,
        name="attend",
        compiler_params=pltpu.CompilerParams(vmem_limit_bytes=LIMIT),
    )(q, k, v, start, index)


def attend_back_kernel(
    q_ref, k_ref, v_ref, start_ref, index_ref, log_ref, dots_ref, d_ref, dq_ref, dk_ref, dv_ref
):
    s = lax.axis_index("seq")
    groups, span = k_ref.shape[:2]
    start = start_ref[...]
    index = index_ref[...]
    log_total = log_ref[...]
    dots = dots_ref[...]
    queries = q_ref[...]
    grads = d_ref[...]
    rows = queries.shape[0]
    dq_ref[...] = jnp.zeros_like(dq_ref)

    def step(g, carry):
        keys = k_ref[g]
        scores = contract_last(keys, queries)
        key = g * span + lax.broadcasted_iota(jnp.int32, (span, rows), 0)
        probs = jnp.where((key >= start) & (key <= index), jnp.exp(scores - log_total), 0.0)
        d_probs = contract_last(v_ref[g], grads)
        d_scores = (probs * (d_probs - dots)).astype(jnp.bfloat16)
        dv_ref[g] = jnp.dot(
            probs.astype(jnp.bfloat16), grads, preferred_element_type=jnp.float32
        ).astype(dv_ref.dtype)
        dk_ref[g] = jnp.dot(d_scores, queries, preferred_element_type=jnp.float32).astype(
            dk_ref.dtype
        )
        dq_ref[...] += contract_first(keys, d_scores)
        return carry

    lax.fori_loop(0, s + 1, step, 0)

    def blank(g, carry):
        dk_ref[g] = jnp.zeros(dk_ref.shape[1:], dk_ref.dtype)
        dv_ref[g] = jnp.zeros(dv_ref.shape[1:], dv_ref.dtype)
        return carry

    lax.fori_loop(s + 1, groups, blank, 0)


def attend_back(q, k, v, start, index, log_total, dots, grads):
    rows, width = q.shape
    return pl.pallas_call(
        attend_back_kernel,
        out_shape=[
            jax.ShapeDtypeStruct((width, rows), jnp.float32),
            jax.ShapeDtypeStruct(k.shape, jnp.bfloat16),
            jax.ShapeDtypeStruct(v.shape, jnp.bfloat16),
        ],
        in_specs=[pl.BlockSpec(memory_space=VMEM)] * 8,
        out_specs=[pl.BlockSpec(memory_space=VMEM)] * 3,
        name="attend_back",
        compiler_params=pltpu.CompilerParams(vmem_limit_bytes=LIMIT),
    )(q, k, v, start, index, log_total, dots, grads)


def flat(ref):
    return ref[...].reshape(1, ref.shape[0])


def front_kernel(
    nseq,
    heads,
    qcount,
    scale,
    x_ref,
    ids_ref,
    w_key_ref,
    w_value_ref,
    gain_in_ref,
    gain_q_ref,
    gain_k_ref,
    w_query_far,
    w_out_far,
    o_proj,
    o_q,
    o_k,
    o_v,
    o_start,
    o_index,
    o_log,
    o_att,
    o_q_lin,
    o_k_lin,
    o_cos,
    o_sin,
    o_attn_t,
    w_query,
    w_out,
    k_all,
    v_all,
    send,
    recv,
    local_sem,
):
    f32, bf16 = jnp.float32, jnp.bfloat16
    bits = nseq.bit_length() - 1
    ups, downs = seq_orders(bits)
    links = Links(nseq, heads, send, recv)
    s, h = links.s, links.h
    rows, model = x_ref.shape
    width = w_key_ref.shape[1]
    gain_q, gain_k = flat(gain_q_ref), flat(gain_k_ref)
    half = width // 2
    total = ids_ref.shape[0] * ids_ref.shape[1]
    load_q = pltpu.make_async_copy(w_query_far, w_query, local_sem.at[0])
    load_q.start()
    load_o = pltpu.make_async_copy(w_out_far, w_out, local_sem.at[1])
    load_o.start()
    partners = [related(h, j) for j in range(1, heads)]
    greet([links.across(b) for b in range(bits)] + [(s, o) for o in partners])

    which = s * heads + h
    mine = ids_ref[pl.ds(which, 1), :].astype(f32)
    column = jnp.broadcast_to(mine, (rows, rows)).T[:, 0:1]
    first = jnp.full((rows, rows), float(total), f32)
    for r in range(ids_ref.shape[0]):
        here = ids_ref[r : r + 1, :].astype(f32)
        at = (r * rows + lax.broadcasted_iota(jnp.int32, (1, rows), 1)).astype(f32)
        first = jnp.minimum(first, jnp.where(column == here, at, float(total)))
    start = jnp.min(first, axis=1, keepdims=True)
    index = (which * rows + lax.broadcasted_iota(jnp.int32, (rows, 1), 0)).astype(f32)
    freq = jnp.exp(
        lax.broadcasted_iota(jnp.int32, (1, half), 1).astype(f32)
        * (-2.0 * math.log(1000000.0) / width)
    )
    angle = (index - start) * freq
    turns = jnp.round(angle * (1.0 / (2.0 * math.pi)))
    angle = (angle - turns * 6.28125) - turns * (2.0 * math.pi - 6.28125)
    cosines, sines = jnp.cos(angle), jnp.sin(angle)
    o_cos[...] = cosines
    o_sin[...] = sines
    start_row = jnp.broadcast_to(start, (rows, rows)).T[0:1, :].astype(jnp.int32)
    index_row = which * rows + lax.broadcasted_iota(jnp.int32, (1, rows), 1)
    for j in range(qcount):
        o_start[:, pl.ds(j * rows, rows)] = start_row
        o_index[:, pl.ds(j * rows, rows)] = index_row

    attn_in = norm_rows(x_ref[...].astype(f32), flat(gain_in_ref)).astype(bf16)
    k_lin = jnp.dot(attn_in, w_key_ref[...], preferred_element_type=f32)
    k_all[s, h] = rotate(norm_rows(k_lin, gain_k), cosines, sines).astype(bf16)
    o_k_lin[...] = k_lin
    v_all[s, h] = jnp.dot(attn_in, w_value_ref[...], preferred_element_type=f32).astype(bf16)

    both = ((k_all, ups), (v_all, downs))

    def pass_on(a, mask, j, bit):
        buf = both[a][0]
        block = buf.at[related(s, mask), related(h, j)]
        return links.go(block, block, links.across(bit))

    over_head = {}
    for j in range(1, heads):
        for a in range(2):
            block = both[a][0].at[s, h]
            over_head[a, j] = links.go(block, block, (s, partners[j - 1]))
    arriving = {}

    def spread(a, mask, j, stage):
        order = both[a][1]
        for later in range(stage, len(order)):
            bit = order[later]
            arriving[a, mask | (1 << bit), j] = pass_on(a, mask, j, bit)

    for a in range(2):
        spread(a, 0, 0, 0)

    load_q.wait()
    q_lin = jnp.dot(attn_in, w_query[...], preferred_element_type=f32)
    o_q_lin[...] = q_lin
    for j in range(1, heads):
        for a in range(2):
            over_head[a, j].wait_recv()
            spread(a, 0, j, 0)
    for j in range(qcount):
        part = norm_rows(q_lin[:, j * width : (j + 1) * width], gain_q)
        o_q[pl.ds(j * rows, rows), :] = (rotate(part, cosines, sines) * scale).astype(bf16)

    queries = o_q[...]
    starts = o_start[...]
    indices = o_index[...]
    o_att[...] = jnp.zeros_like(o_att)
    o_log[...] = jnp.zeros_like(o_log)
    span = heads * rows

    def attend_group(g):
        scores = contract_last(k_all[g].reshape(span, width), queries)
        key = g * span + lax.broadcasted_iota(jnp.int32, scores.shape, 0)
        terms = jnp.where((key >= starts) & (key <= indices), jnp.exp(scores), 0.0)
        o_att[...] += contract_first(v_all[g].reshape(span, width), terms.astype(bf16))
        o_log[...] += jnp.sum(terms, axis=0, keepdims=True)

    pairs = {}

    def to_pair(a, mask):
        block = both[a][0].at[related(s, mask)]
        pairs[a, mask] = links.go(block, block, links.across(0))

    def attend_if(g):
        pl.when(g <= s)(functools.partial(attend_group, g))

    def attend_pair(mask):
        for a in range(2):
            pairs[a, mask].wait_recv()
        attend_if(related(s, mask | 1))

    for a in range(2):
        to_pair(a, 0)
    attend_group(s)
    whole = {}
    ready = [0]
    for stage in range(len(ups)):
        for lower in subsets(range(stage)):
            masks = []
            for a in range(2):
                order = both[a][1]
                mask = sum(1 << order[i] for i in range(stage) if lower >> i & 1)
                masks.append(mask | (1 << order[stage]))
            for j in range(heads):
                for a in range(2):
                    arriving[a, masks[a], j].wait_recv()
                    spread(a, masks[a], j, stage + 1)
            for a in range(2):
                to_pair(a, masks[a])
                whole[masks[a]] = whole.get(masks[a], 0) + 1
            done = [m for m in whole if whole[m] == 2]
            for m in done:
                del whole[m]
                attend_if(related(s, m))
            if done:
                attend_pair(ready.pop(0))
                ready.extend(done)
    o_attn_t[...] = attn_in.T.reshape(o_attn_t.shape)

    for m in ready:
        attend_pair(m)
    mass = o_log[...]
    keep_k = pltpu.make_async_copy(k_all, o_k, local_sem.at[2])
    keep_v = pltpu.make_async_copy(v_all, o_v, local_sem.at[3])
    keep_k.start()
    keep_v.start()
    o_log[...] = jnp.log(mass)
    attended = o_att[...] / mass
    o_att[...] = attended
    load_o.wait()
    proj = jnp.zeros((rows, model), f32)
    for j in range(qcount):
        part = attended[:, j * rows : (j + 1) * rows].T.astype(bf16)
        proj = proj + jnp.dot(
            part, w_out[pl.ds(j * width, width), :], preferred_element_type=f32
        )
    o_proj[...] = proj
    keep_k.wait()
    keep_v.wait()
    links.finish()


def front(nseq, heads, qcount, scale, cid, x, ids, w_key, w_value, gain_in, gain_q, gain_k, w_query, w_out):
    f32, bf16, i32 = jnp.float32, jnp.bfloat16, jnp.int32
    rows, model = x.shape
    width = w_key.shape[1]
    stacked = qcount * rows
    some = nseq // 2
    messages = 2 * (heads - 1) + 2 * heads * (some - 1) + 2 * some
    vm = pl.BlockSpec(memory_space=VMEM)
    anywhere = pl.BlockSpec(memory_space=pl.ANY)
    everyone = (nseq, heads, rows, width)

    def kernel(*refs):
        front_kernel(nseq, heads, qcount, scale, *refs)

    shape = jax.ShapeDtypeStruct
    return pl.pallas_call(
        kernel,
        out_shape=[
            shape((rows, model), f32),
            shape((stacked, width), bf16),
            shape(everyone, bf16),
            shape(everyone, bf16),
            shape((1, stacked), i32),
            shape((1, stacked), i32),
            shape((1, stacked), f32),
            shape((width, stacked), f32),
            shape((rows, qcount * width), f32),
            shape((rows, width), f32),
            shape((rows, width // 2), f32),
            shape((rows, width // 2), f32),
            shape((nseq, model // nseq, rows), bf16),
        ],
        in_specs=[vm] * 7 + [anywhere] * 2,
        out_specs=[vm] * 2 + [anywhere] * 2 + [vm] * 9,
        scratch_shapes=[
            VMEM(w_query.shape, bf16),
            VMEM(w_out.shape, bf16),
            VMEM(everyone, bf16),
            VMEM(everyone, bf16),
            pltpu.SemaphoreType.DMA((messages,)),
            pltpu.SemaphoreType.DMA((messages,)),
            pltpu.SemaphoreType.DMA((4,)),
        ],
        name="front",
        compiler_params=pltpu.CompilerParams(
            collective_id=cid, has_side_effects=True, vmem_limit_bytes=LIMIT
        ),
    )(
        x,
        ids.reshape(nseq * heads, rows),
        w_key,
        w_value,
        gain_in,
        gain_q,
        gain_k,
        w_query,
        w_out,
    )


class Sum:
    def __init__(self, links, part, boxes, order):
        self.links, self.part, self.boxes, self.order = links, part, boxes, order
        self.used = 0
        self.slot = {}
        self.waiting = {}

    def current(self, mask):
        if mask in self.slot:
            return self.boxes.at[self.slot[mask]]
        return self.part(mask)

    def masks(self, stage):
        rest = self.order[stage + 1 :]
        weight = lambda m: sum(1 << (len(rest) - i) for i, b in enumerate(rest) if m >> b & 1)
        return sorted(subsets(rest), key=weight, reverse=True)

    def send(self, stage, mask):
        bit = self.order[stage]
        where = self.used
        self.used += 1
        copy = self.links.go(
            self.current(mask | (1 << bit)), self.boxes.at[where], self.links.across(bit)
        )
        self.waiting[stage, mask] = (copy, where)

    def start(self):
        for mask in self.masks(0):
            self.send(0, mask)

    def steps(self, stage, kept=None):
        def step(mask):
            copy, where = self.waiting.pop((stage, mask))
            mine = kept(mask) if kept is not None else self.current(mask)
            copy.wait_recv()
            self.boxes[where] = self.boxes[where] + mine[...]
            self.slot[mask] = where
            if stage + 1 < len(self.order):
                bit = 1 << self.order[stage + 1]
                if mask & bit:
                    self.send(stage + 1, mask & ~bit)

        return [functools.partial(step, mask) for mask in self.masks(stage)]

    def last(self, kept=None):
        copy, where = self.waiting.pop((len(self.order) - 1, 0))
        mine = kept(0) if kept is not None else self.current(0)
        copy.wait_recv()
        return self.boxes[where].astype(jnp.float32) + mine[...].astype(jnp.float32)


def in_turn(*lists):
    for group in itertools.zip_longest(*lists):
        for step in group:
            if step is not None:
                step()


def split_rows(rows):
    return (rows // 2 + 15) // 16 * 16


class Links:
    def __init__(self, nseq, heads, send, recv):
        self.s, self.h = place()
        self.nseq, self.heads = nseq, heads
        self.send, self.recv = send, recv
        self.count = 0
        self.started = []
        self.others = [lax.rem(self.h + d, heads) for d in range(1, heads)]

    def greet(self, more=()):
        bits = self.nseq.bit_length() - 1
        near = [self.across(b) for b in range(bits)]
        greet(near + [(self.s, o) for o in self.others] + list(more))

    def across(self, bit):
        return (related(self.s, 1 << bit), self.h)

    def go(self, src, dst, target):
        k = self.count
        self.count += 1
        copy = remote(src, dst, self.send.at[k], self.recv.at[k], target)
        copy.start()
        self.started.append(copy)
        return copy

    def over_heads(self, src, boxes):
        return [self.go(src.at[o], boxes.at[d], (self.s, o)) for d, o in enumerate(self.others)]

    def finish(self):
        for copy in self.started:
            copy.wait_send()


def back_norm(v, gain, d_out):
    scale = lax.rsqrt(jnp.mean(v * v, axis=-1, keepdims=True) + EPS)
    unit = v * scale
    inner = d_out * gain
    d_v = scale * (inner - unit * jnp.mean(inner * unit, axis=-1, keepdims=True))
    return d_v, jnp.sum(d_out * unit, axis=0, keepdims=True)


def back_rotate(d, cosines, sines):
    half = d.shape[-1] // 2
    first, second = d[:, :half], d[:, half:]
    return jnp.concatenate(
        [first * cosines + second * sines, second * cosines - first * sines], axis=-1
    )


def tail_kernel(
    nseq,
    heads,
    qcount,
    scale,
    q_ref,
    start_ref,
    index_ref,
    log_ref,
    att_ref,
    d_proj_ref,
    k_lin_ref,
    cos_ref,
    sin_ref,
    gain_q_ref,
    gain_k_ref,
    gain_in_ref,
    gains_ref,
    k_far,
    v_far,
    w_out_far,
    q_lin_far,
    attn_t_far,
    x_far,
    d_hid_far,
    w_query_far,
    w_key_far,
    w_value_far,
    d_gate_ref,
    d_up_ref,
    d_down_first,
    d_down_second,
    o_tokens,
    o_qkv,
    o_out,
    o_gate,
    o_up,
    o_down,
    o_gains,
    k_ref,
    v_ref,
    w_out_ref,
    q_lin_ref,
    attn_t_ref,
    x_ref,
    d_hid_ref,
    w_qkv_ref,
    dk,
    dv,
    dq_t,
    grads,
    grads_t,
    box_k,
    box_v,
    zbox_k,
    zbox_v,
    dw_out,
    box_out,
    zbox_out,
    mid_out,
    end_out,
    dw_qkv,
    box_qkv,
    zsrc_qkv,
    zbox_qkv,
    d_qkv,
    keep_gate_first,
    keep_gate_second,
    keep_up_first,
    keep_up_second,
    keep_down_first,
    keep_down_second,
    box_gate_first,
    box_gate_second,
    box_up_first,
    box_up_second,
    box_down_first,
    box_down_second,
    gsum,
    gbox,
    gzbox,
    send,
    recv,
    local_sem,
):
    f32, bf16 = jnp.float32, jnp.bfloat16
    bits = nseq.bit_length() - 1
    ups, downs = seq_orders(bits)
    links = Links(nseq, heads, send, recv)
    s, h = links.s, links.h
    rows, model = d_proj_ref.shape
    width = k_lin_ref.shape[1]
    gain_q, gain_k = flat(gain_q_ref), flat(gain_k_ref)
    groups, span = k_ref.shape[:2]
    loads = []

    def load(src, dst):
        copy = pltpu.make_async_copy(src, dst, local_sem.at[len(loads)])
        copy.start()
        loads.append(copy)
        return copy

    load_o = load(w_out_far, w_out_ref)
    load_k = load(k_far, k_ref)
    load_v = load(v_far, v_ref)
    plane = subsets(ups)[1:]
    links.greet([(related(s, m), links.h) for m in plane if m & (m - 1)])

    held = subsets(ups)
    ffn = []
    split = keep_gate_first.shape[1]
    for src, keep, box, order, low, past in (
        (d_gate_ref, keep_gate_first, box_gate_first, ups, 0, 1),
        (d_gate_ref, keep_gate_second, box_gate_second, downs, split, 1),
        (d_up_ref, keep_up_first, box_up_first, [0] + ups, 0, 0),
        (d_up_ref, keep_up_second, box_up_second, [0] + downs, split, 0),
        (d_down_first, keep_down_first, box_down_first, ups[1:], 0, 2),
        (d_down_second, keep_down_second, box_down_second, downs[1:], 0, 2),
    ):
        here = pl.ds(low, keep.shape[1])

        def part(m, src=src, here=here, past=past, order=order):
            if past == 0:
                return src.at[related(s, m), here]
            if past == 1:
                return src.at[held.index(m), here]
            return src.at[0 if m else 1, here]

        total = Sum(links, part, box, order)
        kept = subsets(order[1:])
        total.loads = [load(part(m), keep.at[i]) for i, m in enumerate(kept)]
        total.kept = lambda m, keep=keep, kept=kept: keep.at[kept.index(m)]
        ffn.append(total)
    gate, up, down = ffn[0:2], ffn[2:4], ffn[4:6]
    for total in up + gate + down:
        total.start()

    def settle(pair, stage, first=False):
        if first:
            for total in pair:
                for copy in total.loads:
                    copy.wait()
        in_turn(*[total.steps(stage, total.kept if first else None) for total in pair])

    def put(pair, out, first=False):
        at = 0
        for total in pair:
            value = total.last(total.kept if first else None).astype(out.dtype)
            out[pl.ds(at, value.shape[0]), :] = value
            at += value.shape[0]

    load_q = load(q_lin_far, q_lin_ref)
    load_a = load(attn_t_far, attn_t_ref)
    load_x = load(x_far, x_ref)
    load_d = load(d_hid_far, d_hid_ref)
    load_w = []
    at = 0
    for far in (w_query_far, w_key_far, w_value_far):
        load_w.append(load(far, w_qkv_ref.at[:, pl.ds(at, far.shape[1])]))
        at += far.shape[1]

    d_proj = d_proj_ref[...]

    out_rows = dw_out.shape[1] * dw_out.shape[2]
    for j in range(nseq):
        head, low = divmod(j * out_rows, width)
        mixed_t = att_ref[low : low + out_rows, pl.ds(head * rows, rows)].astype(bf16)
        dw_out[j] = (
            jnp.dot(mixed_t, d_proj, preferred_element_type=f32)
            .astype(bf16)
            .reshape(dw_out.shape[1:])
        )

    sum_out = Sum(links, lambda m: dw_out.at[related(s, m)], box_out, [0])
    sum_out.masks = lambda stage: held
    sum_out.start()

    load_o.wait()
    for j in range(qcount):
        part = w_out_ref[pl.ds(j * width, width), :]
        grads[pl.ds(j * rows, rows), :] = contract_last(d_proj, part).astype(bf16)
        grads_t[:, pl.ds(j * rows, rows)] = contract_last(part, d_proj).astype(bf16)
    in_turn(sum_out.steps(0))
    z_out = [
        links.go(box_out.at[:, o], zbox_out.at[d], (s, o)) for d, o in enumerate(links.others)
    ]
    dots = jnp.sum(grads_t[...].astype(f32) * att_ref[...], axis=0, keepdims=True)
    start = start_ref[...]
    index = index_ref[...]
    log_total = log_ref[...]
    dq_t[...] = jnp.zeros_like(dq_t)
    load_k.wait()
    load_v.wait()

    def step(g, carry):
        keys = k_ref[g]
        queries = q_ref[...]
        scores = contract_last(keys, queries)
        key = g * span + lax.broadcasted_iota(jnp.int32, scores.shape, 0)
        probs = jnp.where((key >= start) & (key <= index), jnp.exp(scores - log_total), 0.0)
        d_probs = jnp.dot(v_ref[g], grads_t[...], preferred_element_type=f32)
        d_scores = (probs * (d_probs - dots)).astype(bf16)
        dv[g] = (
            jnp.dot(probs.astype(bf16), grads[...], preferred_element_type=f32)
            .astype(bf16)
            .reshape(dv.shape[1:])
        )
        dk[g] = (
            jnp.dot(d_scores, queries, preferred_element_type=f32)
            .astype(bf16)
            .reshape(dk.shape[1:])
        )
        dq_t[...] += contract_first(keys, d_scores)
        return carry

    def blank(g, carry):
        dk[g] = jnp.zeros(dk.shape[1:], bf16)
        dv[g] = jnp.zeros(dv.shape[1:], bf16)
        return carry

    low = lax.rem(s, 2)
    theirs = s // 2 + low
    lax.fori_loop(0, theirs, lambda i, c: step(2 * i + 1 - low, c), 0)
    lax.fori_loop(theirs, groups // 2, lambda i, c: blank(2 * i + 1 - low, c), 0)

    kv = []
    for j in list(range(1, heads)) + [0]:
        owner = lax.rem(h + j, heads)
        for far, box, order in ((dk, box_k, ups), (dv, box_v, downs)):
            kv.append(
                Sum(
                    links,
                    lambda m, far=far, owner=owner: far.at[related(s, m), owner],
                    box.at[j],
                    [0] + order,
                )
            )
    for mask_index in range(len(held)):
        for total in kv:
            total.send(0, total.masks(0)[mask_index])
    lax.fori_loop(0, s // 2 + 1, lambda i, c: step(2 * i + low, c), 0)
    lax.fori_loop(s // 2 + 1, groups // 2, lambda i, c: blank(2 * i + low, c), 0)

    in_turn(*[total.steps(0) for total in kv])

    load_q.wait()
    cosines, sines = cos_ref[...], sin_ref[...]
    d_gain_q = jnp.zeros((1, width), f32)
    for j in range(qcount):
        d_rot = dq_t[:, pl.ds(j * rows, rows)].T * scale
        d_lin, terms = back_norm(
            q_lin_ref[:, pl.ds(j * width, width)],
            gain_q,
            back_rotate(d_rot, cosines, sines),
        )
        d_qkv[:, pl.ds(j * width, width)] = d_lin.astype(bf16)
        d_gain_q = d_gain_q + terms

    for stage in range(1, bits - 1):
        in_turn(*[total.steps(stage) for total in kv])
    settle(gate, 0, True)

    arriving = {}
    for i, total in enumerate(kv):
        for m in total.steps(bits - 1):
            m()
        j = (i // 2 + 1) % heads
        if j:
            zbox = (zbox_k, zbox_v)[i % 2]
            arriving[i % 2, j] = links.go(
                total.current(0), zbox.at[j - 1], (s, links.others[j - 1])
            )
    for d, copy in enumerate(z_out):
        copy.wait_recv()
    own = box_out[:, h].astype(f32)
    for d in range(heads - 1):
        own = own + zbox_out[d].astype(f32)
    mid_out[...] = own.astype(bf16)
    sum_end = Sum(links, lambda m: mid_out.at[held.index(m)], end_out, downs)
    sum_end.start()


    settle(up, 0, True)

    def whole(i, zbox):
        total = kv[len(kv) - 2 + i].current(0)[...].astype(f32)
        for j in range(1, heads):
            arriving[i, j].wait_recv()
            total = total + zbox[j - 1].astype(f32)
        return total

    d_keys = whole(0, zbox_k)
    d_lin, d_gain_k = back_norm(
        k_lin_ref[...], gain_k, back_rotate(d_keys, cosines, sines)
    )
    qw = qcount * width
    d_qkv[:, pl.ds(qw, width)] = d_lin.astype(bf16)
    d_values = whole(1, zbox_v)
    d_qkv[:, pl.ds(qw + width, width)] = d_values.astype(bf16)

    pieces, _, block_rows, cut = dw_qkv.shape
    load_a.wait()
    qkv = []
    for j in range(pieces):
        cols = pl.ds(j * cut, cut)

        def qkv_block(g, carry, j=j, cols=cols):
            dw_qkv[j, g] = jnp.dot(
                attn_t_ref[g], d_qkv[:, cols], preferred_element_type=f32
            ).astype(bf16)
            return carry

        lax.fori_loop(0, nseq, qkv_block, 0)
        total = Sum(
            links,
            lambda m, j=j: dw_qkv.at[j, related(s, m)],
            box_qkv.at[j],
            [0] + (downs if j % 2 else ups),
        )
        total.start()
        qkv.append(total)

    for copy in load_w + [load_x, load_d]:
        copy.wait()
    d_attn_in = contract_last(d_qkv[...], w_qkv_ref[...])
    in_turn(*[total.steps(0) for total in qkv])
    d_x, d_gain_in = back_norm(x_ref[...].astype(f32), flat(gain_in_ref), d_attn_in)
    o_tokens[...] = (d_hid_ref[...] + d_x).astype(o_tokens.dtype)

    gsum[0] = gains_ref[...]
    gsum[0, 0:1, :] = d_gain_in
    gsum[0, 4:5, :width] = d_gain_q
    gsum[0, 5:6, :width] = d_gain_k
    gain_copy = links.go(gsum.at[0], gbox.at[0], links.across(0))
    for stage in range(1, bits - 1):
        in_turn(*[total.steps(stage) for total in qkv])
    gain_copy.wait_recv()
    gsum[1] = gsum[0] + gbox[0]
    gain_plane = [
        links.go(gsum.at[1], gbox.at[1 + i], (related(s, m), h)) for i, m in enumerate(plane)
    ]
    in_turn(sum_end.steps(0))
    settle(up, 1)
    each = block_rows // heads
    z_qkv = []

    for j, total in enumerate(qkv):
        value = total.last()
        for p in range(heads):
            zsrc_qkv[j, p] = value[p * each : (p + 1) * each].astype(bf16)
        z_qkv.append(links.over_heads(zsrc_qkv.at[j], zbox_qkv.at[j]))
    total_gains = gsum[1]
    for i, copy in enumerate(gain_plane):
        copy.wait_recv()
        total_gains = total_gains + gbox[1 + i]
    gsum[2] = total_gains
    gain_z = [
        links.go(gsum.at[2], gzbox.at[d], (s, o)) for d, o in enumerate(links.others)
    ]
    for total in down:
        for copy in total.loads:
            copy.wait()
    put(down, o_down, True)
    put(gate, o_gate)
    put(up, o_up)
    o_out[...] = sum_end.last()
    for j, copies in enumerate(z_qkv):
        total = zsrc_qkv[j, h].astype(f32)
        for d, copy in enumerate(copies):
            copy.wait_recv()
            total = total + zbox_qkv[j, d].astype(f32)
        o_qkv[:, pl.ds(j * cut, cut)] = total
    total = gsum[2]
    for d, copy in enumerate(gain_z):
        copy.wait_recv()
        total = total + gzbox[d]
    o_gains[...] = total
    links.finish()


def tail(nseq, heads, qcount, scale, cid, *arrays):
    (q, _, _, _, att, d_proj, k_lin, _, _, gain_q, _, _, gains, k, v) = arrays[:15]
    (w_out, q_lin, attn_t, x, d_hid, w_query, w_key, w_value, d_gate, _, _, _) = arrays[15:]
    f32, bf16 = jnp.float32, jnp.bfloat16
    rows, model = d_proj.shape
    width = k_lin.shape[1]
    cols = w_query.shape[1] + w_key.shape[1] + w_value.shape[1]
    pieces = 4
    cut = cols // pieces
    out_rows, qkv_rows = w_out.shape[0] // nseq, attn_t.shape[1]
    ffn_block = d_gate.shape[1:]
    some, all_but = nseq // 2, nseq - 1
    out_block = (heads, out_rows // heads, model)
    split = split_rows(ffn_block[0])
    low, high = (split, ffn_block[1]), (ffn_block[0] - split, ffn_block[1])
    parts = [(part, *n) for n in ((2, 3), (4, 7), (1, 1)) for part in (low, high)]
    copies = (
        sum(n for _, _, n in parts)
        + some
        + (heads - 1)
        + (some - 1)
        + 2 * heads * all_but
        + 2 * (heads - 1)
        + pieces * (all_but + heads - 1)
        + some
        + (heads - 1)
    )
    vm = pl.BlockSpec(memory_space=VMEM)
    anywhere = pl.BlockSpec(memory_space=pl.ANY)

    def kernel(*refs):
        tail_kernel(nseq, heads, qcount, scale, *refs)

    return pl.pallas_call(
        kernel,
        out_shape=[
            jax.ShapeDtypeStruct((rows, model), bf16),
            jax.ShapeDtypeStruct((qkv_rows // heads, cols), f32),
            jax.ShapeDtypeStruct(out_block[1:], f32),
            jax.ShapeDtypeStruct(ffn_block, bf16),
            jax.ShapeDtypeStruct(ffn_block, bf16),
            jax.ShapeDtypeStruct(ffn_block, bf16),
            jax.ShapeDtypeStruct(gains.shape, f32),
        ],
        in_specs=[vm] * 13 + [anywhere] * 14,
        out_specs=[vm] * 7,
        scratch_shapes=[
            VMEM(k.shape, bf16),
            VMEM(v.shape, bf16),
            *[VMEM(a.shape, a.dtype) for a in (w_out, q_lin, attn_t, x, d_hid)],
            VMEM((model, cols), bf16),
            VMEM((nseq, heads, rows, width), bf16),
            VMEM((nseq, heads, rows, width), bf16),
            VMEM((width, qcount * rows), f32),
            VMEM((qcount * rows, width), bf16),
            VMEM((width, qcount * rows), bf16),
            VMEM((heads, all_but, rows, width), bf16),
            VMEM((heads, all_but, rows, width), bf16),
            VMEM((heads - 1, rows, width), bf16),
            VMEM((heads - 1, rows, width), bf16),
            VMEM((nseq,) + out_block, bf16),
            VMEM((some,) + out_block, bf16),
            VMEM((heads - 1, some) + out_block[1:], bf16),
            VMEM((some,) + out_block[1:], bf16),
            VMEM((some - 1,) + out_block[1:], bf16),
            VMEM((pieces, nseq, qkv_rows, cut), bf16),
            VMEM((pieces, all_but, qkv_rows, cut), bf16),
            VMEM((pieces, heads, qkv_rows // heads, cut), bf16),
            VMEM((pieces, heads - 1, qkv_rows // heads, cut), bf16),
            VMEM((rows, cols), bf16),
        ]
        + [VMEM((n,) + part, bf16) for part, n, _ in parts]
        + [VMEM((n,) + part, bf16) for part, _, n in parts]
        + [
            VMEM((3,) + gains.shape, f32),
            VMEM((some,) + gains.shape, f32),
            VMEM((heads - 1,) + gains.shape, f32),
            pltpu.SemaphoreType.DMA((copies,)),
            pltpu.SemaphoreType.DMA((copies,)),
            pltpu.SemaphoreType.DMA((10 + sum(n for _, n, _ in parts),)),
        ],
        name="tail",
        compiler_params=pltpu.CompilerParams(
            collective_id=cid, has_side_effects=True, vmem_limit_bytes=62 * 2**20
        ),
    )(*arrays)


CHUNKS, SPANS = 4, 2
ORDER = (
    ("ags", 0, 0, 0), ("ags", 0, 1, 0), ("agw", 0, 0, 0), ("ags", 0, 0, 1), ("agw", 0, 1, 0),
    ("ags", 0, 1, 1), ("agw", 0, 0, 1), ("ags", 0, 0, 2), ("agw", 0, 1, 1), ("ags", 0, 1, 2),
    ("ags", 0, 3, 0), ("ags", 0, 2, 0), ("agw", 0, 1, 2), ("agw", 0, 0, 2), ("fa", 0), ("fb", 0),
    ("agw", 0, 3, 0), ("ags", 0, 3, 1), ("agw", 0, 2, 0), ("ags", 0, 2, 1), ("fc", 0),
    ("agw", 0, 3, 1), ("ags", 0, 3, 2), ("rss", 0, 0, 0), ("agw", 0, 2, 1), ("ags", 0, 2, 2),
    ("rsw", 0, 0, 0), ("rss", 0, 1, 0), ("rss", 0, 0, 1), ("rsw", 0, 1, 0), ("rss", 0, 1, 1),
    ("agw", 0, 3, 2), ("agw", 0, 2, 2), ("fa", 1), ("rsw", 0, 0, 1), ("rss", 0, 0, 2), ("fb", 1),
    ("rsw", 0, 1, 1), ("rss", 0, 1, 2), ("fc", 1), ("rss", 0, 2, 0), ("rsw", 0, 0, 2), ("n", 0),
    ("ags", 1, 0, 0), ("rss", 0, 3, 0), ("rsw", 0, 1, 2), ("rsw", 0, 2, 0), ("n", 1),
    ("rss", 0, 2, 1), ("ags", 1, 1, 0), ("agw", 1, 0, 0), ("rsw", 0, 3, 0), ("ags", 1, 0, 1),
    ("rss", 0, 3, 1), ("rsw", 0, 2, 1), ("rss", 0, 2, 2), ("agw", 1, 1, 0), ("ags", 1, 1, 1),
    ("agw", 1, 0, 1), ("ags", 1, 0, 2), ("rsw", 0, 3, 1), ("rss", 0, 3, 2), ("rsw", 0, 2, 2),
    ("n", 2), ("ags", 1, 2, 0), ("agw", 1, 1, 1), ("ags", 1, 1, 2), ("rsw", 0, 3, 2), ("n", 3),
    ("ags", 1, 3, 0), ("agw", 1, 0, 2), ("agw", 1, 2, 0), ("ags", 1, 2, 1), ("agw", 1, 1, 2),
    ("ga", 0), ("gb", 0), ("agw", 1, 3, 0), ("ags", 1, 3, 1), ("gc", 0), ("rss", 1, 1, 0),
    ("agw", 1, 2, 1), ("ags", 1, 2, 2), ("rss", 1, 0, 0), ("agw", 1, 3, 1), ("ags", 1, 3, 2),
    ("rsw", 1, 1, 0), ("rss", 1, 1, 1), ("agw", 1, 2, 2), ("agw", 1, 3, 2), ("wd", 0), ("wd", 1),
    ("dd", 0), ("rsw", 1, 0, 0), ("rsw", 1, 1, 1), ("rss", 1, 0, 1), ("rss", 1, 1, 2), ("ga", 1),
    ("gb", 1), ("gc", 1), ("rss", 1, 2, 0), ("Dd", 0), ("rsw", 1, 0, 1), ("rsw", 1, 1, 2),
    ("rss", 1, 3, 0), ("rss", 1, 0, 2), ("wg", 0), ("rsw", 1, 2, 0), ("e", 1), ("rss", 1, 2, 1),
    ("wg", 1), ("dg", 0), ("rsw", 1, 3, 0), ("rss", 1, 3, 1), ("rsw", 1, 0, 2), ("e", 0),
    ("rsw", 1, 2, 1), ("rss", 1, 2, 2), ("wu", 0), ("rsw", 1, 3, 1), ("rss", 1, 3, 2), ("wu", 1),
    ("rsw", 1, 2, 2), ("e", 2), ("Dg", 0), ("rsw", 1, 3, 2), ("e", 3), ("D2", 0),
)


def ffn_kernel(
    nseq,
    heads,
    chunks,
    spans,
    proj_ref,
    x_ref,
    cot_ref,
    gain_two_ref,
    gain_three_ref,
    gain_four_ref,
    w_gate_ref,
    w_up_ref,
    w_down_ref,
    o_out,
    o_hid,
    o_proj,
    o_gains,
    o_first,
    o_second,
    o_gate,
    o_up,
    hidden,
    w_gate,
    w_up,
    w_down,
    u_all,
    d_all,
    by_gate,
    by_up,
    act,
    d_gate,
    d_up,
    parts,
    from_left,
    from_right,
    flipped,
    dw_gate,
    dw_up,
    dw_down,
    box_gate,
    box_down,
    box_first,
    box_second,
    sum_send,
    sum_recv,
    ag_send,
    ag_recv,
    rs_send,
    rs_recv,
    local_sem,
):
    f32, bf16 = jnp.float32, jnp.bfloat16
    s, h = place()
    last = heads - 1
    right = (s, lax.rem(h + 1, heads))
    left = (s, lax.rem(h + last, heads))
    rows, model = x_ref.shape
    units = w_gate.shape[0]
    rc = rows // chunks
    each = chunks // spans
    many = rc * heads * each
    tile = 512
    whole_tiles, rest = units // tile, units % tile

    loads = []
    for n, (src, dst) in enumerate(
        ((w_gate_ref, w_gate), (w_up_ref, w_up), (w_down_ref, w_down))
    ):
        copy = pltpu.make_async_copy(src, dst, local_sem.at[n])
        copy.start()
        loads.append(copy)
    bits = nseq.bit_length() - 1
    ups, downs = seq_orders(bits)
    links = Links(nseq, heads, sum_send, sum_recv)
    greet([right, left] + [links.across(b) for b in range(bits)])

    proj = proj_ref[...]
    hid = x_ref[...].astype(f32) + norm_rows(proj, flat(gain_two_ref))
    hidden[...] = hid
    u_local = norm_rows(hid, flat(gain_three_ref)).astype(bf16)
    for c in range(chunks):
        u_all[c, h] = u_local[c * rc : (c + 1) * rc]
    o_gains[...] = jnp.zeros_like(o_gains)

    def lanes(k, c, t):
        buf = d_all if k else u_all
        return (
            (
                (h - t >= 0) & (h < last),
                buf.at[c, jnp.maximum(h - t, 0)],
                0,
                right,
                h - 1 - t >= 0,
                buf.at[c, jnp.maximum(h - 1 - t, 0)],
            ),
            (
                (h + t <= last) & (h > 0),
                buf.at[c, jnp.minimum(h + t, last)],
                1,
                left,
                h + 1 + t <= last,
                buf.at[c, jnp.minimum(h + 1 + t, last)],
            ),
        )

    def ags(k, c, t):
        for on, block, lane, target, _, _ in lanes(k, c, t):
            i = (k, c, lane, t)
            pl.when(on)(remote(block, block, ag_send.at[i], ag_recv.at[i], target).start)

    def agw(k, c, t):
        for _, _, lane, target, on, block in lanes(k, c, t):
            i = (k, c, lane, t)
            pl.when(on)(remote(block, block, ag_send.at[i], ag_recv.at[i], target).wait_recv)

    def rss(k, c, t):
        for on, dest, box, lane, target, at_end in (
            ((t >= h) & (h < last), last - (t - h), from_left, 0, right, h == 0),
            ((t >= last - h) & (h > 0), t - (last - h), from_right, 1, left, h == last),
        ):
            dest = jnp.clip(dest, 0, last)
            i = (k, c, lane, t)
            if t > 0:

                def forward(box=box, dest=dest, i=i, target=target):
                    box[k, c, t - 1] = box[k, c, t - 1] + parts[k, c, dest]
                    remote(
                        box.at[k, c, t - 1], box.at[k, c, t], rs_send.at[i], rs_recv.at[i], target
                    ).start()

                pl.when(on & jnp.logical_not(at_end))(forward)
            pl.when(on & at_end)(
                remote(
                    parts.at[k, c, dest], box.at[k, c, t], rs_send.at[i], rs_recv.at[i], target
                ).start
            )

    def rsw(k, c, t):
        for on, box, lane, target in (
            ((t >= h - 1) & (h > 0), from_left, 0, right),
            ((t >= last - h - 1) & (h < last), from_right, 1, left),
        ):
            i = (k, c, lane, t)
            block = box.at[k, c, t]
            pl.when(on)(remote(block, block, rs_send.at[i], rs_recv.at[i], target).wait_recv)

    def summed(k, c):
        zero = jnp.zeros((rc, model), f32)
        return (
            parts[k, c, h].astype(f32)
            + jnp.where(h > 0, from_left[k, c, last - 1].astype(f32), zero)
            + jnp.where(h < last, from_right[k, c, last - 1].astype(f32), zero)
        )

    def over_tiles(lo, hi, body):
        def step(i, carry):
            body(pl.ds(pl.multiple_of(i * tile, tile), tile))
            return carry

        lax.fori_loop(lo, hi, step, 0)
        if hi == whole_tiles and rest:
            body(pl.ds(whole_tiles * tile, rest))

    arrived = set()

    def need(n):
        if n not in arrived:
            arrived.add(n)
            loads[n].wait()

    def span_rows(buf, p):
        return buf[pl.ds(p * each, each)].reshape(many, model)

    def place_parts(k, p, cols, value):
        parts[k, pl.ds(p * each, each), :, :, cols] = value.astype(bf16).reshape(
            each, heads, rc, value.shape[1]
        )

    def forward_tiles(c, lo, hi):
        need(0)
        need(1)

        def body(cols):
            u = span_rows(u_all, c)
            gate = contract_last(u, w_gate[cols, :])
            up = contract_last(u, w_up[cols, :])
            root = math.sqrt(2.0 / math.pi)
            square = gate * gate
            curve = jnp.tanh(root * gate * (1.0 + 0.044715 * square))
            half = 0.5 * (1.0 + curve)
            gelu = gate * half
            slope = half + 0.5 * gate * (1.0 - curve * curve) * (
                root * (1.0 + 3 * 0.044715 * square)
            )
            by_gate[pl.ds(c * many, many), cols] = slope * up
            by_up[pl.ds(c * many, many), cols] = gelu
            act[pl.ds(c * many, many), cols] = (gelu * up).astype(bf16)

        over_tiles(lo, hi, body)

    wide = (model // 2 + 127) // 128 * 128

    def over_columns(body):
        body(pl.ds(0, wide))
        body(pl.ds(wide, model - wide))

    def down_rows(c):
        need(2)

        def body(cols):
            place_parts(
                0,
                c,
                cols,
                jnp.dot(
                    act[pl.ds(c * many, many), :], w_down[:, cols], preferred_element_type=f32
                ),
            )

        over_columns(body)

    def turn(c):
        here = pl.ds(c * rc, rc)
        ffn_out = summed(0, c)
        upstream = cot_ref[here, :].astype(f32)
        o_out[here, :] = (hidden[here, :] + norm_rows(ffn_out, flat(gain_four_ref))).astype(
            o_out.dtype
        )
        d_out, terms = back_norm(ffn_out, flat(gain_four_ref), upstream)
        d_all[c, h] = d_out.astype(bf16)
        o_gains[3:4, :] += terms

    def back_tiles(c, lo, hi):
        def body(cols):
            d_act = contract_last(span_rows(d_all, c), w_down[cols, :])
            d_gate[pl.ds(c * many, many), cols] = (
                d_act * by_gate[pl.ds(c * many, many), cols]
            ).astype(bf16)
            d_up[pl.ds(c * many, many), cols] = (
                d_act * by_up[pl.ds(c * many, many), cols]
            ).astype(bf16)

        over_tiles(lo, hi, body)

    def back_rows(c):
        def body(cols):
            part = jnp.dot(
                d_gate[pl.ds(c * many, many), :], w_gate[:, cols], preferred_element_type=f32
            )
            part = part + jnp.dot(
                d_up[pl.ds(c * many, many), :], w_up[:, cols], preferred_element_type=f32
            )
            place_parts(1, c, cols, part)

        over_columns(body)

    def finish_rows(c):
        here = pl.ds(c * rc, rc)
        d_in, terms = back_norm(hidden[here, :], flat(gain_three_ref), summed(1, c))
        o_gains[2:3, :] += terms
        d_hid = cot_ref[here, :].astype(f32) + d_in
        o_hid[here, :] = d_hid
        d_proj, terms = back_norm(proj_ref[here, :], flat(gain_two_ref), d_hid)
        o_proj[here, :] = d_proj.astype(o_proj.dtype)
        o_gains[1:2, :] += terms

    stores = []

    def flip(source):
        for p in range(spans):
            flipped[:, pl.ds(p * many, many)] = span_rows(source, p).T

    def weight_grad(right_ref, dst, half):
        def body(cols):
            value = jnp.dot(flipped[...], right_ref[:, cols], preferred_element_type=f32)
            dst[:, :, cols] = value.astype(bf16).reshape(dst.shape[:2] + (value.shape[1],))

        over_tiles(half_tiles if half else 0, whole_tiles if half else half_tiles, body)

    half_tiles = (whole_tiles + 1) // 2
    held = subsets(ups)
    sum_gate = Sum(links, lambda m: dw_gate.at[related(s, m)], box_gate, [0])
    sum_down = Sum(links, lambda m: dw_down.at[related(s, m)], box_down, [0])
    for total in (sum_gate, sum_down):
        total.masks = lambda stage: held
    def store(src, dst):
        copy = pltpu.make_async_copy(src, dst, local_sem.at[3 + len(stores)])
        copy.start()
        stores.append(copy)

    split = box_first.shape[1]
    pieces = []
    for box, order, low in ((box_first, ups, 0), (box_second, downs, split)):
        here = pl.ds(low, box.shape[1])
        pieces.append(
            Sum(links, lambda m, here=here: box_down.at[held.index(m), here], box, order)
        )

    for event in ORDER:
        kind, args = event[0], event[1:]
        if kind == "ags":
            ags(*args)
        elif kind == "agw":
            agw(*args)
        elif kind == "rss":
            rss(*args)
        elif kind == "rsw":
            rsw(*args)
        elif kind == "fa":
            forward_tiles(args[0], 0, half_tiles)
        elif kind == "fb":
            forward_tiles(args[0], half_tiles, whole_tiles)
        elif kind == "fc":
            down_rows(args[0])
        elif kind == "n":
            turn(args[0])
        elif kind == "ga":
            back_tiles(args[0], 0, half_tiles)
        elif kind == "gb":
            back_tiles(args[0], half_tiles, whole_tiles)
        elif kind == "gc":
            back_rows(args[0])
        elif kind == "e":
            finish_rows(args[0])
        elif kind == "wd":
            if args[0] == 0:
                flip(d_all)
            weight_grad(act, dw_down, args[0])
        elif kind == "wg":
            if args[0] == 0:
                flip(u_all)
            weight_grad(d_gate, dw_gate, args[0])
        elif kind == "wu":
            weight_grad(d_up, dw_up, args[0])
            if args[0] == 1:
                store(dw_up, o_up)
        elif kind == "dd":
            sum_down.start()
        elif kind == "dg":
            sum_gate.start()
        elif kind == "Dg":
            in_turn(sum_gate.steps(0))
            store(box_gate, o_gate)
        elif kind == "Dd":
            in_turn(sum_down.steps(0))
            for total in pieces:
                for m in total.masks(0):
                    total.send(0, m)
        else:
            for total, out in zip(pieces, (o_first, o_second)):
                for m in total.masks(0):
                    copy, where = total.waiting.pop((0, m))
                    copy.wait_recv()
                    total.boxes[where] = total.boxes[where] + total.current(m)[...]
                store(total.boxes, out)

    for event in ORDER:
        if event[0] == "ags":
            k, c, t = event[1:]
            for on, block, lane, target, _, _ in lanes(k, c, t):
                i = (k, c, lane, t)
                pl.when(on)(remote(block, block, ag_send.at[i], ag_recv.at[i], target).wait_send)
        elif event[0] == "rss":
            k, c, t = event[1:]
            for on, box, lane, target in (
                ((t >= h) & (h < last), from_left, 0, right),
                ((t >= last - h) & (h > 0), from_right, 1, left),
            ):
                i = (k, c, lane, t)
                block = box.at[k, c, t]
                pl.when(on)(remote(block, block, rs_send.at[i], rs_recv.at[i], target).wait_send)
    for n in range(3):
        need(n)
    for copy in stores:
        copy.wait()
    links.finish()


def feed_forward(nseq, heads, cid, *arrays):
    _, x, _, _, _, _, w_gate, w_up, w_down = arrays
    f32, bf16 = jnp.float32, jnp.bfloat16
    rows, model = x.shape
    units = w_gate.shape[0]
    chunks = CHUNKS
    rc = rows // chunks
    group = rows * heads
    vm = pl.BlockSpec(memory_space=VMEM)
    anywhere = pl.BlockSpec(memory_space=pl.ANY)
    block = (model // nseq, units)
    some = nseq // 2
    half = jax.ShapeDtypeStruct((some,) + block, bf16)
    split = split_rows(block[0])
    parts = [(split, units), (block[0] - split, units)]
    messages = 3 * some
    hops = (2, chunks, 2, heads - 1)
    return pl.pallas_call(
        functools.partial(ffn_kernel, nseq, heads, CHUNKS, SPANS),
        out_shape=[
            jax.ShapeDtypeStruct((rows, model), bf16),
            jax.ShapeDtypeStruct((rows, model), f32),
            jax.ShapeDtypeStruct((rows, model), bf16),
            jax.ShapeDtypeStruct((8, model), f32),
            *[jax.ShapeDtypeStruct((some // 2,) + part, bf16) for part in parts],
            half,
            jax.ShapeDtypeStruct((nseq,) + block, bf16),
        ],
        in_specs=[vm] * 6 + [anywhere] * 3,
        out_specs=[vm] * 4 + [anywhere] * 4,
        scratch_shapes=[
            VMEM((rows, model), f32),
            VMEM(w_gate.shape, bf16),
            VMEM(w_up.shape, bf16),
            VMEM(w_down.shape, bf16),
            VMEM((chunks, heads, rc, model), bf16),
            VMEM((chunks, heads, rc, model), bf16),
            VMEM((group, units), f32),
            VMEM((group, units), f32),
            VMEM((group, units), bf16),
            VMEM((group, units), bf16),
            VMEM((group, units), bf16),
            VMEM((2, chunks, heads, rc, model), bf16),
            VMEM((2, chunks, heads - 1, rc, model), bf16),
            VMEM((2, chunks, heads - 1, rc, model), bf16),
            VMEM((model, group), bf16),
            VMEM((nseq,) + block, bf16),
            VMEM((nseq,) + block, bf16),
            VMEM((nseq,) + block, bf16),
            VMEM((some,) + block, bf16),
            VMEM((some,) + block, bf16),
            *[VMEM((some // 2,) + part, bf16) for part in parts],
            pltpu.SemaphoreType.DMA((messages,)),
            pltpu.SemaphoreType.DMA((messages,)),
            pltpu.SemaphoreType.DMA(hops),
            pltpu.SemaphoreType.DMA(hops),
            pltpu.SemaphoreType.DMA(hops),
            pltpu.SemaphoreType.DMA(hops),
            pltpu.SemaphoreType.DMA((7,)),
        ],
        name="feed_forward",
        compiler_params=pltpu.CompilerParams(
            collective_id=cid, has_side_effects=True, vmem_limit_bytes=62 * 2**20
        ),
    )(*arrays)


def finish_kernel(nseq, qw, width, each, few, *refs):
    out, tokens, qkv, w_out, gate, up, down, gains = refs[:8]
    o_out, o_tokens, o_query, o_key, o_value, o_w_out, o_gate, o_up, o_down = refs[8:17]
    o_gains = refs[17:]
    s, h = place()
    which = s * lax.axis_size("head") + h
    o_out[...] = out[...]
    o_tokens[...] = tokens[...]
    o_query[...] = qkv[:, :qw]
    o_key[...] = qkv[:, qw : qw + width]
    o_value[...] = qkv[:, qw + width :]
    o_w_out[...] = w_out[...]
    o_gate[...] = gate[...].astype(jnp.float32)
    o_up[...] = up[...].astype(jnp.float32)
    o_down[...] = down[...].astype(jnp.float32)
    model = gains.shape[1]
    wide = pltpu.roll(gains[...], lax.rem(model - which * each, model), 1)
    narrow = pltpu.roll(gains[...], lax.rem(model - which * few, model), 1)
    for i in range(4):
        o_gains[i][...] = wide[i : i + 1, :each]
    for i in range(4, 6):
        o_gains[i][...] = narrow[i : i + 1, :few]


def finish(nseq, qw, width, each, few, *arrays):
    out, tokens, qkv, w_out, gate, up, down, gains = arrays
    vm = pl.BlockSpec(memory_space=VMEM)
    shape = lambda a: jax.ShapeDtypeStruct(a.shape, a.dtype)
    f32 = jnp.float32
    rows = qkv.shape[0]
    wide, narrow = jax.ShapeDtypeStruct((1, each), f32), jax.ShapeDtypeStruct((1, few), f32)
    return pl.pallas_call(
        functools.partial(finish_kernel, nseq, qw, width, each, few),
        out_shape=[shape(out), shape(tokens)]
        + [jax.ShapeDtypeStruct((rows, n), f32) for n in (qw, width, width)]
        + [jax.ShapeDtypeStruct(a.shape, f32) for a in (w_out, gate, up, down)]
        + [wide] * 4
        + [narrow] * 2,
        in_specs=[vm] * 8,
        out_specs=[vm] * 15,
        name="finish",
        compiler_params=pltpu.CompilerParams(vmem_limit_bytes=LIMIT),
    )(*arrays)


def local(
    tokens,
    segment_ids,
    w_query,
    w_key,
    w_value,
    w_out,
    w_gate,
    w_up,
    w_down,
    gain_attn_in,
    gain_attn_out,
    gain_ffn_in,
    gain_ffn_out,
    gain_query,
    gain_key,
    cotangent,
):
    heads = lax.axis_size("head")
    nseq = lax.axis_size("seq")
    head_index = lax.axis_index("head")
    seq_index = lax.axis_index("seq")
    bits = nseq.bit_length() - 1
    local_rows, model = tokens.shape
    width = gain_query.shape[0]
    qcount = w_query.shape[1] // width
    group = local_rows * heads
    total = segment_ids.shape[0]
    hidden_units = w_gate.shape[1]
    scale = 1.0 / math.sqrt(width)
    bf16 = jnp.bfloat16
    if (nseq, heads) == (8, 4) and (model // nseq) % 16 == 0:
        qw = qcount * width
        each, few = model // (nseq * heads), width // (nseq * heads)
        (
            projected,
            queries,
            keys,
            values,
            starts,
            index,
            log_total,
            attended_t,
            q_linear,
            k_linear,
            cosines,
            sines,
            attn_t,
        ) = front(
            nseq,
            heads,
            qcount,
            scale,
            11,
            tokens,
            segment_ids,
            w_key,
            w_value,
            gain_attn_in,
            gain_query,
            gain_key,
            w_query,
            w_out,
        )
        output, d_hidden, d_projected, gains, down_first, down_second, half_gate, all_up = feed_forward(
            nseq,
            heads,
            10,
            projected,
            tokens,
            cotangent,
            gain_attn_out,
            gain_ffn_in,
            gain_ffn_out,
            w_gate.T,
            w_up.T,
            w_down,
        )
        grad_tokens, sum_qkv, sum_out, sum_gate, sum_up, sum_down, sum_gains = tail(
            nseq,
            heads,
            qcount,
            scale,
            9,
            queries,
            starts,
            index,
            log_total,
            attended_t,
            d_projected,
            k_linear,
            cosines,
            sines,
            gain_query,
            gain_key,
            gain_attn_in,
            gains,
            keys.reshape(nseq, group, width),
            values.reshape(nseq, group, width),
            w_out,
            q_linear,
            attn_t,
            tokens,
            d_hidden,
            w_query,
            w_key,
            w_value,
            half_gate,
            all_up,
            down_first,
            down_second,
        )
        (
            output,
            grad_tokens,
            sum_query,
            sum_key,
            sum_value,
            sum_out,
            sum_gate,
            sum_up,
            sum_down,
            *sum_gains,
        ) = finish(
            nseq,
            qw,
            width,
            each,
            few,
            output,
            grad_tokens,
            sum_qkv,
            sum_out,
            sum_gate,
            sum_up,
            sum_down,
            sum_gains,
        )
        return (
            output,
            grad_tokens,
            sum_query,
            sum_key,
            sum_value,
            sum_out,
            sum_gate,
            sum_up,
            sum_down.T,
            *[g[0] for g in sum_gains],
        )
    first_row = (seq_index * heads + head_index) * local_rows
    my_index = first_row + jnp.arange(local_rows, dtype=jnp.int32)
    my_ids = lax.dynamic_slice_in_dim(segment_ids, first_row, local_rows)
    my_starts = jnp.min(
        jnp.where(
            my_ids[:, None] == segment_ids[None, :],
            jnp.arange(total, dtype=jnp.int32)[None, :],
            total,
        ),
        axis=1,
    )
    cosines, sines = rope_tables(my_index - my_starts, width)

    def query_path(linear, gain):
        shaped = linear.reshape(local_rows, qcount, width)
        turned = rotate(norm_rows(shaped, gain), cosines[:, None, :], sines[:, None, :])
        return turned.reshape(local_rows, qcount * width)

    def key_path(linear, gain):
        return rotate(norm_rows(linear, gain), cosines, sines)

    def gated(gate, up):
        return jax.nn.gelu(gate, approximate=True) * up

    def stacked(v):
        return v.reshape(local_rows, qcount, width).transpose(1, 0, 2).reshape(-1, width)

    def unstacked(v):
        return v.reshape(qcount, local_rows, width).transpose(1, 0, 2).reshape(local_rows, -1)

    inputs = tokens.astype(jnp.float32)
    attn_in = norm_rows(inputs, gain_attn_in).astype(bf16)
    k_linear = jnp.dot(attn_in, w_key, preferred_element_type=jnp.float32)
    keys_local = key_path(k_linear, gain_key).astype(bf16)
    values_local = jnp.dot(attn_in, w_value, preferred_element_type=jnp.float32).astype(bf16)
    q_linear = jnp.dot(attn_in, w_query, preferred_element_type=jnp.float32)
    queries_local = query_path(q_linear, gain_query).astype(bf16)
    queries = stacked(queries_local) * jnp.asarray(scale, bf16)
    keys, values = gather_all([keys_local, values_local], nseq, heads, 1)
    keys = keys.reshape(nseq, group, width)
    values = values.reshape(nseq, group, width)
    starts = jnp.tile(my_starts, qcount)[None, :]
    index = jnp.tile(my_index, qcount)[None, :]
    attended_t, log_total = attend(queries, keys, values, starts, index)
    attended = attended_t.T
    mixed_local = unstacked(attended.astype(bf16))
    projected = jnp.dot(mixed_local, w_out, preferred_element_type=jnp.float32)
    hidden = inputs + norm_rows(projected, gain_attn_out)
    ffn_in = norm_rows(hidden, gain_ffn_in).astype(bf16)
    ffn_rows = line_gather(ffn_in, heads, 2).reshape(group, model)
    gate = jnp.dot(ffn_rows, w_gate, preferred_element_type=jnp.float32)
    up = jnp.dot(ffn_rows, w_up, preferred_element_type=jnp.float32)
    activated = gated(gate, up).astype(bf16)
    ffn_out = line_scatter(
        jnp.dot(activated, w_down, preferred_element_type=jnp.float32)
        .astype(bf16)
        .reshape(heads, local_rows, model),
        heads,
        3,
    )
    output = hidden + norm_rows(ffn_out, gain_ffn_out)
    upstream = cotangent.astype(jnp.float32)
    unused, back_four = jax.vjp(norm_rows, ffn_out, gain_ffn_out)
    d_ffn_out, d_gain_four = back_four(upstream)
    d_ffn_rows = line_gather(d_ffn_out.astype(bf16), heads, 4).reshape(group, model)
    d_activated = contract_last(d_ffn_rows, w_down)
    d_w_down = contract_first(d_ffn_rows, activated)
    unused, back_gate = jax.vjp(gated, gate, up)
    d_gate, d_up = back_gate(d_activated)
    d_gate = d_gate.astype(bf16)
    d_up = d_up.astype(bf16)
    d_ffn_in = line_scatter(
        (contract_last(d_gate, w_gate) + contract_last(d_up, w_up))
        .astype(bf16)
        .reshape(heads, local_rows, model),
        heads,
        5,
    )
    d_w_gate = contract_first(ffn_rows, d_gate)
    d_w_up = contract_first(ffn_rows, d_up)
    unused, back_three = jax.vjp(norm_rows, hidden, gain_ffn_in)
    d_hidden_part, d_gain_three = back_three(d_ffn_in)
    d_hidden = upstream + d_hidden_part
    unused, back_two = jax.vjp(norm_rows, projected, gain_attn_out)
    d_projected, d_gain_two = back_two(d_hidden)
    d_projected = d_projected.astype(bf16)
    qw = qcount * width
    d_w_out = contract_first(mixed_local, d_projected)
    d_mixed = contract_last(d_projected, w_out).astype(bf16)
    grad_attended = stacked(d_mixed)
    row_dots = jnp.sum(grad_attended.astype(jnp.float32) * attended, axis=1)[None, :]
    d_queries_t, d_keys, d_values = attend_back(
        queries, keys, values, starts, index, log_total, row_dots, grad_attended
    )
    shape = (nseq, heads, local_rows, width)
    ups, downs = seq_orders(bits)
    d_keys, d_values = scatter_all(
        [d_keys.reshape(shape), d_values.reshape(shape)],
        [True, True],
        [[0] + ups, [0] + downs],
        nseq,
        heads,
        6,
        "scatter_keys",
    )
    d_query_rot = unstacked((d_queries_t.T * scale).astype(bf16)).astype(jnp.float32)
    unused, back_query = jax.vjp(query_path, q_linear, gain_query)
    d_q_linear, d_gain_query = back_query(d_query_rot)
    unused, back_key = jax.vjp(key_path, k_linear, gain_key)
    d_k_linear, d_gain_key = back_key(d_keys)
    d_qkv = jnp.concatenate([d_q_linear, d_k_linear, d_values], axis=1).astype(bf16)
    qw = qcount * width
    d_w_qkv = contract_first(attn_in, d_qkv)
    d_attn_in = (
        contract_last(d_qkv[:, :qw], w_query)
        + contract_last(d_qkv[:, qw : qw + width], w_key)
        + contract_last(d_qkv[:, qw + width :], w_value)
    )
    unused, back_one = jax.vjp(norm_rows, inputs, gain_attn_in)
    d_inputs, d_gain_one = back_one(d_attn_in)
    grad_tokens = (d_hidden + d_inputs).astype(bf16)

    def cut(v):
        return v.reshape(nseq, heads, -1)

    wide = jnp.stack([cut(d_gain_one), cut(d_gain_two), cut(d_gain_three), cut(d_gain_four)], 2)
    narrow = jnp.stack([cut(d_gain_query), cut(d_gain_key)], 2)
    each, few = wide.shape[-1], narrow.shape[-1]
    gains = jnp.concatenate(
        [
            jnp.pad(wide, ((0, 0), (0, 0), (0, 0), (0, 128 - each))),
            jnp.pad(narrow, ((0, 0), (0, 0), (0, 2), (0, 128 - few))),
        ],
        axis=2,
    )
    sum_qkv, sum_out, sum_gains = scatter_all(
        [
            d_w_qkv.astype(bf16).reshape(nseq, heads, -1, d_qkv.shape[1]),
            d_w_out.astype(bf16).reshape(nseq, heads, -1, model),
            gains,
        ],
        [True, True, True],
        [[0] + ups, [0] + downs, [0] + downs],
        nseq,
        heads,
        7,
        "scatter_attn",
    )
    sum_gate, sum_up, sum_down = scatter_all(
        [
            d.astype(bf16).reshape(nseq, model // nseq, hidden_units)
            for d in (d_w_gate, d_w_up, d_w_down)
        ],
        [False, False, False],
        [[0] + ups, [0] + downs, [0] + ups],
        nseq,
        heads,
        8,
        "scatter_ffn",
    )
    return (
        output.astype(bf16),
        grad_tokens,
        sum_qkv[:, :qw],
        sum_qkv[:, qw : qw + width],
        sum_qkv[:, qw + width :],
        sum_out,
        sum_gate,
        sum_up,
        sum_down.T,
        sum_gains[0, :each],
        sum_gains[1, :each],
        sum_gains[2, :each],
        sum_gains[3, :each],
        sum_gains[4, :few],
        sum_gains[5, :few],
    )


def solution(mesh):
    rows = P(("seq", "head"), None)
    in_specs = (
        rows,
        P(),
        P(),
        P(),
        P(),
        P(),
        P(None, "head"),
        P(None, "head"),
        P("head", None),
        P(),
        P(),
        P(),
        P(),
        P(),
        P(),
        rows,
    )
    out_specs = (
        rows,
        rows,
        rows,
        rows,
        rows,
        rows,
        P("seq", "head"),
        P("seq", "head"),
        P("head", "seq"),
    ) + (P(("seq", "head")),) * 6
    return jax.shard_map(local, mesh=mesh, in_specs=in_specs, out_specs=out_specs, check_vma=False)
```

```python
import functools
import itertools
import math

import jax
import jax.numpy as jnp
from jax import lax
from jax.experimental import pallas as pl
from jax.experimental.pallas import tpu as pltpu
from jax.sharding import PartitionSpec as P

EPS = 1e-06
MESH = pl.DeviceIdType.MESH
VMEM = pltpu.VMEM
LIMIT = 56 * 2**20


def norm_rows(v, gain):
    return v * lax.rsqrt(jnp.mean(v * v, axis=-1, keepdims=True) + EPS) * gain


def rotate(v, cosines, sines):
    half = v.shape[-1] // 2
    first = v[..., :half]
    second = v[..., half:]
    return jnp.concatenate(
        [first * cosines - second * sines, second * cosines + first * sines], axis=-1
    )


def rope_tables(positions, width):
    half = width // 2
    freq = jnp.exp(jnp.arange(half, dtype=jnp.float32) * (-2.0 * math.log(1000000.0) / width))
    angle = positions.astype(jnp.float32)[:, None] * freq[None, :]
    return (jnp.cos(angle), jnp.sin(angle))


def contract_first(left, right):
    return lax.dot_general(
        left, right, (((0,), (0,)), ((), ())), preferred_element_type=jnp.float32
    )


def contract_last(left, right):
    return lax.dot_general(
        left, right, (((1,), (1,)), ((), ())), preferred_element_type=jnp.float32
    )


def place():
    return lax.axis_index("seq"), lax.axis_index("head")


def related(s, mask):
    out = s
    bit = 0
    while mask >> bit:
        if (mask >> bit) & 1:
            step = 1 << bit
            out = out + (1 - 2 * ((s // step) % 2)) * step
        bit += 1
    return out


def subsets(bits):
    out = [0]
    for bit in bits:
        out = out + [m | (1 << bit) for m in out]
    return out


def greet(targets):
    barrier = pltpu.get_barrier_semaphore()
    for target in targets:
        pl.semaphore_signal(barrier, inc=1, device_id=target, device_id_type=MESH)
    pl.semaphore_wait(barrier, len(targets))


def remote(src, dst, send, recv, target):
    return pltpu.make_async_remote_copy(
        src_ref=src,
        dst_ref=dst,
        send_sem=send,
        recv_sem=recv,
        device_id=target,
        device_id_type=MESH,
    )


def seq_orders(bits):
    upper = list(range(1, bits))
    return upper, upper[::-1]


def gather_kernel(nseq, heads, local_refs, out_refs, send, recv):
    bits = nseq.bit_length() - 1
    s, h = place()
    others = [lax.rem(h + d, heads) for d in range(1, heads)]
    greet([(related(s, 1 << b), h) for b in range(bits)] + [(s, o) for o in others])
    count = [0]
    started = []

    def go(src, dst, target):
        k = count[0]
        count[0] += 1
        copy = remote(src, dst, send.at[k], recv.at[k], target)
        copy.start()
        started.append(copy)
        return copy

    first = []
    for a in range(len(out_refs)):
        out_refs[a][s, h] = local_refs[a][...]
        first.append(
            [go(local_refs[a], out_refs[a].at[s, h], (s, o)) for o in others]
        )
    orders = [o + [0] for o in seq_orders(bits)]
    held = [{0: first[a]} for a in range(len(out_refs))]
    for stage in range(bits):
        for a in range(len(out_refs)):
            bit = orders[a % 2][stage]
            target = (related(s, 1 << bit), h)
            arrived = {}
            for mask in list(held[a]):
                for copy in held[a][mask]:
                    copy.wait_recv()
                held[a][mask] = []
                group = related(s, mask)
                copy = go(out_refs[a].at[group], out_refs[a].at[group], target)
                arrived[mask | (1 << bit)] = [copy]
            held[a].update(arrived)
    for a in range(len(out_refs)):
        for mask in held[a]:
            for copy in held[a][mask]:
                copy.wait_recv()
    for copy in started:
        copy.wait_send()


def gather_all(arrays, nseq, heads, cid):
    n = len(arrays)
    total = n * (heads - 1 + nseq - 1)

    def kernel(*refs):
        gather_kernel(nseq, heads, refs[:n], refs[n : 2 * n], refs[2 * n], refs[2 * n + 1])

    return pl.pallas_call(
        kernel,
        out_shape=[jax.ShapeDtypeStruct((nseq, heads) + a.shape, a.dtype) for a in arrays],
        in_specs=[pl.BlockSpec(memory_space=VMEM)] * n,
        out_specs=[pl.BlockSpec(memory_space=VMEM)] * n,
        scratch_shapes=[pltpu.SemaphoreType.DMA((total,)), pltpu.SemaphoreType.DMA((total,))],
        name="gather_all",
        compiler_params=pltpu.CompilerParams(
            collective_id=cid, has_side_effects=True, vmem_limit_bytes=LIMIT
        ),
    )(*arrays)


def line_gather_kernel(heads, x_ref, out_ref, send, recv):
    s, h = place()
    right = (s, lax.rem(h + 1, heads))
    left = (s, lax.rem(h + heads - 1, heads))
    greet([right, left])
    out_ref[h] = x_ref[...]
    for step in range(heads - 1):
        to_right = remote(
            out_ref.at[jnp.maximum(h - step, 0)],
            out_ref.at[jnp.maximum(h - step, 0)],
            send.at[0, step],
            recv.at[0, step],
            right,
        )
        to_left = remote(
            out_ref.at[jnp.minimum(h + step, heads - 1)],
            out_ref.at[jnp.minimum(h + step, heads - 1)],
            send.at[1, step],
            recv.at[1, step],
            left,
        )
        pl.when((h - step >= 0) & (h < heads - 1))(to_right.start)
        pl.when((h + step <= heads - 1) & (h > 0))(to_left.start)
        pl.when(h - 1 - step >= 0)(
            remote(
                out_ref.at[jnp.maximum(h - 1 - step, 0)],
                out_ref.at[jnp.maximum(h - 1 - step, 0)],
                send.at[0, step],
                recv.at[0, step],
                right,
            ).wait_recv
        )
        pl.when(h + 1 + step <= heads - 1)(
            remote(
                out_ref.at[jnp.minimum(h + 1 + step, heads - 1)],
                out_ref.at[jnp.minimum(h + 1 + step, heads - 1)],
                send.at[1, step],
                recv.at[1, step],
                left,
            ).wait_recv
        )
        pl.when((h - step >= 0) & (h < heads - 1))(to_right.wait_send)
        pl.when((h + step <= heads - 1) & (h > 0))(to_left.wait_send)


def line_gather(x, heads, cid):
    return pl.pallas_call(
        functools.partial(line_gather_kernel, heads),
        out_shape=jax.ShapeDtypeStruct((heads,) + x.shape, x.dtype),
        in_specs=[pl.BlockSpec(memory_space=VMEM)],
        out_specs=pl.BlockSpec(memory_space=VMEM),
        scratch_shapes=[
            pltpu.SemaphoreType.DMA((2, heads - 1)),
            pltpu.SemaphoreType.DMA((2, heads - 1)),
        ],
        name="line_gather",
        compiler_params=pltpu.CompilerParams(
            collective_id=cid, has_side_effects=True, vmem_limit_bytes=LIMIT
        ),
    )(x)


def line_scatter_kernel(heads, parts, out_ref, from_left, from_right, send, recv):
    s, h = place()
    last = heads - 1
    right = (s, lax.rem(h + 1, heads))
    left = (s, lax.rem(h + heads - 1, heads))
    greet([right, left])
    f32 = jnp.float32
    for step in range(heads - 1):
        r_dest = jnp.clip(last - (step - h), 0, last)
        l_dest = jnp.clip(step - (last - h), 0, last)
        r_on = (step >= h) & (h < last)
        l_on = (step >= last - h) & (h > 0)
        for on, dest, box, lane, target, first in (
            (r_on, r_dest, from_left, 0, right, step == h),
            (l_on, l_dest, from_right, 1, left, step == last - h),
        ):
            at_end = (h == 0) if lane == 0 else (h == last)
            if step > 0:

                def add(box=box, dest=dest):
                    box[step - 1] = (
                        box[step - 1].astype(f32) + parts[dest].astype(f32)
                    ).astype(box.dtype)

                pl.when(on & jnp.logical_not(at_end))(add)
                pl.when(on & jnp.logical_not(at_end))(
                    remote(
                        box.at[step - 1], box.at[step], send.at[lane, step], recv.at[lane, step], target
                    ).start
                )
            pl.when(on & at_end)(
                remote(
                    parts.at[dest], box.at[step], send.at[lane, step], recv.at[lane, step], target
                ).start
            )
        r_in = (step >= h - 1) & (h > 0)
        l_in = (step >= last - h - 1) & (h < last)
        pl.when(r_in)(
            remote(
                from_left.at[step], from_left.at[step], send.at[0, step], recv.at[0, step], right
            ).wait_recv
        )
        pl.when(l_in)(
            remote(
                from_right.at[step], from_right.at[step], send.at[1, step], recv.at[1, step], left
            ).wait_recv
        )
    for step in range(heads - 1):
        for on, box, lane, target in (
            ((step >= h) & (h < last), from_left, 0, right),
            ((step >= last - h) & (h > 0), from_right, 1, left),
        ):
            pl.when(on)(
                remote(
                    box.at[step], box.at[step], send.at[lane, step], recv.at[lane, step], target
                ).wait_send
            )
    out_ref[...] = parts[h].astype(f32)

    def add_left():
        out_ref[...] += from_left[heads - 2].astype(f32)

    def add_right():
        out_ref[...] += from_right[heads - 2].astype(f32)

    pl.when(h > 0)(add_left)
    pl.when(h < last)(add_right)


def line_scatter(parts, heads, cid):
    block = parts.shape[1:]
    return pl.pallas_call(
        functools.partial(line_scatter_kernel, heads),
        out_shape=jax.ShapeDtypeStruct(block, jnp.float32),
        in_specs=[pl.BlockSpec(memory_space=VMEM)],
        out_specs=pl.BlockSpec(memory_space=VMEM),
        scratch_shapes=[
            VMEM((heads - 1,) + block, parts.dtype),
            VMEM((heads - 1,) + block, parts.dtype),
            pltpu.SemaphoreType.DMA((2, heads - 1)),
            pltpu.SemaphoreType.DMA((2, heads - 1)),
        ],
        name="line_scatter",
        compiler_params=pltpu.CompilerParams(
            collective_id=cid, has_side_effects=True, vmem_limit_bytes=LIMIT
        ),
    )(parts)


def scatter_kernel(nseq, heads, zs, orders, parts, outs, boxes, zboxes, send, recv):
    bits = nseq.bit_length() - 1
    s, h = place()
    f32 = jnp.float32
    others = [lax.rem(h + d, heads) for d in range(1, heads)]
    greet(
        [(related(s, 1 << b), h) for b in range(bits)]
        + ([(s, o) for o in others] if any(zs) else [])
    )
    count = [0]
    started = []

    def go(src, dst, target):
        k = count[0]
        count[0] += 1
        copy = remote(src, dst, send.at[k], recv.at[k], target)
        copy.start()
        started.append(copy)
        return copy

    n = len(parts)
    offsets = [0] * n
    slot = [{} for _ in range(n)]
    waiting = [{} for _ in range(n)]

    def current(a, mask):
        if mask in slot[a]:
            return boxes[a].at[slot[a][mask]]
        return parts[a].at[related(s, mask)]

    def launch(a, stage):
        bit = orders[a][stage]
        rest = orders[a][stage + 1 :]
        target = (related(s, 1 << bit), h)
        after = 1 << rest[0] if rest else 0
        masks = sorted(subsets(rest), key=lambda m: 0 if m & after else 1)
        for mask in masks:
            where = offsets[a]
            offsets[a] += 1
            waiting[a][mask] = (
                go(current(a, mask | (1 << bit)), boxes[a].at[where], target),
                where,
            )

    def settle(a, mask):
        copy, where = waiting[a].pop(mask)
        mine = current(a, mask)
        copy.wait_recv()
        boxes[a][where] = (boxes[a][where].astype(f32) + mine[...].astype(f32)).astype(
            boxes[a].dtype
        )
        slot[a][mask] = where

    for a in range(n):
        launch(a, 0)
    for stage in range(bits):
        for a in range(n):
            for mask in list(waiting[a]):
                settle(a, mask)
            if stage + 1 < bits:
                launch(a, stage + 1)
    arriving = []
    for a in range(n):
        if not zs[a]:
            continue
        mine = current(a, 0)
        arriving.append(
            [
                go(mine.at[o], zboxes[a].at[d], (s, o))
                for d, o in enumerate(others)
            ]
        )
    z = 0
    for a in range(n):
        if zs[a]:
            total = current(a, 0)[h].astype(f32)
            for d, copy in enumerate(arriving[z]):
                copy.wait_recv()
                total = total + zboxes[a][d].astype(f32)
            outs[a][...] = total
            z += 1
        else:
            outs[a][...] = current(a, 0)[...].astype(f32)
    for copy in started:
        copy.wait_send()


def scatter_all(arrays, zs, orders, nseq, heads, cid, name):
    n = len(arrays)
    total = sum((nseq - 1) + (heads - 1 if z else 0) for z in zs)
    blocks = [a.shape[2:] if z else a.shape[1:] for a, z in zip(arrays, zs)]

    def kernel(*refs):
        scatter_kernel(
            nseq,
            heads,
            zs,
            orders,
            refs[:n],
            refs[n : 2 * n],
            refs[2 * n : 3 * n],
            refs[3 * n : 4 * n],
            refs[4 * n],
            refs[4 * n + 1],
        )

    return pl.pallas_call(
        kernel,
        out_shape=[jax.ShapeDtypeStruct(b, jnp.float32) for b in blocks],
        in_specs=[pl.BlockSpec(memory_space=VMEM)] * n,
        out_specs=[pl.BlockSpec(memory_space=VMEM)] * n,
        scratch_shapes=[VMEM((nseq - 1,) + a.shape[1:], a.dtype) for a in arrays]
        + [
            VMEM((heads - 1,) + b, a.dtype) if z else VMEM((8, 128), jnp.float32)
            for a, b, z in zip(arrays, blocks, zs)
        ]
        + [pltpu.SemaphoreType.DMA((total,)), pltpu.SemaphoreType.DMA((total,))],
        name=name,
        compiler_params=pltpu.CompilerParams(
            collective_id=cid, has_side_effects=True, vmem_limit_bytes=LIMIT
        ),
    )(*arrays)


def attend_kernel(q_ref, k_ref, v_ref, start_ref, index_ref, out_ref, log_ref):
    s = lax.axis_index("seq")
    span = k_ref.shape[1]
    start = start_ref[...]
    index = index_ref[...]
    queries = q_ref[...]
    rows = queries.shape[0]
    out_ref[...] = jnp.zeros_like(out_ref)

    def step(g, mass):
        scores = contract_last(k_ref[g], queries)
        key = g * span + lax.broadcasted_iota(jnp.int32, (span, rows), 0)
        terms = jnp.where((key >= start) & (key <= index), jnp.exp(scores), 0.0)
        out_ref[...] += contract_first(v_ref[g], terms.astype(jnp.bfloat16))
        return mass + jnp.sum(terms, axis=0, keepdims=True)

    mass = lax.fori_loop(0, s + 1, step, jnp.zeros((1, rows), jnp.float32))
    out_ref[...] = out_ref[...] / mass
    log_ref[...] = jnp.log(mass)


def attend(q, k, v, start, index):
    rows, width = q.shape
    return pl.pallas_call(
        attend_kernel,
        out_shape=[
            jax.ShapeDtypeStruct((width, rows), jnp.float32),
            jax.ShapeDtypeStruct((1, rows), jnp.float32),
        ],
        in_specs=[pl.BlockSpec(memory_space=VMEM)] * 5,
        out_specs=[pl.BlockSpec(memory_space=VMEM)] * 2,
        name="attend",
        compiler_params=pltpu.CompilerParams(vmem_limit_bytes=LIMIT),
    )(q, k, v, start, index)


def attend_back_kernel(
    q_ref, k_ref, v_ref, start_ref, index_ref, log_ref, dots_ref, d_ref, dq_ref, dk_ref, dv_ref
):
    s = lax.axis_index("seq")
    groups, span = k_ref.shape[:2]
    start = start_ref[...]
    index = index_ref[...]
    log_total = log_ref[...]
    dots = dots_ref[...]
    queries = q_ref[...]
    grads = d_ref[...]
    rows = queries.shape[0]
    dq_ref[...] = jnp.zeros_like(dq_ref)

    def step(g, carry):
        keys = k_ref[g]
        scores = contract_last(keys, queries)
        key = g * span + lax.broadcasted_iota(jnp.int32, (span, rows), 0)
        probs = jnp.where((key >= start) & (key <= index), jnp.exp(scores - log_total), 0.0)
        d_probs = contract_last(v_ref[g], grads)
        d_scores = (probs * (d_probs - dots)).astype(jnp.bfloat16)
        dv_ref[g] = jnp.dot(
            probs.astype(jnp.bfloat16), grads, preferred_element_type=jnp.float32
        ).astype(dv_ref.dtype)
        dk_ref[g] = jnp.dot(d_scores, queries, preferred_element_type=jnp.float32).astype(
            dk_ref.dtype
        )
        dq_ref[...] += contract_first(keys, d_scores)
        return carry

    lax.fori_loop(0, s + 1, step, 0)

    def blank(g, carry):
        dk_ref[g] = jnp.zeros(dk_ref.shape[1:], dk_ref.dtype)
        dv_ref[g] = jnp.zeros(dv_ref.shape[1:], dv_ref.dtype)
        return carry

    lax.fori_loop(s + 1, groups, blank, 0)


def attend_back(q, k, v, start, index, log_total, dots, grads):
    rows, width = q.shape
    return pl.pallas_call(
        attend_back_kernel,
        out_shape=[
            jax.ShapeDtypeStruct((width, rows), jnp.float32),
            jax.ShapeDtypeStruct(k.shape, jnp.bfloat16),
            jax.ShapeDtypeStruct(v.shape, jnp.bfloat16),
        ],
        in_specs=[pl.BlockSpec(memory_space=VMEM)] * 8,
        out_specs=[pl.BlockSpec(memory_space=VMEM)] * 3,
        name="attend_back",
        compiler_params=pltpu.CompilerParams(vmem_limit_bytes=LIMIT),
    )(q, k, v, start, index, log_total, dots, grads)


def flat(ref):
    return ref[...].reshape(1, ref.shape[0])


def front_kernel(
    nseq,
    heads,
    qcount,
    scale,
    x_ref,
    ids_ref,
    w_key_ref,
    w_value_ref,
    gain_in_ref,
    gain_q_ref,
    gain_k_ref,
    w_query_far,
    w_out_far,
    o_proj,
    o_q,
    o_k,
    o_v,
    o_start,
    o_index,
    o_log,
    o_att,
    o_q_lin,
    o_k_lin,
    o_cos,
    o_sin,
    o_attn_t,
    w_query,
    w_out,
    k_all,
    v_all,
    send,
    recv,
    local_sem,
):
    f32, bf16 = jnp.float32, jnp.bfloat16
    bits = nseq.bit_length() - 1
    ups, downs = seq_orders(bits)
    links = Links(nseq, heads, send, recv)
    s, h = links.s, links.h
    rows, model = x_ref.shape
    width = w_key_ref.shape[1]
    gain_q, gain_k = flat(gain_q_ref), flat(gain_k_ref)
    half = width // 2
    total = ids_ref.shape[0] * ids_ref.shape[1]
    load_q = pltpu.make_async_copy(w_query_far, w_query, local_sem.at[0])
    load_q.start()
    load_o = pltpu.make_async_copy(w_out_far, w_out, local_sem.at[1])
    load_o.start()
    partners = [related(h, j) for j in range(1, heads)]
    greet([links.across(b) for b in range(bits)] + [(s, o) for o in partners])

    which = s * heads + h
    mine = ids_ref[pl.ds(which, 1), :].astype(f32)
    column = jnp.broadcast_to(mine, (rows, rows)).T[:, 0:1]
    first = jnp.full((rows, rows), float(total), f32)
    for r in range(ids_ref.shape[0]):
        here = ids_ref[r : r + 1, :].astype(f32)
        at = (r * rows + lax.broadcasted_iota(jnp.int32, (1, rows), 1)).astype(f32)
        first = jnp.minimum(first, jnp.where(column == here, at, float(total)))
    start = jnp.min(first, axis=1, keepdims=True)
    index = (which * rows + lax.broadcasted_iota(jnp.int32, (rows, 1), 0)).astype(f32)
    freq = jnp.exp(
        lax.broadcasted_iota(jnp.int32, (1, half), 1).astype(f32)
        * (-2.0 * math.log(1000000.0) / width)
    )
    angle = (index - start) * freq
    turns = jnp.round(angle * (1.0 / (2.0 * math.pi)))
    angle = (angle - turns * 6.28125) - turns * (2.0 * math.pi - 6.28125)
    cosines, sines = jnp.cos(angle), jnp.sin(angle)
    o_cos[...] = cosines
    o_sin[...] = sines
    start_row = jnp.broadcast_to(start, (rows, rows)).T[0:1, :].astype(jnp.int32)
    index_row = which * rows + lax.broadcasted_iota(jnp.int32, (1, rows), 1)
    for j in range(qcount):
        o_start[:, pl.ds(j * rows, rows)] = start_row
        o_index[:, pl.ds(j * rows, rows)] = index_row

    attn_in = norm_rows(x_ref[...].astype(f32), flat(gain_in_ref)).astype(bf16)
    k_lin = jnp.dot(attn_in, w_key_ref[...], preferred_element_type=f32)
    k_all[s, h] = rotate(norm_rows(k_lin, gain_k), cosines, sines).astype(bf16)
    o_k_lin[...] = k_lin
    v_all[s, h] = jnp.dot(attn_in, w_value_ref[...], preferred_element_type=f32).astype(bf16)

    both = ((k_all, ups), (v_all, downs))

    def pass_on(a, mask, j, bit):
        buf = both[a][0]
        block = buf.at[related(s, mask), related(h, j)]
        return links.go(block, block, links.across(bit))

    over_head = {}
    for j in range(1, heads):
        for a in range(2):
            block = both[a][0].at[s, h]
            over_head[a, j] = links.go(block, block, (s, partners[j - 1]))
    arriving = {}

    def spread(a, mask, j, stage):
        order = both[a][1]
        for later in range(stage, len(order)):
            bit = order[later]
            arriving[a, mask | (1 << bit), j] = pass_on(a, mask, j, bit)

    for a in range(2):
        spread(a, 0, 0, 0)

    load_q.wait()
    q_lin = jnp.dot(attn_in, w_query[...], preferred_element_type=f32)
    o_q_lin[...] = q_lin
    for j in range(1, heads):
        for a in range(2):
            over_head[a, j].wait_recv()
            spread(a, 0, j, 0)
    for j in range(qcount):
        part = norm_rows(q_lin[:, j * width : (j + 1) * width], gain_q)
        o_q[pl.ds(j * rows, rows), :] = (rotate(part, cosines, sines) * scale).astype(bf16)

    pairs = []

    def to_pair(a, mask):
        block = both[a][0].at[related(s, mask)]
        pairs.append(links.go(block, block, links.across(0)))

    for a in range(2):
        to_pair(a, 0)
    for stage in range(len(ups)):
        for lower in subsets(range(stage)):
            masks = []
            for a in range(2):
                order = both[a][1]
                mask = sum(1 << order[i] for i in range(stage) if lower >> i & 1)
                masks.append(mask | (1 << order[stage]))
            for j in range(heads):
                for a in range(2):
                    arriving[a, masks[a], j].wait_recv()
                    spread(a, masks[a], j, stage + 1)
            for a in range(2):
                to_pair(a, masks[a])
    for j in range(1):
        o_attn_t[...] = attn_in.T.reshape(o_attn_t.shape)

    queries = o_q[...]
    starts = o_start[...]
    indices = o_index[...]
    o_att[...] = jnp.zeros_like(o_att)
    span = heads * rows
    low = lax.rem(s, 2)

    def attend_group(g, mass):
        scores = contract_last(k_all[g].reshape(span, width), queries)
        key = g * span + lax.broadcasted_iota(jnp.int32, scores.shape, 0)
        terms = jnp.where((key >= starts) & (key <= indices), jnp.exp(scores), 0.0)
        o_att[...] += contract_first(v_all[g].reshape(span, width), terms.astype(bf16))
        return mass + jnp.sum(terms, axis=0, keepdims=True)

    mass = lax.fori_loop(
        0,
        s // 2 + 1,
        lambda i, m: attend_group(2 * i + low, m),
        jnp.zeros((1, qcount * rows), f32),
    )
    for copy in pairs:
        copy.wait_recv()
    mass = lax.fori_loop(
        0, s // 2 + low, lambda i, m: attend_group(2 * i + 1 - low, m), mass
    )
    keep_k = pltpu.make_async_copy(k_all, o_k, local_sem.at[2])
    keep_v = pltpu.make_async_copy(v_all, o_v, local_sem.at[3])
    keep_k.start()
    keep_v.start()
    o_log[...] = jnp.log(mass)
    attended = o_att[...] / mass
    o_att[...] = attended
    load_o.wait()
    proj = jnp.zeros((rows, model), f32)
    for j in range(qcount):
        part = attended[:, j * rows : (j + 1) * rows].T.astype(bf16)
        proj = proj + jnp.dot(
            part, w_out[pl.ds(j * width, width), :], preferred_element_type=f32
        )
    o_proj[...] = proj
    keep_k.wait()
    keep_v.wait()
    links.finish()


def front(nseq, heads, qcount, scale, cid, x, ids, w_key, w_value, gain_in, gain_q, gain_k, w_query, w_out):
    f32, bf16, i32 = jnp.float32, jnp.bfloat16, jnp.int32
    rows, model = x.shape
    width = w_key.shape[1]
    stacked = qcount * rows
    some = nseq // 2
    messages = 2 * (heads - 1) + 2 * heads * (some - 1) + 2 * some
    vm = pl.BlockSpec(memory_space=VMEM)
    anywhere = pl.BlockSpec(memory_space=pl.ANY)
    everyone = (nseq, heads, rows, width)

    def kernel(*refs):
        front_kernel(nseq, heads, qcount, scale, *refs)

    shape = jax.ShapeDtypeStruct
    return pl.pallas_call(
        kernel,
        out_shape=[
            shape((rows, model), f32),
            shape((stacked, width), bf16),
            shape(everyone, bf16),
            shape(everyone, bf16),
            shape((1, stacked), i32),
            shape((1, stacked), i32),
            shape((1, stacked), f32),
            shape((width, stacked), f32),
            shape((rows, qcount * width), f32),
            shape((rows, width), f32),
            shape((rows, width // 2), f32),
            shape((rows, width // 2), f32),
            shape((nseq, model // nseq, rows), bf16),
        ],
        in_specs=[vm] * 7 + [anywhere] * 2,
        out_specs=[vm] * 2 + [anywhere] * 2 + [vm] * 9,
        scratch_shapes=[
            VMEM(w_query.shape, bf16),
            VMEM(w_out.shape, bf16),
            VMEM(everyone, bf16),
            VMEM(everyone, bf16),
            pltpu.SemaphoreType.DMA((messages,)),
            pltpu.SemaphoreType.DMA((messages,)),
            pltpu.SemaphoreType.DMA((4,)),
        ],
        name="front",
        compiler_params=pltpu.CompilerParams(
            collective_id=cid, has_side_effects=True, vmem_limit_bytes=LIMIT
        ),
    )(
        x,
        ids.reshape(nseq * heads, rows),
        w_key,
        w_value,
        gain_in,
        gain_q,
        gain_k,
        w_query,
        w_out,
    )


class Sum:
    def __init__(self, links, part, boxes, order):
        self.links, self.part, self.boxes, self.order = links, part, boxes, order
        self.used = 0
        self.slot = {}
        self.waiting = {}

    def current(self, mask):
        if mask in self.slot:
            return self.boxes.at[self.slot[mask]]
        return self.part(mask)

    def masks(self, stage):
        rest = self.order[stage + 1 :]
        weight = lambda m: sum(1 << (len(rest) - i) for i, b in enumerate(rest) if m >> b & 1)
        return sorted(subsets(rest), key=weight, reverse=True)

    def send(self, stage, mask):
        bit = self.order[stage]
        where = self.used
        self.used += 1
        copy = self.links.go(
            self.current(mask | (1 << bit)), self.boxes.at[where], self.links.across(bit)
        )
        self.waiting[stage, mask] = (copy, where)

    def start(self):
        for mask in self.masks(0):
            self.send(0, mask)

    def steps(self, stage, kept=None):
        def step(mask):
            copy, where = self.waiting.pop((stage, mask))
            mine = kept(mask) if kept is not None else self.current(mask)
            copy.wait_recv()
            self.boxes[where] = self.boxes[where] + mine[...]
            self.slot[mask] = where
            if stage + 1 < len(self.order):
                bit = 1 << self.order[stage + 1]
                if mask & bit:
                    self.send(stage + 1, mask & ~bit)

        return [functools.partial(step, mask) for mask in self.masks(stage)]

    def last(self, kept=None):
        copy, where = self.waiting.pop((len(self.order) - 1, 0))
        mine = kept(0) if kept is not None else self.current(0)
        copy.wait_recv()
        return self.boxes[where].astype(jnp.float32) + mine[...].astype(jnp.float32)


def in_turn(*lists):
    for group in itertools.zip_longest(*lists):
        for step in group:
            if step is not None:
                step()


def split_rows(rows):
    return (rows // 2 + 15) // 16 * 16


class Links:
    def __init__(self, nseq, heads, send, recv):
        self.s, self.h = place()
        self.nseq, self.heads = nseq, heads
        self.send, self.recv = send, recv
        self.count = 0
        self.started = []
        self.others = [lax.rem(self.h + d, heads) for d in range(1, heads)]

    def greet(self, more=()):
        bits = self.nseq.bit_length() - 1
        near = [self.across(b) for b in range(bits)]
        greet(near + [(self.s, o) for o in self.others] + list(more))

    def across(self, bit):
        return (related(self.s, 1 << bit), self.h)

    def go(self, src, dst, target):
        k = self.count
        self.count += 1
        copy = remote(src, dst, self.send.at[k], self.recv.at[k], target)
        copy.start()
        self.started.append(copy)
        return copy

    def over_heads(self, src, boxes):
        return [self.go(src.at[o], boxes.at[d], (self.s, o)) for d, o in enumerate(self.others)]

    def finish(self):
        for copy in self.started:
            copy.wait_send()


def back_norm(v, gain, d_out):
    scale = lax.rsqrt(jnp.mean(v * v, axis=-1, keepdims=True) + EPS)
    unit = v * scale
    inner = d_out * gain
    d_v = scale * (inner - unit * jnp.mean(inner * unit, axis=-1, keepdims=True))
    return d_v, jnp.sum(d_out * unit, axis=0, keepdims=True)


def back_rotate(d, cosines, sines):
    half = d.shape[-1] // 2
    first, second = d[:, :half], d[:, half:]
    return jnp.concatenate(
        [first * cosines + second * sines, second * cosines - first * sines], axis=-1
    )


def tail_kernel(
    nseq,
    heads,
    qcount,
    scale,
    q_ref,
    start_ref,
    index_ref,
    log_ref,
    att_ref,
    d_proj_ref,
    k_lin_ref,
    cos_ref,
    sin_ref,
    gain_q_ref,
    gain_k_ref,
    gain_in_ref,
    gains_ref,
    k_far,
    v_far,
    w_out_far,
    q_lin_far,
    attn_t_far,
    x_far,
    d_hid_far,
    w_query_far,
    w_key_far,
    w_value_far,
    d_gate_ref,
    d_up_ref,
    d_down_first,
    d_down_second,
    o_tokens,
    o_qkv,
    o_out,
    o_gate,
    o_up,
    o_down,
    o_gains,
    k_ref,
    v_ref,
    w_out_ref,
    q_lin_ref,
    attn_t_ref,
    x_ref,
    d_hid_ref,
    w_qkv_ref,
    dk,
    dv,
    dq_t,
    grads,
    grads_t,
    box_k,
    box_v,
    zbox_k,
    zbox_v,
    dw_out,
    box_out,
    zbox_out,
    mid_out,
    end_out,
    dw_qkv,
    box_qkv,
    zsrc_qkv,
    zbox_qkv,
    d_qkv,
    keep_gate_first,
    keep_gate_second,
    keep_up_first,
    keep_up_second,
    keep_down_first,
    keep_down_second,
    box_gate_first,
    box_gate_second,
    box_up_first,
    box_up_second,
    box_down_first,
    box_down_second,
    gsum,
    gbox,
    gzbox,
    send,
    recv,
    local_sem,
):
    f32, bf16 = jnp.float32, jnp.bfloat16
    bits = nseq.bit_length() - 1
    ups, downs = seq_orders(bits)
    links = Links(nseq, heads, send, recv)
    s, h = links.s, links.h
    rows, model = d_proj_ref.shape
    width = k_lin_ref.shape[1]
    gain_q, gain_k = flat(gain_q_ref), flat(gain_k_ref)
    groups, span = k_ref.shape[:2]
    loads = []

    def load(src, dst):
        copy = pltpu.make_async_copy(src, dst, local_sem.at[len(loads)])
        copy.start()
        loads.append(copy)
        return copy

    load_o = load(w_out_far, w_out_ref)
    load_k = load(k_far, k_ref)
    load_v = load(v_far, v_ref)
    plane = subsets(ups)[1:]
    links.greet([(related(s, m), links.h) for m in plane if m & (m - 1)])

    held = subsets(ups)
    ffn = []
    split = keep_gate_first.shape[1]
    for src, keep, box, order, low, past in (
        (d_gate_ref, keep_gate_first, box_gate_first, ups, 0, 1),
        (d_gate_ref, keep_gate_second, box_gate_second, downs, split, 1),
        (d_up_ref, keep_up_first, box_up_first, [0] + ups, 0, 0),
        (d_up_ref, keep_up_second, box_up_second, [0] + downs, split, 0),
        (d_down_first, keep_down_first, box_down_first, ups[1:], 0, 2),
        (d_down_second, keep_down_second, box_down_second, downs[1:], 0, 2),
    ):
        here = pl.ds(low, keep.shape[1])

        def part(m, src=src, here=here, past=past, order=order):
            if past == 0:
                return src.at[related(s, m), here]
            if past == 1:
                return src.at[held.index(m), here]
            return src.at[0 if m else 1, here]

        total = Sum(links, part, box, order)
        kept = subsets(order[1:])
        total.loads = [load(part(m), keep.at[i]) for i, m in enumerate(kept)]
        total.kept = lambda m, keep=keep, kept=kept: keep.at[kept.index(m)]
        ffn.append(total)
    gate, up, down = ffn[0:2], ffn[2:4], ffn[4:6]
    for total in up + gate + down:
        total.start()

    def settle(pair, stage, first=False):
        if first:
            for total in pair:
                for copy in total.loads:
                    copy.wait()
        in_turn(*[total.steps(stage, total.kept if first else None) for total in pair])

    def put(pair, out, first=False):
        at = 0
        for total in pair:
            value = total.last(total.kept if first else None).astype(out.dtype)
            out[pl.ds(at, value.shape[0]), :] = value
            at += value.shape[0]

    load_q = load(q_lin_far, q_lin_ref)
    load_a = load(attn_t_far, attn_t_ref)
    load_x = load(x_far, x_ref)
    load_d = load(d_hid_far, d_hid_ref)
    load_w = []
    at = 0
    for far in (w_query_far, w_key_far, w_value_far):
        load_w.append(load(far, w_qkv_ref.at[:, pl.ds(at, far.shape[1])]))
        at += far.shape[1]

    d_proj = d_proj_ref[...]

    out_rows = dw_out.shape[1] * dw_out.shape[2]

    def out_block(j, carry):
        low = pl.multiple_of((j * out_rows) % width, out_rows)
        head = pl.multiple_of((j * out_rows) // width * rows, rows)
        mixed_t = att_ref[pl.ds(low, out_rows), pl.ds(head, rows)].astype(bf16)
        dw_out[j] = (
            jnp.dot(mixed_t, d_proj, preferred_element_type=f32)
            .astype(bf16)
            .reshape(dw_out.shape[1:])
        )
        return carry

    lax.fori_loop(0, nseq, out_block, 0)
    sum_out = Sum(links, lambda m: dw_out.at[related(s, m)], box_out, [0])
    sum_out.masks = lambda stage: held
    sum_out.start()

    load_o.wait()

    def back_out(j, carry):
        part = w_out_ref[pl.ds(pl.multiple_of(j * width, width), width), :]
        here = pl.ds(pl.multiple_of(j * rows, rows), rows)
        grads[here, :] = contract_last(d_proj, part).astype(bf16)
        grads_t[:, here] = contract_last(part, d_proj).astype(bf16)
        return carry

    lax.fori_loop(0, qcount, back_out, 0)
    in_turn(sum_out.steps(0))
    z_out = [
        links.go(box_out.at[:, o], zbox_out.at[d], (s, o)) for d, o in enumerate(links.others)
    ]
    dots = jnp.sum(grads_t[...].astype(f32) * att_ref[...], axis=0, keepdims=True)
    start = start_ref[...]
    index = index_ref[...]
    log_total = log_ref[...]
    dq_t[...] = jnp.zeros_like(dq_t)
    load_k.wait()
    load_v.wait()

    def step(g, carry):
        keys = k_ref[g]
        queries = q_ref[...]
        scores = contract_last(keys, queries)
        key = g * span + lax.broadcasted_iota(jnp.int32, scores.shape, 0)
        probs = jnp.where((key >= start) & (key <= index), jnp.exp(scores - log_total), 0.0)
        d_probs = jnp.dot(v_ref[g], grads_t[...], preferred_element_type=f32)
        d_scores = (probs * (d_probs - dots)).astype(bf16)
        dv[g] = (
            jnp.dot(probs.astype(bf16), grads[...], preferred_element_type=f32)
            .astype(bf16)
            .reshape(dv.shape[1:])
        )
        dk[g] = (
            jnp.dot(d_scores, queries, preferred_element_type=f32)
            .astype(bf16)
            .reshape(dk.shape[1:])
        )
        dq_t[...] += contract_first(keys, d_scores)
        return carry

    def blank(g, carry):
        dk[g] = jnp.zeros(dk.shape[1:], bf16)
        dv[g] = jnp.zeros(dv.shape[1:], bf16)
        return carry

    lax.fori_loop(0, s + 1, step, 0)
    lax.fori_loop(s + 1, groups, blank, 0)

    kv = []
    for j in list(range(1, heads)) + [0]:
        owner = lax.rem(h + j, heads)
        for far, box, order in ((dk, box_k, ups), (dv, box_v, downs)):
            kv.append(
                Sum(
                    links,
                    lambda m, far=far, owner=owner: far.at[related(s, m), owner],
                    box.at[j],
                    [0] + order,
                )
            )
    for mask_index in range(len(held)):
        for total in kv:
            total.send(0, total.masks(0)[mask_index])

    in_turn(*[total.steps(0) for total in kv])

    load_q.wait()
    cosines, sines = cos_ref[...], sin_ref[...]
    d_gain_q = jnp.zeros((1, width), f32)
    for j in range(qcount):
        d_rot = dq_t[:, pl.ds(j * rows, rows)].T * scale
        d_lin, terms = back_norm(
            q_lin_ref[:, pl.ds(j * width, width)],
            gain_q,
            back_rotate(d_rot, cosines, sines),
        )
        d_qkv[:, pl.ds(j * width, width)] = d_lin.astype(bf16)
        d_gain_q = d_gain_q + terms

    for stage in range(1, bits - 1):
        in_turn(*[total.steps(stage) for total in kv])
    settle(gate, 0, True)

    arriving = {}
    for i, total in enumerate(kv):
        for m in total.steps(bits - 1):
            m()
        j = (i // 2 + 1) % heads
        if j:
            zbox = (zbox_k, zbox_v)[i % 2]
            arriving[i % 2, j] = links.go(
                total.current(0), zbox.at[j - 1], (s, links.others[j - 1])
            )
    for d, copy in enumerate(z_out):
        copy.wait_recv()
    own = box_out[:, h].astype(f32)
    for d in range(heads - 1):
        own = own + zbox_out[d].astype(f32)
    mid_out[...] = own.astype(bf16)
    sum_end = Sum(links, lambda m: mid_out.at[held.index(m)], end_out, downs)
    sum_end.start()


    settle(up, 0, True)

    def whole(i, zbox):
        total = kv[len(kv) - 2 + i].current(0)[...].astype(f32)
        for j in range(1, heads):
            arriving[i, j].wait_recv()
            total = total + zbox[j - 1].astype(f32)
        return total

    d_keys = whole(0, zbox_k)
    d_lin, d_gain_k = back_norm(
        k_lin_ref[...], gain_k, back_rotate(d_keys, cosines, sines)
    )
    qw = qcount * width
    d_qkv[:, pl.ds(qw, width)] = d_lin.astype(bf16)
    d_values = whole(1, zbox_v)
    d_qkv[:, pl.ds(qw + width, width)] = d_values.astype(bf16)

    pieces, _, block_rows, cut = dw_qkv.shape
    load_a.wait()
    qkv = []
    for j in range(pieces):
        cols = pl.ds(j * cut, cut)

        def qkv_block(g, carry, j=j, cols=cols):
            dw_qkv[j, g] = jnp.dot(
                attn_t_ref[g], d_qkv[:, cols], preferred_element_type=f32
            ).astype(bf16)
            return carry

        lax.fori_loop(0, nseq, qkv_block, 0)
        total = Sum(
            links,
            lambda m, j=j: dw_qkv.at[j, related(s, m)],
            box_qkv.at[j],
            [0] + (downs if j % 2 else ups),
        )
        total.start()
        qkv.append(total)

    for copy in load_w + [load_x, load_d]:
        copy.wait()
    d_attn_in = contract_last(d_qkv[...], w_qkv_ref[...])
    in_turn(*[total.steps(0) for total in qkv])
    d_x, d_gain_in = back_norm(x_ref[...].astype(f32), flat(gain_in_ref), d_attn_in)
    o_tokens[...] = (d_hid_ref[...] + d_x).astype(o_tokens.dtype)

    gsum[0] = gains_ref[...]
    gsum[0, 0:1, :] = d_gain_in
    gsum[0, 4:5, :width] = d_gain_q
    gsum[0, 5:6, :width] = d_gain_k
    gain_copy = links.go(gsum.at[0], gbox.at[0], links.across(0))
    for stage in range(1, bits - 1):
        in_turn(*[total.steps(stage) for total in qkv])
    gain_copy.wait_recv()
    gsum[1] = gsum[0] + gbox[0]
    gain_plane = [
        links.go(gsum.at[1], gbox.at[1 + i], (related(s, m), h)) for i, m in enumerate(plane)
    ]
    in_turn(sum_end.steps(0))
    settle(up, 1)
    each = block_rows // heads
    z_qkv = []

    for j, total in enumerate(qkv):
        value = total.last()
        for p in range(heads):
            zsrc_qkv[j, p] = value[p * each : (p + 1) * each].astype(bf16)
        z_qkv.append(links.over_heads(zsrc_qkv.at[j], zbox_qkv.at[j]))
    total_gains = gsum[1]
    for i, copy in enumerate(gain_plane):
        copy.wait_recv()
        total_gains = total_gains + gbox[1 + i]
    gsum[2] = total_gains
    gain_z = [
        links.go(gsum.at[2], gzbox.at[d], (s, o)) for d, o in enumerate(links.others)
    ]
    for total in down:
        for copy in total.loads:
            copy.wait()
    put(down, o_down, True)
    put(gate, o_gate)
    put(up, o_up)
    o_out[...] = sum_end.last()
    for j, copies in enumerate(z_qkv):
        total = zsrc_qkv[j, h].astype(f32)
        for d, copy in enumerate(copies):
            copy.wait_recv()
            total = total + zbox_qkv[j, d].astype(f32)
        o_qkv[:, pl.ds(j * cut, cut)] = total
    total = gsum[2]
    for d, copy in enumerate(gain_z):
        copy.wait_recv()
        total = total + gzbox[d]
    o_gains[...] = total
    links.finish()


def tail(nseq, heads, qcount, scale, cid, *arrays):
    (q, _, _, _, att, d_proj, k_lin, _, _, gain_q, _, _, gains, k, v) = arrays[:15]
    (w_out, q_lin, attn_t, x, d_hid, w_query, w_key, w_value, d_gate, _, _, _) = arrays[15:]
    f32, bf16 = jnp.float32, jnp.bfloat16
    rows, model = d_proj.shape
    width = k_lin.shape[1]
    cols = w_query.shape[1] + w_key.shape[1] + w_value.shape[1]
    pieces = 4
    cut = cols // pieces
    out_rows, qkv_rows = w_out.shape[0] // nseq, attn_t.shape[1]
    ffn_block = d_gate.shape[1:]
    some, all_but = nseq // 2, nseq - 1
    out_block = (heads, out_rows // heads, model)
    split = split_rows(ffn_block[0])
    low, high = (split, ffn_block[1]), (ffn_block[0] - split, ffn_block[1])
    parts = [(part, *n) for n in ((2, 3), (4, 7), (1, 1)) for part in (low, high)]
    copies = (
        sum(n for _, _, n in parts)
        + some
        + (heads - 1)
        + (some - 1)
        + 2 * heads * all_but
        + 2 * (heads - 1)
        + pieces * (all_but + heads - 1)
        + some
        + (heads - 1)
    )
    vm = pl.BlockSpec(memory_space=VMEM)
    anywhere = pl.BlockSpec(memory_space=pl.ANY)

    def kernel(*refs):
        tail_kernel(nseq, heads, qcount, scale, *refs)

    return pl.pallas_call(
        kernel,
        out_shape=[
            jax.ShapeDtypeStruct((rows, model), bf16),
            jax.ShapeDtypeStruct((qkv_rows // heads, cols), f32),
            jax.ShapeDtypeStruct(out_block[1:], f32),
            jax.ShapeDtypeStruct(ffn_block, bf16),
            jax.ShapeDtypeStruct(ffn_block, bf16),
            jax.ShapeDtypeStruct(ffn_block, bf16),
            jax.ShapeDtypeStruct(gains.shape, f32),
        ],
        in_specs=[vm] * 13 + [anywhere] * 14,
        out_specs=[vm] * 7,
        scratch_shapes=[
            VMEM(k.shape, bf16),
            VMEM(v.shape, bf16),
            *[VMEM(a.shape, a.dtype) for a in (w_out, q_lin, attn_t, x, d_hid)],
            VMEM((model, cols), bf16),
            VMEM((nseq, heads, rows, width), bf16),
            VMEM((nseq, heads, rows, width), bf16),
            VMEM((width, qcount * rows), f32),
            VMEM((qcount * rows, width), bf16),
            VMEM((width, qcount * rows), bf16),
            VMEM((heads, all_but, rows, width), bf16),
            VMEM((heads, all_but, rows, width), bf16),
            VMEM((heads - 1, rows, width), bf16),
            VMEM((heads - 1, rows, width), bf16),
            VMEM((nseq,) + out_block, bf16),
            VMEM((some,) + out_block, bf16),
            VMEM((heads - 1, some) + out_block[1:], bf16),
            VMEM((some,) + out_block[1:], bf16),
            VMEM((some - 1,) + out_block[1:], bf16),
            VMEM((pieces, nseq, qkv_rows, cut), bf16),
            VMEM((pieces, all_but, qkv_rows, cut), bf16),
            VMEM((pieces, heads, qkv_rows // heads, cut), bf16),
            VMEM((pieces, heads - 1, qkv_rows // heads, cut), bf16),
            VMEM((rows, cols), bf16),
        ]
        + [VMEM((n,) + part, bf16) for part, n, _ in parts]
        + [VMEM((n,) + part, bf16) for part, _, n in parts]
        + [
            VMEM((3,) + gains.shape, f32),
            VMEM((some,) + gains.shape, f32),
            VMEM((heads - 1,) + gains.shape, f32),
            pltpu.SemaphoreType.DMA((copies,)),
            pltpu.SemaphoreType.DMA((copies,)),
            pltpu.SemaphoreType.DMA((10 + sum(n for _, n, _ in parts),)),
        ],
        name="tail",
        compiler_params=pltpu.CompilerParams(
            collective_id=cid, has_side_effects=True, vmem_limit_bytes=62 * 2**20
        ),
    )(*arrays)


CHUNKS, SPANS = 4, 2
ORDER = (
    ("ags", 0, 0, 0), ("ags", 0, 1, 0), ("agw", 0, 0, 0), ("ags", 0, 0, 1), ("agw", 0, 1, 0),
    ("ags", 0, 1, 1), ("agw", 0, 0, 1), ("ags", 0, 0, 2), ("agw", 0, 1, 1), ("ags", 0, 1, 2),
    ("ags", 0, 3, 0), ("ags", 0, 2, 0), ("agw", 0, 1, 2), ("agw", 0, 0, 2), ("fa", 0), ("fb", 0),
    ("agw", 0, 3, 0), ("ags", 0, 3, 1), ("agw", 0, 2, 0), ("ags", 0, 2, 1), ("fc", 0),
    ("agw", 0, 3, 1), ("ags", 0, 3, 2), ("rss", 0, 0, 0), ("agw", 0, 2, 1), ("ags", 0, 2, 2),
    ("rsw", 0, 0, 0), ("rss", 0, 1, 0), ("rss", 0, 0, 1), ("rsw", 0, 1, 0), ("rss", 0, 1, 1),
    ("agw", 0, 3, 2), ("agw", 0, 2, 2), ("fa", 1), ("rsw", 0, 0, 1), ("rss", 0, 0, 2), ("fb", 1),
    ("rsw", 0, 1, 1), ("rss", 0, 1, 2), ("fc", 1), ("rss", 0, 2, 0), ("rsw", 0, 0, 2), ("n", 0),
    ("ags", 1, 0, 0), ("rss", 0, 3, 0), ("rsw", 0, 1, 2), ("rsw", 0, 2, 0), ("n", 1),
    ("rss", 0, 2, 1), ("ags", 1, 1, 0), ("agw", 1, 0, 0), ("rsw", 0, 3, 0), ("ags", 1, 0, 1),
    ("rss", 0, 3, 1), ("rsw", 0, 2, 1), ("rss", 0, 2, 2), ("agw", 1, 1, 0), ("ags", 1, 1, 1),
    ("agw", 1, 0, 1), ("ags", 1, 0, 2), ("rsw", 0, 3, 1), ("rss", 0, 3, 2), ("rsw", 0, 2, 2),
    ("n", 2), ("ags", 1, 2, 0), ("agw", 1, 1, 1), ("ags", 1, 1, 2), ("rsw", 0, 3, 2), ("n", 3),
    ("ags", 1, 3, 0), ("agw", 1, 0, 2), ("agw", 1, 2, 0), ("ags", 1, 2, 1), ("agw", 1, 1, 2),
    ("ga", 0), ("gb", 0), ("agw", 1, 3, 0), ("ags", 1, 3, 1), ("gc", 0), ("rss", 1, 1, 0),
    ("agw", 1, 2, 1), ("ags", 1, 2, 2), ("rss", 1, 0, 0), ("agw", 1, 3, 1), ("ags", 1, 3, 2),
    ("rsw", 1, 1, 0), ("rss", 1, 1, 1), ("agw", 1, 2, 2), ("agw", 1, 3, 2), ("wd", 0), ("wd", 1),
    ("dd", 0), ("rsw", 1, 0, 0), ("rsw", 1, 1, 1), ("rss", 1, 0, 1), ("rss", 1, 1, 2), ("ga", 1),
    ("gb", 1), ("gc", 1), ("rss", 1, 2, 0), ("Dd", 0), ("rsw", 1, 0, 1), ("rsw", 1, 1, 2),
    ("rss", 1, 3, 0), ("rss", 1, 0, 2), ("wg", 0), ("rsw", 1, 2, 0), ("e", 1), ("rss", 1, 2, 1),
    ("wg", 1), ("dg", 0), ("rsw", 1, 3, 0), ("rss", 1, 3, 1), ("rsw", 1, 0, 2), ("e", 0),
    ("rsw", 1, 2, 1), ("rss", 1, 2, 2), ("wu", 0), ("rsw", 1, 3, 1), ("rss", 1, 3, 2), ("wu", 1),
    ("rsw", 1, 2, 2), ("e", 2), ("Dg", 0), ("rsw", 1, 3, 2), ("e", 3), ("D2", 0),
)


def ffn_kernel(
    nseq,
    heads,
    chunks,
    spans,
    proj_ref,
    x_ref,
    cot_ref,
    gain_two_ref,
    gain_three_ref,
    gain_four_ref,
    w_gate_ref,
    w_up_ref,
    w_down_ref,
    o_out,
    o_hid,
    o_proj,
    o_gains,
    o_first,
    o_second,
    o_gate,
    o_up,
    hidden,
    w_gate,
    w_up,
    w_down,
    u_all,
    d_all,
    by_gate,
    by_up,
    act,
    d_gate,
    d_up,
    parts,
    from_left,
    from_right,
    flipped,
    dw_gate,
    dw_up,
    dw_down,
    box_gate,
    box_down,
    box_first,
    box_second,
    sum_send,
    sum_recv,
    ag_send,
    ag_recv,
    rs_send,
    rs_recv,
    local_sem,
):
    f32, bf16 = jnp.float32, jnp.bfloat16
    s, h = place()
    last = heads - 1
    right = (s, lax.rem(h + 1, heads))
    left = (s, lax.rem(h + last, heads))
    rows, model = x_ref.shape
    units = w_gate.shape[0]
    rc = rows // chunks
    each = chunks // spans
    many = rc * heads * each

    loads = []
    for n, (src, dst) in enumerate(
        ((w_gate_ref, w_gate), (w_up_ref, w_up), (w_down_ref, w_down))
    ):
        copy = pltpu.make_async_copy(src, dst, local_sem.at[n])
        copy.start()
        loads.append(copy)
    bits = nseq.bit_length() - 1
    ups, downs = seq_orders(bits)
    links = Links(nseq, heads, sum_send, sum_recv)
    greet([right, left] + [links.across(b) for b in range(bits)])

    proj = proj_ref[...]
    hid = x_ref[...].astype(f32) + norm_rows(proj, flat(gain_two_ref))
    hidden[...] = hid
    u_local = norm_rows(hid, flat(gain_three_ref)).astype(bf16)
    for c in range(chunks):
        u_all[c, h] = u_local[c * rc : (c + 1) * rc]
    o_gains[...] = jnp.zeros_like(o_gains)

    def lanes(k, c, t):
        buf = d_all if k else u_all
        return (
            (
                (h - t >= 0) & (h < last),
                buf.at[c, jnp.maximum(h - t, 0)],
                0,
                right,
                h - 1 - t >= 0,
                buf.at[c, jnp.maximum(h - 1 - t, 0)],
            ),
            (
                (h + t <= last) & (h > 0),
                buf.at[c, jnp.minimum(h + t, last)],
                1,
                left,
                h + 1 + t <= last,
                buf.at[c, jnp.minimum(h + 1 + t, last)],
            ),
        )

    def ags(k, c, t):
        for on, block, lane, target, _, _ in lanes(k, c, t):
            i = (k, c, lane, t)
            pl.when(on)(remote(block, block, ag_send.at[i], ag_recv.at[i], target).start)

    def agw(k, c, t):
        for _, _, lane, target, on, block in lanes(k, c, t):
            i = (k, c, lane, t)
            pl.when(on)(remote(block, block, ag_send.at[i], ag_recv.at[i], target).wait_recv)

    def rss(k, c, t):
        for on, dest, box, lane, target, at_end in (
            ((t >= h) & (h < last), last - (t - h), from_left, 0, right, h == 0),
            ((t >= last - h) & (h > 0), t - (last - h), from_right, 1, left, h == last),
        ):
            dest = jnp.clip(dest, 0, last)
            i = (k, c, lane, t)
            if t > 0:

                def forward(box=box, dest=dest, i=i, target=target):
                    box[k, c, t - 1] = box[k, c, t - 1] + parts[k, c, dest]
                    remote(
                        box.at[k, c, t - 1], box.at[k, c, t], rs_send.at[i], rs_recv.at[i], target
                    ).start()

                pl.when(on & jnp.logical_not(at_end))(forward)
            pl.when(on & at_end)(
                remote(
                    parts.at[k, c, dest], box.at[k, c, t], rs_send.at[i], rs_recv.at[i], target
                ).start
            )

    def rsw(k, c, t):
        for on, box, lane, target in (
            ((t >= h - 1) & (h > 0), from_left, 0, right),
            ((t >= last - h - 1) & (h < last), from_right, 1, left),
        ):
            i = (k, c, lane, t)
            block = box.at[k, c, t]
            pl.when(on)(remote(block, block, rs_send.at[i], rs_recv.at[i], target).wait_recv)

    def summed(k, c):
        zero = jnp.zeros((rc, model), f32)
        return (
            parts[k, c, h].astype(f32)
            + jnp.where(h > 0, from_left[k, c, last - 1].astype(f32), zero)
            + jnp.where(h < last, from_right[k, c, last - 1].astype(f32), zero)
        )

    def over_tiles(second, body, tile):
        whole_tiles, rest = units // tile, units % tile
        middle = (whole_tiles + 1) // 2

        def step(i, carry):
            body(pl.ds(pl.multiple_of(i * tile, tile), tile))
            return carry

        lax.fori_loop(middle if second else 0, whole_tiles if second else middle, step, 0)
        if second and rest:
            body(pl.ds(whole_tiles * tile, rest))

    arrived = set()

    def need(n):
        if n not in arrived:
            arrived.add(n)
            loads[n].wait()

    def span_rows(buf, p):
        return buf[pl.ds(p * each, each)].reshape(many, model)

    def place_parts(k, p, cols, value):
        parts[k, pl.ds(p * each, each), :, :, cols] = value.astype(bf16).reshape(
            each, heads, rc, value.shape[1]
        )

    def forward_tiles(c, second):
        need(0)
        need(1)

        def body(cols):
            u = span_rows(u_all, c)
            gate = contract_last(u, w_gate[cols, :])
            up = contract_last(u, w_up[cols, :])
            root = math.sqrt(2.0 / math.pi)
            square = gate * gate
            curve = jnp.tanh(root * gate * (1.0 + 0.044715 * square))
            half = 0.5 * (1.0 + curve)
            gelu = gate * half
            slope = half + 0.5 * gate * (1.0 - curve * curve) * (
                root * (1.0 + 3 * 0.044715 * square)
            )
            by_gate[pl.ds(c * many, many), cols] = slope * up
            by_up[pl.ds(c * many, many), cols] = gelu
            act[pl.ds(c * many, many), cols] = (gelu * up).astype(bf16)

        over_tiles(second, body, 512)

    wide = (model // 2 + 127) // 128 * 128

    def over_columns(body):
        body(pl.ds(0, wide))
        body(pl.ds(wide, model - wide))

    def down_rows(c):
        need(2)

        def body(cols):
            place_parts(
                0,
                c,
                cols,
                jnp.dot(
                    act[pl.ds(c * many, many), :], w_down[:, cols], preferred_element_type=f32
                ),
            )

        over_columns(body)

    def turn(c):
        here = pl.ds(c * rc, rc)
        ffn_out = summed(0, c)
        upstream = cot_ref[here, :].astype(f32)
        o_out[here, :] = (hidden[here, :] + norm_rows(ffn_out, flat(gain_four_ref))).astype(
            o_out.dtype
        )
        d_out, terms = back_norm(ffn_out, flat(gain_four_ref), upstream)
        d_all[c, h] = d_out.astype(bf16)
        o_gains[3:4, :] += terms

    def back_tiles(c, second):
        def body(cols):
            d_act = contract_last(span_rows(d_all, c), w_down[cols, :])
            d_gate[pl.ds(c * many, many), cols] = (
                d_act * by_gate[pl.ds(c * many, many), cols]
            ).astype(bf16)
            d_up[pl.ds(c * many, many), cols] = (
                d_act * by_up[pl.ds(c * many, many), cols]
            ).astype(bf16)

        over_tiles(second, body, 512)

    def back_rows(c):
        def body(cols):
            part = jnp.dot(
                d_gate[pl.ds(c * many, many), :], w_gate[:, cols], preferred_element_type=f32
            )
            part = part + jnp.dot(
                d_up[pl.ds(c * many, many), :], w_up[:, cols], preferred_element_type=f32
            )
            place_parts(1, c, cols, part)

        over_columns(body)

    def finish_rows(c):
        here = pl.ds(c * rc, rc)
        d_in, terms = back_norm(hidden[here, :], flat(gain_three_ref), summed(1, c))
        o_gains[2:3, :] += terms
        d_hid = cot_ref[here, :].astype(f32) + d_in
        o_hid[here, :] = d_hid
        d_proj, terms = back_norm(proj_ref[here, :], flat(gain_two_ref), d_hid)
        o_proj[here, :] = d_proj.astype(o_proj.dtype)
        o_gains[1:2, :] += terms

    stores = []

    def flip(source):
        for p in range(spans):
            flipped[:, pl.ds(p * many, many)] = span_rows(source, p).T

    def weight_grad(right_ref, dst, half):
        def body(cols):
            value = jnp.dot(flipped[...], right_ref[:, cols], preferred_element_type=f32)
            dst[:, :, cols] = value.astype(bf16).reshape(dst.shape[:2] + (value.shape[1],))

        over_tiles(half, body, 512)

    held = subsets(ups)
    sum_gate = Sum(links, lambda m: dw_gate.at[related(s, m)], box_gate, [0])
    sum_down = Sum(links, lambda m: dw_down.at[related(s, m)], box_down, [0])
    for total in (sum_gate, sum_down):
        total.masks = lambda stage: held
    def store(src, dst):
        copy = pltpu.make_async_copy(src, dst, local_sem.at[3 + len(stores)])
        copy.start()
        stores.append(copy)

    split = box_first.shape[1]
    pieces = []
    for box, order, low in ((box_first, ups, 0), (box_second, downs, split)):
        here = pl.ds(low, box.shape[1])
        pieces.append(
            Sum(links, lambda m, here=here: box_down.at[held.index(m), here], box, order)
        )

    for event in ORDER:
        kind, args = event[0], event[1:]
        if kind == "ags":
            ags(*args)
        elif kind == "agw":
            agw(*args)
        elif kind == "rss":
            rss(*args)
        elif kind == "rsw":
            rsw(*args)
        elif kind == "fa":
            forward_tiles(args[0], False)
        elif kind == "fb":
            forward_tiles(args[0], True)
        elif kind == "fc":
            down_rows(args[0])
        elif kind == "n":
            turn(args[0])
        elif kind == "ga":
            back_tiles(args[0], False)
        elif kind == "gb":
            back_tiles(args[0], True)
        elif kind == "gc":
            back_rows(args[0])
        elif kind == "e":
            finish_rows(args[0])
        elif kind == "wd":
            if args[0] == 0:
                flip(d_all)
            weight_grad(act, dw_down, args[0])
        elif kind == "wg":
            if args[0] == 0:
                flip(u_all)
            weight_grad(d_gate, dw_gate, args[0])
        elif kind == "wu":
            weight_grad(d_up, dw_up, args[0])
            if args[0] == 1:
                store(dw_up, o_up)
        elif kind == "dd":
            sum_down.start()
        elif kind == "dg":
            sum_gate.start()
        elif kind == "Dg":
            in_turn(sum_gate.steps(0))
            store(box_gate, o_gate)
        elif kind == "Dd":
            in_turn(sum_down.steps(0))
            for total in pieces:
                for m in total.masks(0):
                    total.send(0, m)
        else:
            for total, out in zip(pieces, (o_first, o_second)):
                for m in total.masks(0):
                    copy, where = total.waiting.pop((0, m))
                    copy.wait_recv()
                    total.boxes[where] = total.boxes[where] + total.current(m)[...]
                store(total.boxes, out)

    for event in ORDER:
        if event[0] == "ags":
            k, c, t = event[1:]
            for on, block, lane, target, _, _ in lanes(k, c, t):
                i = (k, c, lane, t)
                pl.when(on)(remote(block, block, ag_send.at[i], ag_recv.at[i], target).wait_send)
        elif event[0] == "rss":
            k, c, t = event[1:]
            for on, box, lane, target in (
                ((t >= h) & (h < last), from_left, 0, right),
                ((t >= last - h) & (h > 0), from_right, 1, left),
            ):
                i = (k, c, lane, t)
                block = box.at[k, c, t]
                pl.when(on)(remote(block, block, rs_send.at[i], rs_recv.at[i], target).wait_send)
    for n in range(3):
        need(n)
    for copy in stores:
        copy.wait()
    links.finish()


def feed_forward(nseq, heads, cid, *arrays):
    _, x, _, _, _, _, w_gate, w_up, w_down = arrays
    f32, bf16 = jnp.float32, jnp.bfloat16
    rows, model = x.shape
    units = w_gate.shape[0]
    chunks = CHUNKS
    rc = rows // chunks
    group = rows * heads
    vm = pl.BlockSpec(memory_space=VMEM)
    anywhere = pl.BlockSpec(memory_space=pl.ANY)
    block = (model // nseq, units)
    some = nseq // 2
    half = jax.ShapeDtypeStruct((some,) + block, bf16)
    split = split_rows(block[0])
    parts = [(split, units), (block[0] - split, units)]
    messages = 3 * some
    hops = (2, chunks, 2, heads - 1)
    return pl.pallas_call(
        functools.partial(ffn_kernel, nseq, heads, CHUNKS, SPANS),
        out_shape=[
            jax.ShapeDtypeStruct((rows, model), bf16),
            jax.ShapeDtypeStruct((rows, model), f32),
            jax.ShapeDtypeStruct((rows, model), bf16),
            jax.ShapeDtypeStruct((8, model), f32),
            *[jax.ShapeDtypeStruct((some // 2,) + part, bf16) for part in parts],
            half,
            jax.ShapeDtypeStruct((nseq,) + block, bf16),
        ],
        in_specs=[vm] * 6 + [anywhere] * 3,
        out_specs=[vm] * 4 + [anywhere] * 4,
        scratch_shapes=[
            VMEM((rows, model), f32),
            VMEM(w_gate.shape, bf16),
            VMEM(w_up.shape, bf16),
            VMEM(w_down.shape, bf16),
            VMEM((chunks, heads, rc, model), bf16),
            VMEM((chunks, heads, rc, model), bf16),
            VMEM((group, units), f32),
            VMEM((group, units), f32),
            VMEM((group, units), bf16),
            VMEM((group, units), bf16),
            VMEM((group, units), bf16),
            VMEM((2, chunks, heads, rc, model), bf16),
            VMEM((2, chunks, heads - 1, rc, model), bf16),
            VMEM((2, chunks, heads - 1, rc, model), bf16),
            VMEM((model, group), bf16),
            VMEM((nseq,) + block, bf16),
            VMEM((nseq,) + block, bf16),
            VMEM((nseq,) + block, bf16),
            VMEM((some,) + block, bf16),
            VMEM((some,) + block, bf16),
            *[VMEM((some // 2,) + part, bf16) for part in parts],
            pltpu.SemaphoreType.DMA((messages,)),
            pltpu.SemaphoreType.DMA((messages,)),
            pltpu.SemaphoreType.DMA(hops),
            pltpu.SemaphoreType.DMA(hops),
            pltpu.SemaphoreType.DMA(hops),
            pltpu.SemaphoreType.DMA(hops),
            pltpu.SemaphoreType.DMA((7,)),
        ],
        name="feed_forward",
        compiler_params=pltpu.CompilerParams(
            collective_id=cid, has_side_effects=True, vmem_limit_bytes=62 * 2**20
        ),
    )(*arrays)


def finish_kernel(nseq, qw, width, each, few, *refs):
    out, tokens, qkv, w_out, gate, up, down, gains = refs[:8]
    o_out, o_tokens, o_query, o_key, o_value, o_w_out, o_gate, o_up, o_down = refs[8:17]
    o_gains = refs[17:]
    s, h = place()
    which = s * lax.axis_size("head") + h
    o_out[...] = out[...]
    o_tokens[...] = tokens[...]
    o_query[...] = qkv[:, :qw]
    o_key[...] = qkv[:, qw : qw + width]
    o_value[...] = qkv[:, qw + width :]
    o_w_out[...] = w_out[...]
    o_gate[...] = gate[...].astype(jnp.float32)
    o_up[...] = up[...].astype(jnp.float32)
    o_down[...] = down[...].astype(jnp.float32)
    model = gains.shape[1]
    wide = pltpu.roll(gains[...], lax.rem(model - which * each, model), 1)
    narrow = pltpu.roll(gains[...], lax.rem(model - which * few, model), 1)
    for i in range(4):
        o_gains[i][...] = wide[i : i + 1, :each]
    for i in range(4, 6):
        o_gains[i][...] = narrow[i : i + 1, :few]


def finish(nseq, qw, width, each, few, *arrays):
    out, tokens, qkv, w_out, gate, up, down, gains = arrays
    vm = pl.BlockSpec(memory_space=VMEM)
    shape = lambda a: jax.ShapeDtypeStruct(a.shape, a.dtype)
    f32 = jnp.float32
    rows = qkv.shape[0]
    wide, narrow = jax.ShapeDtypeStruct((1, each), f32), jax.ShapeDtypeStruct((1, few), f32)
    return pl.pallas_call(
        functools.partial(finish_kernel, nseq, qw, width, each, few),
        out_shape=[shape(out), shape(tokens)]
        + [jax.ShapeDtypeStruct((rows, n), f32) for n in (qw, width, width)]
        + [jax.ShapeDtypeStruct(a.shape, f32) for a in (w_out, gate, up, down)]
        + [wide] * 4
        + [narrow] * 2,
        in_specs=[vm] * 8,
        out_specs=[vm] * 15,
        name="finish",
        compiler_params=pltpu.CompilerParams(vmem_limit_bytes=LIMIT),
    )(*arrays)


def local(
    tokens,
    segment_ids,
    w_query,
    w_key,
    w_value,
    w_out,
    w_gate,
    w_up,
    w_down,
    gain_attn_in,
    gain_attn_out,
    gain_ffn_in,
    gain_ffn_out,
    gain_query,
    gain_key,
    cotangent,
):
    heads = lax.axis_size("head")
    nseq = lax.axis_size("seq")
    head_index = lax.axis_index("head")
    seq_index = lax.axis_index("seq")
    bits = nseq.bit_length() - 1
    local_rows, model = tokens.shape
    width = gain_query.shape[0]
    qcount = w_query.shape[1] // width
    group = local_rows * heads
    total = segment_ids.shape[0]
    hidden_units = w_gate.shape[1]
    scale = 1.0 / math.sqrt(width)
    bf16 = jnp.bfloat16
    if (nseq, heads) == (8, 4) and (model // nseq) % 16 == 0:
        qw = qcount * width
        each, few = model // (nseq * heads), width // (nseq * heads)
        (
            projected,
            queries,
            keys,
            values,
            starts,
            index,
            log_total,
            attended_t,
            q_linear,
            k_linear,
            cosines,
            sines,
            attn_t,
        ) = front(
            nseq,
            heads,
            qcount,
            scale,
            11,
            tokens,
            segment_ids,
            w_key,
            w_value,
            gain_attn_in,
            gain_query,
            gain_key,
            w_query,
            w_out,
        )
        output, d_hidden, d_projected, gains, down_first, down_second, half_gate, all_up = feed_forward(
            nseq,
            heads,
            10,
            projected,
            tokens,
            cotangent,
            gain_attn_out,
            gain_ffn_in,
            gain_ffn_out,
            w_gate.T,
            w_up.T,
            w_down,
        )
        grad_tokens, sum_qkv, sum_out, sum_gate, sum_up, sum_down, sum_gains = tail(
            nseq,
            heads,
            qcount,
            scale,
            9,
            queries,
            starts,
            index,
            log_total,
            attended_t,
            d_projected,
            k_linear,
            cosines,
            sines,
            gain_query,
            gain_key,
            gain_attn_in,
            gains,
            keys.reshape(nseq, group, width),
            values.reshape(nseq, group, width),
            w_out,
            q_linear,
            attn_t,
            tokens,
            d_hidden,
            w_query,
            w_key,
            w_value,
            half_gate,
            all_up,
            down_first,
            down_second,
        )
        (
            output,
            grad_tokens,
            sum_query,
            sum_key,
            sum_value,
            sum_out,
            sum_gate,
            sum_up,
            sum_down,
            *sum_gains,
        ) = finish(
            nseq,
            qw,
            width,
            each,
            few,
            output,
            grad_tokens,
            sum_qkv,
            sum_out,
            sum_gate,
            sum_up,
            sum_down,
            sum_gains,
        )
        return (
            output,
            grad_tokens,
            sum_query,
            sum_key,
            sum_value,
            sum_out,
            sum_gate,
            sum_up,
            sum_down.T,
            *[g[0] for g in sum_gains],
        )
    first_row = (seq_index * heads + head_index) * local_rows
    my_index = first_row + jnp.arange(local_rows, dtype=jnp.int32)
    my_ids = lax.dynamic_slice_in_dim(segment_ids, first_row, local_rows)
    my_starts = jnp.min(
        jnp.where(
            my_ids[:, None] == segment_ids[None, :],
            jnp.arange(total, dtype=jnp.int32)[None, :],
            total,
        ),
        axis=1,
    )
    cosines, sines = rope_tables(my_index - my_starts, width)

    def query_path(linear, gain):
        shaped = linear.reshape(local_rows, qcount, width)
        turned = rotate(norm_rows(shaped, gain), cosines[:, None, :], sines[:, None, :])
        return turned.reshape(local_rows, qcount * width)

    def key_path(linear, gain):
        return rotate(norm_rows(linear, gain), cosines, sines)

    def gated(gate, up):
        return jax.nn.gelu(gate, approximate=True) * up

    def stacked(v):
        return v.reshape(local_rows, qcount, width).transpose(1, 0, 2).reshape(-1, width)

    def unstacked(v):
        return v.reshape(qcount, local_rows, width).transpose(1, 0, 2).reshape(local_rows, -1)

    inputs = tokens.astype(jnp.float32)
    attn_in = norm_rows(inputs, gain_attn_in).astype(bf16)
    k_linear = jnp.dot(attn_in, w_key, preferred_element_type=jnp.float32)
    keys_local = key_path(k_linear, gain_key).astype(bf16)
    values_local = jnp.dot(attn_in, w_value, preferred_element_type=jnp.float32).astype(bf16)
    q_linear = jnp.dot(attn_in, w_query, preferred_element_type=jnp.float32)
    queries_local = query_path(q_linear, gain_query).astype(bf16)
    queries = stacked(queries_local) * jnp.asarray(scale, bf16)
    keys, values = gather_all([keys_local, values_local], nseq, heads, 1)
    keys = keys.reshape(nseq, group, width)
    values = values.reshape(nseq, group, width)
    starts = jnp.tile(my_starts, qcount)[None, :]
    index = jnp.tile(my_index, qcount)[None, :]
    attended_t, log_total = attend(queries, keys, values, starts, index)
    attended = attended_t.T
    mixed_local = unstacked(attended.astype(bf16))
    projected = jnp.dot(mixed_local, w_out, preferred_element_type=jnp.float32)
    hidden = inputs + norm_rows(projected, gain_attn_out)
    ffn_in = norm_rows(hidden, gain_ffn_in).astype(bf16)
    ffn_rows = line_gather(ffn_in, heads, 2).reshape(group, model)
    gate = jnp.dot(ffn_rows, w_gate, preferred_element_type=jnp.float32)
    up = jnp.dot(ffn_rows, w_up, preferred_element_type=jnp.float32)
    activated = gated(gate, up).astype(bf16)
    ffn_out = line_scatter(
        jnp.dot(activated, w_down, preferred_element_type=jnp.float32)
        .astype(bf16)
        .reshape(heads, local_rows, model),
        heads,
        3,
    )
    output = hidden + norm_rows(ffn_out, gain_ffn_out)
    upstream = cotangent.astype(jnp.float32)
    unused, back_four = jax.vjp(norm_rows, ffn_out, gain_ffn_out)
    d_ffn_out, d_gain_four = back_four(upstream)
    d_ffn_rows = line_gather(d_ffn_out.astype(bf16), heads, 4).reshape(group, model)
    d_activated = contract_last(d_ffn_rows, w_down)
    d_w_down = contract_first(d_ffn_rows, activated)
    unused, back_gate = jax.vjp(gated, gate, up)
    d_gate, d_up = back_gate(d_activated)
    d_gate = d_gate.astype(bf16)
    d_up = d_up.astype(bf16)
    d_ffn_in = line_scatter(
        (contract_last(d_gate, w_gate) + contract_last(d_up, w_up))
        .astype(bf16)
        .reshape(heads, local_rows, model),
        heads,
        5,
    )
    d_w_gate = contract_first(ffn_rows, d_gate)
    d_w_up = contract_first(ffn_rows, d_up)
    unused, back_three = jax.vjp(norm_rows, hidden, gain_ffn_in)
    d_hidden_part, d_gain_three = back_three(d_ffn_in)
    d_hidden = upstream + d_hidden_part
    unused, back_two = jax.vjp(norm_rows, projected, gain_attn_out)
    d_projected, d_gain_two = back_two(d_hidden)
    d_projected = d_projected.astype(bf16)
    qw = qcount * width
    d_w_out = contract_first(mixed_local, d_projected)
    d_mixed = contract_last(d_projected, w_out).astype(bf16)
    grad_attended = stacked(d_mixed)
    row_dots = jnp.sum(grad_attended.astype(jnp.float32) * attended, axis=1)[None, :]
    d_queries_t, d_keys, d_values = attend_back(
        queries, keys, values, starts, index, log_total, row_dots, grad_attended
    )
    shape = (nseq, heads, local_rows, width)
    ups, downs = seq_orders(bits)
    d_keys, d_values = scatter_all(
        [d_keys.reshape(shape), d_values.reshape(shape)],
        [True, True],
        [[0] + ups, [0] + downs],
        nseq,
        heads,
        6,
        "scatter_keys",
    )
    d_query_rot = unstacked((d_queries_t.T * scale).astype(bf16)).astype(jnp.float32)
    unused, back_query = jax.vjp(query_path, q_linear, gain_query)
    d_q_linear, d_gain_query = back_query(d_query_rot)
    unused, back_key = jax.vjp(key_path, k_linear, gain_key)
    d_k_linear, d_gain_key = back_key(d_keys)
    d_qkv = jnp.concatenate([d_q_linear, d_k_linear, d_values], axis=1).astype(bf16)
    qw = qcount * width
    d_w_qkv = contract_first(attn_in, d_qkv)
    d_attn_in = (
        contract_last(d_qkv[:, :qw], w_query)
        + contract_last(d_qkv[:, qw : qw + width], w_key)
        + contract_last(d_qkv[:, qw + width :], w_value)
    )
    unused, back_one = jax.vjp(norm_rows, inputs, gain_attn_in)
    d_inputs, d_gain_one = back_one(d_attn_in)
    grad_tokens = (d_hidden + d_inputs).astype(bf16)

    def cut(v):
        return v.reshape(nseq, heads, -1)

    wide = jnp.stack([cut(d_gain_one), cut(d_gain_two), cut(d_gain_three), cut(d_gain_four)], 2)
    narrow = jnp.stack([cut(d_gain_query), cut(d_gain_key)], 2)
    each, few = wide.shape[-1], narrow.shape[-1]
    gains = jnp.concatenate(
        [
            jnp.pad(wide, ((0, 0), (0, 0), (0, 0), (0, 128 - each))),
            jnp.pad(narrow, ((0, 0), (0, 0), (0, 2), (0, 128 - few))),
        ],
        axis=2,
    )
    sum_qkv, sum_out, sum_gains = scatter_all(
        [
            d_w_qkv.astype(bf16).reshape(nseq, heads, -1, d_qkv.shape[1]),
            d_w_out.astype(bf16).reshape(nseq, heads, -1, model),
            gains,
        ],
        [True, True, True],
        [[0] + ups, [0] + downs, [0] + downs],
        nseq,
        heads,
        7,
        "scatter_attn",
    )
    sum_gate, sum_up, sum_down = scatter_all(
        [
            d.astype(bf16).reshape(nseq, model // nseq, hidden_units)
            for d in (d_w_gate, d_w_up, d_w_down)
        ],
        [False, False, False],
        [[0] + ups, [0] + downs, [0] + ups],
        nseq,
        heads,
        8,
        "scatter_ffn",
    )
    return (
        output.astype(bf16),
        grad_tokens,
        sum_qkv[:, :qw],
        sum_qkv[:, qw : qw + width],
        sum_qkv[:, qw + width :],
        sum_out,
        sum_gate,
        sum_up,
        sum_down.T,
        sum_gains[0, :each],
        sum_gains[1, :each],
        sum_gains[2, :each],
        sum_gains[3, :each],
        sum_gains[4, :few],
        sum_gains[5, :few],
    )


def solution(mesh):
    rows = P(("seq", "head"), None)
    in_specs = (
        rows,
        P(),
        P(),
        P(),
        P(),
        P(),
        P(None, "head"),
        P(None, "head"),
        P("head", None),
        P(),
        P(),
        P(),
        P(),
        P(),
        P(),
        rows,
    )
    out_specs = (
        rows,
        rows,
        rows,
        rows,
        rows,
        rows,
        P("seq", "head"),
        P("seq", "head"),
        P("head", "seq"),
    ) + (P(("seq", "head")),) * 6
    return jax.shard_map(local, mesh=mesh, in_specs=in_specs, out_specs=out_specs, check_vma=False)
```

```python
import functools
import itertools
import math

import jax
import jax.numpy as jnp
from jax import lax
from jax.experimental import pallas as pl
from jax.experimental.pallas import tpu as pltpu
from jax.sharding import PartitionSpec as P

EPS = 1e-06
MESH = pl.DeviceIdType.MESH
VMEM = pltpu.VMEM
LIMIT = 56 * 2**20


def norm_rows(v, gain):
    return v * lax.rsqrt(jnp.mean(v * v, axis=-1, keepdims=True) + EPS) * gain


def rotate(v, cosines, sines):
    half = v.shape[-1] // 2
    first = v[..., :half]
    second = v[..., half:]
    return jnp.concatenate(
        [first * cosines - second * sines, second * cosines + first * sines], axis=-1
    )


def rope_tables(positions, width):
    half = width // 2
    freq = jnp.exp(jnp.arange(half, dtype=jnp.float32) * (-2.0 * math.log(1000000.0) / width))
    angle = positions.astype(jnp.float32)[:, None] * freq[None, :]
    return (jnp.cos(angle), jnp.sin(angle))


def contract_first(left, right):
    return lax.dot_general(
        left, right, (((0,), (0,)), ((), ())), preferred_element_type=jnp.float32
    )


def contract_last(left, right):
    return lax.dot_general(
        left, right, (((1,), (1,)), ((), ())), preferred_element_type=jnp.float32
    )


def place():
    return lax.axis_index("seq"), lax.axis_index("head")


def related(s, mask):
    out = s
    bit = 0
    while mask >> bit:
        if (mask >> bit) & 1:
            step = 1 << bit
            out = out + (1 - 2 * ((s // step) % 2)) * step
        bit += 1
    return out


def subsets(bits):
    out = [0]
    for bit in bits:
        out = out + [m | (1 << bit) for m in out]
    return out


def greet(targets):
    barrier = pltpu.get_barrier_semaphore()
    for target in targets:
        pl.semaphore_signal(barrier, inc=1, device_id=target, device_id_type=MESH)
    pl.semaphore_wait(barrier, len(targets))


def remote(src, dst, send, recv, target):
    return pltpu.make_async_remote_copy(
        src_ref=src,
        dst_ref=dst,
        send_sem=send,
        recv_sem=recv,
        device_id=target,
        device_id_type=MESH,
    )


def seq_orders(bits):
    upper = list(range(1, bits))
    return upper, upper[::-1]


def gather_kernel(nseq, heads, local_refs, out_refs, send, recv):
    bits = nseq.bit_length() - 1
    s, h = place()
    others = [lax.rem(h + d, heads) for d in range(1, heads)]
    greet([(related(s, 1 << b), h) for b in range(bits)] + [(s, o) for o in others])
    count = [0]
    started = []

    def go(src, dst, target):
        k = count[0]
        count[0] += 1
        copy = remote(src, dst, send.at[k], recv.at[k], target)
        copy.start()
        started.append(copy)
        return copy

    first = []
    for a in range(len(out_refs)):
        out_refs[a][s, h] = local_refs[a][...]
        first.append(
            [go(local_refs[a], out_refs[a].at[s, h], (s, o)) for o in others]
        )
    orders = [o + [0] for o in seq_orders(bits)]
    held = [{0: first[a]} for a in range(len(out_refs))]
    for stage in range(bits):
        for a in range(len(out_refs)):
            bit = orders[a % 2][stage]
            target = (related(s, 1 << bit), h)
            arrived = {}
            for mask in list(held[a]):
                for copy in held[a][mask]:
                    copy.wait_recv()
                held[a][mask] = []
                group = related(s, mask)
                copy = go(out_refs[a].at[group], out_refs[a].at[group], target)
                arrived[mask | (1 << bit)] = [copy]
            held[a].update(arrived)
    for a in range(len(out_refs)):
        for mask in held[a]:
            for copy in held[a][mask]:
                copy.wait_recv()
    for copy in started:
        copy.wait_send()


def gather_all(arrays, nseq, heads, cid):
    n = len(arrays)
    total = n * (heads - 1 + nseq - 1)

    def kernel(*refs):
        gather_kernel(nseq, heads, refs[:n], refs[n : 2 * n], refs[2 * n], refs[2 * n + 1])

    return pl.pallas_call(
        kernel,
        out_shape=[jax.ShapeDtypeStruct((nseq, heads) + a.shape, a.dtype) for a in arrays],
        in_specs=[pl.BlockSpec(memory_space=VMEM)] * n,
        out_specs=[pl.BlockSpec(memory_space=VMEM)] * n,
        scratch_shapes=[pltpu.SemaphoreType.DMA((total,)), pltpu.SemaphoreType.DMA((total,))],
        name="gather_all",
        compiler_params=pltpu.CompilerParams(
            collective_id=cid, has_side_effects=True, vmem_limit_bytes=LIMIT
        ),
    )(*arrays)


def line_gather_kernel(heads, x_ref, out_ref, send, recv):
    s, h = place()
    right = (s, lax.rem(h + 1, heads))
    left = (s, lax.rem(h + heads - 1, heads))
    greet([right, left])
    out_ref[h] = x_ref[...]
    for step in range(heads - 1):
        to_right = remote(
            out_ref.at[jnp.maximum(h - step, 0)],
            out_ref.at[jnp.maximum(h - step, 0)],
            send.at[0, step],
            recv.at[0, step],
            right,
        )
        to_left = remote(
            out_ref.at[jnp.minimum(h + step, heads - 1)],
            out_ref.at[jnp.minimum(h + step, heads - 1)],
            send.at[1, step],
            recv.at[1, step],
            left,
        )
        pl.when((h - step >= 0) & (h < heads - 1))(to_right.start)
        pl.when((h + step <= heads - 1) & (h > 0))(to_left.start)
        pl.when(h - 1 - step >= 0)(
            remote(
                out_ref.at[jnp.maximum(h - 1 - step, 0)],
                out_ref.at[jnp.maximum(h - 1 - step, 0)],
                send.at[0, step],
                recv.at[0, step],
                right,
            ).wait_recv
        )
        pl.when(h + 1 + step <= heads - 1)(
            remote(
                out_ref.at[jnp.minimum(h + 1 + step, heads - 1)],
                out_ref.at[jnp.minimum(h + 1 + step, heads - 1)],
                send.at[1, step],
                recv.at[1, step],
                left,
            ).wait_recv
        )
        pl.when((h - step >= 0) & (h < heads - 1))(to_right.wait_send)
        pl.when((h + step <= heads - 1) & (h > 0))(to_left.wait_send)


def line_gather(x, heads, cid):
    return pl.pallas_call(
        functools.partial(line_gather_kernel, heads),
        out_shape=jax.ShapeDtypeStruct((heads,) + x.shape, x.dtype),
        in_specs=[pl.BlockSpec(memory_space=VMEM)],
        out_specs=pl.BlockSpec(memory_space=VMEM),
        scratch_shapes=[
            pltpu.SemaphoreType.DMA((2, heads - 1)),
            pltpu.SemaphoreType.DMA((2, heads - 1)),
        ],
        name="line_gather",
        compiler_params=pltpu.CompilerParams(
            collective_id=cid, has_side_effects=True, vmem_limit_bytes=LIMIT
        ),
    )(x)


def line_scatter_kernel(heads, parts, out_ref, from_left, from_right, send, recv):
    s, h = place()
    last = heads - 1
    right = (s, lax.rem(h + 1, heads))
    left = (s, lax.rem(h + heads - 1, heads))
    greet([right, left])
    f32 = jnp.float32
    for step in range(heads - 1):
        r_dest = jnp.clip(last - (step - h), 0, last)
        l_dest = jnp.clip(step - (last - h), 0, last)
        r_on = (step >= h) & (h < last)
        l_on = (step >= last - h) & (h > 0)
        for on, dest, box, lane, target, first in (
            (r_on, r_dest, from_left, 0, right, step == h),
            (l_on, l_dest, from_right, 1, left, step == last - h),
        ):
            at_end = (h == 0) if lane == 0 else (h == last)
            if step > 0:

                def add(box=box, dest=dest):
                    box[step - 1] = (
                        box[step - 1].astype(f32) + parts[dest].astype(f32)
                    ).astype(box.dtype)

                pl.when(on & jnp.logical_not(at_end))(add)
                pl.when(on & jnp.logical_not(at_end))(
                    remote(
                        box.at[step - 1], box.at[step], send.at[lane, step], recv.at[lane, step], target
                    ).start
                )
            pl.when(on & at_end)(
                remote(
                    parts.at[dest], box.at[step], send.at[lane, step], recv.at[lane, step], target
                ).start
            )
        r_in = (step >= h - 1) & (h > 0)
        l_in = (step >= last - h - 1) & (h < last)
        pl.when(r_in)(
            remote(
                from_left.at[step], from_left.at[step], send.at[0, step], recv.at[0, step], right
            ).wait_recv
        )
        pl.when(l_in)(
            remote(
                from_right.at[step], from_right.at[step], send.at[1, step], recv.at[1, step], left
            ).wait_recv
        )
    for step in range(heads - 1):
        for on, box, lane, target in (
            ((step >= h) & (h < last), from_left, 0, right),
            ((step >= last - h) & (h > 0), from_right, 1, left),
        ):
            pl.when(on)(
                remote(
                    box.at[step], box.at[step], send.at[lane, step], recv.at[lane, step], target
                ).wait_send
            )
    out_ref[...] = parts[h].astype(f32)

    def add_left():
        out_ref[...] += from_left[heads - 2].astype(f32)

    def add_right():
        out_ref[...] += from_right[heads - 2].astype(f32)

    pl.when(h > 0)(add_left)
    pl.when(h < last)(add_right)


def line_scatter(parts, heads, cid):
    block = parts.shape[1:]
    return pl.pallas_call(
        functools.partial(line_scatter_kernel, heads),
        out_shape=jax.ShapeDtypeStruct(block, jnp.float32),
        in_specs=[pl.BlockSpec(memory_space=VMEM)],
        out_specs=pl.BlockSpec(memory_space=VMEM),
        scratch_shapes=[
            VMEM((heads - 1,) + block, parts.dtype),
            VMEM((heads - 1,) + block, parts.dtype),
            pltpu.SemaphoreType.DMA((2, heads - 1)),
            pltpu.SemaphoreType.DMA((2, heads - 1)),
        ],
        name="line_scatter",
        compiler_params=pltpu.CompilerParams(
            collective_id=cid, has_side_effects=True, vmem_limit_bytes=LIMIT
        ),
    )(parts)


def scatter_kernel(nseq, heads, zs, orders, parts, outs, boxes, zboxes, send, recv):
    bits = nseq.bit_length() - 1
    s, h = place()
    f32 = jnp.float32
    others = [lax.rem(h + d, heads) for d in range(1, heads)]
    greet(
        [(related(s, 1 << b), h) for b in range(bits)]
        + ([(s, o) for o in others] if any(zs) else [])
    )
    count = [0]
    started = []

    def go(src, dst, target):
        k = count[0]
        count[0] += 1
        copy = remote(src, dst, send.at[k], recv.at[k], target)
        copy.start()
        started.append(copy)
        return copy

    n = len(parts)
    offsets = [0] * n
    slot = [{} for _ in range(n)]
    waiting = [{} for _ in range(n)]

    def current(a, mask):
        if mask in slot[a]:
            return boxes[a].at[slot[a][mask]]
        return parts[a].at[related(s, mask)]

    def launch(a, stage):
        bit = orders[a][stage]
        rest = orders[a][stage + 1 :]
        target = (related(s, 1 << bit), h)
        after = 1 << rest[0] if rest else 0
        masks = sorted(subsets(rest), key=lambda m: 0 if m & after else 1)
        for mask in masks:
            where = offsets[a]
            offsets[a] += 1
            waiting[a][mask] = (
                go(current(a, mask | (1 << bit)), boxes[a].at[where], target),
                where,
            )

    def settle(a, mask):
        copy, where = waiting[a].pop(mask)
        mine = current(a, mask)
        copy.wait_recv()
        boxes[a][where] = (boxes[a][where].astype(f32) + mine[...].astype(f32)).astype(
            boxes[a].dtype
        )
        slot[a][mask] = where

    for a in range(n):
        launch(a, 0)
    for stage in range(bits):
        for a in range(n):
            for mask in list(waiting[a]):
                settle(a, mask)
            if stage + 1 < bits:
                launch(a, stage + 1)
    arriving = []
    for a in range(n):
        if not zs[a]:
            continue
        mine = current(a, 0)
        arriving.append(
            [
                go(mine.at[o], zboxes[a].at[d], (s, o))
                for d, o in enumerate(others)
            ]
        )
    z = 0
    for a in range(n):
        if zs[a]:
            total = current(a, 0)[h].astype(f32)
            for d, copy in enumerate(arriving[z]):
                copy.wait_recv()
                total = total + zboxes[a][d].astype(f32)
            outs[a][...] = total
            z += 1
        else:
            outs[a][...] = current(a, 0)[...].astype(f32)
    for copy in started:
        copy.wait_send()


def scatter_all(arrays, zs, orders, nseq, heads, cid, name):
    n = len(arrays)
    total = sum((nseq - 1) + (heads - 1 if z else 0) for z in zs)
    blocks = [a.shape[2:] if z else a.shape[1:] for a, z in zip(arrays, zs)]

    def kernel(*refs):
        scatter_kernel(
            nseq,
            heads,
            zs,
            orders,
            refs[:n],
            refs[n : 2 * n],
            refs[2 * n : 3 * n],
            refs[3 * n : 4 * n],
            refs[4 * n],
            refs[4 * n + 1],
        )

    return pl.pallas_call(
        kernel,
        out_shape=[jax.ShapeDtypeStruct(b, jnp.float32) for b in blocks],
        in_specs=[pl.BlockSpec(memory_space=VMEM)] * n,
        out_specs=[pl.BlockSpec(memory_space=VMEM)] * n,
        scratch_shapes=[VMEM((nseq - 1,) + a.shape[1:], a.dtype) for a in arrays]
        + [
            VMEM((heads - 1,) + b, a.dtype) if z else VMEM((8, 128), jnp.float32)
            for a, b, z in zip(arrays, blocks, zs)
        ]
        + [pltpu.SemaphoreType.DMA((total,)), pltpu.SemaphoreType.DMA((total,))],
        name=name,
        compiler_params=pltpu.CompilerParams(
            collective_id=cid, has_side_effects=True, vmem_limit_bytes=LIMIT
        ),
    )(*arrays)


def attend_kernel(q_ref, k_ref, v_ref, start_ref, index_ref, out_ref, log_ref):
    s = lax.axis_index("seq")
    span = k_ref.shape[1]
    start = start_ref[...]
    index = index_ref[...]
    queries = q_ref[...]
    rows = queries.shape[0]
    out_ref[...] = jnp.zeros_like(out_ref)

    def step(g, mass):
        scores = contract_last(k_ref[g], queries)
        key = g * span + lax.broadcasted_iota(jnp.int32, (span, rows), 0)
        terms = jnp.where((key >= start) & (key <= index), jnp.exp(scores), 0.0)
        out_ref[...] += contract_first(v_ref[g], terms.astype(jnp.bfloat16))
        return mass + jnp.sum(terms, axis=0, keepdims=True)

    mass = lax.fori_loop(0, s + 1, step, jnp.zeros((1, rows), jnp.float32))
    out_ref[...] = out_ref[...] / mass
    log_ref[...] = jnp.log(mass)


def attend(q, k, v, start, index):
    rows, width = q.shape
    return pl.pallas_call(
        attend_kernel,
        out_shape=[
            jax.ShapeDtypeStruct((width, rows), jnp.float32),
            jax.ShapeDtypeStruct((1, rows), jnp.float32),
        ],
        in_specs=[pl.BlockSpec(memory_space=VMEM)] * 5,
        out_specs=[pl.BlockSpec(memory_space=VMEM)] * 2,
        name="attend",
        compiler_params=pltpu.CompilerParams(vmem_limit_bytes=LIMIT),
    )(q, k, v, start, index)


def attend_back_kernel(
    q_ref, k_ref, v_ref, start_ref, index_ref, log_ref, dots_ref, d_ref, dq_ref, dk_ref, dv_ref
):
    s = lax.axis_index("seq")
    groups, span = k_ref.shape[:2]
    start = start_ref[...]
    index = index_ref[...]
    log_total = log_ref[...]
    dots = dots_ref[...]
    queries = q_ref[...]
    grads = d_ref[...]
    rows = queries.shape[0]
    dq_ref[...] = jnp.zeros_like(dq_ref)

    def step(g, carry):
        keys = k_ref[g]
        scores = contract_last(keys, queries)
        key = g * span + lax.broadcasted_iota(jnp.int32, (span, rows), 0)
        probs = jnp.where((key >= start) & (key <= index), jnp.exp(scores - log_total), 0.0)
        d_probs = contract_last(v_ref[g], grads)
        d_scores = (probs * (d_probs - dots)).astype(jnp.bfloat16)
        dv_ref[g] = jnp.dot(
            probs.astype(jnp.bfloat16), grads, preferred_element_type=jnp.float32
        ).astype(dv_ref.dtype)
        dk_ref[g] = jnp.dot(d_scores, queries, preferred_element_type=jnp.float32).astype(
            dk_ref.dtype
        )
        dq_ref[...] += contract_first(keys, d_scores)
        return carry

    lax.fori_loop(0, s + 1, step, 0)

    def blank(g, carry):
        dk_ref[g] = jnp.zeros(dk_ref.shape[1:], dk_ref.dtype)
        dv_ref[g] = jnp.zeros(dv_ref.shape[1:], dv_ref.dtype)
        return carry

    lax.fori_loop(s + 1, groups, blank, 0)


def attend_back(q, k, v, start, index, log_total, dots, grads):
    rows, width = q.shape
    return pl.pallas_call(
        attend_back_kernel,
        out_shape=[
            jax.ShapeDtypeStruct((width, rows), jnp.float32),
            jax.ShapeDtypeStruct(k.shape, jnp.bfloat16),
            jax.ShapeDtypeStruct(v.shape, jnp.bfloat16),
        ],
        in_specs=[pl.BlockSpec(memory_space=VMEM)] * 8,
        out_specs=[pl.BlockSpec(memory_space=VMEM)] * 3,
        name="attend_back",
        compiler_params=pltpu.CompilerParams(vmem_limit_bytes=LIMIT),
    )(q, k, v, start, index, log_total, dots, grads)


def flat(ref):
    return ref[...].reshape(1, ref.shape[0])


def front_kernel(
    nseq,
    heads,
    qcount,
    scale,
    x_ref,
    ids_ref,
    w_key_ref,
    w_value_ref,
    gain_in_ref,
    gain_q_ref,
    gain_k_ref,
    w_query_far,
    w_out_far,
    o_proj,
    o_q,
    o_k,
    o_v,
    o_start,
    o_index,
    o_log,
    o_att,
    o_q_lin,
    o_k_lin,
    o_cos,
    o_sin,
    o_attn_t,
    w_query,
    w_out,
    k_all,
    v_all,
    send,
    recv,
    local_sem,
):
    f32, bf16 = jnp.float32, jnp.bfloat16
    bits = nseq.bit_length() - 1
    ups, downs = seq_orders(bits)
    links = Links(nseq, heads, send, recv)
    s, h = links.s, links.h
    rows, model = x_ref.shape
    width = w_key_ref.shape[1]
    gain_q, gain_k = flat(gain_q_ref), flat(gain_k_ref)
    half = width // 2
    total = ids_ref.shape[0] * ids_ref.shape[1]
    load_q = pltpu.make_async_copy(w_query_far, w_query, local_sem.at[0])
    load_q.start()
    load_o = pltpu.make_async_copy(w_out_far, w_out, local_sem.at[1])
    load_o.start()
    partners = [related(h, j) for j in range(1, heads)]
    greet([links.across(b) for b in range(bits)] + [(s, o) for o in partners])

    which = s * heads + h
    mine = ids_ref[pl.ds(which, 1), :].astype(f32)
    column = jnp.broadcast_to(mine, (rows, rows)).T[:, 0:1]
    first = jnp.full((rows, rows), float(total), f32)
    for r in range(ids_ref.shape[0]):
        here = ids_ref[r : r + 1, :].astype(f32)
        at = (r * rows + lax.broadcasted_iota(jnp.int32, (1, rows), 1)).astype(f32)
        first = jnp.minimum(first, jnp.where(column == here, at, float(total)))
    start = jnp.min(first, axis=1, keepdims=True)
    index = (which * rows + lax.broadcasted_iota(jnp.int32, (rows, 1), 0)).astype(f32)
    freq = jnp.exp(
        lax.broadcasted_iota(jnp.int32, (1, half), 1).astype(f32)
        * (-2.0 * math.log(1000000.0) / width)
    )
    angle = (index - start) * freq
    turns = jnp.round(angle * (1.0 / (2.0 * math.pi)))
    angle = (angle - turns * 6.28125) - turns * (2.0 * math.pi - 6.28125)
    cosines, sines = jnp.cos(angle), jnp.sin(angle)
    o_cos[...] = cosines
    o_sin[...] = sines
    start_row = jnp.broadcast_to(start, (rows, rows)).T[0:1, :].astype(jnp.int32)
    index_row = which * rows + lax.broadcasted_iota(jnp.int32, (1, rows), 1)
    for j in range(qcount):
        o_start[:, pl.ds(j * rows, rows)] = start_row
        o_index[:, pl.ds(j * rows, rows)] = index_row

    attn_in = norm_rows(x_ref[...].astype(f32), flat(gain_in_ref)).astype(bf16)
    k_lin = jnp.dot(attn_in, w_key_ref[...], preferred_element_type=f32)
    k_all[s, h] = rotate(norm_rows(k_lin, gain_k), cosines, sines).astype(bf16)
    o_k_lin[...] = k_lin
    v_all[s, h] = jnp.dot(attn_in, w_value_ref[...], preferred_element_type=f32).astype(bf16)

    both = ((k_all, ups), (v_all, downs))

    def pass_on(a, mask, j, bit):
        buf = both[a][0]
        block = buf.at[related(s, mask), related(h, j)]
        return links.go(block, block, links.across(bit))

    over_head = {}
    for j in range(1, heads):
        for a in range(2):
            block = both[a][0].at[s, h]
            over_head[a, j] = links.go(block, block, (s, partners[j - 1]))
    arriving = {}

    def spread(a, mask, j, stage):
        order = both[a][1]
        for later in range(stage, len(order)):
            bit = order[later]
            arriving[a, mask | (1 << bit), j] = pass_on(a, mask, j, bit)

    for a in range(2):
        spread(a, 0, 0, 0)

    load_q.wait()
    q_lin = jnp.dot(attn_in, w_query[...], preferred_element_type=f32)
    o_q_lin[...] = q_lin
    for j in range(1, heads):
        for a in range(2):
            over_head[a, j].wait_recv()
            spread(a, 0, j, 0)
    for j in range(qcount):
        part = norm_rows(q_lin[:, j * width : (j + 1) * width], gain_q)
        o_q[pl.ds(j * rows, rows), :] = (rotate(part, cosines, sines) * scale).astype(bf16)

    pairs = []

    def to_pair(a, mask):
        block = both[a][0].at[related(s, mask)]
        pairs.append(links.go(block, block, links.across(0)))

    for a in range(2):
        to_pair(a, 0)
    for stage in range(len(ups)):
        for lower in subsets(range(stage)):
            masks = []
            for a in range(2):
                order = both[a][1]
                mask = sum(1 << order[i] for i in range(stage) if lower >> i & 1)
                masks.append(mask | (1 << order[stage]))
            for j in range(heads):
                for a in range(2):
                    arriving[a, masks[a], j].wait_recv()
                    spread(a, masks[a], j, stage + 1)
            for a in range(2):
                to_pair(a, masks[a])
    for j in range(1):
        o_attn_t[...] = attn_in.T.reshape(o_attn_t.shape)

    queries = o_q[...]
    starts = o_start[...]
    indices = o_index[...]
    o_att[...] = jnp.zeros_like(o_att)
    span = heads * rows
    low = lax.rem(s, 2)

    def attend_group(g, mass):
        scores = contract_last(k_all[g].reshape(span, width), queries)
        key = g * span + lax.broadcasted_iota(jnp.int32, scores.shape, 0)
        terms = jnp.where((key >= starts) & (key <= indices), jnp.exp(scores), 0.0)
        o_att[...] += contract_first(v_all[g].reshape(span, width), terms.astype(bf16))
        return mass + jnp.sum(terms, axis=0, keepdims=True)

    mass = lax.fori_loop(
        0,
        s // 2 + 1,
        lambda i, m: attend_group(2 * i + low, m),
        jnp.zeros((1, qcount * rows), f32),
    )
    for copy in pairs:
        copy.wait_recv()
    keep_k = pltpu.make_async_copy(k_all, o_k, local_sem.at[2])
    keep_v = pltpu.make_async_copy(v_all, o_v, local_sem.at[3])
    keep_k.start()
    keep_v.start()
    mass = lax.fori_loop(
        0, s // 2 + low, lambda i, m: attend_group(2 * i + 1 - low, m), mass
    )
    o_log[...] = jnp.log(mass)
    attended = o_att[...] / mass
    o_att[...] = attended
    load_o.wait()
    proj = jnp.zeros((rows, model), f32)
    for j in range(qcount):
        part = attended[:, j * rows : (j + 1) * rows].T.astype(bf16)
        proj = proj + jnp.dot(
            part, w_out[pl.ds(j * width, width), :], preferred_element_type=f32
        )
    o_proj[...] = proj
    keep_k.wait()
    keep_v.wait()
    links.finish()


def front(nseq, heads, qcount, scale, cid, x, ids, w_key, w_value, gain_in, gain_q, gain_k, w_query, w_out):
    f32, bf16, i32 = jnp.float32, jnp.bfloat16, jnp.int32
    rows, model = x.shape
    width = w_key.shape[1]
    stacked = qcount * rows
    some = nseq // 2
    messages = 2 * (heads - 1) + 2 * heads * (some - 1) + 2 * some
    vm = pl.BlockSpec(memory_space=VMEM)
    anywhere = pl.BlockSpec(memory_space=pl.ANY)
    everyone = (nseq, heads, rows, width)

    def kernel(*refs):
        front_kernel(nseq, heads, qcount, scale, *refs)

    shape = jax.ShapeDtypeStruct
    return pl.pallas_call(
        kernel,
        out_shape=[
            shape((rows, model), f32),
            shape((stacked, width), bf16),
            shape(everyone, bf16),
            shape(everyone, bf16),
            shape((1, stacked), i32),
            shape((1, stacked), i32),
            shape((1, stacked), f32),
            shape((width, stacked), f32),
            shape((rows, qcount * width), f32),
            shape((rows, width), f32),
            shape((rows, width // 2), f32),
            shape((rows, width // 2), f32),
            shape((nseq, model // nseq, rows), bf16),
        ],
        in_specs=[vm] * 7 + [anywhere] * 2,
        out_specs=[vm] * 2 + [anywhere] * 2 + [vm] * 9,
        scratch_shapes=[
            VMEM(w_query.shape, bf16),
            VMEM(w_out.shape, bf16),
            VMEM(everyone, bf16),
            VMEM(everyone, bf16),
            pltpu.SemaphoreType.DMA((messages,)),
            pltpu.SemaphoreType.DMA((messages,)),
            pltpu.SemaphoreType.DMA((4,)),
        ],
        name="front",
        compiler_params=pltpu.CompilerParams(
            collective_id=cid, has_side_effects=True, vmem_limit_bytes=LIMIT
        ),
    )(
        x,
        ids.reshape(nseq * heads, rows),
        w_key,
        w_value,
        gain_in,
        gain_q,
        gain_k,
        w_query,
        w_out,
    )


class Sum:
    def __init__(self, links, part, boxes, order):
        self.links, self.part, self.boxes, self.order = links, part, boxes, order
        self.used = 0
        self.slot = {}
        self.waiting = {}

    def current(self, mask):
        if mask in self.slot:
            return self.boxes.at[self.slot[mask]]
        return self.part(mask)

    def masks(self, stage):
        rest = self.order[stage + 1 :]
        weight = lambda m: sum(1 << (len(rest) - i) for i, b in enumerate(rest) if m >> b & 1)
        return sorted(subsets(rest), key=weight, reverse=True)

    def send(self, stage, mask):
        bit = self.order[stage]
        where = self.used
        self.used += 1
        copy = self.links.go(
            self.current(mask | (1 << bit)), self.boxes.at[where], self.links.across(bit)
        )
        self.waiting[stage, mask] = (copy, where)

    def start(self):
        for mask in self.masks(0):
            self.send(0, mask)

    def steps(self, stage, kept=None):
        def step(mask):
            copy, where = self.waiting.pop((stage, mask))
            mine = kept(mask) if kept is not None else self.current(mask)
            copy.wait_recv()
            self.boxes[where] = self.boxes[where] + mine[...]
            self.slot[mask] = where
            if stage + 1 < len(self.order):
                bit = 1 << self.order[stage + 1]
                if mask & bit:
                    self.send(stage + 1, mask & ~bit)

        return [functools.partial(step, mask) for mask in self.masks(stage)]

    def last(self, kept=None):
        copy, where = self.waiting.pop((len(self.order) - 1, 0))
        mine = kept(0) if kept is not None else self.current(0)
        copy.wait_recv()
        return self.boxes[where].astype(jnp.float32) + mine[...].astype(jnp.float32)


def in_turn(*lists):
    for group in itertools.zip_longest(*lists):
        for step in group:
            if step is not None:
                step()


def split_rows(rows):
    return (rows // 2 + 15) // 16 * 16


class Links:
    def __init__(self, nseq, heads, send, recv):
        self.s, self.h = place()
        self.nseq, self.heads = nseq, heads
        self.send, self.recv = send, recv
        self.count = 0
        self.started = []
        self.others = [lax.rem(self.h + d, heads) for d in range(1, heads)]

    def greet(self, more=()):
        bits = self.nseq.bit_length() - 1
        near = [self.across(b) for b in range(bits)]
        greet(near + [(self.s, o) for o in self.others] + list(more))

    def across(self, bit):
        return (related(self.s, 1 << bit), self.h)

    def go(self, src, dst, target):
        k = self.count
        self.count += 1
        copy = remote(src, dst, self.send.at[k], self.recv.at[k], target)
        copy.start()
        self.started.append(copy)
        return copy

    def over_heads(self, src, boxes):
        return [self.go(src.at[o], boxes.at[d], (self.s, o)) for d, o in enumerate(self.others)]

    def finish(self):
        for copy in self.started:
            copy.wait_send()


def back_norm(v, gain, d_out):
    scale = lax.rsqrt(jnp.mean(v * v, axis=-1, keepdims=True) + EPS)
    unit = v * scale
    inner = d_out * gain
    d_v = scale * (inner - unit * jnp.mean(inner * unit, axis=-1, keepdims=True))
    return d_v, jnp.sum(d_out * unit, axis=0, keepdims=True)


def back_rotate(d, cosines, sines):
    half = d.shape[-1] // 2
    first, second = d[:, :half], d[:, half:]
    return jnp.concatenate(
        [first * cosines + second * sines, second * cosines - first * sines], axis=-1
    )


def tail_kernel(
    nseq,
    heads,
    qcount,
    scale,
    q_ref,
    start_ref,
    index_ref,
    log_ref,
    att_ref,
    d_proj_ref,
    k_lin_ref,
    cos_ref,
    sin_ref,
    gain_q_ref,
    gain_k_ref,
    gain_in_ref,
    gains_ref,
    k_far,
    v_far,
    w_out_far,
    q_lin_far,
    attn_t_far,
    x_far,
    d_hid_far,
    w_query_far,
    w_key_far,
    w_value_far,
    d_gate_ref,
    d_up_ref,
    d_down_first,
    d_down_second,
    o_tokens,
    o_qkv,
    o_out,
    o_gate,
    o_up,
    o_down,
    o_gains,
    k_ref,
    v_ref,
    w_out_ref,
    q_lin_ref,
    attn_t_ref,
    x_ref,
    d_hid_ref,
    w_qkv_ref,
    dk,
    dv,
    dq_t,
    grads,
    grads_t,
    box_k,
    box_v,
    zbox_k,
    zbox_v,
    dw_out,
    box_out,
    zbox_out,
    mid_out,
    end_out,
    dw_qkv,
    box_qkv,
    zsrc_qkv,
    zbox_qkv,
    d_qkv,
    keep_gate_first,
    keep_gate_second,
    keep_up_first,
    keep_up_second,
    keep_down_first,
    keep_down_second,
    box_gate_first,
    box_gate_second,
    box_up_first,
    box_up_second,
    box_down_first,
    box_down_second,
    gsum,
    gbox,
    gzbox,
    send,
    recv,
    local_sem,
):
    f32, bf16 = jnp.float32, jnp.bfloat16
    bits = nseq.bit_length() - 1
    ups, downs = seq_orders(bits)
    links = Links(nseq, heads, send, recv)
    s, h = links.s, links.h
    rows, model = d_proj_ref.shape
    width = k_lin_ref.shape[1]
    gain_q, gain_k = flat(gain_q_ref), flat(gain_k_ref)
    groups, span = k_ref.shape[:2]
    loads = []

    def load(src, dst):
        copy = pltpu.make_async_copy(src, dst, local_sem.at[len(loads)])
        copy.start()
        loads.append(copy)
        return copy

    load_o = load(w_out_far, w_out_ref)
    load_k = load(k_far, k_ref)
    load_v = load(v_far, v_ref)
    plane = subsets(ups)[1:]
    links.greet([(related(s, m), links.h) for m in plane if m & (m - 1)])

    held = subsets(ups)
    ffn = []
    split = keep_gate_first.shape[1]
    for src, keep, box, order, low, past in (
        (d_gate_ref, keep_gate_first, box_gate_first, ups, 0, 1),
        (d_gate_ref, keep_gate_second, box_gate_second, downs, split, 1),
        (d_up_ref, keep_up_first, box_up_first, [0] + ups, 0, 0),
        (d_up_ref, keep_up_second, box_up_second, [0] + downs, split, 0),
        (d_down_first, keep_down_first, box_down_first, ups[1:], 0, 2),
        (d_down_second, keep_down_second, box_down_second, downs[1:], 0, 2),
    ):
        here = pl.ds(low, keep.shape[1])

        def part(m, src=src, here=here, past=past, order=order):
            if past == 0:
                return src.at[related(s, m), here]
            if past == 1:
                return src.at[held.index(m), here]
            return src.at[0 if m else 1, here]

        total = Sum(links, part, box, order)
        kept = subsets(order[1:])
        total.loads = [load(part(m), keep.at[i]) for i, m in enumerate(kept)]
        total.kept = lambda m, keep=keep, kept=kept: keep.at[kept.index(m)]
        ffn.append(total)
    gate, up, down = ffn[0:2], ffn[2:4], ffn[4:6]
    for total in up + gate + down:
        total.start()

    def settle(pair, stage, first=False):
        if first:
            for total in pair:
                for copy in total.loads:
                    copy.wait()
        in_turn(*[total.steps(stage, total.kept if first else None) for total in pair])

    def put(pair, out, first=False):
        at = 0
        for total in pair:
            value = total.last(total.kept if first else None).astype(out.dtype)
            out[pl.ds(at, value.shape[0]), :] = value
            at += value.shape[0]

    load_q = load(q_lin_far, q_lin_ref)
    load_a = load(attn_t_far, attn_t_ref)
    load_x = load(x_far, x_ref)
    load_d = load(d_hid_far, d_hid_ref)
    load_w = []
    at = 0
    for far in (w_query_far, w_key_far, w_value_far):
        load_w.append(load(far, w_qkv_ref.at[:, pl.ds(at, far.shape[1])]))
        at += far.shape[1]

    d_proj = d_proj_ref[...]

    out_rows = dw_out.shape[1] * dw_out.shape[2]

    def out_block(j, carry):
        low = pl.multiple_of((j * out_rows) % width, out_rows)
        head = pl.multiple_of((j * out_rows) // width * rows, rows)
        mixed_t = att_ref[pl.ds(low, out_rows), pl.ds(head, rows)].astype(bf16)
        dw_out[j] = (
            jnp.dot(mixed_t, d_proj, preferred_element_type=f32)
            .astype(bf16)
            .reshape(dw_out.shape[1:])
        )
        return carry

    lax.fori_loop(0, nseq, out_block, 0)
    sum_out = Sum(links, lambda m: dw_out.at[related(s, m)], box_out, [0])
    sum_out.masks = lambda stage: held
    sum_out.start()

    load_o.wait()

    def back_out(j, carry):
        part = w_out_ref[pl.ds(pl.multiple_of(j * width, width), width), :]
        here = pl.ds(pl.multiple_of(j * rows, rows), rows)
        grads[here, :] = contract_last(d_proj, part).astype(bf16)
        grads_t[:, here] = contract_last(part, d_proj).astype(bf16)
        return carry

    lax.fori_loop(0, qcount, back_out, 0)
    in_turn(sum_out.steps(0))
    z_out = [
        links.go(box_out.at[:, o], zbox_out.at[d], (s, o)) for d, o in enumerate(links.others)
    ]
    dots = jnp.sum(grads_t[...].astype(f32) * att_ref[...], axis=0, keepdims=True)
    start = start_ref[...]
    index = index_ref[...]
    log_total = log_ref[...]
    dq_t[...] = jnp.zeros_like(dq_t)
    load_k.wait()
    load_v.wait()

    def step(g, carry):
        keys = k_ref[g]
        queries = q_ref[...]
        scores = contract_last(keys, queries)
        key = g * span + lax.broadcasted_iota(jnp.int32, scores.shape, 0)
        probs = jnp.where((key >= start) & (key <= index), jnp.exp(scores - log_total), 0.0)
        d_probs = jnp.dot(v_ref[g], grads_t[...], preferred_element_type=f32)
        d_scores = (probs * (d_probs - dots)).astype(bf16)
        dv[g] = (
            jnp.dot(probs.astype(bf16), grads[...], preferred_element_type=f32)
            .astype(bf16)
            .reshape(dv.shape[1:])
        )
        dk[g] = (
            jnp.dot(d_scores, queries, preferred_element_type=f32)
            .astype(bf16)
            .reshape(dk.shape[1:])
        )
        dq_t[...] += contract_first(keys, d_scores)
        return carry

    def blank(g, carry):
        dk[g] = jnp.zeros(dk.shape[1:], bf16)
        dv[g] = jnp.zeros(dv.shape[1:], bf16)
        return carry

    lax.fori_loop(0, s + 1, step, 0)
    lax.fori_loop(s + 1, groups, blank, 0)

    kv = []
    for j in list(range(1, heads)) + [0]:
        owner = lax.rem(h + j, heads)
        for far, box, order in ((dk, box_k, ups), (dv, box_v, downs)):
            kv.append(
                Sum(
                    links,
                    lambda m, far=far, owner=owner: far.at[related(s, m), owner],
                    box.at[j],
                    [0] + order,
                )
            )
    for mask_index in range(len(held)):
        for total in kv:
            total.send(0, total.masks(0)[mask_index])

    in_turn(*[total.steps(0) for total in kv])

    load_q.wait()
    cosines, sines = cos_ref[...], sin_ref[...]
    d_gain_q = jnp.zeros((1, width), f32)
    for j in range(qcount):
        d_rot = dq_t[:, pl.ds(j * rows, rows)].T * scale
        d_lin, terms = back_norm(
            q_lin_ref[:, pl.ds(j * width, width)],
            gain_q,
            back_rotate(d_rot, cosines, sines),
        )
        d_qkv[:, pl.ds(j * width, width)] = d_lin.astype(bf16)
        d_gain_q = d_gain_q + terms

    for stage in range(1, bits - 1):
        in_turn(*[total.steps(stage) for total in kv])
    settle(gate, 0, True)

    arriving = {}
    for i, total in enumerate(kv):
        for m in total.steps(bits - 1):
            m()
        j = (i // 2 + 1) % heads
        if j:
            zbox = (zbox_k, zbox_v)[i % 2]
            arriving[i % 2, j] = links.go(
                total.current(0), zbox.at[j - 1], (s, links.others[j - 1])
            )
    for d, copy in enumerate(z_out):
        copy.wait_recv()
    own = box_out[:, h].astype(f32)
    for d in range(heads - 1):
        own = own + zbox_out[d].astype(f32)
    mid_out[...] = own.astype(bf16)
    sum_end = Sum(links, lambda m: mid_out.at[held.index(m)], end_out, downs)
    sum_end.start()


    settle(up, 0, True)

    def whole(i, zbox):
        total = kv[len(kv) - 2 + i].current(0)[...].astype(f32)
        for j in range(1, heads):
            arriving[i, j].wait_recv()
            total = total + zbox[j - 1].astype(f32)
        return total

    d_keys = whole(0, zbox_k)
    d_lin, d_gain_k = back_norm(
        k_lin_ref[...], gain_k, back_rotate(d_keys, cosines, sines)
    )
    qw = qcount * width
    d_qkv[:, pl.ds(qw, width)] = d_lin.astype(bf16)
    d_values = whole(1, zbox_v)
    d_qkv[:, pl.ds(qw + width, width)] = d_values.astype(bf16)

    pieces, _, block_rows, cut = dw_qkv.shape
    load_a.wait()
    qkv = []
    for j in range(pieces):
        cols = pl.ds(j * cut, cut)

        def qkv_block(g, carry, j=j, cols=cols):
            dw_qkv[j, g] = jnp.dot(
                attn_t_ref[g], d_qkv[:, cols], preferred_element_type=f32
            ).astype(bf16)
            return carry

        lax.fori_loop(0, nseq, qkv_block, 0)
        total = Sum(
            links,
            lambda m, j=j: dw_qkv.at[j, related(s, m)],
            box_qkv.at[j],
            [0] + (downs if j % 2 else ups),
        )
        total.start()
        qkv.append(total)

    for copy in load_w + [load_x, load_d]:
        copy.wait()
    d_attn_in = contract_last(d_qkv[...], w_qkv_ref[...])
    in_turn(*[total.steps(0) for total in qkv])
    d_x, d_gain_in = back_norm(x_ref[...].astype(f32), flat(gain_in_ref), d_attn_in)
    o_tokens[...] = (d_hid_ref[...] + d_x).astype(o_tokens.dtype)

    gsum[0] = gains_ref[...]
    gsum[0, 0:1, :] = d_gain_in
    gsum[0, 4:5, :width] = d_gain_q
    gsum[0, 5:6, :width] = d_gain_k
    gain_copy = links.go(gsum.at[0], gbox.at[0], links.across(0))
    for stage in range(1, bits - 1):
        in_turn(*[total.steps(stage) for total in qkv])
    gain_copy.wait_recv()
    gsum[1] = gsum[0] + gbox[0]
    gain_plane = [
        links.go(gsum.at[1], gbox.at[1 + i], (related(s, m), h)) for i, m in enumerate(plane)
    ]
    in_turn(sum_end.steps(0))
    settle(up, 1)
    each = block_rows // heads
    z_qkv = []

    for j, total in enumerate(qkv):
        value = total.last()
        for p in range(heads):
            zsrc_qkv[j, p] = value[p * each : (p + 1) * each].astype(bf16)
        z_qkv.append(links.over_heads(zsrc_qkv.at[j], zbox_qkv.at[j]))
    total_gains = gsum[1]
    for i, copy in enumerate(gain_plane):
        copy.wait_recv()
        total_gains = total_gains + gbox[1 + i]
    gsum[2] = total_gains
    gain_z = [
        links.go(gsum.at[2], gzbox.at[d], (s, o)) for d, o in enumerate(links.others)
    ]
    for total in down:
        for copy in total.loads:
            copy.wait()
    put(down, o_down, True)
    put(gate, o_gate)
    put(up, o_up)
    o_out[...] = sum_end.last()
    for j, copies in enumerate(z_qkv):
        total = zsrc_qkv[j, h].astype(f32)
        for d, copy in enumerate(copies):
            copy.wait_recv()
            total = total + zbox_qkv[j, d].astype(f32)
        o_qkv[:, pl.ds(j * cut, cut)] = total
    total = gsum[2]
    for d, copy in enumerate(gain_z):
        copy.wait_recv()
        total = total + gzbox[d]
    o_gains[...] = total
    links.finish()


def tail(nseq, heads, qcount, scale, cid, *arrays):
    (q, _, _, _, att, d_proj, k_lin, _, _, gain_q, _, _, gains, k, v) = arrays[:15]
    (w_out, q_lin, attn_t, x, d_hid, w_query, w_key, w_value, d_gate, _, _, _) = arrays[15:]
    f32, bf16 = jnp.float32, jnp.bfloat16
    rows, model = d_proj.shape
    width = k_lin.shape[1]
    cols = w_query.shape[1] + w_key.shape[1] + w_value.shape[1]
    pieces = 4
    cut = cols // pieces
    out_rows, qkv_rows = w_out.shape[0] // nseq, attn_t.shape[1]
    ffn_block = d_gate.shape[1:]
    some, all_but = nseq // 2, nseq - 1
    out_block = (heads, out_rows // heads, model)
    split = split_rows(ffn_block[0])
    low, high = (split, ffn_block[1]), (ffn_block[0] - split, ffn_block[1])
    parts = [(part, *n) for n in ((2, 3), (4, 7), (1, 1)) for part in (low, high)]
    copies = (
        sum(n for _, _, n in parts)
        + some
        + (heads - 1)
        + (some - 1)
        + 2 * heads * all_but
        + 2 * (heads - 1)
        + pieces * (all_but + heads - 1)
        + some
        + (heads - 1)
    )
    vm = pl.BlockSpec(memory_space=VMEM)
    anywhere = pl.BlockSpec(memory_space=pl.ANY)

    def kernel(*refs):
        tail_kernel(nseq, heads, qcount, scale, *refs)

    return pl.pallas_call(
        kernel,
        out_shape=[
            jax.ShapeDtypeStruct((rows, model), bf16),
            jax.ShapeDtypeStruct((qkv_rows // heads, cols), f32),
            jax.ShapeDtypeStruct(out_block[1:], f32),
            jax.ShapeDtypeStruct(ffn_block, bf16),
            jax.ShapeDtypeStruct(ffn_block, bf16),
            jax.ShapeDtypeStruct(ffn_block, bf16),
            jax.ShapeDtypeStruct(gains.shape, f32),
        ],
        in_specs=[vm] * 13 + [anywhere] * 14,
        out_specs=[vm] * 7,
        scratch_shapes=[
            VMEM(k.shape, bf16),
            VMEM(v.shape, bf16),
            *[VMEM(a.shape, a.dtype) for a in (w_out, q_lin, attn_t, x, d_hid)],
            VMEM((model, cols), bf16),
            VMEM((nseq, heads, rows, width), bf16),
            VMEM((nseq, heads, rows, width), bf16),
            VMEM((width, qcount * rows), f32),
            VMEM((qcount * rows, width), bf16),
            VMEM((width, qcount * rows), bf16),
            VMEM((heads, all_but, rows, width), bf16),
            VMEM((heads, all_but, rows, width), bf16),
            VMEM((heads - 1, rows, width), bf16),
            VMEM((heads - 1, rows, width), bf16),
            VMEM((nseq,) + out_block, bf16),
            VMEM((some,) + out_block, bf16),
            VMEM((heads - 1, some) + out_block[1:], bf16),
            VMEM((some,) + out_block[1:], bf16),
            VMEM((some - 1,) + out_block[1:], bf16),
            VMEM((pieces, nseq, qkv_rows, cut), bf16),
            VMEM((pieces, all_but, qkv_rows, cut), bf16),
            VMEM((pieces, heads, qkv_rows // heads, cut), bf16),
            VMEM((pieces, heads - 1, qkv_rows // heads, cut), bf16),
            VMEM((rows, cols), bf16),
        ]
        + [VMEM((n,) + part, bf16) for part, n, _ in parts]
        + [VMEM((n,) + part, bf16) for part, _, n in parts]
        + [
            VMEM((3,) + gains.shape, f32),
            VMEM((some,) + gains.shape, f32),
            VMEM((heads - 1,) + gains.shape, f32),
            pltpu.SemaphoreType.DMA((copies,)),
            pltpu.SemaphoreType.DMA((copies,)),
            pltpu.SemaphoreType.DMA((10 + sum(n for _, n, _ in parts),)),
        ],
        name="tail",
        compiler_params=pltpu.CompilerParams(
            collective_id=cid, has_side_effects=True, vmem_limit_bytes=62 * 2**20
        ),
    )(*arrays)


CHUNKS, SPANS = 4, 2
ORDER = (
    ("ags", 0, 0, 0), ("ags", 0, 1, 0), ("agw", 0, 0, 0), ("ags", 0, 0, 1), ("agw", 0, 1, 0),
    ("ags", 0, 1, 1), ("agw", 0, 0, 1), ("ags", 0, 0, 2), ("agw", 0, 1, 1), ("ags", 0, 1, 2),
    ("ags", 0, 3, 0), ("ags", 0, 2, 0), ("agw", 0, 1, 2), ("agw", 0, 0, 2), ("fa", 0), ("fb", 0),
    ("agw", 0, 3, 0), ("ags", 0, 3, 1), ("agw", 0, 2, 0), ("ags", 0, 2, 1), ("fc", 0),
    ("agw", 0, 3, 1), ("ags", 0, 3, 2), ("rss", 0, 0, 0), ("agw", 0, 2, 1), ("ags", 0, 2, 2),
    ("rsw", 0, 0, 0), ("rss", 0, 1, 0), ("rss", 0, 0, 1), ("rsw", 0, 1, 0), ("rss", 0, 1, 1),
    ("agw", 0, 3, 2), ("agw", 0, 2, 2), ("fa", 1), ("rsw", 0, 0, 1), ("rss", 0, 0, 2), ("fb", 1),
    ("rsw", 0, 1, 1), ("rss", 0, 1, 2), ("fc", 1), ("rss", 0, 2, 0), ("rsw", 0, 0, 2), ("n", 0),
    ("ags", 1, 0, 0), ("rss", 0, 3, 0), ("rsw", 0, 1, 2), ("rsw", 0, 2, 0), ("n", 1),
    ("rss", 0, 2, 1), ("ags", 1, 1, 0), ("agw", 1, 0, 0), ("rsw", 0, 3, 0), ("ags", 1, 0, 1),
    ("rss", 0, 3, 1), ("rsw", 0, 2, 1), ("rss", 0, 2, 2), ("agw", 1, 1, 0), ("ags", 1, 1, 1),
    ("agw", 1, 0, 1), ("ags", 1, 0, 2), ("rsw", 0, 3, 1), ("rss", 0, 3, 2), ("rsw", 0, 2, 2),
    ("n", 2), ("ags", 1, 2, 0), ("agw", 1, 1, 1), ("ags", 1, 1, 2), ("rsw", 0, 3, 2), ("n", 3),
    ("ags", 1, 3, 0), ("agw", 1, 0, 2), ("agw", 1, 2, 0), ("ags", 1, 2, 1), ("agw", 1, 1, 2),
    ("ga", 0), ("gb", 0), ("agw", 1, 3, 0), ("ags", 1, 3, 1), ("gc", 0), ("rss", 1, 1, 0),
    ("agw", 1, 2, 1), ("ags", 1, 2, 2), ("rss", 1, 0, 0), ("agw", 1, 3, 1), ("ags", 1, 3, 2),
    ("rsw", 1, 1, 0), ("rss", 1, 1, 1), ("agw", 1, 2, 2), ("agw", 1, 3, 2), ("wd", 0), ("wd", 1),
    ("dd", 0), ("rsw", 1, 0, 0), ("rsw", 1, 1, 1), ("rss", 1, 0, 1), ("rss", 1, 1, 2), ("ga", 1),
    ("gb", 1), ("gc", 1), ("rss", 1, 2, 0), ("Dd", 0), ("rsw", 1, 0, 1), ("rsw", 1, 1, 2),
    ("rss", 1, 3, 0), ("rss", 1, 0, 2), ("wg", 0), ("rsw", 1, 2, 0), ("e", 1), ("rss", 1, 2, 1),
    ("wg", 1), ("dg", 0), ("rsw", 1, 3, 0), ("rss", 1, 3, 1), ("rsw", 1, 0, 2), ("e", 0),
    ("rsw", 1, 2, 1), ("rss", 1, 2, 2), ("wu", 0), ("rsw", 1, 3, 1), ("rss", 1, 3, 2), ("wu", 1),
    ("rsw", 1, 2, 2), ("e", 2), ("Dg", 0), ("rsw", 1, 3, 2), ("e", 3), ("D2", 0),
)


def ffn_kernel(
    nseq,
    heads,
    chunks,
    spans,
    proj_ref,
    x_ref,
    cot_ref,
    gain_two_ref,
    gain_three_ref,
    gain_four_ref,
    w_gate_ref,
    w_up_ref,
    w_down_ref,
    o_out,
    o_hid,
    o_proj,
    o_gains,
    o_first,
    o_second,
    o_gate,
    o_up,
    hidden,
    w_gate,
    w_up,
    w_down,
    u_all,
    d_all,
    by_gate,
    by_up,
    act,
    d_gate,
    d_up,
    parts,
    from_left,
    from_right,
    flipped,
    dw_gate,
    dw_up,
    dw_down,
    box_gate,
    box_down,
    box_first,
    box_second,
    sum_send,
    sum_recv,
    ag_send,
    ag_recv,
    rs_send,
    rs_recv,
    local_sem,
):
    f32, bf16 = jnp.float32, jnp.bfloat16
    s, h = place()
    last = heads - 1
    right = (s, lax.rem(h + 1, heads))
    left = (s, lax.rem(h + last, heads))
    rows, model = x_ref.shape
    units = w_gate.shape[0]
    rc = rows // chunks
    each = chunks // spans
    many = rc * heads * each

    loads = []
    for n, (src, dst) in enumerate(
        ((w_gate_ref, w_gate), (w_up_ref, w_up), (w_down_ref, w_down))
    ):
        copy = pltpu.make_async_copy(src, dst, local_sem.at[n])
        copy.start()
        loads.append(copy)
    bits = nseq.bit_length() - 1
    ups, downs = seq_orders(bits)
    links = Links(nseq, heads, sum_send, sum_recv)
    greet([right, left] + [links.across(b) for b in range(bits)])

    proj = proj_ref[...]
    hid = x_ref[...].astype(f32) + norm_rows(proj, flat(gain_two_ref))
    hidden[...] = hid
    u_local = norm_rows(hid, flat(gain_three_ref)).astype(bf16)
    for c in range(chunks):
        u_all[c, h] = u_local[c * rc : (c + 1) * rc]
    o_gains[...] = jnp.zeros_like(o_gains)

    def lanes(k, c, t):
        buf = d_all if k else u_all
        return (
            (
                (h - t >= 0) & (h < last),
                buf.at[c, jnp.maximum(h - t, 0)],
                0,
                right,
                h - 1 - t >= 0,
                buf.at[c, jnp.maximum(h - 1 - t, 0)],
            ),
            (
                (h + t <= last) & (h > 0),
                buf.at[c, jnp.minimum(h + t, last)],
                1,
                left,
                h + 1 + t <= last,
                buf.at[c, jnp.minimum(h + 1 + t, last)],
            ),
        )

    def ags(k, c, t):
        for on, block, lane, target, _, _ in lanes(k, c, t):
            i = (k, c, lane, t)
            pl.when(on)(remote(block, block, ag_send.at[i], ag_recv.at[i], target).start)

    def agw(k, c, t):
        for _, _, lane, target, on, block in lanes(k, c, t):
            i = (k, c, lane, t)
            pl.when(on)(remote(block, block, ag_send.at[i], ag_recv.at[i], target).wait_recv)

    def rss(k, c, t):
        for on, dest, box, lane, target, at_end in (
            ((t >= h) & (h < last), last - (t - h), from_left, 0, right, h == 0),
            ((t >= last - h) & (h > 0), t - (last - h), from_right, 1, left, h == last),
        ):
            dest = jnp.clip(dest, 0, last)
            i = (k, c, lane, t)
            if t > 0:

                def forward(box=box, dest=dest, i=i, target=target):
                    box[k, c, t - 1] = box[k, c, t - 1] + parts[k, c, dest]
                    remote(
                        box.at[k, c, t - 1], box.at[k, c, t], rs_send.at[i], rs_recv.at[i], target
                    ).start()

                pl.when(on & jnp.logical_not(at_end))(forward)
            pl.when(on & at_end)(
                remote(
                    parts.at[k, c, dest], box.at[k, c, t], rs_send.at[i], rs_recv.at[i], target
                ).start
            )

    def rsw(k, c, t):
        for on, box, lane, target in (
            ((t >= h - 1) & (h > 0), from_left, 0, right),
            ((t >= last - h - 1) & (h < last), from_right, 1, left),
        ):
            i = (k, c, lane, t)
            block = box.at[k, c, t]
            pl.when(on)(remote(block, block, rs_send.at[i], rs_recv.at[i], target).wait_recv)

    def summed(k, c):
        zero = jnp.zeros((rc, model), f32)
        return (
            parts[k, c, h].astype(f32)
            + jnp.where(h > 0, from_left[k, c, last - 1].astype(f32), zero)
            + jnp.where(h < last, from_right[k, c, last - 1].astype(f32), zero)
        )

    def over_tiles(second, body, tile):
        whole_tiles, rest = units // tile, units % tile
        middle = (whole_tiles + 1) // 2

        def step(i, carry):
            body(pl.ds(pl.multiple_of(i * tile, tile), tile))
            return carry

        lax.fori_loop(middle if second else 0, whole_tiles if second else middle, step, 0)
        if second and rest:
            body(pl.ds(whole_tiles * tile, rest))

    arrived = set()

    def need(n):
        if n not in arrived:
            arrived.add(n)
            loads[n].wait()

    def span_rows(buf, p):
        return buf[pl.ds(p * each, each)].reshape(many, model)

    def place_parts(k, p, cols, value):
        parts[k, pl.ds(p * each, each), :, :, cols] = value.astype(bf16).reshape(
            each, heads, rc, value.shape[1]
        )

    def forward_tiles(c, second):
        need(0)
        need(1)

        def body(cols):
            u = span_rows(u_all, c)
            gate = contract_last(u, w_gate[cols, :])
            up = contract_last(u, w_up[cols, :])
            root = math.sqrt(2.0 / math.pi)
            square = gate * gate
            curve = jnp.tanh(root * gate * (1.0 + 0.044715 * square))
            half = 0.5 * (1.0 + curve)
            gelu = gate * half
            slope = half + 0.5 * gate * (1.0 - curve * curve) * (
                root * (1.0 + 3 * 0.044715 * square)
            )
            by_gate[pl.ds(c * many, many), cols] = slope * up
            by_up[pl.ds(c * many, many), cols] = gelu
            act[pl.ds(c * many, many), cols] = (gelu * up).astype(bf16)

        over_tiles(second, body, 512)

    wide = (model // 2 + 127) // 128 * 128

    def over_columns(body):
        body(pl.ds(0, wide))
        body(pl.ds(wide, model - wide))

    def down_rows(c):
        need(2)

        def body(cols):
            place_parts(
                0,
                c,
                cols,
                jnp.dot(
                    act[pl.ds(c * many, many), :], w_down[:, cols], preferred_element_type=f32
                ),
            )

        over_columns(body)

    def turn(c):
        here = pl.ds(c * rc, rc)
        ffn_out = summed(0, c)
        upstream = cot_ref[here, :].astype(f32)
        o_out[here, :] = (hidden[here, :] + norm_rows(ffn_out, flat(gain_four_ref))).astype(
            o_out.dtype
        )
        d_out, terms = back_norm(ffn_out, flat(gain_four_ref), upstream)
        d_all[c, h] = d_out.astype(bf16)
        o_gains[3:4, :] += terms

    def back_tiles(c, second):
        def body(cols):
            d_act = contract_last(span_rows(d_all, c), w_down[cols, :])
            d_gate[pl.ds(c * many, many), cols] = (
                d_act * by_gate[pl.ds(c * many, many), cols]
            ).astype(bf16)
            d_up[pl.ds(c * many, many), cols] = (
                d_act * by_up[pl.ds(c * many, many), cols]
            ).astype(bf16)

        over_tiles(second, body, 512)

    def back_rows(c):
        def body(cols):
            part = jnp.dot(
                d_gate[pl.ds(c * many, many), :], w_gate[:, cols], preferred_element_type=f32
            )
            part = part + jnp.dot(
                d_up[pl.ds(c * many, many), :], w_up[:, cols], preferred_element_type=f32
            )
            place_parts(1, c, cols, part)

        over_columns(body)

    def finish_rows(c):
        here = pl.ds(c * rc, rc)
        d_in, terms = back_norm(hidden[here, :], flat(gain_three_ref), summed(1, c))
        o_gains[2:3, :] += terms
        d_hid = cot_ref[here, :].astype(f32) + d_in
        o_hid[here, :] = d_hid
        d_proj, terms = back_norm(proj_ref[here, :], flat(gain_two_ref), d_hid)
        o_proj[here, :] = d_proj.astype(o_proj.dtype)
        o_gains[1:2, :] += terms

    stores = []

    def flip(source):
        for p in range(spans):
            flipped[:, pl.ds(p * many, many)] = span_rows(source, p).T

    def weight_grad(right_ref, dst, half):
        def body(cols):
            value = jnp.dot(flipped[...], right_ref[:, cols], preferred_element_type=f32)
            dst[:, :, cols] = value.astype(bf16).reshape(dst.shape[:2] + (value.shape[1],))

        over_tiles(half, body, 512)

    held = subsets(ups)
    sum_gate = Sum(links, lambda m: dw_gate.at[related(s, m)], box_gate, [0])
    sum_down = Sum(links, lambda m: dw_down.at[related(s, m)], box_down, [0])
    for total in (sum_gate, sum_down):
        total.masks = lambda stage: held
    def store(src, dst):
        copy = pltpu.make_async_copy(src, dst, local_sem.at[3 + len(stores)])
        copy.start()
        stores.append(copy)

    split = box_first.shape[1]
    pieces = []
    for box, order, low in ((box_first, ups, 0), (box_second, downs, split)):
        here = pl.ds(low, box.shape[1])
        pieces.append(
            Sum(links, lambda m, here=here: box_down.at[held.index(m), here], box, order)
        )

    for event in ORDER:
        kind, args = event[0], event[1:]
        if kind == "ags":
            ags(*args)
        elif kind == "agw":
            agw(*args)
        elif kind == "rss":
            rss(*args)
        elif kind == "rsw":
            rsw(*args)
        elif kind == "fa":
            forward_tiles(args[0], False)
        elif kind == "fb":
            forward_tiles(args[0], True)
        elif kind == "fc":
            down_rows(args[0])
        elif kind == "n":
            turn(args[0])
        elif kind == "ga":
            back_tiles(args[0], False)
        elif kind == "gb":
            back_tiles(args[0], True)
        elif kind == "gc":
            back_rows(args[0])
        elif kind == "e":
            finish_rows(args[0])
        elif kind == "wd":
            if args[0] == 0:
                flip(d_all)
            weight_grad(act, dw_down, args[0])
        elif kind == "wg":
            if args[0] == 0:
                flip(u_all)
            weight_grad(d_gate, dw_gate, args[0])
        elif kind == "wu":
            weight_grad(d_up, dw_up, args[0])
            if args[0] == 1:
                store(dw_up, o_up)
        elif kind == "dd":
            sum_down.start()
        elif kind == "dg":
            sum_gate.start()
        elif kind == "Dg":
            in_turn(sum_gate.steps(0))
            store(box_gate, o_gate)
        elif kind == "Dd":
            in_turn(sum_down.steps(0))
            for total in pieces:
                for m in total.masks(0):
                    total.send(0, m)
        else:
            for total, out in zip(pieces, (o_first, o_second)):
                for m in total.masks(0):
                    copy, where = total.waiting.pop((0, m))
                    copy.wait_recv()
                    total.boxes[where] = total.boxes[where] + total.current(m)[...]
                store(total.boxes, out)

    for event in ORDER:
        if event[0] == "ags":
            k, c, t = event[1:]
            for on, block, lane, target, _, _ in lanes(k, c, t):
                i = (k, c, lane, t)
                pl.when(on)(remote(block, block, ag_send.at[i], ag_recv.at[i], target).wait_send)
        elif event[0] == "rss":
            k, c, t = event[1:]
            for on, box, lane, target in (
                ((t >= h) & (h < last), from_left, 0, right),
                ((t >= last - h) & (h > 0), from_right, 1, left),
            ):
                i = (k, c, lane, t)
                block = box.at[k, c, t]
                pl.when(on)(remote(block, block, rs_send.at[i], rs_recv.at[i], target).wait_send)
    for n in range(3):
        need(n)
    for copy in stores:
        copy.wait()
    links.finish()


def feed_forward(nseq, heads, cid, *arrays):
    _, x, _, _, _, _, w_gate, w_up, w_down = arrays
    f32, bf16 = jnp.float32, jnp.bfloat16
    rows, model = x.shape
    units = w_gate.shape[0]
    chunks = CHUNKS
    rc = rows // chunks
    group = rows * heads
    vm = pl.BlockSpec(memory_space=VMEM)
    anywhere = pl.BlockSpec(memory_space=pl.ANY)
    block = (model // nseq, units)
    some = nseq // 2
    half = jax.ShapeDtypeStruct((some,) + block, bf16)
    split = split_rows(block[0])
    parts = [(split, units), (block[0] - split, units)]
    messages = 3 * some
    hops = (2, chunks, 2, heads - 1)
    return pl.pallas_call(
        functools.partial(ffn_kernel, nseq, heads, CHUNKS, SPANS),
        out_shape=[
            jax.ShapeDtypeStruct((rows, model), bf16),
            jax.ShapeDtypeStruct((rows, model), f32),
            jax.ShapeDtypeStruct((rows, model), bf16),
            jax.ShapeDtypeStruct((8, model), f32),
            *[jax.ShapeDtypeStruct((some // 2,) + part, bf16) for part in parts],
            half,
            jax.ShapeDtypeStruct((nseq,) + block, bf16),
        ],
        in_specs=[vm] * 6 + [anywhere] * 3,
        out_specs=[vm] * 4 + [anywhere] * 4,
        scratch_shapes=[
            VMEM((rows, model), f32),
            VMEM(w_gate.shape, bf16),
            VMEM(w_up.shape, bf16),
            VMEM(w_down.shape, bf16),
            VMEM((chunks, heads, rc, model), bf16),
            VMEM((chunks, heads, rc, model), bf16),
            VMEM((group, units), f32),
            VMEM((group, units), f32),
            VMEM((group, units), bf16),
            VMEM((group, units), bf16),
            VMEM((group, units), bf16),
            VMEM((2, chunks, heads, rc, model), bf16),
            VMEM((2, chunks, heads - 1, rc, model), bf16),
            VMEM((2, chunks, heads - 1, rc, model), bf16),
            VMEM((model, group), bf16),
            VMEM((nseq,) + block, bf16),
            VMEM((nseq,) + block, bf16),
            VMEM((nseq,) + block, bf16),
            VMEM((some,) + block, bf16),
            VMEM((some,) + block, bf16),
            *[VMEM((some // 2,) + part, bf16) for part in parts],
            pltpu.SemaphoreType.DMA((messages,)),
            pltpu.SemaphoreType.DMA((messages,)),
            pltpu.SemaphoreType.DMA(hops),
            pltpu.SemaphoreType.DMA(hops),
            pltpu.SemaphoreType.DMA(hops),
            pltpu.SemaphoreType.DMA(hops),
            pltpu.SemaphoreType.DMA((7,)),
        ],
        name="feed_forward",
        compiler_params=pltpu.CompilerParams(
            collective_id=cid, has_side_effects=True, vmem_limit_bytes=62 * 2**20
        ),
    )(*arrays)


def finish_kernel(nseq, qw, width, each, few, *refs):
    out, tokens, qkv, w_out, gate, up, down, gains = refs[:8]
    o_out, o_tokens, o_query, o_key, o_value, o_w_out, o_gate, o_up, o_down = refs[8:17]
    o_gains = refs[17:]
    s, h = place()
    which = s * lax.axis_size("head") + h
    o_out[...] = out[...]
    o_tokens[...] = tokens[...]
    o_query[...] = qkv[:, :qw]
    o_key[...] = qkv[:, qw : qw + width]
    o_value[...] = qkv[:, qw + width :]
    o_w_out[...] = w_out[...]
    o_gate[...] = gate[...].astype(jnp.float32)
    o_up[...] = up[...].astype(jnp.float32)
    o_down[...] = down[...].astype(jnp.float32)
    model = gains.shape[1]
    wide = pltpu.roll(gains[...], lax.rem(model - which * each, model), 1)
    narrow = pltpu.roll(gains[...], lax.rem(model - which * few, model), 1)
    for i in range(4):
        o_gains[i][...] = wide[i : i + 1, :each]
    for i in range(4, 6):
        o_gains[i][...] = narrow[i : i + 1, :few]


def finish(nseq, qw, width, each, few, *arrays):
    out, tokens, qkv, w_out, gate, up, down, gains = arrays
    vm = pl.BlockSpec(memory_space=VMEM)
    shape = lambda a: jax.ShapeDtypeStruct(a.shape, a.dtype)
    f32 = jnp.float32
    rows = qkv.shape[0]
    wide, narrow = jax.ShapeDtypeStruct((1, each), f32), jax.ShapeDtypeStruct((1, few), f32)
    return pl.pallas_call(
        functools.partial(finish_kernel, nseq, qw, width, each, few),
        out_shape=[shape(out), shape(tokens)]
        + [jax.ShapeDtypeStruct((rows, n), f32) for n in (qw, width, width)]
        + [jax.ShapeDtypeStruct(a.shape, f32) for a in (w_out, gate, up, down)]
        + [wide] * 4
        + [narrow] * 2,
        in_specs=[vm] * 8,
        out_specs=[vm] * 15,
        name="finish",
        compiler_params=pltpu.CompilerParams(vmem_limit_bytes=LIMIT),
    )(*arrays)


def local(
    tokens,
    segment_ids,
    w_query,
    w_key,
    w_value,
    w_out,
    w_gate,
    w_up,
    w_down,
    gain_attn_in,
    gain_attn_out,
    gain_ffn_in,
    gain_ffn_out,
    gain_query,
    gain_key,
    cotangent,
):
    heads = lax.axis_size("head")
    nseq = lax.axis_size("seq")
    head_index = lax.axis_index("head")
    seq_index = lax.axis_index("seq")
    bits = nseq.bit_length() - 1
    local_rows, model = tokens.shape
    width = gain_query.shape[0]
    qcount = w_query.shape[1] // width
    group = local_rows * heads
    total = segment_ids.shape[0]
    hidden_units = w_gate.shape[1]
    scale = 1.0 / math.sqrt(width)
    bf16 = jnp.bfloat16
    if (nseq, heads) == (8, 4) and (model // nseq) % 16 == 0:
        qw = qcount * width
        each, few = model // (nseq * heads), width // (nseq * heads)
        (
            projected,
            queries,
            keys,
            values,
            starts,
            index,
            log_total,
            attended_t,
            q_linear,
            k_linear,
            cosines,
            sines,
            attn_t,
        ) = front(
            nseq,
            heads,
            qcount,
            scale,
            11,
            tokens,
            segment_ids,
            w_key,
            w_value,
            gain_attn_in,
            gain_query,
            gain_key,
            w_query,
            w_out,
        )
        output, d_hidden, d_projected, gains, down_first, down_second, half_gate, all_up = feed_forward(
            nseq,
            heads,
            10,
            projected,
            tokens,
            cotangent,
            gain_attn_out,
            gain_ffn_in,
            gain_ffn_out,
            w_gate.T,
            w_up.T,
            w_down,
        )
        grad_tokens, sum_qkv, sum_out, sum_gate, sum_up, sum_down, sum_gains = tail(
            nseq,
            heads,
            qcount,
            scale,
            9,
            queries,
            starts,
            index,
            log_total,
            attended_t,
            d_projected,
            k_linear,
            cosines,
            sines,
            gain_query,
            gain_key,
            gain_attn_in,
            gains,
            keys.reshape(nseq, group, width),
            values.reshape(nseq, group, width),
            w_out,
            q_linear,
            attn_t,
            tokens,
            d_hidden,
            w_query,
            w_key,
            w_value,
            half_gate,
            all_up,
            down_first,
            down_second,
        )
        (
            output,
            grad_tokens,
            sum_query,
            sum_key,
            sum_value,
            sum_out,
            sum_gate,
            sum_up,
            sum_down,
            *sum_gains,
        ) = finish(
            nseq,
            qw,
            width,
            each,
            few,
            output,
            grad_tokens,
            sum_qkv,
            sum_out,
            sum_gate,
            sum_up,
            sum_down,
            sum_gains,
        )
        return (
            output,
            grad_tokens,
            sum_query,
            sum_key,
            sum_value,
            sum_out,
            sum_gate,
            sum_up,
            sum_down.T,
            *[g[0] for g in sum_gains],
        )
    first_row = (seq_index * heads + head_index) * local_rows
    my_index = first_row + jnp.arange(local_rows, dtype=jnp.int32)
    my_ids = lax.dynamic_slice_in_dim(segment_ids, first_row, local_rows)
    my_starts = jnp.min(
        jnp.where(
            my_ids[:, None] == segment_ids[None, :],
            jnp.arange(total, dtype=jnp.int32)[None, :],
            total,
        ),
        axis=1,
    )
    cosines, sines = rope_tables(my_index - my_starts, width)

    def query_path(linear, gain):
        shaped = linear.reshape(local_rows, qcount, width)
        turned = rotate(norm_rows(shaped, gain), cosines[:, None, :], sines[:, None, :])
        return turned.reshape(local_rows, qcount * width)

    def key_path(linear, gain):
        return rotate(norm_rows(linear, gain), cosines, sines)

    def gated(gate, up):
        return jax.nn.gelu(gate, approximate=True) * up

    def stacked(v):
        return v.reshape(local_rows, qcount, width).transpose(1, 0, 2).reshape(-1, width)

    def unstacked(v):
        return v.reshape(qcount, local_rows, width).transpose(1, 0, 2).reshape(local_rows, -1)

    inputs = tokens.astype(jnp.float32)
    attn_in = norm_rows(inputs, gain_attn_in).astype(bf16)
    k_linear = jnp.dot(attn_in, w_key, preferred_element_type=jnp.float32)
    keys_local = key_path(k_linear, gain_key).astype(bf16)
    values_local = jnp.dot(attn_in, w_value, preferred_element_type=jnp.float32).astype(bf16)
    q_linear = jnp.dot(attn_in, w_query, preferred_element_type=jnp.float32)
    queries_local = query_path(q_linear, gain_query).astype(bf16)
    queries = stacked(queries_local) * jnp.asarray(scale, bf16)
    keys, values = gather_all([keys_local, values_local], nseq, heads, 1)
    keys = keys.reshape(nseq, group, width)
    values = values.reshape(nseq, group, width)
    starts = jnp.tile(my_starts, qcount)[None, :]
    index = jnp.tile(my_index, qcount)[None, :]
    attended_t, log_total = attend(queries, keys, values, starts, index)
    attended = attended_t.T
    mixed_local = unstacked(attended.astype(bf16))
    projected = jnp.dot(mixed_local, w_out, preferred_element_type=jnp.float32)
    hidden = inputs + norm_rows(projected, gain_attn_out)
    ffn_in = norm_rows(hidden, gain_ffn_in).astype(bf16)
    ffn_rows = line_gather(ffn_in, heads, 2).reshape(group, model)
    gate = jnp.dot(ffn_rows, w_gate, preferred_element_type=jnp.float32)
    up = jnp.dot(ffn_rows, w_up, preferred_element_type=jnp.float32)
    activated = gated(gate, up).astype(bf16)
    ffn_out = line_scatter(
        jnp.dot(activated, w_down, preferred_element_type=jnp.float32)
        .astype(bf16)
        .reshape(heads, local_rows, model),
        heads,
        3,
    )
    output = hidden + norm_rows(ffn_out, gain_ffn_out)
    upstream = cotangent.astype(jnp.float32)
    unused, back_four = jax.vjp(norm_rows, ffn_out, gain_ffn_out)
    d_ffn_out, d_gain_four = back_four(upstream)
    d_ffn_rows = line_gather(d_ffn_out.astype(bf16), heads, 4).reshape(group, model)
    d_activated = contract_last(d_ffn_rows, w_down)
    d_w_down = contract_first(d_ffn_rows, activated)
    unused, back_gate = jax.vjp(gated, gate, up)
    d_gate, d_up = back_gate(d_activated)
    d_gate = d_gate.astype(bf16)
    d_up = d_up.astype(bf16)
    d_ffn_in = line_scatter(
        (contract_last(d_gate, w_gate) + contract_last(d_up, w_up))
        .astype(bf16)
        .reshape(heads, local_rows, model),
        heads,
        5,
    )
    d_w_gate = contract_first(ffn_rows, d_gate)
    d_w_up = contract_first(ffn_rows, d_up)
    unused, back_three = jax.vjp(norm_rows, hidden, gain_ffn_in)
    d_hidden_part, d_gain_three = back_three(d_ffn_in)
    d_hidden = upstream + d_hidden_part
    unused, back_two = jax.vjp(norm_rows, projected, gain_attn_out)
    d_projected, d_gain_two = back_two(d_hidden)
    d_projected = d_projected.astype(bf16)
    qw = qcount * width
    d_w_out = contract_first(mixed_local, d_projected)
    d_mixed = contract_last(d_projected, w_out).astype(bf16)
    grad_attended = stacked(d_mixed)
    row_dots = jnp.sum(grad_attended.astype(jnp.float32) * attended, axis=1)[None, :]
    d_queries_t, d_keys, d_values = attend_back(
        queries, keys, values, starts, index, log_total, row_dots, grad_attended
    )
    shape = (nseq, heads, local_rows, width)
    ups, downs = seq_orders(bits)
    d_keys, d_values = scatter_all(
        [d_keys.reshape(shape), d_values.reshape(shape)],
        [True, True],
        [[0] + ups, [0] + downs],
        nseq,
        heads,
        6,
        "scatter_keys",
    )
    d_query_rot = unstacked((d_queries_t.T * scale).astype(bf16)).astype(jnp.float32)
    unused, back_query = jax.vjp(query_path, q_linear, gain_query)
    d_q_linear, d_gain_query = back_query(d_query_rot)
    unused, back_key = jax.vjp(key_path, k_linear, gain_key)
    d_k_linear, d_gain_key = back_key(d_keys)
    d_qkv = jnp.concatenate([d_q_linear, d_k_linear, d_values], axis=1).astype(bf16)
    qw = qcount * width
    d_w_qkv = contract_first(attn_in, d_qkv)
    d_attn_in = (
        contract_last(d_qkv[:, :qw], w_query)
        + contract_last(d_qkv[:, qw : qw + width], w_key)
        + contract_last(d_qkv[:, qw + width :], w_value)
    )
    unused, back_one = jax.vjp(norm_rows, inputs, gain_attn_in)
    d_inputs, d_gain_one = back_one(d_attn_in)
    grad_tokens = (d_hidden + d_inputs).astype(bf16)

    def cut(v):
        return v.reshape(nseq, heads, -1)

    wide = jnp.stack([cut(d_gain_one), cut(d_gain_two), cut(d_gain_three), cut(d_gain_four)], 2)
    narrow = jnp.stack([cut(d_gain_query), cut(d_gain_key)], 2)
    each, few = wide.shape[-1], narrow.shape[-1]
    gains = jnp.concatenate(
        [
            jnp.pad(wide, ((0, 0), (0, 0), (0, 0), (0, 128 - each))),
            jnp.pad(narrow, ((0, 0), (0, 0), (0, 2), (0, 128 - few))),
        ],
        axis=2,
    )
    sum_qkv, sum_out, sum_gains = scatter_all(
        [
            d_w_qkv.astype(bf16).reshape(nseq, heads, -1, d_qkv.shape[1]),
            d_w_out.astype(bf16).reshape(nseq, heads, -1, model),
            gains,
        ],
        [True, True, True],
        [[0] + ups, [0] + downs, [0] + downs],
        nseq,
        heads,
        7,
        "scatter_attn",
    )
    sum_gate, sum_up, sum_down = scatter_all(
        [
            d.astype(bf16).reshape(nseq, model // nseq, hidden_units)
            for d in (d_w_gate, d_w_up, d_w_down)
        ],
        [False, False, False],
        [[0] + ups, [0] + downs, [0] + ups],
        nseq,
        heads,
        8,
        "scatter_ffn",
    )
    return (
        output.astype(bf16),
        grad_tokens,
        sum_qkv[:, :qw],
        sum_qkv[:, qw : qw + width],
        sum_qkv[:, qw + width :],
        sum_out,
        sum_gate,
        sum_up,
        sum_down.T,
        sum_gains[0, :each],
        sum_gains[1, :each],
        sum_gains[2, :each],
        sum_gains[3, :each],
        sum_gains[4, :few],
        sum_gains[5, :few],
    )


def solution(mesh):
    rows = P(("seq", "head"), None)
    in_specs = (
        rows,
        P(),
        P(),
        P(),
        P(),
        P(),
        P(None, "head"),
        P(None, "head"),
        P("head", None),
        P(),
        P(),
        P(),
        P(),
        P(),
        P(),
        rows,
    )
    out_specs = (
        rows,
        rows,
        rows,
        rows,
        rows,
        rows,
        P("seq", "head"),
        P("seq", "head"),
        P("head", "seq"),
    ) + (P(("seq", "head")),) * 6
    return jax.shard_map(local, mesh=mesh, in_specs=in_specs, out_specs=out_specs, check_vma=False)
```
